32 devices in a mesh: grp: 4 (over y, core), ep: 8 (over z, x).
Axes of the slice: x: 2, y: 2, z: 4, core: 2. Of those that a mesh axis runs over, the one named last changes fastest.
Arguments:
- hidden_in: bfloat16 [4096, 2048], P(('grp', 'ep')), may hold values from -6 to 6
- segments: int32 [4096], P('grp'), may hold values from 0 to 71, as said below
- routes: int32 [4096, 4], P('grp'), may hold values from 0 to 7, all different within a row; in each aligned block of 128 rows (0 to 127, 128 to 255, ...) at most 128 rows name the same one
- cotangent: bfloat16 [4096, 2048], P(('grp', 'ep')), may hold values from -6 to 6
- norm1_gain: float32 [2048], replicated, may hold values from 0.5 to 1.5
- w_qkv: bfloat16 [2048, 16, 384], P(None, 'ep'), may hold values from -0.125 to 0.125
- b_qkv: float32 [16, 384], P('ep'), may hold values from -1.75 to 1.75
- w_out: bfloat16 [16, 128, 2048], P('ep'), may hold values from -1 to 1
- norm2_gain: float32 [2048], replicated, may hold values from 0.5 to 1.5
- router: bfloat16 [2048, 8], replicated, may hold values from -0.0625 to 0.0625
- shared_gate_up: bfloat16 [2, 2048, 5632], P(None, None, 'ep'), may hold values from -0.125 to 0.125
- shared_down: bfloat16 [5632, 2048], P('ep'), may hold values from -0.15625 to 0.15625
- shared_gate: bfloat16 [2048], replicated, may hold values from -0.125 to 0.125
- expert_gate_up: bfloat16 [8, 2, 2048, 1408], P('ep'), may hold values from -0.125 to 0.125
- expert_down: bfloat16 [8, 1408, 2048], P('ep'), may hold values from -0.625 to 0.625
Outputs:
- layer_out: bfloat16 [4096, 2048], P(('grp', 'ep'))
- grad_x: float32 [4096, 2048], P(('grp', 'ep'))
- grad_norm1_gain: float32 [2048], replicated
- grad_w_qkv: float32 [2048, 16, 384], P('grp', 'ep')
- grad_b_qkv: float32 [16, 384], P('ep', 'grp')
- grad_w_out: float32 [16, 128, 2048], P('ep', None, 'grp')
- grad_norm2_gain: float32 [2048], replicated
- grad_router: float32 [2048, 8], replicated
- grad_shared_gate_up: float32 [2, 2048, 5632], P(None, 'grp', 'ep')
- grad_shared_down: float32 [5632, 2048], P('ep', 'grp')
- grad_shared_gate: float32 [2048], replicated
- grad_expert_gate_up: float32 [8, 2, 2048, 1408], P('ep', None, 'grp')
- grad_expert_down: float32 [8, 1408, 2048], P('ep', None, 'grp')
The draws below stay inside these ranges and needn't reach their ends.
Inputs may be any that keep to these rules, and one draw needn't show every extreme that they name: `routes`: each row names 4 different experts. In the rows of one device (aligned blocks of 128 rows) no expert is named by more than 128 rows, a bound that some block reaches of some device in every draw. `segments`: segment numbers never fall. Each sequence of 1024 tokens (those of one index of grp) begins a new document, and its first document has exactly 800 tokens; the others have 60 to 800, but the last of a sequence may be cut shorter. Sequence s numbers its last document (s + 1) * 18 - 1.
All inputs are finite; a program needn't handle non-finite values.
Results may differ from the reference program's by a relative error of at most 0.019.
Values may be sent and summed in bfloat16 or wider, within the bound.
A program may use at most 320 MiB of HBM per device.

```python
import math
import jax
import jax.numpy as jnp
import numpy as np
from jax import lax

D = 2048
H = 16
HD = 128
FFE = 1408
FS = 5632
TOP = 4
DOC_MAX = 800
DOC_MIN = 60
TOK_DEV = 128
SEQ = 1024
TOKENS = 4096
EXPERTS = 8
CAP = 128
N_EP = 8


def draw_segments(key, part):
    key = jax.random.fold_in(key, 7)
    seq_count = TOKENS // SEQ
    doc_slots = SEQ // DOC_MIN + 1
    doc_lengths = jax.random.randint(key, (seq_count, doc_slots), DOC_MIN, DOC_MAX + 1)
    doc_lengths = doc_lengths.at[:, 0].set(DOC_MAX)
    doc_ends = jnp.cumsum(doc_lengths, axis=1)
    position = jnp.arange(SEQ, dtype=jnp.int32)
    local_ids = jnp.sum((doc_ends[:, None, :] <= position[None, :, None]).astype(jnp.int32), -1)
    last_ids = local_ids[:, -1:]
    local_ids = jnp.where(local_ids == last_ids, doc_slots - 1, local_ids)
    offsets = jnp.arange(seq_count, dtype=jnp.int32)[:, None] * doc_slots
    return (local_ids + offsets).reshape(-1).astype(jnp.int32)


def block_scale(rng, dims, cuts, low, largest):
    level, own = 1.0, jax.random.fold_in(rng, 6)
    for dim, shards_of in cuts:
        heights = jnp.exp(jax.random.uniform(jax.random.fold_in(own, dim), (shards_of,), jnp.float32, low / len(cuts), largest / len(cuts)))
        level = level * jnp.repeat(heights, dims[dim] // shards_of).reshape([-1 if axis == dim else 1 for axis in range(len(dims))])
    return level


def routed_block(key, own, number, rows, count, top, reach, lean):
    order = jax.random.permutation(key, count)
    heavy_load, usual = portions_of(count, rows * top, reach, lean, True), portions_of(count, rows * top, reach, lean, False)
    places = jnp.arange(count)

    def named(lengths, rotation):
        used = int((lengths > 0).sum())
        fixed = max(1, used // 4)
        shifted = fixed + (places - fixed + rotation * (used - fixed)) % max(1, count - fixed)
        return jnp.zeros((count,), jnp.int32).at[order[jnp.where(places < fixed, places, shifted)]].set(jnp.asarray(lengths, jnp.int32))

    lengths = jnp.where(number % 4 == 0, named(heavy_load, number // 4), named(usual, number - number // 4 - 1))
    mixed = jax.random.permutation(jax.random.fold_in(own, 3), count)
    source_of, receiver = mixed[0:count // 2 * 2:2], mixed[1:count // 2 * 2:2]
    slack = jnp.minimum(lengths[source_of] - 1, reach - lengths[receiver]) // 2
    slack = jnp.where((source_of == order[0]) | (receiver == order[0]) | (lengths[receiver] == 0), 0, jnp.maximum(slack, 0))
    shifted = jax.random.randint(jax.random.fold_in(own, 4), (count // 2,), 0, 1 << 20) % (slack + 1)
    lengths = lengths.at[source_of].add(-shifted).at[receiver].add(shifted)
    labels = jnp.searchsorted(jnp.cumsum(lengths), jnp.arange(rows * top), side="right").astype(jnp.int32)
    listing = labels.reshape(top, rows).T
    listing = listing[jax.random.permutation(jax.random.fold_in(own, 1), rows)]
    rotation = jax.random.randint(jax.random.fold_in(own, 2), (rows, 1), 0, top)
    return jnp.take_along_axis(listing, (jnp.arange(top)[None, :] + rotation) % top, axis=1)


def portions_of(amount, total, reach, skew, full):
    loads = [(1 << 20) // math.isqrt(standing ** skew) + 1 for standing in range(1, amount + 1)]
    largest = reach if full else min(reach, max(-(-total // amount), total * loads[0] // sum(loads)))
    least = 1 if total - largest >= amount - 1 else 0
    given, rest = [largest] + [least] * (amount - 1), total - largest - least * (amount - 1)
    while rest > 0:
        free = [i for i in range(1, amount) if given[i] < largest] or [i for i in range(1, amount) if given[i] < reach]
        whole, left = sum([loads[i] for i in free]), rest
        for i in free:
            addition = min(reach - given[i], max(1, left * loads[i] // whole), rest)
            given[i] = given[i] + addition
            rest = rest - addition
    return np.array(given)


def noise(own_key, extent, deviation, reach, shards=(), held_as=jnp.bfloat16):
    level = block_scale(own_key, extent, shards, -0.22, 0.18) if shards else 1.0
    array = jax.random.normal(own_key, extent, jnp.float32) * deviation * level
    return jnp.minimum(jnp.maximum(array, -reach), reach).astype(held_as)


def setup_inputs(seed: int = 0) -> dict:
    seeds = jax.random.split(jax.random.key(seed), 16)
    hidden_in = noise(seeds[0], (TOKENS, D), 1.0, 6.0, ((0, 32),))
    segments = draw_segments(jax.random.fold_in(seeds[15], 71), 0)
    routes_keys = jax.random.split(jax.random.fold_in(seeds[2], 1), TOKENS // TOK_DEV)
    routes_turns = jax.random.permutation(jax.random.fold_in(seeds[2], 3), TOKENS // TOK_DEV)
    routes = jax.vmap(lambda own, number: routed_block(jax.random.fold_in(seeds[2], 2), own, number, TOK_DEV, EXPERTS, TOP, CAP, 2))(routes_keys, routes_turns).reshape((TOKENS, TOP))
    cotangent = noise(seeds[3], (TOKENS, D), 1.0, 6.0, ((0, 32),))
    norm1_gain = jnp.clip(1.0 + 0.1 * jax.random.normal(seeds[4], (D,), jnp.float32), 0.5, 1.5)
    w_qkv = noise(seeds[5], (D, H, 3 * HD), D ** -0.5, 0.125, ((1, 8),))
    b_qkv = noise(seeds[6], (H, 3 * HD), 0.3, 1.75, ((0, 8),), jnp.float32)
    w_out = noise(seeds[7], (H, HD, D), (H * HD // 64) ** -0.5, 1.0, ((0, 8),))
    norm2_gain = jnp.clip(1.0 + 0.1 * jax.random.normal(seeds[8], (D,), jnp.float32), 0.5, 1.5)
    router = noise(seeds[9], (D, EXPERTS), (0.5 / D ** 0.5), 0.0625)
    shared_gate_up = noise(seeds[10], (2, D, FS), D ** -0.5, 0.125, ((2, 8),))
    shared_down = noise(seeds[11], (FS, D), (FS // 4) ** -0.5, 0.15625, ((0, 8),))
    shared_gate = noise(seeds[12], (D,), D ** -0.5, 0.125)
    expert_gate_up = noise(seeds[13], (EXPERTS, 2, D, FFE), D ** -0.5, 0.125, ((0, 8),))
    expert_down = noise(seeds[14], (EXPERTS, FFE, D), (FFE // 16) ** -0.5, 0.625, ((0, 8),))
    return {"hidden_in": hidden_in, "segments": segments, "routes": routes, "cotangent": cotangent, "norm1_gain": norm1_gain, "w_qkv": w_qkv, "b_qkv": b_qkv, "w_out": w_out, "norm2_gain": norm2_gain, "router": router, "shared_gate_up": shared_gate_up, "shared_down": shared_down, "shared_gate": shared_gate, "expert_gate_up": expert_gate_up, "expert_down": expert_down}


EPS = 1e-06
THETA = 1000000.0
NEGATIVE = -1e+30
HIGHEST = lax.Precision.HIGHEST

@jax.custom_vjp
def low(v):
    return lax.optimization_barrier(v.astype(jnp.bfloat16)).astype(jnp.float32)

@jax.custom_vjp
def low_back(v):
    return v

def low_keep(v):
    return (low(v), None)

def low_pass(kept, grad):
    return (grad,)

def back_keep(v):
    return (v, None)

def back_low(kept, grad):
    return (low(grad),)
low.defvjp(low_keep, low_pass)
low_back.defvjp(back_keep, back_low)

def normalize(values, gain):
    return values * lax.rsqrt(lax.optimization_barrier(jnp.mean(values * values, -1, keepdims=True)) + EPS) * gain

def rope_tables(segment_ids, head_dim):
    token_count = segment_ids.shape[0]
    position = jnp.arange(token_count, dtype=jnp.int32)
    change = jnp.concatenate([jnp.ones((1,), dtype=bool), segment_ids[1:] != segment_ids[:-1]])
    starts = lax.cummax(jnp.where(change, position, 0), axis=0)
    offset = (position - starts).astype(jnp.float32)
    half_dim = head_dim // 2
    inverse = THETA ** (-2.0 * jnp.arange(half_dim, dtype=jnp.float32) / head_dim)
    angles = offset[:, None] * inverse[None, :]
    angles = jnp.concatenate([angles, angles], 1)
    return (jnp.cos(angles), jnp.sin(angles))

def rotate(values, cosine, sine):
    half_dim = values.shape[-1] // 2
    turned = jnp.concatenate([-values[..., half_dim:], values[..., :half_dim]], -1)
    return values * cosine[:, None, :] + turned * sine[:, None, :]

def attend(queries, key_rows, values, segment_ids):
    seq_length, head_count, head_dim = queries.shape
    block_rows = min(512, seq_length)
    block_count = seq_length // block_rows
    position = jnp.arange(seq_length, dtype=jnp.int32)
    score_scale = 1.0 / math.sqrt(head_dim)

    def one_block(pieces):
        query_block, segment_block, position_block = pieces
        scores = low_back(jnp.einsum('qhc,khc->hqk', query_block, key_rows, precision=HIGHEST) * score_scale)
        allowed = (segment_block[:, None] == segment_ids[None, :]) & (position[None, :] <= position_block[:, None])
        scores = jnp.where(allowed[None], scores, NEGATIVE)
        weights = low(jax.nn.softmax(scores, axis=-1))
        return jnp.einsum('hqk,khc->qhc', weights, values, precision=HIGHEST)
    result = lax.map(jax.checkpoint(one_block), (queries.reshape(block_count, block_rows, head_count, head_dim), segment_ids.reshape(block_count, block_rows), position.reshape(block_count, block_rows)))
    return result.reshape(seq_length, head_count, head_dim)

def layer(params, pieces):
    norm1_gain, w_qkv, b_qkv, w_out, norm2_gain, router, shared_gate_up, shared_down, shared_gate, expert_gate_up, expert_down = params
    tokens, segment_ids, cosine, sine, route_ids, route_place, slot_entry, slot_valid = pieces
    head_dim = w_out.shape[1]
    top_count = route_ids.shape[1]
    normed_one = low(normalize(tokens, norm1_gain))
    projected = low_back(jnp.einsum('td,dhc->thc', normed_one, w_qkv, precision=HIGHEST) + b_qkv)
    queries = low(rotate(projected[..., :head_dim], cosine, sine))
    key_rows = low(rotate(projected[..., head_dim:2 * head_dim], cosine, sine))
    values = low(projected[..., 2 * head_dim:])
    attended = low_back(low(attend(queries, key_rows, values, segment_ids)))
    attn_branch = low_back(jnp.einsum('thc,hcd->td', attended, w_out, precision=HIGHEST))
    residual = tokens + attn_branch
    normed_two = low(normalize(residual, norm2_gain))
    route_probs = jax.nn.softmax(jnp.dot(normed_two, router, precision=HIGHEST), axis=-1)
    gate_values = jnp.take_along_axis(route_probs, route_ids, 1)
    shared_weight = jax.nn.sigmoid(jnp.dot(normed_two, shared_gate, precision=HIGHEST))
    shared_pre = low_back(jnp.einsum('td,kdf->ktf', normed_two, shared_gate_up, precision=HIGHEST))
    shared_act = low(jax.nn.silu(shared_pre[0]) * shared_pre[1])
    shared_branch = low_back(jnp.dot(shared_act, shared_down, precision=HIGHEST))

    def one_expert(parts):
        gate_up, down_proj, entry_ids, entry_valid = parts
        expert_input = low_back(normed_two[entry_ids // top_count]) * entry_valid[:, None]
        expert_pre = low_back(jnp.einsum('rd,kdf->rkf', expert_input, gate_up, precision=HIGHEST))
        expert_act = low(jax.nn.silu(expert_pre[:, 0]) * expert_pre[:, 1])
        return low_back(low(jnp.dot(expert_act, down_proj, precision=HIGHEST)))
    expert_rows = lax.map(jax.checkpoint(one_expert), (expert_gate_up, expert_down, slot_entry, slot_valid))
    routed = expert_rows[route_ids.reshape(-1), route_place].reshape(route_ids.shape[0], top_count, -1)
    expert_branch = lax.optimization_barrier(jnp.sum(gate_values[..., None] * routed, 1))
    return residual + shared_weight[:, None] * shared_branch + expert_branch

def reference(hidden_in, segments, routes, cotangent, norm1_gain, w_qkv, b_qkv, w_out, norm2_gain, router, shared_gate_up, shared_down, shared_gate, expert_gate_up, expert_down):
    seq_count = TOKENS // SEQ
    cosine, sine = rope_tables(segments, HD)
    flat_routes = routes.reshape(seq_count, N_EP, TOK_DEV * TOP)
    one_hot = (flat_routes[..., None] == jnp.arange(EXPERTS, dtype=jnp.int32)).astype(jnp.int32)
    ranks = lax.optimization_barrier(jnp.sum(one_hot * (jnp.cumsum(one_hot, 2) - 1), -1))
    places = (jnp.arange(N_EP, dtype=jnp.int32)[None, :, None] * CAP + ranks).reshape(seq_count, SEQ * TOP).astype(jnp.int32)
    route_flat = routes.reshape(seq_count, SEQ * TOP)

    def slot_tables(route_row, place_row):
        entries = jnp.zeros((EXPERTS, N_EP * CAP), jnp.int32).at[route_row, place_row].set(jnp.arange(SEQ * TOP, dtype=jnp.int32))
        validity = jnp.zeros((EXPERTS, N_EP * CAP), jnp.float32).at[route_row, place_row].set(1.0)
        return (entries, validity)
    slot_entry, slot_valid = jax.vmap(slot_tables)(route_flat, places)

    def forward(hidden, *params):

        def one_sequence(pieces):
            return layer(params, pieces)
        return lax.map(jax.checkpoint(one_sequence), (hidden.reshape(seq_count, SEQ, D), segments.reshape(seq_count, SEQ), cosine.reshape(seq_count, SEQ, HD), sine.reshape(seq_count, SEQ, HD), routes.reshape(seq_count, SEQ, TOP), places, slot_entry, slot_valid))
    result, pull_back = jax.vjp(forward, hidden_in.astype(jnp.float32), norm1_gain.astype(jnp.float32), w_qkv.astype(jnp.float32), b_qkv.astype(jnp.float32), w_out.astype(jnp.float32), norm2_gain.astype(jnp.float32), router.astype(jnp.float32), shared_gate_up.astype(jnp.float32), shared_down.astype(jnp.float32), shared_gate.astype(jnp.float32), expert_gate_up.astype(jnp.float32), expert_down.astype(jnp.float32))
    grads = pull_back(cotangent.astype(jnp.float32).reshape(seq_count, SEQ, D))
    return (result.reshape(TOKENS, D).astype(jnp.bfloat16), grads[0].reshape(TOKENS, D), grads[1], grads[2], grads[3], grads[4], grads[5], grads[6], grads[7], grads[8], grads[9], grads[10], grads[11])
```

```python
import functools
import math

import jax
import jax.numpy as jnp
from jax import lax
from jax.experimental import pallas as pl
from jax.experimental.pallas import tpu as pltpu
from jax.sharding import PartitionSpec as P

EPS = 1e-06
THETA = 1000000.0
NEGATIVE = -1e30
BF16 = jnp.bfloat16
F32 = jnp.float32
LANES = 128
MIB = 1024 * 1024
KERNEL_COST = pl.CostEstimate(flops=10**6, bytes_accessed=10**5, transcendentals=0)


def dot(lhs, rhs):
    return jnp.dot(lhs, rhs, preferred_element_type=F32)


def dot_nt(lhs, rhs):
    return lax.dot_general(lhs, rhs, (((1,), (1,)), ((), ())), preferred_element_type=F32)


def dot_tn(lhs, rhs):
    return lax.dot_general(lhs, rhs, (((0,), (0,)), ((), ())), preferred_element_type=F32)


def tied(*arrays):
    return lax.optimization_barrier(arrays)


def sum_all(value, axes):
    for axis in axes:
        size = lax.axis_size(axis)
        step = 1
        while step < size:
            value = value + lax.ppermute(value, axis, [(i, i ^ step) for i in range(size)])
            step *= 2
    return value


class GrpReduce:
    def __init__(self, rows, produce):
        self.rows, self.produce = rows, produce
        self.size = lax.axis_size("grp")
        self.planes = self.size // 2
        mine = lax.axis_index("grp")
        self.core, self.plane = mine % 2, mine // 2
        self.far = [(self.plane + k) % self.planes for k in range(1, self.planes)]

    def after(self, token):
        self.rows = tied(self.rows, token)[0]

    def to_partner(self, value):
        return lax.ppermute(value, "grp", [(i, i ^ 1) for i in range(self.size)])

    def away(self):
        return [
            self.produce(self.rows, 2 * plane + 1 - self.core).astype(BF16) for plane in self.far
        ]

    def pass_on(self, arrived):
        return [
            (self.produce(self.rows, 2 * plane + self.core) + value.astype(F32)).astype(BF16)
            for plane, value in zip(self.far, arrived)
        ]

    def to_planes(self, values):
        sent = []
        for k, value in enumerate(values):
            shift = 2 * (k + 1)
            pairs = [(j, (j + shift) % self.size) for j in range(self.size)]
            sent.append(lax.ppermute(value, "grp", pairs))
        return sent

    def own(self):
        away = self.produce(self.rows, 2 * self.plane + 1 - self.core).astype(BF16)
        kept = self.produce(self.rows, 2 * self.plane + self.core)
        return kept + self.to_partner(away).astype(F32)


def add_all(value, others):
    for other in others:
        value = value + other.astype(F32)
    return value


def flat_tied(first, groups):
    flat = [value for group in groups for value in group]
    first, *flat = tied(first, *flat)
    result = []
    for group in groups:
        result.append(flat[: len(group)])
        flat = flat[len(group) :]
    return first, result


def columns_of(array, member):
    size = array.shape[1] // lax.axis_size("grp")
    return lax.dynamic_slice_in_dim(array, member * size, size, 1)


MESH = pl.DeviceIdType.MESH


def ring_places(count):
    here = lax.axis_index("ep")
    if count != 8:
        return here, lambda spot: spot
    x, z = here % 2, here // 2

    def index_at(spot):
        side = spot // 4
        return 2 * (spot + side * (7 - 2 * spot)) + side

    return z + x * (7 - 2 * z), index_at


def slot_index(count, slot):
    place, index_at = ring_places(count)
    offset = jnp.where(slot == count - 1, count // 2, (slot // 2 + 1) * (2 * (slot % 2) - 1))
    offset = jnp.where(slot == count - 2, 0, offset)
    return index_at((place + offset + count) % count)


def when(condition):
    if isinstance(condition, bool):
        return (lambda run: run()) if condition else (lambda run: None)
    return pl.when(condition)


def rows_at(slot, size):
    return pl.ds(pl.multiple_of(slot * size, size), size)


class KernelRing:
    def __init__(self, buffer, count, size, send_sems, recv_sems):
        place, index_at = ring_places(count)
        self.buffer, self.count, self.size = buffer, count, size
        self.half = count // 2
        self.send_sems, self.recv_sems = send_sems, recv_sems
        self.right = index_at((place + 1) % count)
        self.left = index_at((place + count - 1) % count)

    def own(self):
        return slice((self.count - 2) * self.size, (self.count - 1) * self.size)

    def copy(self, source, target, neighbour, step, way):
        return pltpu.make_async_remote_copy(
            src_ref=self.buffer.at[source],
            dst_ref=self.buffer.at[target],
            send_sem=self.send_sems.at[step, way],
            recv_sem=self.recv_sems.at[step, way],
            device_id={"ep": neighbour},
            device_id_type=MESH,
        )

    def sends(self, step):
        before = lax.rem(step + self.half - 1, self.half)
        copies = []
        for way, neighbour in enumerate((self.right, self.left)):
            source = jnp.where(step == 0, self.count - 2, 2 * before + way)
            copies.append(
                self.copy(
                    rows_at(source, self.size), rows_at(2 * step + way, self.size),
                    neighbour, step, way,
                )
            )
        return copies

    def last_sends(self):
        middle = self.size // 2
        copies = []
        for way, neighbour in enumerate((self.right, self.left)):
            source = (self.count - 4 + way) * self.size + way * middle
            target = (self.count - 1) * self.size + way * middle
            copies.append(
                self.copy(
                    pl.ds(source, middle), pl.ds(target, middle), neighbour, self.half - 1, way
                )
            )
        return copies

    def start(self):
        for copy in self.sends(0):
            copy.start()

    def arrive(self, i):
        @when(i < self.half - 1)
        def _():
            for copy in self.sends(i):
                copy.wait_recv()

        @when(i == self.half - 1)
        def _():
            for copy in self.last_sends():
                copy.wait_recv()

    def forward(self, i):
        @when(i < self.half - 2)
        def _():
            for copy in self.sends(i + 1):
                copy.start()

        @when(i == self.half - 2)
        def _():
            for copy in self.last_sends():
                copy.start()

    def finish(self):
        for step in range(self.half - 1):
            for copy in self.sends(step):
                copy.wait_send()
        for copy in self.last_sends():
            copy.wait_send()


class Exchange:
    def __init__(self, count, source_at, target_at, send_sems, recv_sems):
        self.count = count
        self.place, self.index_at = ring_places(count)
        self.source_at, self.target_at = source_at, target_at
        self.send_sems, self.recv_sems = send_sems, recv_sems

    def copy(self, slot):
        way = slot % 2
        far = slot // 2 + 1
        farthest = slot == self.count - 1
        offset = jnp.where(farthest, self.count // 2, far * (2 * way - 1))
        landing = jnp.where(farthest, slot, slot + 1 - 2 * way)
        return pltpu.make_async_remote_copy(
            src_ref=self.source_at(slot),
            dst_ref=self.target_at(landing),
            send_sem=self.send_sems.at[slot],
            recv_sem=self.recv_sems.at[landing],
            device_id={"ep": self.index_at((self.place + offset + self.count) % self.count)},
            device_id_type=MESH,
        )

    def arrived(self, slot):
        return pltpu.make_async_remote_copy(
            src_ref=self.source_at(slot),
            dst_ref=self.target_at(slot),
            send_sem=self.send_sems.at[slot],
            recv_sem=self.recv_sems.at[slot],
            device_id={"ep": self.index_at((self.place + 1) % self.count)},
            device_id_type=MESH,
        )

    def others(self):
        return [slot for slot in range(self.count) if slot != self.count - 2]


def greet(axis, count):
    barrier = pltpu.get_barrier_semaphore()
    here = lax.axis_index(axis)
    for step in range(1, count):
        pl.semaphore_signal(
            barrier, inc=1, device_id={axis: (here + step) % count}, device_id_type=MESH
        )


def block_rows_of(count):
    return 256 if count % 256 == 0 else 128


def attend_forward_kernel(
    count, grp_count, heads, scale, hidden, first_gain, gain, w, b, segments, row_segments, w_out,
    q_out, k_out, v_out, attended_out, log_out, residual_out, normed_out, cosine, sine, starts,
    x_out, w_all_out, row_positions, xs, w_all, received, x_send, x_recv, w_send, w_recv, plane_send, plane_recv, core_send,
    core_recv, hand_send, hand_recv, x_sems, w_sems, own_sem,
):
    size, width = hidden.shape
    half = count // 2
    rows = 2 * size
    dim = LANES
    inner_size = heads * dim
    planes = grp_count // 2
    mine = lax.axis_index("grp")
    core, plane = mine % 2, mine // 2
    part_width = width // grp_count

    own_columns = pl.ds(pl.multiple_of(mine * part_width, part_width), part_width)
    ring_x = KernelRing(xs, count, size, x_send, x_recv)
    ring_w = KernelRing(w_all.at[0], count, inner_size, w_send, w_recv)
    load = pltpu.make_async_copy(
        w_out.at[:, own_columns], w_all.at[0, ring_w.own()], own_sem.at[0]
    )
    load.start()
    greet("ep", count)
    greet("grp", grp_count)
    own_hidden = hidden[...].astype(F32)
    mean = jnp.sum(own_hidden * own_hidden, -1, keepdims=True) * (1.0 / width)
    xs[ring_x.own(), :] = (own_hidden * lax.rsqrt(mean + EPS) * first_gain[...]).astype(BF16)
    pl.semaphore_wait(pltpu.get_barrier_semaphore(), count - 1 + grp_count - 1)
    ring_x.start()
    load.wait()
    ring_w.start()

    for slot in range(count):
        row_positions[:, slot * size : (slot + 1) * size] = slot_index(
            count, slot
        ) * size + lax.broadcasted_iota(jnp.int32, (1, size), 1)
    lane = lax.broadcasted_iota(jnp.int32, (size, dim), 1)
    low_half = lane < dim // 2
    index = jnp.where(low_half, lane, lane - dim // 2).astype(F32)
    inverse = jnp.exp(index * (-2.0 * math.log(THETA) / dim))

    def tables(slot, carry):
        block = slot_index(count, slot)
        here, there = rows_at(slot, size), rows_at(block, size)
        before = jnp.where(row_segments[...] < segments[there, :], 1.0, 0.0)
        start = jnp.sum(before, -1, keepdims=True)
        starts[here, :] = start.astype(jnp.int32)
        position = (block * size + lax.broadcasted_iota(jnp.int32, (size, 1), 0)).astype(F32)
        angle = (position - start) * inverse
        cosine[here, :] = jnp.cos(angle)
        sine[here, :] = jnp.where(low_half, -jnp.sin(angle), jnp.sin(angle))
        return carry

    lax.fori_loop(0, count, tables, 0)

    def to_plane(step, i):
        here = rows_at(i, 2 * inner_size)
        landing = (planes - step) % planes
        return pltpu.make_async_remote_copy(
            src_ref=w_all.at[0, here],
            dst_ref=w_all.at[landing, here],
            send_sem=plane_send.at[step - 1, i],
            recv_sem=plane_recv.at[landing - 1, i],
            device_id={"grp": (mine + 2 * step) % grp_count},
            device_id_type=MESH,
        )

    def to_core(j):
        return pltpu.make_async_remote_copy(
            src_ref=w_all.at[j],
            dst_ref=w_all.at[planes + j],
            send_sem=core_send.at[j],
            recv_sem=core_recv.at[j],
            device_id={"grp": mine + 1 - 2 * core},
            device_id_type=MESH,
        )

    def store_x(i):
        here = rows_at(i, rows)
        return pltpu.make_async_copy(xs.at[here], x_out.at[here], x_sems.at[i])

    def store_w(j):
        return pltpu.make_async_copy(w_all.at[j], w_all_out.at[j], w_sems.at[j])

    def project(i, carry):
        here = rows_at(i, rows)
        ring_x.arrive(i)
        ring_x.forward(i)
        store_x(i).start()
        ring_w.arrive(i)
        ring_w.forward(i)
        for step in range(1, planes):
            to_plane(step, i).start()
        projected = dot(xs[here, :], w[...]) + b[...]
        cos, sin = cosine[here, :], sine[here, :]
        for h in range(heads):
            base = 3 * dim * h
            query = projected[:, base : base + dim]
            key = projected[:, base + dim : base + 2 * dim]
            q_out[h, here, :] = (query * cos + pltpu.roll(query, dim // 2, 1) * sin).astype(BF16)
            k_out[h, here, :] = (key * cos + pltpu.roll(key, dim // 2, 1) * sin).astype(BF16)
            v_out[h, here, :] = projected[:, base + 2 * dim : base + 3 * dim].astype(BF16)
        return carry

    lax.fori_loop(0, half, project, 0)
    to_core(0).start()
    store_w(0).start()

    exchange = Exchange(
        count,
        lambda slot: attended_out.at[rows_at(slot, size)],
        lambda slot: received.at[slot],
        hand_send,
        hand_recv,
    )

    def attend(step, carry):
        i = half - 1 - step
        here = rows_at(i, rows)
        count_up = lax.broadcasted_iota(jnp.int32, (size, 1), 0)
        own = jnp.concatenate(
            [slot_index(count, 2 * i + k) * size + count_up for k in range(2)], 0
        )
        start = starts[here, :]
        keys_at = row_positions[...]
        allowed = (keys_at <= own) & (keys_at >= start)
        for h in range(heads):
            scores = dot_nt(q_out[h, here, :], k_out[h]) * scale
            scores = jnp.where(allowed, scores, NEGATIVE)
            highest = jnp.max(scores, -1, keepdims=True)
            expo = jnp.exp(scores - highest)
            total = jnp.sum(expo, -1, keepdims=True)
            weights = (expo * (1.0 / total)).astype(BF16)
            attended_out[here, h * dim : (h + 1) * dim] = dot(weights, v_out[h]).astype(BF16)
            log_out[h, here, :] = highest + jnp.log(total)
        exchange.copy(2 * i + 1).start()

        @pl.when(i < half - 1)
        def _():
            exchange.copy(2 * i).start()

        return carry

    lax.fori_loop(0, half, attend, 0)
    received[count - 2] = attended_out[ring_x.own(), :]
    for j in range(1, planes):
        for i in range(half):
            to_plane((planes - j) % planes, i).wait_recv()
        to_core(j).start()
        store_w(j).start()
    for slot in exchange.others():
        exchange.arrived(slot).wait_recv()
    for j in range(planes):
        to_core(j).wait_recv()
        store_w(planes + j).start()
    mixed = jnp.concatenate([received[slot] for slot in range(count)], 1)
    square = jnp.zeros((size, 1), F32)
    for j in range(grp_count):
        member = 2 * ((plane + j % planes) % planes) + (core if j < planes else 1 - core)
        columns = pl.ds(pl.multiple_of(member * part_width, part_width), part_width)
        piece = hidden[:, columns].astype(F32) + dot(mixed, w_all[j])
        residual_out[:, columns] = piece
        square = square + jnp.sum(piece * piece, -1, keepdims=True)
    factor = lax.rsqrt(square * (1.0 / width) + EPS)
    normed_out[...] = (residual_out[...] * factor * gain[...]).astype(BF16)

    for i in range(half):
        store_x(i).wait()
        for step in range(1, planes):
            to_plane(step, i).wait_send()
    for j in range(grp_count):
        store_w(j).wait()
    for j in range(planes):
        to_core(j).wait_send()
    for slot in exchange.others():
        exchange.copy(slot).wait_send()
    ring_x.finish()
    ring_w.finish()


def attend_forward(
    count, grp_count, hidden, first_gain, gain, w, b, w_out, segments, scale
):
    size, width = hidden.shape
    tokens = size * count
    heads = w.shape[1] // (3 * LANES)
    half, planes = count // 2, grp_count // 2
    anywhere = pl.BlockSpec(memory_space=pl.ANY)
    whole = pl.BlockSpec(memory_space=pltpu.VMEM)
    shape = jax.ShapeDtypeStruct
    w_all_shape = (grp_count, count * heads * LANES, width // grp_count)
    dma = pltpu.SemaphoreType.DMA
    return pl.pallas_call(
        functools.partial(attend_forward_kernel, count, grp_count, heads, scale),
        in_specs=[whole] * 7 + [anywhere],
        out_specs=[whole] * 10 + [anywhere] * 2,
        out_shape=(
            shape((heads, tokens, LANES), BF16),
            shape((heads, tokens, LANES), BF16),
            shape((heads, tokens, LANES), BF16),
            shape((tokens, heads * LANES), BF16),
            shape((heads, tokens, 1), F32),
            shape((size, width), F32),
            shape((size, width), BF16),
            shape((tokens, LANES), F32),
            shape((tokens, LANES), F32),
            shape((tokens, 1), jnp.int32),
            shape((tokens, width), BF16),
            shape(w_all_shape, BF16),
        ),
        scratch_shapes=[
            pltpu.VMEM((1, tokens), jnp.int32),
            pltpu.VMEM((tokens, width), BF16),
            pltpu.VMEM(w_all_shape, BF16),
            pltpu.VMEM((count, size, heads * LANES), BF16),
            dma((half, 2)),
            dma((half, 2)),
            dma((half, 2)),
            dma((half, 2)),
            dma((max(planes - 1, 1), half)),
            dma((max(planes - 1, 1), half)),
            dma((planes,)),
            dma((planes,)),
            dma((count,)),
            dma((count,)),
            dma((half,)),
            dma((grp_count,)),
            dma((1,)),
        ],
        compiler_params=pltpu.CompilerParams(
            collective_id=1, has_side_effects=True, vmem_limit_bytes=56 * MIB
        ),
        cost_estimate=KERNEL_COST,
        name="attend_forward",
    )(hidden, first_gain[None, :], gain[None, :], w, b, segments[:, None], segments[None, :], w_out)


def attend_backward_kernel(
    count, grp_count, heads, scale, g_own, w_all, w, cosine, sine, q, k, v, row_logs, row_starts,
    g_out, bias_out, branch_out, group_out, row_positions, positions, g_att, dk, dv, outbox, gs,
    send_sems, recv_sems, ring_send, ring_recv, store_sems,
):
    size, width = g_own.shape
    tokens = size * count
    rows = block_rows_of(tokens)
    dim = LANES
    inner_size = heads * dim
    planes = grp_count // 2
    mine = lax.axis_index("grp")
    core, plane = mine % 2, mine // 2
    part_width = width // grp_count

    ring = KernelRing(gs, count, size, ring_send, ring_recv)

    def store(i):
        here = rows_at(i, 2 * size)
        return pltpu.make_async_copy(gs.at[here], group_out.at[here], store_sems.at[i])

    def next_pair(i):
        ring.arrive(i)
        ring.forward(i)
        store(i).start()

    greet("ep", count)
    gs[ring.own(), :] = g_own[...]
    for slot in range(count):
        first = slot_index(count, slot) * size
        row_positions[:, slot * size : (slot + 1) * size] = first + lax.broadcasted_iota(
            jnp.int32, (1, size), 1
        )
        positions[slot * size : (slot + 1) * size, :] = first + lax.broadcasted_iota(
            jnp.int32, (size, 1), 0
        )
    own_rows = None
    for j in range(grp_count):
        member = 2 * ((plane + j % planes) % planes) + (core if j < planes else 1 - core)
        columns = pl.ds(pl.multiple_of(member * part_width, part_width), part_width)
        piece = dot_nt(g_own[:, columns], w_all[j])
        own_rows = piece if own_rows is None else own_rows + piece
    own_rows = own_rows.astype(BF16)
    for slot in range(count):
        outbox[slot] = own_rows[:, slot * inner_size : (slot + 1) * inner_size]
    exchange = Exchange(
        count,
        lambda slot: outbox.at[slot],
        lambda slot: g_att.at[rows_at(slot, size)],
        send_sems,
        recv_sems,
    )
    pl.semaphore_wait(pltpu.get_barrier_semaphore(), count - 1)
    for slot in exchange.others():
        exchange.copy(slot).start()
    ring.start()
    g_att[(count - 2) * size : (count - 1) * size, :] = outbox[count - 2]
    dk[...] = jnp.zeros_like(dk)
    dv[...] = jnp.zeros_like(dv)
    for slot in exchange.others():
        exchange.arrived(slot).wait_recv()

    def scores_back(i, carry):
        here = rows_at(i, rows)
        own, start = row_positions[:, here], row_starts[:, here]
        keys_at = positions[...]
        allowed = (keys_at <= own) & (keys_at >= start)
        cos, sin = cosine[here, :], sine[here, :]
        for h in range(heads):
            query = q[h, here, :]
            g_block = g_att[here, h * dim : (h + 1) * dim]
            scores = dot_nt(k[h], query) * scale - row_logs[h, :, here]
            weights = jnp.exp(jnp.where(allowed, scores, NEGATIVE))
            g_weights = dot_nt(v[h], g_block)
            inner = jnp.sum(weights * g_weights, 0, keepdims=True)
            g_scores = (weights * (g_weights - inner)).astype(BF16)
            g_query = dot_tn(g_scores, k[h]) * scale
            g_query = g_query * cos - pltpu.roll(g_query, dim // 2, 1) * sin
            g_out[here, 3 * dim * h : 3 * dim * h + dim] = g_query.astype(BF16)
            dk[h] += dot(g_scores, query)
            dv[h] += dot(weights.astype(BF16), g_block)

        @pl.when(i == 1)
        def _():
            next_pair(0)

        return carry

    lax.fori_loop(0, tokens // rows, scores_back, 0)
    next_pair(1)
    bias_out[...] = jnp.zeros_like(bias_out)

    def finish(i, carry):
        here = rows_at(i, rows)
        cos, sin = cosine[here, :], sine[here, :]
        for h in range(heads):
            base = 3 * dim * h
            g_key = dk[h, here, :] * scale
            g_key = g_key * cos - pltpu.roll(g_key, dim // 2, 1) * sin
            g_out[here, base + dim : base + 2 * dim] = g_key.astype(BF16)
            g_out[here, base + 2 * dim : base + 3 * dim] = dv[h, here, :].astype(BF16)
        g_here = g_out[here, :]
        bias_out[...] += jnp.sum(g_here.astype(F32), 0, keepdims=True)
        branch_out[here, :] = dot_nt(g_here, w[...]).astype(BF16)
        return carry

    lax.fori_loop(0, tokens // rows, finish, 0)
    for i in range(2, count // 2):
        next_pair(i)
    for slot in exchange.others():
        exchange.copy(slot).wait_send()
    ring.finish()
    for i in range(count // 2):
        store(i).wait()


def attend_backward(
    count, grp_count, g_own, w_all, w, cosine, sine, q, k, v, logs, starts, scale
):
    size, width = g_own.shape
    heads, tokens, _ = q.shape
    whole = pl.BlockSpec(memory_space=pltpu.VMEM)
    shape = jax.ShapeDtypeStruct
    dma = pltpu.SemaphoreType.DMA
    return pl.pallas_call(
        functools.partial(attend_backward_kernel, count, grp_count, heads, scale),
        in_specs=[whole] * 10,
        out_specs=[whole] * 3 + [pl.BlockSpec(memory_space=pl.ANY)],
        out_shape=(
            shape((tokens, 3 * LANES * heads), BF16),
            shape((1, 3 * LANES * heads), F32),
            shape((tokens, width), BF16),
            shape((tokens, width), BF16),
        ),
        scratch_shapes=[
            pltpu.VMEM((1, tokens), jnp.int32),
            pltpu.VMEM((tokens, 1), jnp.int32),
            pltpu.VMEM((tokens, heads * LANES), BF16),
            pltpu.VMEM((heads, tokens, LANES), F32),
            pltpu.VMEM((heads, tokens, LANES), F32),
            pltpu.VMEM((count, size, heads * LANES), BF16),
            pltpu.VMEM((tokens, width), BF16),
            dma((count,)),
            dma((count,)),
            dma((count // 2, 2)),
            dma((count // 2, 2)),
            dma((count // 2,)),
        ],
        compiler_params=pltpu.CompilerParams(
            collective_id=2, has_side_effects=True, vmem_limit_bytes=56 * MIB
        ),
        cost_estimate=KERNEL_COST,
        name="attend_backward",
    )(
        g_own, w_all, w, cosine, sine, q, k, v,
        logs.reshape(heads, 1, tokens), starts.reshape(1, tokens),
    )


def reduce_kernel(count, number, *refs):
    parts, outs = refs[:number], refs[number : 2 * number]
    to_right = refs[2 * number : 3 * number]
    to_left = refs[3 * number : 4 * number]
    send_sems, recv_sems = refs[4 * number :]
    half = count // 2
    size = outs[0].shape[0]
    middle = size // 2
    place, index_at = ring_places(count)
    neighbours = (index_at((place + 1) % count), index_at((place + count - 1) % count))
    barrier = pltpu.get_barrier_semaphore()
    for neighbour in neighbours:
        pl.semaphore_signal(barrier, inc=1, device_id={"ep": neighbour}, device_id_type=MESH)
    pl.semaphore_wait(barrier, 2)

    def copy(a, step, way):
        held = (to_right, to_left)[way][a]
        if step == 0:
            cut = pl.ds(way * middle, middle)
            source = parts[a].at[pl.ds((count - 1) * size + way * middle, middle)]
            target = held.at[0, cut]
        else:
            source, target = held.at[step - 1], held.at[step]
        return pltpu.make_async_remote_copy(
            src_ref=source,
            dst_ref=target,
            send_sem=send_sems.at[a, step, way],
            recv_sem=recv_sems.at[a, step, way],
            device_id={"ep": neighbours[way]},
            device_id_type=MESH,
        )

    for a in range(number):
        for way in range(2):
            copy(a, 0, way).start()
    for step in range(1, half):
        far = half - step
        for a in range(number):
            for way in range(2):
                held = (to_right, to_left)[way][a]
                first = (2 * far - 1 - way) * size
                copy(a, step - 1, way).wait_recv()
                if step == 1:
                    here = slice(way * middle, (way + 1) * middle)
                    rest = slice((1 - way) * middle, (2 - way) * middle)
                    own = parts[a][first + way * middle : first + (way + 1) * middle, :]
                    held[0, here] = (own.astype(F32) + held[0, here].astype(F32)).astype(BF16)
                    held[0, rest] = parts[a][
                        first + (1 - way) * middle : first + (2 - way) * middle, :
                    ]
                else:
                    own = parts[a][first : first + size, :]
                    held[step - 1] = (own.astype(F32) + held[step - 1].astype(F32)).astype(BF16)
                copy(a, step, way).start()
    for a in range(number):
        own = parts[a][(count - 2) * size : (count - 1) * size, :].astype(F32)
        for way in range(2):
            copy(a, half - 1, way).wait_recv()
            own = own + (to_right, to_left)[way][a][half - 1].astype(F32)
        outs[a][...] = own
    for a in range(number):
        for step in range(half):
            for way in range(2):
                copy(a, step, way).wait_send()


def reduce_rows(count, call, *parts):
    tokens, width = parts[0].shape
    size, number, half = tokens // count, len(parts), count // 2
    return pl.pallas_call(
        functools.partial(reduce_kernel, count, number),
        in_specs=[pl.BlockSpec(memory_space=pltpu.VMEM)] * number,
        out_specs=[pl.BlockSpec(memory_space=pltpu.VMEM)] * number,
        out_shape=[jax.ShapeDtypeStruct((size, width), F32)] * number,
        scratch_shapes=[pltpu.VMEM((half, size, width), BF16)] * (2 * number)
        + [pltpu.SemaphoreType.DMA((number, half, 2))] * 2,
        compiler_params=pltpu.CompilerParams(
            collective_id=call, has_side_effects=True, vmem_limit_bytes=56 * MIB
        ),
        cost_estimate=KERNEL_COST,
        name="reduce_rows",
    )(*parts)


def tiles_of(width):
    tiles, start = [], 0
    while width - start > 384:
        tiles.append((start, 256))
        start += 256
    tiles.append((start, width - start))
    return tiles


def experts_kernel(
    count, expert_count, x_own, cot_own, routes, routes_w, gate_up_e, down_e, gate_up_s, down_s,
    act_e_out, grad_e_out, act_s_out, grad_s_out, part_out, branch_out, logits_out, x_out,
    cot_out,
    xs, cots, gate_e, up_e, held_e, gate_s, up_s, held_s, act_e, grad_e, act_s, grad_s, part,
    branch, logits_held, x_send, x_recv, cot_send, cot_recv, weight_sems, out_sems, x_sems,
):
    half = count // 2
    size = x_own.shape[0]
    rows = 2 * size
    ring_x = KernelRing(xs, count, size, x_send, x_recv)
    ring_cot = KernelRing(cots, count, size, cot_send, cot_recv)

    barrier = pltpu.get_barrier_semaphore()
    for neighbour in (ring_x.left, ring_x.right):
        pl.semaphore_signal(barrier, inc=1, device_id={"ep": neighbour}, device_id_type=MESH)
    loads = [
        pltpu.make_async_copy(source, target, weight_sems.at[i])
        for i, (source, target) in enumerate(
            [
                (gate_up_e.at[0, 0], gate_e),
                (gate_up_e.at[0, 1], up_e),
                (down_e.at[0], held_e),
                (gate_up_s.at[0], gate_s),
                (gate_up_s.at[1], up_s),
                (down_s, held_s),
            ]
        )
    ]
    for load in loads:
        load.start()
    xs[ring_x.own(), :] = x_own[...]
    cots[ring_x.own(), :] = cot_own[...]
    pl.semaphore_wait(barrier, 2)
    ring_x.start()
    ring_cot.start()

    def stores(i):
        here = rows_at(i, rows)
        slot = lax.rem(i, 2)
        pieces = [
            (act_e.at[slot], act_e_out.at[here]),
            (grad_e.at[slot, 0], grad_e_out.at[0, here]),
            (grad_e.at[slot, 1], grad_e_out.at[1, here]),
            (act_s.at[slot], act_s_out.at[here]),
            (grad_s.at[slot, 0], grad_s_out.at[0, here]),
            (grad_s.at[slot, 1], grad_s_out.at[1, here]),
            (part.at[slot], part_out.at[here]),
            (branch.at[slot], branch_out.at[here]),
            (logits_held.at[slot], logits_out.at[here]),
        ]
        return [
            pltpu.make_async_copy(source, target, out_sems.at[slot, k])
            for k, (source, target) in enumerate(pieces)
        ]

    def store_rows(i):
        here = rows_at(i, rows)
        return [
            pltpu.make_async_copy(xs.at[here], x_out.at[here], x_sems.at[0, i]),
            pltpu.make_async_copy(cots.at[here], cot_out.at[here], x_sems.at[1, i]),
        ]

    sections = (
        (gate_e, up_e, held_e, act_e, grad_e, dot, dot_nt),
        (gate_s, up_s, held_s, act_s, grad_s, dot_nt, dot),
    )
    mine = lax.axis_index("ep")
    onehot = (lax.broadcasted_iota(jnp.int32, (1, LANES), 1) == mine).astype(F32)

    def one_pair(i, carry):
        slot = lax.rem(i, 2)
        here = rows_at(i, rows)
        ring_x.arrive(i)
        ring_x.forward(i)
        ring_cot.arrive(i)
        ring_cot.forward(i)
        for copy in store_rows(i):
            copy.start()

        @pl.when(i == 0)
        def _():
            for load in loads:
                load.wait()

        @pl.when(i >= 2)
        def _():
            for copy in stores(i - 2):
                copy.wait()

        lane = lax.broadcasted_iota(jnp.int32, (rows, LANES), 1)
        inputs, cotangent = xs[here, :], cots[here, :]
        logits = dot(inputs, routes_w[...])
        routed = jnp.where(lane < expert_count, logits, NEGATIVE)
        expo = jnp.exp(routed - jnp.max(routed, -1, keepdims=True))
        probs = expo * (1.0 / jnp.sum(expo, -1, keepdims=True))
        named = jnp.concatenate(
            [routes[rows_at(slot_index(count, 2 * i + k), size), :] for k in range(2)], 0
        )
        hits = jnp.sum(jnp.where(named == mine, 1.0, 0.0), -1, keepdims=True)
        own_prob = jnp.sum(probs * onehot, -1, keepdims=True) * hits
        share_logit = jnp.sum(jnp.where(lane == expert_count, logits, 0.0), -1, keepdims=True)
        share = 1.0 / (1.0 + jnp.exp(-share_logit))

        inner = []
        total, out_total = None, None
        for s, (gate_w, up_w, down_w, act_out, grad_out, ahead, back_dot) in enumerate(sections):
            factor = own_prob if s == 0 else share
            dots = jnp.zeros((rows, 1), F32)
            for start, width in tiles_of(down_w.shape[0]):
                cut = pl.ds(start, width)
                piece = (slice(None), cut) if s == 0 else (cut, slice(None))
                gate = ahead(inputs, gate_w[piece])
                up = ahead(inputs, up_w[piece])
                grad = dot_nt(cotangent, down_w[cut, :])
                sigma = 0.5 * jnp.tanh(0.5 * gate) + 0.5
                silu = gate * sigma
                act = (silu * up).astype(BF16).astype(F32)
                dots = dots + jnp.sum(grad * act, -1, keepdims=True)
                scaled = grad * factor
                act_out[slot, :, cut] = (act * factor).astype(BF16)
                grad_out[slot, 0, :, cut] = (
                    scaled * up * (sigma + silu * (1.0 - sigma))
                ).astype(BF16)
                grad_out[slot, 1, :, cut] = (scaled * silu).astype(BF16)
            inner.append(dots)
            back = back_dot(grad_out[slot, 0], gate_w[...]) + back_dot(
                grad_out[slot, 1], up_w[...]
            )
            total = back if total is None else total + back
            out_piece = dot(act_out[slot], down_w[...])
            out_total = out_piece if out_total is None else out_total + out_piece
        branch[slot] = out_total.astype(BF16)
        grad_logits = own_prob * inner[0] * (onehot - probs)
        grad_share = share * (1.0 - share) * inner[1]
        grad_logits = grad_logits + jnp.where(lane == expert_count, grad_share, 0.0)
        high = grad_logits.astype(BF16)
        low = (grad_logits - high.astype(F32)).astype(BF16)
        total = total + dot_nt(high, routes_w[...]) + dot_nt(low, routes_w[...])
        logits_held[slot, :, :LANES] = high
        logits_held[slot, :, LANES:] = low
        part[slot] = total.astype(BF16)
        for copy in stores(i):
            copy.start()
        return carry

    lax.fori_loop(0, half, one_pair, 0)
    for i in range(half):
        for copy in store_rows(i):
            copy.wait()
    for i in range(max(half - 2, 0), half):
        for copy in stores(i):
            copy.wait()
    ring_x.finish()
    ring_cot.finish()


def experts(
    count, expert_count, x_own, cot_own, routes, routes_w, gate_up_e, down_e, gate_up_s, down_s
):
    size, width = x_own.shape
    tokens, rows, half = size * count, 2 * size, count // 2
    wide, narrow = down_e.shape[1], down_s.shape[0]
    anywhere = pl.BlockSpec(memory_space=pl.ANY)
    whole = pl.BlockSpec(memory_space=pltpu.VMEM)
    shape = jax.ShapeDtypeStruct
    dma = pltpu.SemaphoreType.DMA
    return pl.pallas_call(
        functools.partial(experts_kernel, count, expert_count),
        in_specs=[whole] * 4 + [anywhere] * 4,
        out_specs=[anywhere] * 9,
        out_shape=(
            shape((tokens, wide), BF16),
            shape((2, tokens, wide), BF16),
            shape((tokens, narrow), BF16),
            shape((2, tokens, narrow), BF16),
            shape((tokens, width), BF16),
            shape((tokens, width), BF16),
            shape((tokens, 2 * LANES), BF16),
            shape((tokens, width), BF16),
            shape((tokens, width), BF16),
        ),
        scratch_shapes=[
            pltpu.VMEM((tokens, width), BF16),
            pltpu.VMEM((tokens, width), BF16),
            pltpu.VMEM((width, wide), BF16),
            pltpu.VMEM((width, wide), BF16),
            pltpu.VMEM((wide, width), BF16),
            pltpu.VMEM((narrow, width), BF16),
            pltpu.VMEM((narrow, width), BF16),
            pltpu.VMEM((narrow, width), BF16),
            pltpu.VMEM((2, rows, wide), BF16),
            pltpu.VMEM((2, 2, rows, wide), BF16),
            pltpu.VMEM((2, rows, narrow), BF16),
            pltpu.VMEM((2, 2, rows, narrow), BF16),
            pltpu.VMEM((2, rows, width), BF16),
            pltpu.VMEM((2, rows, width), BF16),
            pltpu.VMEM((2, rows, 2 * LANES), BF16),
            dma((half, 2)),
            dma((half, 2)),
            dma((half, 2)),
            dma((half, 2)),
            dma((6,)),
            dma((2, 9)),
            dma((2, half)),
        ],
        compiler_params=pltpu.CompilerParams(
            collective_id=0, has_side_effects=True, vmem_limit_bytes=60 * MIB
        ),
        cost_estimate=KERNEL_COST,
        name="experts",
    )(x_own, cot_own, routes, routes_w, gate_up_e, down_e, gate_up_s, down_s)


def norm_of(values):
    factor = lax.rsqrt(jnp.mean(values * values, -1, keepdims=True) + EPS)
    return values * factor, factor


def norm_back(grad_out, normal, factor, gain):
    scaled = grad_out * gain
    return factor * (scaled - normal * jnp.mean(scaled * normal, -1, keepdims=True))


def local(
    hidden_in, segments, routes, cotangent, norm1_gain, w_qkv, b_qkv, w_out, norm2_gain, router,
    shared_gate_up, shared_down, shared_gate, expert_gate_up, expert_down,
):
    tokens_here, width = hidden_in.shape
    ep_count = lax.axis_size("ep")
    grp_count = lax.axis_size("grp")
    expert_count = router.shape[1]
    heads, qkv_dim = b_qkv.shape
    head_dim = qkv_dim // 3
    scale = 1.0 / math.sqrt(head_dim)
    slice_width = width // grp_count
    routes_w = jnp.concatenate(
        [router, shared_gate[:, None], jnp.zeros((width, LANES - 1 - expert_count), BF16)], 1
    )
    w_flat = w_qkv.reshape(width, heads * qkv_dim)
    b_flat = b_qkv.reshape(1, heads * qkv_dim)
    w_out_flat = w_out.reshape(heads * head_dim, width)

    (
        queries, key_rows, values, attended, logs, residual, normed_two, cosine, sine, starts,
        group_one, w_all,
    ) = attend_forward(
        ep_count, grp_count, hidden_in, norm1_gain, norm2_gain, w_flat, b_flat, w_out_flat,
        segments, scale,
    )

    (
        expert_act, expert_grad, shared_act, shared_grad, part, out_parts, grad_logits,
        group_two, group_cot,
    ) = experts(
        ep_count, expert_count, normed_two, cotangent, routes, routes_w,
        expert_gate_up, expert_down, jnp.swapaxes(shared_gate_up, 1, 2), shared_down,
    )

    def expert_gate_up_grad(rows, member):
        columns = columns_of(rows, member)
        return jnp.stack([dot_tn(columns, expert_grad[k]) for k in range(2)], 0)

    def shared_gate_up_grad(rows, member):
        columns = columns_of(rows, member)
        return jnp.stack([dot_tn(shared_grad[k], columns) for k in range(2)], 0)

    def down_grad(act):
        return lambda rows, member: dot_tn(act, columns_of(rows, member))

    sums = [
        GrpReduce(group_two, expert_gate_up_grad),
        GrpReduce(group_cot, down_grad(expert_act)),
        GrpReduce(group_two, shared_gate_up_grad),
        GrpReduce(group_cot, down_grad(shared_act)),
    ]
    part, aways = flat_tied(part, [item.away() for item in sums])
    arrived = [[item.to_partner(v) for v in values_] for item, values_ in zip(sums, aways)]
    (grad_normed_two,) = reduce_rows(ep_count, 3, part)
    normal_two, factor_two = norm_of(residual)
    grad_y = cotangent.astype(F32)
    grad_residual = grad_y + norm_back(grad_normed_two, normal_two, factor_two, norm2_gain)
    grad_norm2 = jnp.sum(grad_normed_two * normal_two, 0)
    for item in sums:
        item.after(grad_normed_two)
    own_attn, passed = flat_tied(
        grad_residual.astype(BF16),
        [item.pass_on(values_) for item, values_ in zip(sums, arrived)],
    )
    from_planes = [item.to_planes(values_) for item, values_ in zip(sums, passed)]

    grad_qkv, grad_bias, grad_branch, group_attn = attend_backward(
        ep_count, grp_count, own_attn, w_all, w_flat, cosine, sine, queries, key_rows, values,
        logs, starts, scale,
    )
    grad_norm1 = jnp.zeros((width,), F32)

    def w_qkv_grad(rows, member):
        nonlocal grad_norm1
        piece = dot_tn(columns_of(rows, member), grad_qkv)
        start = member * slice_width
        weights = lax.dynamic_slice_in_dim(w_flat, start, slice_width, 0).astype(F32)
        inner = jnp.sum(weights * piece, -1)
        grad_norm1 = lax.dynamic_update_slice_in_dim(grad_norm1, inner, start, 0)
        return piece

    more = [
        GrpReduce(group_one, w_qkv_grad),
        GrpReduce(group_attn, lambda rows, member: dot_tn(attended, columns_of(rows, member))),
    ]
    grad_branch, aways = flat_tied(grad_branch, [item.away() for item in more])
    arrived = [[item.to_partner(v) for v in values_] for item, values_ in zip(more, aways)]
    grad_normed_one, out_sum = reduce_rows(ep_count, 4, grad_branch, out_parts)
    layer_out = (residual + out_sum).astype(BF16)
    normal_one, factor_one = norm_of(hidden_in.astype(F32))
    grad_x = grad_residual + norm_back(grad_normed_one, normal_one, factor_one, norm1_gain)

    for item in more + sums:
        item.after(grad_normed_one)
    from_planes = [
        item.to_planes(item.pass_on(values_)) for item, values_ in zip(more, arrived)
    ] + from_planes
    (
        grad_w_qkv, grad_w_out, grad_expert_gate_up, grad_expert_down, grad_shared_gate_up,
        grad_shared_down,
    ) = [
        add_all(item.own(), values_) for item, values_ in zip(more + sums, from_planes)
    ]
    grad_routes = dot_tn(grad_logits, group_two)
    grad_routes = grad_routes[: expert_count + 1] + grad_routes[LANES : LANES + expert_count + 1]
    small = jnp.concatenate([grad_norm2[None], (grad_norm1 / norm1_gain)[None], grad_routes], 0)
    small = sum_all(small, ("ep", "grp"))
    bias_total = sum_all(grad_bias, ("grp",)).reshape(heads, grp_count, qkv_dim // grp_count)
    grad_b = lax.dynamic_index_in_dim(bias_total, lax.axis_index("grp"), 1, keepdims=False)
    grad_shared_gate_up = jnp.swapaxes(grad_shared_gate_up, 1, 2)

    return (
        layer_out,
        grad_x,
        small[1],
        grad_w_qkv.reshape(slice_width, heads, qkv_dim),
        grad_b,
        grad_w_out.reshape(heads, head_dim, slice_width),
        small[0],
        small[2 : expert_count + 2].T,
        grad_shared_gate_up,
        grad_shared_down,
        small[expert_count + 2],
        grad_expert_gate_up[None],
        grad_expert_down[None],
    )


def solution(mesh):
    in_specs = (
        P(("grp", "ep"), None),
        P("grp"),
        P("grp", None),
        P(("grp", "ep"), None),
        P(),
        P(None, "ep", None),
        P("ep", None),
        P("ep", None, None),
        P(),
        P(),
        P(None, None, "ep"),
        P("ep", None),
        P(),
        P("ep", None, None, None),
        P("ep", None, None),
    )
    out_specs = (
        P(("grp", "ep"), None),
        P(("grp", "ep"), None),
        P(),
        P("grp", "ep", None),
        P("ep", "grp"),
        P("ep", None, "grp"),
        P(),
        P(),
        P(None, "grp", "ep"),
        P("ep", "grp"),
        P(),
        P("ep", None, "grp", None),
        P("ep", None, "grp"),
    )
    return jax.shard_map(local, mesh=mesh, in_specs=in_specs, out_specs=out_specs, check_vma=False)
```

```python
import functools
import math

import jax
import jax.numpy as jnp
from jax import lax
from jax.experimental import pallas as pl
from jax.experimental.pallas import tpu as pltpu
from jax.sharding import PartitionSpec as P

EPS = 1e-06
THETA = 1000000.0
NEGATIVE = -1e30
BF16 = jnp.bfloat16
F32 = jnp.float32
LANES = 128
MIB = 1024 * 1024
KERNEL_COST = pl.CostEstimate(flops=10**6, bytes_accessed=10**5, transcendentals=0)


def dot(lhs, rhs):
    return jnp.dot(lhs, rhs, preferred_element_type=F32)


def dot_nt(lhs, rhs):
    return lax.dot_general(lhs, rhs, (((1,), (1,)), ((), ())), preferred_element_type=F32)


def dot_tn(lhs, rhs):
    return lax.dot_general(lhs, rhs, (((0,), (0,)), ((), ())), preferred_element_type=F32)


def tied(*arrays):
    return lax.optimization_barrier(arrays)


class GrpReduce:
    def __init__(self, rows, produce):
        self.rows, self.produce = rows, produce
        self.size = lax.axis_size("grp")
        self.planes = self.size // 2
        mine = lax.axis_index("grp")
        self.core, self.plane = mine % 2, mine // 2
        self.far = [(self.plane + k) % self.planes for k in range(1, self.planes)]

    def after(self, token):
        self.rows = tied(self.rows, token)[0]

    def to_partner(self, value):
        return lax.ppermute(value, "grp", [(i, i ^ 1) for i in range(self.size)])

    def away(self):
        return [
            self.produce(self.rows, 2 * plane + 1 - self.core).astype(BF16) for plane in self.far
        ]

    def pass_on(self, arrived):
        return [
            (self.produce(self.rows, 2 * plane + self.core) + value.astype(F32)).astype(BF16)
            for plane, value in zip(self.far, arrived)
        ]

    def own(self):
        away = self.produce(self.rows, 2 * self.plane + 1 - self.core).astype(BF16)
        kept = self.produce(self.rows, 2 * self.plane + self.core)
        return kept + self.to_partner(away).astype(F32)


def add_all(value, others):
    for other in others:
        value = value + other.astype(F32)
    return value


def flat_tied(first, groups):
    flat = [value for group in groups for value in group]
    first, *flat = tied(first, *flat)
    result = []
    for group in groups:
        result.append(flat[: len(group)])
        flat = flat[len(group) :]
    return first, result


def columns_of(array, member):
    size = array.shape[1] // lax.axis_size("grp")
    return lax.dynamic_slice_in_dim(array, member * size, size, 1)


MESH = pl.DeviceIdType.MESH


def ring_places(count):
    here = lax.axis_index("ep")
    if count != 8:
        return here, lambda spot: spot
    x, z = here % 2, here // 2

    def index_at(spot):
        side = spot // 4
        return 2 * (spot + side * (7 - 2 * spot)) + side

    return z + x * (7 - 2 * z), index_at


def slot_index(count, slot):
    place, index_at = ring_places(count)
    offset = jnp.where(slot == count - 1, count // 2, (slot // 2 + 1) * (2 * (slot % 2) - 1))
    offset = jnp.where(slot == count - 2, 0, offset)
    return index_at((place + offset + count) % count)


def when(condition):
    if isinstance(condition, bool):
        return (lambda run: run()) if condition else (lambda run: None)
    return pl.when(condition)


def rows_at(slot, size):
    return pl.ds(pl.multiple_of(slot * size, size), size)


class KernelRing:
    def __init__(self, buffer, count, size, send_sems, recv_sems):
        place, index_at = ring_places(count)
        self.buffer, self.count, self.size = buffer, count, size
        self.half = count // 2
        self.send_sems, self.recv_sems = send_sems, recv_sems
        self.right = index_at((place + 1) % count)
        self.left = index_at((place + count - 1) % count)

    def own(self):
        return slice((self.count - 2) * self.size, (self.count - 1) * self.size)

    def copy(self, source, target, neighbour, step, way):
        return pltpu.make_async_remote_copy(
            src_ref=self.buffer.at[source],
            dst_ref=self.buffer.at[target],
            send_sem=self.send_sems.at[step, way],
            recv_sem=self.recv_sems.at[step, way],
            device_id={"ep": neighbour},
            device_id_type=MESH,
        )

    def sends(self, step):
        before = lax.rem(step + self.half - 1, self.half)
        copies = []
        for way, neighbour in enumerate((self.right, self.left)):
            source = jnp.where(step == 0, self.count - 2, 2 * before + way)
            copies.append(
                self.copy(
                    rows_at(source, self.size), rows_at(2 * step + way, self.size),
                    neighbour, step, way,
                )
            )
        return copies

    def last_sends(self):
        middle = self.size // 2
        copies = []
        for way, neighbour in enumerate((self.right, self.left)):
            source = (self.count - 4 + way) * self.size + way * middle
            target = (self.count - 1) * self.size + way * middle
            copies.append(
                self.copy(
                    pl.ds(source, middle), pl.ds(target, middle), neighbour, self.half - 1, way
                )
            )
        return copies

    def start(self):
        for copy in self.sends(0):
            copy.start()

    def arrive(self, i):
        @when(i < self.half - 1)
        def _():
            for copy in self.sends(i):
                copy.wait_recv()

        @when(i == self.half - 1)
        def _():
            for copy in self.last_sends():
                copy.wait_recv()

    def forward(self, i):
        @when(i < self.half - 2)
        def _():
            for copy in self.sends(i + 1):
                copy.start()

        @when(i == self.half - 2)
        def _():
            for copy in self.last_sends():
                copy.start()

    def finish(self):
        for step in range(self.half - 1):
            for copy in self.sends(step):
                copy.wait_send()
        for copy in self.last_sends():
            copy.wait_send()


class Exchange:
    def __init__(self, count, source_at, target_at, send_sems, recv_sems):
        self.count = count
        self.place, self.index_at = ring_places(count)
        self.source_at, self.target_at = source_at, target_at
        self.send_sems, self.recv_sems = send_sems, recv_sems

    def copy(self, slot):
        way = slot % 2
        far = slot // 2 + 1
        farthest = slot == self.count - 1
        offset = jnp.where(farthest, self.count // 2, far * (2 * way - 1))
        landing = jnp.where(farthest, slot, slot + 1 - 2 * way)
        return pltpu.make_async_remote_copy(
            src_ref=self.source_at(slot),
            dst_ref=self.target_at(landing),
            send_sem=self.send_sems.at[slot],
            recv_sem=self.recv_sems.at[landing],
            device_id={"ep": self.index_at((self.place + offset + self.count) % self.count)},
            device_id_type=MESH,
        )

    def arrived(self, slot):
        return pltpu.make_async_remote_copy(
            src_ref=self.source_at(slot),
            dst_ref=self.target_at(slot),
            send_sem=self.send_sems.at[slot],
            recv_sem=self.recv_sems.at[slot],
            device_id={"ep": self.index_at((self.place + 1) % self.count)},
            device_id_type=MESH,
        )

    def others(self):
        return [slot for slot in range(self.count) if slot != self.count - 2]


class PlaneCopies:
    def __init__(self, sources, targets, planes, sems):
        mine, size = lax.axis_index("grp"), lax.axis_size("grp")
        self.copies = []
        for i, (source, target) in enumerate(zip(sources, targets)):
            shift = 2 * (i % (planes - 1) + 1)
            self.copies.append(
                pltpu.make_async_remote_copy(
                    src_ref=source,
                    dst_ref=target,
                    send_sem=sems.at[0, i],
                    recv_sem=sems.at[1, i],
                    device_id={"grp": (mine + shift) % size},
                    device_id_type=MESH,
                )
            )

    def start(self):
        for copy in self.copies:
            copy.start()

    def finish(self):
        for copy in self.copies:
            copy.wait()


def greet(axis, count):
    barrier = pltpu.get_barrier_semaphore()
    here = lax.axis_index(axis)
    for step in range(1, count):
        pl.semaphore_signal(
            barrier, inc=1, device_id={axis: (here + step) % count}, device_id_type=MESH
        )


def block_rows_of(count):
    return 256 if count % 256 == 0 else 128


def attend_forward_kernel(
    count, grp_count, heads, scale, hidden, first_gain, gain, w, b, segments, row_segments, w_out,
    q_out, k_out, v_out, attended_out, log_out, residual_out, normed_out, cosine, sine, starts,
    x_out, w_all_out, row_positions, xs, w_all, received, x_send, x_recv, w_send, w_recv, plane_send, plane_recv, core_send,
    core_recv, hand_send, hand_recv, x_sems, w_sems, own_sem,
):
    size, width = hidden.shape
    half = count // 2
    rows = 2 * size
    dim = LANES
    inner_size = heads * dim
    planes = grp_count // 2
    mine = lax.axis_index("grp")
    core, plane = mine % 2, mine // 2
    part_width = width // grp_count

    own_columns = pl.ds(pl.multiple_of(mine * part_width, part_width), part_width)
    ring_x = KernelRing(xs, count, size, x_send, x_recv)
    ring_w = KernelRing(w_all.at[0], count, inner_size, w_send, w_recv)
    load = pltpu.make_async_copy(
        w_out.at[:, own_columns], w_all.at[0, ring_w.own()], own_sem.at[0]
    )
    load.start()
    greet("ep", count)
    greet("grp", grp_count)
    own_hidden = hidden[...].astype(F32)
    mean = jnp.sum(own_hidden * own_hidden, -1, keepdims=True) * (1.0 / width)
    xs[ring_x.own(), :] = (own_hidden * lax.rsqrt(mean + EPS) * first_gain[...]).astype(BF16)
    pl.semaphore_wait(pltpu.get_barrier_semaphore(), count - 1 + grp_count - 1)
    ring_x.start()

    for slot in range(count):
        row_positions[:, slot * size : (slot + 1) * size] = slot_index(
            count, slot
        ) * size + lax.broadcasted_iota(jnp.int32, (1, size), 1)
    lane = lax.broadcasted_iota(jnp.int32, (size, dim), 1)
    low_half = lane < dim // 2
    index = jnp.where(low_half, lane, lane - dim // 2).astype(F32)
    inverse = jnp.exp(index * (-2.0 * math.log(THETA) / dim))

    def tables(slot, carry):
        block = slot_index(count, slot)
        here, there = rows_at(slot, size), rows_at(block, size)
        before = jnp.where(row_segments[...] < segments[there, :], 1.0, 0.0)
        start = jnp.sum(before, -1, keepdims=True)
        starts[here, :] = start.astype(jnp.int32)
        position = (block * size + lax.broadcasted_iota(jnp.int32, (size, 1), 0)).astype(F32)
        angle = (position - start) * inverse
        cosine[here, :] = jnp.cos(angle)
        sine[here, :] = jnp.where(low_half, -jnp.sin(angle), jnp.sin(angle))
        return carry

    lax.fori_loop(0, count, tables, 0)

    def to_plane(step, i):
        here = rows_at(i, 2 * inner_size)
        landing = (planes - step) % planes
        return pltpu.make_async_remote_copy(
            src_ref=w_all.at[0, here],
            dst_ref=w_all.at[landing, here],
            send_sem=plane_send.at[step - 1, i],
            recv_sem=plane_recv.at[landing - 1, i],
            device_id={"grp": (mine + 2 * step) % grp_count},
            device_id_type=MESH,
        )

    def to_core(j):
        return pltpu.make_async_remote_copy(
            src_ref=w_all.at[j],
            dst_ref=w_all.at[planes + j],
            send_sem=core_send.at[j],
            recv_sem=core_recv.at[j],
            device_id={"grp": mine + 1 - 2 * core},
            device_id_type=MESH,
        )

    def store_x(i):
        here = rows_at(i, rows)
        return pltpu.make_async_copy(xs.at[here], x_out.at[here], x_sems.at[i])

    def store_w(j):
        return pltpu.make_async_copy(w_all.at[j], w_all_out.at[j], w_sems.at[j])

    def project(i, carry):
        here = rows_at(i, rows)
        ring_x.arrive(i)
        ring_x.forward(i)
        store_x(i).start()

        @pl.when(i == half - 2)
        def _():
            load.wait()
            ring_w.start()

        projected = dot(xs[here, :], w[...]) + b[...]
        cos, sin = cosine[here, :], sine[here, :]
        for h in range(heads):
            base = 3 * dim * h
            query = projected[:, base : base + dim]
            key = projected[:, base + dim : base + 2 * dim]
            q_out[h, here, :] = (query * cos + pltpu.roll(query, dim // 2, 1) * sin).astype(BF16)
            k_out[h, here, :] = (key * cos + pltpu.roll(key, dim // 2, 1) * sin).astype(BF16)
            v_out[h, here, :] = projected[:, base + 2 * dim : base + 3 * dim].astype(BF16)
        return carry

    lax.fori_loop(0, half, project, 0)

    exchange = Exchange(
        count,
        lambda slot: attended_out.at[rows_at(slot, size)],
        lambda slot: received.at[slot],
        hand_send,
        hand_recv,
    )

    def attend(step, carry):
        i = half - 1 - step
        here = rows_at(i, rows)
        count_up = lax.broadcasted_iota(jnp.int32, (size, 1), 0)
        own = jnp.concatenate(
            [slot_index(count, 2 * i + k) * size + count_up for k in range(2)], 0
        )
        start = starts[here, :]
        keys_at = row_positions[...]
        allowed = (keys_at <= own) & (keys_at >= start)
        for h in range(heads):
            scores = dot_nt(q_out[h, here, :], k_out[h]) * scale
            scores = jnp.where(allowed, scores, NEGATIVE)
            highest = jnp.max(scores, -1, keepdims=True)
            expo = jnp.exp(scores - highest)
            total = jnp.sum(expo, -1, keepdims=True)
            weights = (expo * (1.0 / total)).astype(BF16)
            attended_out[here, h * dim : (h + 1) * dim] = dot(weights, v_out[h]).astype(BF16)
            log_out[h, here, :] = highest + jnp.log(total)
        exchange.copy(2 * i + 1).start()

        @pl.when(i < half - 1)
        def _():
            exchange.copy(2 * i).start()

        ring_w.arrive(step)
        ring_w.forward(step)
        for k in range(1, planes):
            to_plane(k, step).start()
        return carry

    lax.fori_loop(0, half, attend, 0)
    to_core(0).start()
    store_w(0).start()
    received[count - 2] = attended_out[ring_x.own(), :]
    for j in range(1, planes):
        for i in range(half):
            to_plane((planes - j) % planes, i).wait_recv()
        to_core(j).start()
        store_w(j).start()
    for slot in exchange.others():
        exchange.arrived(slot).wait_recv()
    for j in range(planes):
        to_core(j).wait_recv()
        store_w(planes + j).start()
    mixed = jnp.concatenate([received[slot] for slot in range(count)], 1)
    square = jnp.zeros((size, 1), F32)
    for j in range(grp_count):
        member = 2 * ((plane + j % planes) % planes) + (core if j < planes else 1 - core)
        columns = pl.ds(pl.multiple_of(member * part_width, part_width), part_width)
        piece = hidden[:, columns].astype(F32) + dot(mixed, w_all[j])
        residual_out[:, columns] = piece
        square = square + jnp.sum(piece * piece, -1, keepdims=True)
    factor = lax.rsqrt(square * (1.0 / width) + EPS)
    normed_out[...] = (residual_out[...] * factor * gain[...]).astype(BF16)

    for i in range(half):
        store_x(i).wait()
        for step in range(1, planes):
            to_plane(step, i).wait_send()
    for j in range(grp_count):
        store_w(j).wait()
    for j in range(planes):
        to_core(j).wait_send()
    for slot in exchange.others():
        exchange.copy(slot).wait_send()
    ring_x.finish()
    ring_w.finish()


def attend_forward(
    count, grp_count, hidden, first_gain, gain, w, b, w_out, segments, scale
):
    size, width = hidden.shape
    tokens = size * count
    heads = w.shape[1] // (3 * LANES)
    half, planes = count // 2, grp_count // 2
    anywhere = pl.BlockSpec(memory_space=pl.ANY)
    whole = pl.BlockSpec(memory_space=pltpu.VMEM)
    shape = jax.ShapeDtypeStruct
    w_all_shape = (grp_count, count * heads * LANES, width // grp_count)
    dma = pltpu.SemaphoreType.DMA
    return pl.pallas_call(
        functools.partial(attend_forward_kernel, count, grp_count, heads, scale),
        in_specs=[whole] * 7 + [anywhere],
        out_specs=[whole] * 10 + [anywhere] * 2,
        out_shape=(
            shape((heads, tokens, LANES), BF16),
            shape((heads, tokens, LANES), BF16),
            shape((heads, tokens, LANES), BF16),
            shape((tokens, heads * LANES), BF16),
            shape((heads, tokens, 1), F32),
            shape((size, width), F32),
            shape((size, width), BF16),
            shape((tokens, LANES), F32),
            shape((tokens, LANES), F32),
            shape((tokens, 1), jnp.int32),
            shape((tokens, width), BF16),
            shape(w_all_shape, BF16),
        ),
        scratch_shapes=[
            pltpu.VMEM((1, tokens), jnp.int32),
            pltpu.VMEM((tokens, width), BF16),
            pltpu.VMEM(w_all_shape, BF16),
            pltpu.VMEM((count, size, heads * LANES), BF16),
            dma((half, 2)),
            dma((half, 2)),
            dma((half, 2)),
            dma((half, 2)),
            dma((max(planes - 1, 1), half)),
            dma((max(planes - 1, 1), half)),
            dma((planes,)),
            dma((planes,)),
            dma((count,)),
            dma((count,)),
            dma((half,)),
            dma((grp_count,)),
            dma((1,)),
        ],
        compiler_params=pltpu.CompilerParams(
            collective_id=1, has_side_effects=True, vmem_limit_bytes=56 * MIB
        ),
        cost_estimate=KERNEL_COST,
        name="attend_forward",
    )(hidden, first_gain[None, :], gain[None, :], w, b, segments[:, None], segments[None, :], w_out)


def attend_backward_kernel(
    count, grp_count, heads, scale, g_own, w_all, w, cosine, sine, q, k, v, row_logs, row_starts,
    *refs,
):
    number = (len(refs) - 17) // 2
    bulk, refs = refs[:number], refs[number:]
    g_out, bias_out, branch_out, group_out = refs[:4]
    landed = refs[4 : 4 + number]
    (
        row_positions, positions, g_att, dk, dv, outbox, gs, send_sems, recv_sems, ring_send,
        ring_recv, store_sems, plane_sems,
    ) = refs[4 + number :]
    size, width = g_own.shape
    tokens = size * count
    rows = block_rows_of(tokens)
    dim = LANES
    inner_size = heads * dim
    planes = grp_count // 2
    mine = lax.axis_index("grp")
    core, plane = mine % 2, mine // 2
    part_width = width // grp_count

    ring = KernelRing(gs, count, size, ring_send, ring_recv)

    def store(i):
        here = rows_at(i, 2 * size)
        return pltpu.make_async_copy(gs.at[here], group_out.at[here], store_sems.at[i])

    def next_pair(i):
        ring.arrive(i)
        ring.forward(i)
        store(i).start()

    greet("ep", count)
    greet("grp", grp_count)
    gs[ring.own(), :] = g_own[...]
    pl.semaphore_wait(pltpu.get_barrier_semaphore(), count - 1 + grp_count - 1)
    plane_copies = PlaneCopies(bulk, landed, grp_count // 2, plane_sems)
    ring.start()
    plane_copies.start()
    for slot in range(count):
        first = slot_index(count, slot) * size
        row_positions[:, slot * size : (slot + 1) * size] = first + lax.broadcasted_iota(
            jnp.int32, (1, size), 1
        )
        positions[slot * size : (slot + 1) * size, :] = first + lax.broadcasted_iota(
            jnp.int32, (size, 1), 0
        )
    own_rows = None
    for j in range(grp_count):
        member = 2 * ((plane + j % planes) % planes) + (core if j < planes else 1 - core)
        columns = pl.ds(pl.multiple_of(member * part_width, part_width), part_width)
        piece = dot_nt(g_own[:, columns], w_all[j])
        own_rows = piece if own_rows is None else own_rows + piece
    own_rows = own_rows.astype(BF16)
    for slot in range(count):
        outbox[slot] = own_rows[:, slot * inner_size : (slot + 1) * inner_size]
    exchange = Exchange(
        count,
        lambda slot: outbox.at[slot],
        lambda slot: g_att.at[rows_at(slot, size)],
        send_sems,
        recv_sems,
    )
    for slot in exchange.others():
        exchange.copy(slot).start()
    g_att[(count - 2) * size : (count - 1) * size, :] = outbox[count - 2]
    dk[...] = jnp.zeros_like(dk)
    dv[...] = jnp.zeros_like(dv)
    for slot in exchange.others():
        exchange.arrived(slot).wait_recv()

    def scores_back(i, carry):
        here = rows_at(i, rows)
        own, start = row_positions[:, here], row_starts[:, here]
        keys_at = positions[...]
        allowed = (keys_at <= own) & (keys_at >= start)
        cos, sin = cosine[here, :], sine[here, :]
        for h in range(heads):
            query = q[h, here, :]
            g_block = g_att[here, h * dim : (h + 1) * dim]
            scores = dot_nt(k[h], query) * scale - row_logs[h, :, here]
            weights = jnp.exp(jnp.where(allowed, scores, NEGATIVE))
            g_weights = dot_nt(v[h], g_block)
            inner = jnp.sum(weights * g_weights, 0, keepdims=True)
            g_scores = (weights * (g_weights - inner)).astype(BF16)
            g_query = dot_tn(g_scores, k[h]) * scale
            g_query = g_query * cos - pltpu.roll(g_query, dim // 2, 1) * sin
            g_out[here, 3 * dim * h : 3 * dim * h + dim] = g_query.astype(BF16)
            dk[h] += dot(g_scores, query)
            dv[h] += dot(weights.astype(BF16), g_block)

        @pl.when(i == 0)
        def _():
            next_pair(0)

        @pl.when(i == 2)
        def _():
            next_pair(1)

        return carry

    lax.fori_loop(0, tokens // rows, scores_back, 0)
    bias_out[...] = jnp.zeros_like(bias_out)

    def finish(i, carry):
        here = rows_at(i, rows)
        cos, sin = cosine[here, :], sine[here, :]
        for h in range(heads):
            base = 3 * dim * h
            g_key = dk[h, here, :] * scale
            g_key = g_key * cos - pltpu.roll(g_key, dim // 2, 1) * sin
            g_out[here, base + dim : base + 2 * dim] = g_key.astype(BF16)
            g_out[here, base + 2 * dim : base + 3 * dim] = dv[h, here, :].astype(BF16)
        g_here = g_out[here, :]
        bias_out[...] += jnp.sum(g_here.astype(F32), 0, keepdims=True)
        branch_out[here, :] = dot_nt(g_here, w[...]).astype(BF16)
        return carry

    lax.fori_loop(0, tokens // rows, finish, 0)
    for i in range(2, count // 2):
        next_pair(i)
    for slot in exchange.others():
        exchange.copy(slot).wait_send()
    ring.finish()
    for i in range(count // 2):
        store(i).wait()
    plane_copies.finish()


def attend_backward(
    count, grp_count, g_own, w_all, w, cosine, sine, q, k, v, logs, starts, scale, bulk
):
    size, width = g_own.shape
    heads, tokens, _ = q.shape
    anywhere = pl.BlockSpec(memory_space=pl.ANY)
    whole = pl.BlockSpec(memory_space=pltpu.VMEM)
    shape = jax.ShapeDtypeStruct
    dma = pltpu.SemaphoreType.DMA
    return pl.pallas_call(
        functools.partial(attend_backward_kernel, count, grp_count, heads, scale),
        in_specs=[whole] * 10 + [anywhere] * len(bulk),
        out_specs=[whole] * 3 + [anywhere] * (1 + len(bulk)),
        out_shape=(
            shape((tokens, 3 * LANES * heads), BF16),
            shape((1, 3 * LANES * heads), F32),
            shape((tokens, width), BF16),
            shape((tokens, width), BF16),
            *[shape(value.shape, value.dtype) for value in bulk],
        ),
        scratch_shapes=[
            pltpu.VMEM((1, tokens), jnp.int32),
            pltpu.VMEM((tokens, 1), jnp.int32),
            pltpu.VMEM((tokens, heads * LANES), BF16),
            pltpu.VMEM((heads, tokens, LANES), F32),
            pltpu.VMEM((heads, tokens, LANES), F32),
            pltpu.VMEM((count, size, heads * LANES), BF16),
            pltpu.VMEM((tokens, width), BF16),
            dma((count,)),
            dma((count,)),
            dma((count // 2, 2)),
            dma((count // 2, 2)),
            dma((count // 2,)),
            dma((2, max(len(bulk), 1))),
        ],
        compiler_params=pltpu.CompilerParams(
            collective_id=2, has_side_effects=True, vmem_limit_bytes=56 * MIB
        ),
        cost_estimate=KERNEL_COST,
        name="attend_backward",
    )(
        g_own, w_all, w, cosine, sine, q, k, v,
        logs.reshape(heads, 1, tokens), starts.reshape(1, tokens), *bulk,
    )


def doubling_stages(axes):
    stages = []
    for axis in axes:
        step = 1
        while step < lax.axis_size(axis):
            stages.append((axis, step))
            step *= 2
    return stages


class Doubling:
    def __init__(self, held, arrived, stages, sems):
        self.held, self.arrived, self.stages, self.sems = held, arrived, stages, sems
        self.place = 0

    def copy(self, k):
        axis, step = self.stages[k]
        here = lax.axis_index(axis)
        return pltpu.make_async_remote_copy(
            src_ref=self.held.at[k],
            dst_ref=self.arrived.at[k],
            send_sem=self.sems.at[0, k],
            recv_sem=self.sems.at[1, k],
            device_id={axis: here + step * (1 - 2 * (here // step % 2))},
            device_id_type=MESH,
        )

    def start(self):
        self.copy(0).start()

    def advance(self):
        k = self.place
        if k < len(self.stages):
            self.copy(k).wait_recv()
            self.held[k + 1] = self.held[k] + self.arrived[k]
            if k + 1 < len(self.stages):
                self.copy(k + 1).start()
            self.place += 1

    def finish(self):
        while self.place < len(self.stages):
            self.advance()
        for k in range(len(self.stages)):
            self.copy(k).wait_send()
        return self.held[len(self.stages)]


def reduce_kernel(count, grp_count, number, bulk_number, small_axes, *refs):
    refs = list(refs)

    def take(amount):
        taken = refs[:amount]
        del refs[:amount]
        return taken

    small_number = len(small_axes)
    parts, smalls, bulk = take(number), take(small_number), take(bulk_number)
    outs, small_outs, landed = take(number), take(small_number), take(bulk_number)
    to_right, to_left = take(number), take(number)
    small_held, small_arrived = take(small_number), take(small_number)
    send_sems, recv_sems = take(2)
    small_sems = take(small_number)
    (plane_sems,) = take(1)
    half = count // 2
    size = outs[0].shape[0]
    middle = size // 2
    place, index_at = ring_places(count)
    neighbours = (index_at((place + 1) % count), index_at((place + count - 1) % count))
    greet("ep", count)
    greet("grp", grp_count)
    for held, small in zip(small_held, smalls):
        held[0] = small[...]
    pl.semaphore_wait(pltpu.get_barrier_semaphore(), count - 1 + grp_count - 1)

    def copy(a, step, way):
        held = (to_right, to_left)[way][a]
        if step == 0:
            cut = pl.ds(way * middle, middle)
            source = parts[a].at[pl.ds((count - 1) * size + way * middle, middle)]
            target = held.at[0, cut]
        else:
            source, target = held.at[step - 1], held.at[step]
        return pltpu.make_async_remote_copy(
            src_ref=source,
            dst_ref=target,
            send_sem=send_sems.at[a, step, way],
            recv_sem=recv_sems.at[a, step, way],
            device_id={"ep": neighbours[way]},
            device_id_type=MESH,
        )

    sums = [
        Doubling(held, arrived, doubling_stages(axes), sems)
        for held, arrived, axes, sems in zip(small_held, small_arrived, small_axes, small_sems)
    ]
    for a in range(number):
        for way in range(2):
            copy(a, 0, way).start()
    for item in sums:
        item.start()
    plane_copies = PlaneCopies(bulk, landed, grp_count // 2, plane_sems)
    plane_copies.start()
    for step in range(1, half):
        far = half - step
        for a in range(number):
            for way in range(2):
                held = (to_right, to_left)[way][a]
                first = (2 * far - 1 - way) * size
                copy(a, step - 1, way).wait_recv()
                if step == 1:
                    here = slice(way * middle, (way + 1) * middle)
                    rest = slice((1 - way) * middle, (2 - way) * middle)
                    own = parts[a][first + way * middle : first + (way + 1) * middle, :]
                    held[0, here] = (own.astype(F32) + held[0, here].astype(F32)).astype(BF16)
                    held[0, rest] = parts[a][
                        first + (1 - way) * middle : first + (2 - way) * middle, :
                    ]
                else:
                    own = parts[a][first : first + size, :]
                    held[step - 1] = (own.astype(F32) + held[step - 1].astype(F32)).astype(BF16)
                copy(a, step, way).start()
            for item in sums:
                item.advance()
    for a in range(number):
        own = parts[a][(count - 2) * size : (count - 1) * size, :].astype(F32)
        for way in range(2):
            copy(a, half - 1, way).wait_recv()
            own = own + (to_right, to_left)[way][a][half - 1].astype(F32)
        outs[a][...] = own
    for item, out in zip(sums, small_outs):
        out[...] = item.finish()
    for a in range(number):
        for step in range(half):
            for way in range(2):
                copy(a, step, way).wait_send()
    plane_copies.finish()


def reduce_rows(count, grp_count, call, parts, smalls=(), small_axes=(), bulk=()):
    tokens, width = parts[0].shape
    size, number, half = tokens // count, len(parts), count // 2
    stages = [len(doubling_stages(axes)) for axes in small_axes]
    anywhere = pl.BlockSpec(memory_space=pl.ANY)
    whole = pl.BlockSpec(memory_space=pltpu.VMEM)
    shape = jax.ShapeDtypeStruct
    dma = pltpu.SemaphoreType.DMA
    results = pl.pallas_call(
        functools.partial(
            reduce_kernel, count, grp_count, number, len(bulk), tuple(small_axes)
        ),
        in_specs=[whole] * (number + len(smalls)) + [anywhere] * len(bulk),
        out_specs=[whole] * (number + len(smalls)) + [anywhere] * len(bulk),
        out_shape=[shape((size, width), F32)] * number
        + [shape(value.shape, value.dtype) for value in (*smalls, *bulk)],
        scratch_shapes=[pltpu.VMEM((half, size, width), BF16)] * (2 * number)
        + [pltpu.VMEM((k + 1, *value.shape), F32) for k, value in zip(stages, smalls)]
        + [pltpu.VMEM((k, *value.shape), F32) for k, value in zip(stages, smalls)]
        + [dma((number, half, 2))] * 2
        + [dma((2, k)) for k in stages]
        + [dma((2, max(len(bulk), 1)))],
        compiler_params=pltpu.CompilerParams(
            collective_id=call, has_side_effects=True, vmem_limit_bytes=56 * MIB
        ),
        cost_estimate=KERNEL_COST,
        name="reduce_rows",
    )(*parts, *smalls, *bulk)
    return (
        results[:number],
        results[number : number + len(smalls)],
        results[number + len(smalls) :],
    )


def tiles_of(width):
    tiles, start = [], 0
    while width - start > 384:
        tiles.append((start, 256))
        start += 256
    tiles.append((start, width - start))
    return tiles


def experts_kernel(
    count, expert_count, x_own, cot_own, routes, routes_w, gate_up_e, down_e, gate_up_s, down_s,
    act_e_out, grad_e_out, act_s_out, grad_s_out, part_out, branch_out, logits_out, x_out,
    cot_out,
    xs, cots, gate_e, up_e, held_e, gate_s, up_s, held_s, act_e, grad_e, act_s, grad_s, part,
    branch, logits_held, x_send, x_recv, cot_send, cot_recv, weight_sems, out_sems, x_sems,
):
    half = count // 2
    size = x_own.shape[0]
    rows = 2 * size
    ring_x = KernelRing(xs, count, size, x_send, x_recv)
    ring_cot = KernelRing(cots, count, size, cot_send, cot_recv)

    barrier = pltpu.get_barrier_semaphore()
    for neighbour in (ring_x.left, ring_x.right):
        pl.semaphore_signal(barrier, inc=1, device_id={"ep": neighbour}, device_id_type=MESH)
    loads = [
        pltpu.make_async_copy(source, target, weight_sems.at[i])
        for i, (source, target) in enumerate(
            [
                (gate_up_e.at[0, 0], gate_e),
                (gate_up_e.at[0, 1], up_e),
                (down_e.at[0], held_e),
                (gate_up_s.at[0], gate_s),
                (gate_up_s.at[1], up_s),
                (down_s, held_s),
            ]
        )
    ]
    for load in loads:
        load.start()
    xs[ring_x.own(), :] = x_own[...]
    cots[ring_x.own(), :] = cot_own[...]
    pl.semaphore_wait(barrier, 2)
    ring_x.start()
    ring_cot.start()

    def stores(i):
        here = rows_at(i, rows)
        slot = lax.rem(i, 2)
        pieces = [
            (act_e.at[slot], act_e_out.at[here]),
            (grad_e.at[slot, 0], grad_e_out.at[0, here]),
            (grad_e.at[slot, 1], grad_e_out.at[1, here]),
            (act_s.at[slot], act_s_out.at[here]),
            (grad_s.at[slot, 0], grad_s_out.at[0, here]),
            (grad_s.at[slot, 1], grad_s_out.at[1, here]),
            (part.at[slot], part_out.at[here]),
            (branch.at[slot], branch_out.at[here]),
            (logits_held.at[slot], logits_out.at[here]),
        ]
        return [
            pltpu.make_async_copy(source, target, out_sems.at[slot, k])
            for k, (source, target) in enumerate(pieces)
        ]

    def store_rows(i):
        here = rows_at(i, rows)
        return [
            pltpu.make_async_copy(xs.at[here], x_out.at[here], x_sems.at[0, i]),
            pltpu.make_async_copy(cots.at[here], cot_out.at[here], x_sems.at[1, i]),
        ]

    sections = (
        (gate_e, up_e, held_e, act_e, grad_e, dot, dot_nt),
        (gate_s, up_s, held_s, act_s, grad_s, dot_nt, dot),
    )
    mine = lax.axis_index("ep")
    onehot = (lax.broadcasted_iota(jnp.int32, (1, LANES), 1) == mine).astype(F32)

    def one_pair(i, carry):
        slot = lax.rem(i, 2)
        here = rows_at(i, rows)
        ring_x.arrive(i)
        ring_x.forward(i)
        ring_cot.arrive(i)
        ring_cot.forward(i)
        for copy in store_rows(i):
            copy.start()

        @pl.when(i == 0)
        def _():
            for load in loads:
                load.wait()

        @pl.when(i >= 2)
        def _():
            for copy in stores(i - 2):
                copy.wait()

        lane = lax.broadcasted_iota(jnp.int32, (rows, LANES), 1)
        inputs, cotangent = xs[here, :], cots[here, :]
        logits = dot(inputs, routes_w[...])
        routed = jnp.where(lane < expert_count, logits, NEGATIVE)
        expo = jnp.exp(routed - jnp.max(routed, -1, keepdims=True))
        probs = expo * (1.0 / jnp.sum(expo, -1, keepdims=True))
        named = jnp.concatenate(
            [routes[rows_at(slot_index(count, 2 * i + k), size), :] for k in range(2)], 0
        )
        hits = jnp.sum(jnp.where(named == mine, 1.0, 0.0), -1, keepdims=True)
        own_prob = jnp.sum(probs * onehot, -1, keepdims=True) * hits
        share_logit = jnp.sum(jnp.where(lane == expert_count, logits, 0.0), -1, keepdims=True)
        share = 1.0 / (1.0 + jnp.exp(-share_logit))

        inner = []
        total, out_total = None, None
        for s, (gate_w, up_w, down_w, act_out, grad_out, ahead, back_dot) in enumerate(sections):
            factor = own_prob if s == 0 else share
            dots = jnp.zeros((rows, 1), F32)
            for start, width in tiles_of(down_w.shape[0]):
                cut = pl.ds(start, width)
                piece = (slice(None), cut) if s == 0 else (cut, slice(None))
                gate = ahead(inputs, gate_w[piece])
                up = ahead(inputs, up_w[piece])
                grad = dot_nt(cotangent, down_w[cut, :])
                sigma = 0.5 * jnp.tanh(0.5 * gate) + 0.5
                silu = gate * sigma
                act = (silu * up).astype(BF16).astype(F32)
                dots = dots + jnp.sum(grad * act, -1, keepdims=True)
                scaled = grad * factor
                act_out[slot, :, cut] = (act * factor).astype(BF16)
                grad_out[slot, 0, :, cut] = (
                    scaled * up * (sigma + silu * (1.0 - sigma))
                ).astype(BF16)
                grad_out[slot, 1, :, cut] = (scaled * silu).astype(BF16)
            inner.append(dots)
            back = back_dot(grad_out[slot, 0], gate_w[...]) + back_dot(
                grad_out[slot, 1], up_w[...]
            )
            total = back if total is None else total + back
            out_piece = dot(act_out[slot], down_w[...])
            out_total = out_piece if out_total is None else out_total + out_piece
        branch[slot] = out_total.astype(BF16)
        grad_logits = own_prob * inner[0] * (onehot - probs)
        grad_share = share * (1.0 - share) * inner[1]
        grad_logits = grad_logits + jnp.where(lane == expert_count, grad_share, 0.0)
        high = grad_logits.astype(BF16)
        low = (grad_logits - high.astype(F32)).astype(BF16)
        total = total + dot_nt(high, routes_w[...]) + dot_nt(low, routes_w[...])
        logits_held[slot, :, :LANES] = high
        logits_held[slot, :, LANES:] = low
        part[slot] = total.astype(BF16)
        for copy in stores(i):
            copy.start()
        return carry

    lax.fori_loop(0, half, one_pair, 0)
    for i in range(half):
        for copy in store_rows(i):
            copy.wait()
    for i in range(max(half - 2, 0), half):
        for copy in stores(i):
            copy.wait()
    ring_x.finish()
    ring_cot.finish()


def experts(
    count, expert_count, x_own, cot_own, routes, routes_w, gate_up_e, down_e, gate_up_s, down_s
):
    size, width = x_own.shape
    tokens, rows, half = size * count, 2 * size, count // 2
    wide, narrow = down_e.shape[1], down_s.shape[0]
    anywhere = pl.BlockSpec(memory_space=pl.ANY)
    whole = pl.BlockSpec(memory_space=pltpu.VMEM)
    shape = jax.ShapeDtypeStruct
    dma = pltpu.SemaphoreType.DMA
    return pl.pallas_call(
        functools.partial(experts_kernel, count, expert_count),
        in_specs=[whole] * 4 + [anywhere] * 4,
        out_specs=[anywhere] * 9,
        out_shape=(
            shape((tokens, wide), BF16),
            shape((2, tokens, wide), BF16),
            shape((tokens, narrow), BF16),
            shape((2, tokens, narrow), BF16),
            shape((tokens, width), BF16),
            shape((tokens, width), BF16),
            shape((tokens, 2 * LANES), BF16),
            shape((tokens, width), BF16),
            shape((tokens, width), BF16),
        ),
        scratch_shapes=[
            pltpu.VMEM((tokens, width), BF16),
            pltpu.VMEM((tokens, width), BF16),
            pltpu.VMEM((width, wide), BF16),
            pltpu.VMEM((width, wide), BF16),
            pltpu.VMEM((wide, width), BF16),
            pltpu.VMEM((narrow, width), BF16),
            pltpu.VMEM((narrow, width), BF16),
            pltpu.VMEM((narrow, width), BF16),
            pltpu.VMEM((2, rows, wide), BF16),
            pltpu.VMEM((2, 2, rows, wide), BF16),
            pltpu.VMEM((2, rows, narrow), BF16),
            pltpu.VMEM((2, 2, rows, narrow), BF16),
            pltpu.VMEM((2, rows, width), BF16),
            pltpu.VMEM((2, rows, width), BF16),
            pltpu.VMEM((2, rows, 2 * LANES), BF16),
            dma((half, 2)),
            dma((half, 2)),
            dma((half, 2)),
            dma((half, 2)),
            dma((6,)),
            dma((2, 9)),
            dma((2, half)),
        ],
        compiler_params=pltpu.CompilerParams(
            collective_id=0, has_side_effects=True, vmem_limit_bytes=60 * MIB
        ),
        cost_estimate=KERNEL_COST,
        name="experts",
    )(x_own, cot_own, routes, routes_w, gate_up_e, down_e, gate_up_s, down_s)


def norm_of(values):
    factor = lax.rsqrt(jnp.mean(values * values, -1, keepdims=True) + EPS)
    return values * factor, factor


def norm_back(grad_out, normal, factor, gain):
    scaled = grad_out * gain
    return factor * (scaled - normal * jnp.mean(scaled * normal, -1, keepdims=True))


def local(
    hidden_in, segments, routes, cotangent, norm1_gain, w_qkv, b_qkv, w_out, norm2_gain, router,
    shared_gate_up, shared_down, shared_gate, expert_gate_up, expert_down,
):
    tokens_here, width = hidden_in.shape
    ep_count = lax.axis_size("ep")
    grp_count = lax.axis_size("grp")
    expert_count = router.shape[1]
    heads, qkv_dim = b_qkv.shape
    head_dim = qkv_dim // 3
    scale = 1.0 / math.sqrt(head_dim)
    slice_width = width // grp_count
    routes_w = jnp.concatenate(
        [router, shared_gate[:, None], jnp.zeros((width, LANES - 1 - expert_count), BF16)], 1
    )
    w_flat = w_qkv.reshape(width, heads * qkv_dim)
    b_flat = b_qkv.reshape(1, heads * qkv_dim)
    w_out_flat = w_out.reshape(heads * head_dim, width)

    (
        queries, key_rows, values, attended, logs, residual, normed_two, cosine, sine, starts,
        group_one, w_all,
    ) = attend_forward(
        ep_count, grp_count, hidden_in, norm1_gain, norm2_gain, w_flat, b_flat, w_out_flat,
        segments, scale,
    )

    (
        expert_act, expert_grad, shared_act, shared_grad, part, out_parts, grad_logits,
        group_two, group_cot,
    ) = experts(
        ep_count, expert_count, normed_two, cotangent, routes, routes_w,
        expert_gate_up, expert_down, jnp.swapaxes(shared_gate_up, 1, 2), shared_down,
    )

    def expert_gate_up_grad(rows, member):
        columns = columns_of(rows, member)
        return jnp.stack([dot_tn(columns, expert_grad[k]) for k in range(2)], 0)

    def shared_gate_up_grad(rows, member):
        columns = columns_of(rows, member)
        return jnp.stack([dot_tn(shared_grad[k], columns) for k in range(2)], 0)

    def down_grad(act):
        return lambda rows, member: dot_tn(act, columns_of(rows, member))

    sums = [
        GrpReduce(group_two, expert_gate_up_grad),
        GrpReduce(group_cot, down_grad(expert_act)),
        GrpReduce(group_two, shared_gate_up_grad),
        GrpReduce(group_cot, down_grad(shared_act)),
    ]
    part, aways = flat_tied(part, [item.away() for item in sums])
    arrived = [[item.to_partner(v) for v in values_] for item, values_ in zip(sums, aways)]
    (grad_normed_two,), _, _ = reduce_rows(ep_count, grp_count, 3, [part])
    normal_two, factor_two = norm_of(residual)
    grad_y = cotangent.astype(F32)
    grad_residual = grad_y + norm_back(grad_normed_two, normal_two, factor_two, norm2_gain)
    grad_norm2 = jnp.sum(grad_normed_two * normal_two, 0)
    for item in sums:
        item.after(grad_normed_two)
    own_attn, passed = flat_tied(
        grad_residual.astype(BF16),
        [item.pass_on(values_) for item, values_ in zip(sums, arrived)],
    )
    each = grp_count // 2 - 1

    grad_qkv, grad_bias, grad_branch, group_attn, *landed = attend_backward(
        ep_count, grp_count, own_attn, w_all, w_flat, cosine, sine, queries, key_rows, values,
        logs, starts, scale, passed[0],
    )
    from_planes = [landed]
    grad_norm1 = jnp.zeros((width,), F32)

    def w_qkv_grad(rows, member):
        nonlocal grad_norm1
        piece = dot_tn(columns_of(rows, member), grad_qkv)
        start = member * slice_width
        weights = lax.dynamic_slice_in_dim(w_flat, start, slice_width, 0).astype(F32)
        inner = jnp.sum(weights * piece, -1)
        grad_norm1 = lax.dynamic_update_slice_in_dim(grad_norm1, inner, start, 0)
        return piece

    more = [
        GrpReduce(group_one, w_qkv_grad),
        GrpReduce(group_attn, lambda rows, member: dot_tn(attended, columns_of(rows, member))),
    ]
    aways = [item.away() for item in more]
    arrived = [[item.to_partner(v) for v in values_] for item, values_ in zip(more, aways)]
    more_passed = [item.pass_on(values_) for item, values_ in zip(more, arrived)]
    more_own = [item.own() for item in more]
    grad_routes = dot_tn(grad_logits, group_two)
    grad_routes = grad_routes[: expert_count + 1] + grad_routes[LANES : LANES + expert_count + 1]
    small = jnp.concatenate([grad_norm2[None], (grad_norm1 / norm1_gain)[None], grad_routes], 0)
    bulk = [value for values_ in passed[1:] for value in values_]
    (grad_normed_one, out_sum), (small, bias_total), landed = reduce_rows(
        ep_count, grp_count, 4, [grad_branch, out_parts], [small, grad_bias],
        [("ep", "grp"), ("grp",)], bulk + [value for values_ in more_passed for value in values_],
    )
    from_planes += [landed[i * each : (i + 1) * each] for i in range(5)]
    layer_out = (residual + out_sum).astype(BF16)
    normal_one, factor_one = norm_of(hidden_in.astype(F32))
    grad_x = grad_residual + norm_back(grad_normed_one, normal_one, factor_one, norm1_gain)

    for item in sums:
        item.after(grad_normed_one)
    (
        grad_expert_gate_up, grad_expert_down, grad_shared_gate_up, grad_shared_down,
        grad_w_qkv, grad_w_out,
    ) = [
        add_all(own, values_)
        for own, values_ in zip([item.own() for item in sums] + more_own, from_planes)
    ]
    bias_total = bias_total.reshape(heads, grp_count, qkv_dim // grp_count)
    grad_b = lax.dynamic_index_in_dim(bias_total, lax.axis_index("grp"), 1, keepdims=False)
    grad_shared_gate_up = jnp.swapaxes(grad_shared_gate_up, 1, 2)

    return (
        layer_out,
        grad_x,
        small[1],
        grad_w_qkv.reshape(slice_width, heads, qkv_dim),
        grad_b,
        grad_w_out.reshape(heads, head_dim, slice_width),
        small[0],
        small[2 : expert_count + 2].T,
        grad_shared_gate_up,
        grad_shared_down,
        small[expert_count + 2],
        grad_expert_gate_up[None],
        grad_expert_down[None],
    )


def solution(mesh):
    in_specs = (
        P(("grp", "ep"), None),
        P("grp"),
        P("grp", None),
        P(("grp", "ep"), None),
        P(),
        P(None, "ep", None),
        P("ep", None),
        P("ep", None, None),
        P(),
        P(),
        P(None, None, "ep"),
        P("ep", None),
        P(),
        P("ep", None, None, None),
        P("ep", None, None),
    )
    out_specs = (
        P(("grp", "ep"), None),
        P(("grp", "ep"), None),
        P(),
        P("grp", "ep", None),
        P("ep", "grp"),
        P("ep", None, "grp"),
        P(),
        P(),
        P(None, "grp", "ep"),
        P("ep", "grp"),
        P(),
        P("ep", None, "grp", None),
        P("ep", None, "grp"),
    )
    return jax.shard_map(local, mesh=mesh, in_specs=in_specs, out_specs=out_specs, check_vma=False)
```

```python
import functools
import math

import jax
import jax.numpy as jnp
from jax import lax
from jax.experimental import pallas as pl
from jax.experimental.pallas import tpu as pltpu
from jax.sharding import PartitionSpec as P

EPS = 1e-06
THETA = 1000000.0
NEGATIVE = -1e30
BF16 = jnp.bfloat16
F32 = jnp.float32
LANES = 128
MIB = 1024 * 1024
KERNEL_COST = pl.CostEstimate(flops=10**6, bytes_accessed=10**5, transcendentals=0)


def dot(lhs, rhs):
    return jnp.dot(lhs, rhs, preferred_element_type=F32)


def dot_nt(lhs, rhs):
    return lax.dot_general(lhs, rhs, (((1,), (1,)), ((), ())), preferred_element_type=F32)


def dot_tn(lhs, rhs):
    return lax.dot_general(lhs, rhs, (((0,), (0,)), ((), ())), preferred_element_type=F32)


class GrpReduce:
    def __init__(self, rows, produce):
        self.rows, self.produce = rows, produce
        self.size = lax.axis_size("grp")
        self.planes = self.size // 2
        mine = lax.axis_index("grp")
        self.core, self.plane = mine % 2, mine // 2
        self.far = [(self.plane + k) % self.planes for k in range(1, self.planes)]

    def to_partner(self, value):
        return lax.ppermute(value, "grp", [(i, i ^ 1) for i in range(self.size)])

    def away(self):
        return [
            self.produce(self.rows, 2 * plane + 1 - self.core).astype(BF16) for plane in self.far
        ]

    def pass_on(self, arrived):
        return [
            (self.produce(self.rows, 2 * plane + self.core) + value.astype(F32)).astype(BF16)
            for plane, value in zip(self.far, arrived)
        ]

    def own(self):
        away = self.produce(self.rows, 2 * self.plane + 1 - self.core).astype(BF16)
        kept = self.produce(self.rows, 2 * self.plane + self.core)
        return kept + self.to_partner(away).astype(F32)


def add_all(value, others):
    value = value.astype(F32)
    for other in others:
        value = value + other.astype(F32)
    return value


def columns_of(array, member):
    size = array.shape[1] // lax.axis_size("grp")
    return lax.dynamic_slice_in_dim(array, member * size, size, 1)


MESH = pl.DeviceIdType.MESH


def ring_places(count):
    here = lax.axis_index("ep")
    if count != 8:
        return here, lambda spot: spot
    x, z = here % 2, here // 2

    def index_at(spot):
        side = spot // 4
        return 2 * (spot + side * (7 - 2 * spot)) + side

    return z + x * (7 - 2 * z), index_at


def slot_index(count, slot):
    place, index_at = ring_places(count)
    offset = jnp.where(slot == count - 1, count // 2, (slot // 2 + 1) * (2 * (slot % 2) - 1))
    offset = jnp.where(slot == count - 2, 0, offset)
    return index_at((place + offset + count) % count)


def when(condition):
    if isinstance(condition, bool):
        return (lambda run: run()) if condition else (lambda run: None)
    return pl.when(condition)


def rows_at(slot, size):
    return pl.ds(pl.multiple_of(slot * size, size), size)


class KernelRing:
    def __init__(self, buffer, count, size, send_sems, recv_sems):
        place, index_at = ring_places(count)
        self.buffer, self.count, self.size = buffer, count, size
        self.half = count // 2
        self.send_sems, self.recv_sems = send_sems, recv_sems
        self.right = index_at((place + 1) % count)
        self.left = index_at((place + count - 1) % count)

    def own(self):
        return slice((self.count - 2) * self.size, (self.count - 1) * self.size)

    def copy(self, source, target, neighbour, step, way):
        return pltpu.make_async_remote_copy(
            src_ref=self.buffer.at[source],
            dst_ref=self.buffer.at[target],
            send_sem=self.send_sems.at[step, way],
            recv_sem=self.recv_sems.at[step, way],
            device_id={"ep": neighbour},
            device_id_type=MESH,
        )

    def sends(self, step):
        before = lax.rem(step + self.half - 1, self.half)
        copies = []
        for way, neighbour in enumerate((self.right, self.left)):
            source = jnp.where(step == 0, self.count - 2, 2 * before + way)
            copies.append(
                self.copy(
                    rows_at(source, self.size), rows_at(2 * step + way, self.size),
                    neighbour, step, way,
                )
            )
        return copies

    def last_sends(self):
        middle = self.size // 2
        copies = []
        for way, neighbour in enumerate((self.right, self.left)):
            source = (self.count - 4 + way) * self.size + way * middle
            target = (self.count - 1) * self.size + way * middle
            copies.append(
                self.copy(
                    pl.ds(source, middle), pl.ds(target, middle), neighbour, self.half - 1, way
                )
            )
        return copies

    def start(self):
        for copy in self.sends(0):
            copy.start()

    def arrive(self, i):
        @when(i < self.half - 1)
        def _():
            for copy in self.sends(i):
                copy.wait_recv()

        @when(i == self.half - 1)
        def _():
            for copy in self.last_sends():
                copy.wait_recv()

    def forward(self, i):
        @when(i < self.half - 2)
        def _():
            for copy in self.sends(i + 1):
                copy.start()

        @when(i == self.half - 2)
        def _():
            for copy in self.last_sends():
                copy.start()

    def finish(self):
        for step in range(self.half - 1):
            for copy in self.sends(step):
                copy.wait_send()
        for copy in self.last_sends():
            copy.wait_send()


class Exchange:
    def __init__(self, count, source_at, target_at, send_sems, recv_sems):
        self.count = count
        self.place, self.index_at = ring_places(count)
        self.source_at, self.target_at = source_at, target_at
        self.send_sems, self.recv_sems = send_sems, recv_sems

    def copy(self, slot):
        way = slot % 2
        far = slot // 2 + 1
        farthest = slot == self.count - 1
        offset = jnp.where(farthest, self.count // 2, far * (2 * way - 1))
        landing = jnp.where(farthest, slot, slot + 1 - 2 * way)
        return pltpu.make_async_remote_copy(
            src_ref=self.source_at(slot),
            dst_ref=self.target_at(landing),
            send_sem=self.send_sems.at[slot],
            recv_sem=self.recv_sems.at[landing],
            device_id={"ep": self.index_at((self.place + offset + self.count) % self.count)},
            device_id_type=MESH,
        )

    def arrived(self, slot):
        return pltpu.make_async_remote_copy(
            src_ref=self.source_at(slot),
            dst_ref=self.target_at(slot),
            send_sem=self.send_sems.at[slot],
            recv_sem=self.recv_sems.at[slot],
            device_id={"ep": self.index_at((self.place + 1) % self.count)},
            device_id_type=MESH,
        )

    def others(self):
        return [slot for slot in range(self.count) if slot != self.count - 2]


class PlaneCopies:
    def __init__(self, sources, targets, planes, sems):
        mine, size = lax.axis_index("grp"), lax.axis_size("grp")
        self.copies = []
        for i, (source, target) in enumerate(zip(sources, targets)):
            shift = 2 * (i % (planes - 1) + 1)
            self.copies.append(
                pltpu.make_async_remote_copy(
                    src_ref=source,
                    dst_ref=target,
                    send_sem=sems.at[0, i],
                    recv_sem=sems.at[1, i],
                    device_id={"grp": (mine + shift) % size},
                    device_id_type=MESH,
                )
            )

    def start(self):
        for copy in self.copies:
            copy.start()

    def finish(self):
        for copy in self.copies:
            copy.wait()


def greet(axis, count):
    barrier = pltpu.get_barrier_semaphore()
    here = lax.axis_index(axis)
    for step in range(1, count):
        pl.semaphore_signal(
            barrier, inc=1, device_id={axis: (here + step) % count}, device_id_type=MESH
        )


def block_rows_of(count):
    return 256 if count % 256 == 0 else 128


def attend_forward_kernel(
    count, grp_count, heads, scale, hidden, first_gain, gain, w, b, segments, row_segments, w_out,
    q_out, k_out, v_out, attended_out, log_out, residual_out, normed_out, cosine, sine, row_starts,
    x_out, w_all_out, row_positions, starts, xs, w_all, received, x_send, x_recv, w_send, w_recv, plane_send, plane_recv, core_send,
    core_recv, hand_send, hand_recv, x_sems, w_sems, own_sem,
):
    size, width = hidden.shape
    half = count // 2
    rows = 2 * size
    dim = LANES
    inner_size = heads * dim
    planes = grp_count // 2
    mine = lax.axis_index("grp")
    core, plane = mine % 2, mine // 2
    part_width = width // grp_count

    own_columns = pl.ds(pl.multiple_of(mine * part_width, part_width), part_width)
    ring_x = KernelRing(xs, count, size, x_send, x_recv)
    ring_w = KernelRing(w_all.at[0], count, inner_size, w_send, w_recv)
    load = pltpu.make_async_copy(
        w_out.at[:, own_columns], w_all.at[0, ring_w.own()], own_sem.at[0]
    )
    load.start()
    greet("ep", count)
    greet("grp", grp_count)
    own_hidden = hidden[...].astype(F32)
    mean = jnp.sum(own_hidden * own_hidden, -1, keepdims=True) * (1.0 / width)
    xs[ring_x.own(), :] = (own_hidden * lax.rsqrt(mean + EPS) * first_gain[...]).astype(BF16)
    pl.semaphore_wait(pltpu.get_barrier_semaphore(), count - 1 + grp_count - 1)
    load.wait()
    ring_w.start()
    ring_x.start()

    for slot in range(count):
        row_positions[:, slot * size : (slot + 1) * size] = slot_index(
            count, slot
        ) * size + lax.broadcasted_iota(jnp.int32, (1, size), 1)
    lane = lax.broadcasted_iota(jnp.int32, (size, dim), 1)
    low_half = lane < dim // 2
    index = jnp.where(low_half, lane, lane - dim // 2).astype(F32)
    inverse = jnp.exp(index * (-2.0 * math.log(THETA) / dim))

    def tables(slot, carry):
        block = slot_index(count, slot)
        here, there = rows_at(slot, size), rows_at(block, size)
        before = jnp.where(row_segments[...] < segments[there, :], 1.0, 0.0)
        start = jnp.sum(before, -1, keepdims=True)
        starts[here, :] = start.astype(jnp.int32)
        own_row = row_segments[:, there]
        before = jnp.where(segments[...] < own_row, 1.0, 0.0)
        row_starts[:, here] = jnp.sum(before, 0, keepdims=True).astype(jnp.int32)
        position = (block * size + lax.broadcasted_iota(jnp.int32, (size, 1), 0)).astype(F32)
        angle = (position - start) * inverse
        cosine[here, :] = jnp.cos(angle)
        sine[here, :] = jnp.where(low_half, -jnp.sin(angle), jnp.sin(angle))
        return carry

    lax.fori_loop(0, count, tables, 0)

    def to_plane(step, i):
        here = rows_at(i, 2 * inner_size)
        landing = (planes - step) % planes
        return pltpu.make_async_remote_copy(
            src_ref=w_all.at[0, here],
            dst_ref=w_all.at[landing, here],
            send_sem=plane_send.at[step - 1, i],
            recv_sem=plane_recv.at[landing - 1, i],
            device_id={"grp": (mine + 2 * step) % grp_count},
            device_id_type=MESH,
        )

    def to_core(j):
        return pltpu.make_async_remote_copy(
            src_ref=w_all.at[j],
            dst_ref=w_all.at[planes + j],
            send_sem=core_send.at[j],
            recv_sem=core_recv.at[j],
            device_id={"grp": mine + 1 - 2 * core},
            device_id_type=MESH,
        )

    def store_x(i):
        here = rows_at(i, rows)
        return pltpu.make_async_copy(xs.at[here], x_out.at[here], x_sems.at[i])

    def store_w(j):
        return pltpu.make_async_copy(w_all.at[j], w_all_out.at[j], w_sems.at[j])

    def project(i, carry):
        here = rows_at(i, rows)
        ring_w.arrive(i)
        ring_w.forward(i)
        for step in range(1, planes):
            to_plane(step, i).start()
        ring_x.arrive(i)
        ring_x.forward(i)
        store_x(i).start()
        projected = dot(xs[here, :], w[...]) + b[...]
        cos, sin = cosine[here, :], sine[here, :]
        for h in range(heads):
            base = 3 * dim * h
            query = projected[:, base : base + dim]
            key = projected[:, base + dim : base + 2 * dim]
            q_out[h, here, :] = (query * cos + pltpu.roll(query, dim // 2, 1) * sin).astype(BF16)
            k_out[h, here, :] = (key * cos + pltpu.roll(key, dim // 2, 1) * sin).astype(BF16)
            v_out[h, here, :] = projected[:, base + 2 * dim : base + 3 * dim].astype(BF16)
        return carry

    lax.fori_loop(0, half, project, 0)
    to_core(0).start()
    store_w(0).start()

    exchange = Exchange(
        count,
        lambda slot: attended_out.at[rows_at(slot, size)],
        lambda slot: received.at[slot],
        hand_send,
        hand_recv,
    )

    def attend(step, carry):
        i = half - 1 - step
        here = rows_at(i, rows)
        count_up = lax.broadcasted_iota(jnp.int32, (size, 1), 0)
        own = jnp.concatenate(
            [slot_index(count, 2 * i + k) * size + count_up for k in range(2)], 0
        )
        start = starts[here, :]
        keys_at = row_positions[...]
        allowed = (keys_at <= own) & (keys_at >= start)
        for h in range(heads):
            scores = dot_nt(q_out[h, here, :], k_out[h]) * scale
            scores = jnp.where(allowed, scores, NEGATIVE)
            highest = jnp.max(scores, -1, keepdims=True)
            expo = jnp.exp(scores - highest)
            total = jnp.sum(expo, -1, keepdims=True)
            weights = (expo * (1.0 / total)).astype(BF16)
            attended_out[here, h * dim : (h + 1) * dim] = dot(weights, v_out[h]).astype(BF16)
            logs = jnp.broadcast_to(highest + jnp.log(total), (rows, LANES))
            log_out[h, :, here] = jnp.transpose(logs)[:1, :]
        exchange.copy(2 * i + 1).start()

        @pl.when(i < half - 1)
        def _():
            exchange.copy(2 * i).start()

        return carry

    lax.fori_loop(0, half, attend, 0)
    received[count - 2] = attended_out[ring_x.own(), :]
    for j in range(1, planes):
        for i in range(half):
            to_plane((planes - j) % planes, i).wait_recv()
        to_core(j).start()
        store_w(j).start()
    for slot in exchange.others():
        exchange.arrived(slot).wait_recv()
    for j in range(planes):
        to_core(j).wait_recv()
        store_w(planes + j).start()
    mixed = jnp.concatenate([received[slot] for slot in range(count)], 1)
    square = jnp.zeros((size, 1), F32)
    for j in range(grp_count):
        member = 2 * ((plane + j % planes) % planes) + (core if j < planes else 1 - core)
        columns = pl.ds(pl.multiple_of(member * part_width, part_width), part_width)
        piece = hidden[:, columns].astype(F32) + dot(mixed, w_all[j])
        residual_out[:, columns] = piece
        square = square + jnp.sum(piece * piece, -1, keepdims=True)
    factor = lax.rsqrt(square * (1.0 / width) + EPS)
    normed_out[...] = (residual_out[...] * factor * gain[...]).astype(BF16)

    for i in range(half):
        store_x(i).wait()
        for step in range(1, planes):
            to_plane(step, i).wait_send()
    for j in range(grp_count):
        store_w(j).wait()
    for j in range(planes):
        to_core(j).wait_send()
    for slot in exchange.others():
        exchange.copy(slot).wait_send()
    ring_x.finish()
    ring_w.finish()


def attend_forward(
    count, grp_count, hidden, first_gain, gain, w, b, w_out, segments, scale
):
    size, width = hidden.shape
    tokens = size * count
    heads = w.shape[1] // (3 * LANES)
    half, planes = count // 2, grp_count // 2
    anywhere = pl.BlockSpec(memory_space=pl.ANY)
    whole = pl.BlockSpec(memory_space=pltpu.VMEM)
    shape = jax.ShapeDtypeStruct
    w_all_shape = (grp_count, count * heads * LANES, width // grp_count)
    dma = pltpu.SemaphoreType.DMA
    return pl.pallas_call(
        functools.partial(attend_forward_kernel, count, grp_count, heads, scale),
        in_specs=[whole] * 7 + [anywhere],
        out_specs=[whole] * 10 + [anywhere] * 2,
        out_shape=(
            shape((heads, tokens, LANES), BF16),
            shape((heads, tokens, LANES), BF16),
            shape((heads, tokens, LANES), BF16),
            shape((tokens, heads * LANES), BF16),
            shape((heads, 1, tokens), F32),
            shape((size, width), F32),
            shape((size, width), BF16),
            shape((tokens, LANES), F32),
            shape((tokens, LANES), F32),
            shape((1, tokens), jnp.int32),
            shape((tokens, width), BF16),
            shape(w_all_shape, BF16),
        ),
        scratch_shapes=[
            pltpu.VMEM((1, tokens), jnp.int32),
            pltpu.VMEM((tokens, 1), jnp.int32),
            pltpu.VMEM((tokens, width), BF16),
            pltpu.VMEM(w_all_shape, BF16),
            pltpu.VMEM((count, size, heads * LANES), BF16),
            dma((half, 2)),
            dma((half, 2)),
            dma((half, 2)),
            dma((half, 2)),
            dma((max(planes - 1, 1), half)),
            dma((max(planes - 1, 1), half)),
            dma((planes,)),
            dma((planes,)),
            dma((count,)),
            dma((count,)),
            dma((half,)),
            dma((grp_count,)),
            dma((1,)),
        ],
        compiler_params=pltpu.CompilerParams(
            collective_id=1, has_side_effects=True, vmem_limit_bytes=56 * MIB
        ),
        cost_estimate=KERNEL_COST,
        name="attend_forward",
    )(hidden, first_gain[None, :], gain[None, :], w, b, segments[:, None], segments[None, :], w_out)


def attend_backward_kernel(
    count, grp_count, heads, scale, g_own, w_all, w, cosine, sine, q, k, v, row_logs, row_starts,
    *refs,
):
    number = (len(refs) - 17) // 2
    bulk, refs = refs[:number], refs[number:]
    g_out, bias_out, branch_out, group_out = refs[:4]
    landed = refs[4 : 4 + number]
    (
        row_positions, positions, g_att, dk, dv, outbox, gs, send_sems, recv_sems, ring_send,
        ring_recv, store_sems, plane_sems,
    ) = refs[4 + number :]
    size, width = g_own.shape
    tokens = size * count
    rows = block_rows_of(tokens)
    dim = LANES
    inner_size = heads * dim
    planes = grp_count // 2
    mine = lax.axis_index("grp")
    core, plane = mine % 2, mine // 2
    part_width = width // grp_count

    ring = KernelRing(gs, count, size, ring_send, ring_recv)

    def store(i):
        here = rows_at(i, 2 * size)
        return pltpu.make_async_copy(gs.at[here], group_out.at[here], store_sems.at[i])

    def next_pair(i):
        ring.arrive(i)
        ring.forward(i)
        store(i).start()

    greet("ep", count)
    greet("grp", grp_count)
    gs[ring.own(), :] = g_own[...]
    pl.semaphore_wait(pltpu.get_barrier_semaphore(), count - 1 + grp_count - 1)
    plane_copies = PlaneCopies(bulk, landed, grp_count // 2, plane_sems)
    ring.start()
    plane_copies.start()
    for slot in range(count):
        first = slot_index(count, slot) * size
        row_positions[:, slot * size : (slot + 1) * size] = first + lax.broadcasted_iota(
            jnp.int32, (1, size), 1
        )
        positions[slot * size : (slot + 1) * size, :] = first + lax.broadcasted_iota(
            jnp.int32, (size, 1), 0
        )
    own_rows = None
    for j in range(grp_count):
        member = 2 * ((plane + j % planes) % planes) + (core if j < planes else 1 - core)
        columns = pl.ds(pl.multiple_of(member * part_width, part_width), part_width)
        piece = dot_nt(g_own[:, columns], w_all[j])
        own_rows = piece if own_rows is None else own_rows + piece
    own_rows = own_rows.astype(BF16)
    for slot in range(count):
        outbox[slot] = own_rows[:, slot * inner_size : (slot + 1) * inner_size]
    exchange = Exchange(
        count,
        lambda slot: outbox.at[slot],
        lambda slot: g_att.at[rows_at(slot, size)],
        send_sems,
        recv_sems,
    )
    for slot in exchange.others():
        exchange.copy(slot).start()
    g_att[(count - 2) * size : (count - 1) * size, :] = outbox[count - 2]
    dk[...] = jnp.zeros_like(dk)
    dv[...] = jnp.zeros_like(dv)
    for slot in exchange.others():
        exchange.arrived(slot).wait_recv()

    def scores_back(i, carry):
        here = rows_at(i, rows)
        own, start = row_positions[:, here], row_starts[:, here]
        keys_at = positions[...]
        allowed = (keys_at <= own) & (keys_at >= start)
        cos, sin = cosine[here, :], sine[here, :]
        for h in range(heads):
            query = q[h, here, :]
            g_block = g_att[here, h * dim : (h + 1) * dim]
            scores = dot_nt(k[h], query) * scale - row_logs[h, :, here]
            weights = jnp.exp(jnp.where(allowed, scores, NEGATIVE))
            g_weights = dot_nt(v[h], g_block)
            inner = jnp.sum(weights * g_weights, 0, keepdims=True)
            g_scores = (weights * (g_weights - inner)).astype(BF16)
            g_query = dot_tn(g_scores, k[h]) * scale
            g_query = g_query * cos - pltpu.roll(g_query, dim // 2, 1) * sin
            g_out[here, 3 * dim * h : 3 * dim * h + dim] = g_query.astype(BF16)
            dk[h] += dot(g_scores, query)
            dv[h] += dot(weights.astype(BF16), g_block)

        @pl.when(i == 0)
        def _():
            next_pair(0)

        @pl.when(i == 2)
        def _():
            next_pair(1)

        return carry

    lax.fori_loop(0, tokens // rows, scores_back, 0)
    bias_out[...] = jnp.zeros_like(bias_out)

    def finish(i, carry):
        here = rows_at(i, rows)
        cos, sin = cosine[here, :], sine[here, :]
        for h in range(heads):
            base = 3 * dim * h
            g_key = dk[h, here, :] * scale
            g_key = g_key * cos - pltpu.roll(g_key, dim // 2, 1) * sin
            g_out[here, base + dim : base + 2 * dim] = g_key.astype(BF16)
            g_out[here, base + 2 * dim : base + 3 * dim] = dv[h, here, :].astype(BF16)
        g_here = g_out[here, :]
        bias_out[...] += jnp.sum(g_here.astype(F32), 0, keepdims=True)
        branch_out[here, :] = dot_nt(g_here, w[...]).astype(BF16)
        return carry

    lax.fori_loop(0, tokens // rows, finish, 0)
    for i in range(2, count // 2):
        next_pair(i)
    for slot in exchange.others():
        exchange.copy(slot).wait_send()
    ring.finish()
    for i in range(count // 2):
        store(i).wait()
    plane_copies.finish()


def attend_backward(
    count, grp_count, g_own, w_all, w, cosine, sine, q, k, v, logs, starts, scale, bulk
):
    size, width = g_own.shape
    heads, tokens, _ = q.shape
    anywhere = pl.BlockSpec(memory_space=pl.ANY)
    whole = pl.BlockSpec(memory_space=pltpu.VMEM)
    shape = jax.ShapeDtypeStruct
    dma = pltpu.SemaphoreType.DMA
    return pl.pallas_call(
        functools.partial(attend_backward_kernel, count, grp_count, heads, scale),
        in_specs=[whole] * 10 + [anywhere] * len(bulk),
        out_specs=[whole] * 3 + [anywhere] * (1 + len(bulk)),
        out_shape=(
            shape((tokens, 3 * LANES * heads), BF16),
            shape((1, 3 * LANES * heads), F32),
            shape((tokens, width), BF16),
            shape((tokens, width), BF16),
            *[shape(value.shape, value.dtype) for value in bulk],
        ),
        scratch_shapes=[
            pltpu.VMEM((1, tokens), jnp.int32),
            pltpu.VMEM((tokens, 1), jnp.int32),
            pltpu.VMEM((tokens, heads * LANES), BF16),
            pltpu.VMEM((heads, tokens, LANES), F32),
            pltpu.VMEM((heads, tokens, LANES), F32),
            pltpu.VMEM((count, size, heads * LANES), BF16),
            pltpu.VMEM((tokens, width), BF16),
            dma((count,)),
            dma((count,)),
            dma((count // 2, 2)),
            dma((count // 2, 2)),
            dma((count // 2,)),
            dma((2, max(len(bulk), 1))),
        ],
        compiler_params=pltpu.CompilerParams(
            collective_id=2, has_side_effects=True, vmem_limit_bytes=56 * MIB
        ),
        cost_estimate=KERNEL_COST,
        name="attend_backward",
    )(
        g_own, w_all, w, cosine, sine, q, k, v,
        logs, starts, *bulk,
    )


def doubling_stages(axes):
    stages = []
    for axis in axes:
        step = lax.axis_size(axis) // 2
        while step:
            stages.append((axis, step))
            step //= 2
    return stages


class Doubling:
    def __init__(self, held, arrived, stages, sems):
        self.held, self.arrived, self.stages, self.sems = held, arrived, stages, sems
        self.place = 0

    def copy(self, k):
        axis, step = self.stages[k]
        here = lax.axis_index(axis)
        return pltpu.make_async_remote_copy(
            src_ref=self.held.at[k],
            dst_ref=self.arrived.at[k],
            send_sem=self.sems.at[0, k],
            recv_sem=self.sems.at[1, k],
            device_id={axis: here + step * (1 - 2 * (here // step % 2))},
            device_id_type=MESH,
        )

    def start(self):
        self.copy(0).start()

    def advance(self):
        k = self.place
        if k < len(self.stages):
            self.copy(k).wait_recv()
            self.held[k + 1] = self.held[k] + self.arrived[k]
            if k + 1 < len(self.stages):
                self.copy(k + 1).start()
            self.place += 1

    def finish(self):
        while self.place < len(self.stages):
            self.advance()
        for k in range(len(self.stages)):
            self.copy(k).wait_send()
        return self.held[len(self.stages)]


class RingSum:
    def __init__(self, count, part, out, to_right, to_left, send_sems, recv_sems):
        place, index_at = ring_places(count)
        self.count, self.half, self.size = count, count // 2, out.shape[0]
        self.part, self.out, self.held = part, out, (to_right, to_left)
        self.send_sems, self.recv_sems = send_sems, recv_sems
        self.neighbours = (
            index_at((place + 1) % count), index_at((place + count - 1) % count)
        )

    def copy(self, step, way):
        held, middle = self.held[way], self.size // 2
        if step == 0:
            source = self.part.at[pl.ds((self.count - 1) * self.size + way * middle, middle)]
            target = held.at[0, pl.ds(way * middle, middle)]
        else:
            source, target = held.at[step - 1], held.at[step]
        return pltpu.make_async_remote_copy(
            src_ref=source,
            dst_ref=target,
            send_sem=self.send_sems.at[step, way],
            recv_sem=self.recv_sems.at[step, way],
            device_id={"ep": self.neighbours[way]},
            device_id_type=MESH,
        )

    def start(self):
        for way in range(2):
            self.copy(0, way).start()

    def advance(self, step):
        middle, part = self.size // 2, self.part
        for way in range(2):
            held = self.held[way]
            first = (2 * (self.half - step) - 1 - way) * self.size
            self.copy(step - 1, way).wait_recv()
            if step == 1:
                here = slice(way * middle, (way + 1) * middle)
                rest = slice((1 - way) * middle, (2 - way) * middle)
                own = part[first + way * middle : first + (way + 1) * middle, :]
                held[0, here] = (own.astype(F32) + held[0, here].astype(F32)).astype(BF16)
                held[0, rest] = part[first + (1 - way) * middle : first + (2 - way) * middle, :]
            else:
                own = part[first : first + self.size, :]
                held[step - 1] = (own.astype(F32) + held[step - 1].astype(F32)).astype(BF16)
            self.copy(step, way).start()

    def last(self):
        own = self.part[(self.count - 2) * self.size : (self.count - 1) * self.size, :]
        total = own.astype(F32)
        for way in range(2):
            self.copy(self.half - 1, way).wait_recv()
            total = total + self.held[way][self.half - 1].astype(F32)
        self.out[...] = total

    def finish(self):
        for step in range(self.half):
            for way in range(2):
                self.copy(step, way).wait_send()


def reduce_kernel(count, grp_count, number, bulk_number, small_axes, *refs):
    refs = list(refs)

    def take(amount):
        taken = refs[:amount]
        del refs[:amount]
        return taken

    small_number = len(small_axes)
    parts, smalls, bulk = take(number), take(small_number), take(bulk_number)
    outs, small_outs, landed = take(number), take(small_number), take(bulk_number)
    to_right, to_left = take(number), take(number)
    small_held, small_arrived = take(small_number), take(small_number)
    send_sems, recv_sems = take(2)
    small_sems = take(small_number)
    (plane_sems,) = take(1)
    greet("ep", count)
    greet("grp", grp_count)
    for held, small in zip(small_held, smalls):
        held[0] = small[...]
    pl.semaphore_wait(pltpu.get_barrier_semaphore(), count - 1 + grp_count - 1)
    rings = [
        RingSum(
            count, parts[a], outs[a], to_right[a], to_left[a], send_sems.at[a], recv_sems.at[a]
        )
        for a in range(number)
    ]
    sums = [
        Doubling(held, arrived, doubling_stages(axes), sems)
        for held, arrived, axes, sems in zip(small_held, small_arrived, small_axes, small_sems)
    ]
    for ring in rings:
        ring.start()
    for item in sums:
        item.start()
    plane_copies = PlaneCopies(bulk, landed, grp_count // 2, plane_sems)
    plane_copies.start()
    for step in range(1, count // 2):
        for ring in rings:
            ring.advance(step)
            for item in sums:
                item.advance()
    for ring in rings:
        ring.last()
    for item, out in zip(sums, small_outs):
        out[...] = item.finish()
    for ring in rings:
        ring.finish()
    plane_copies.finish()


def reduce_rows(count, grp_count, call, parts, smalls=(), small_axes=(), bulk=()):
    tokens, width = parts[0].shape
    size, number, half = tokens // count, len(parts), count // 2
    stages = [len(doubling_stages(axes)) for axes in small_axes]
    anywhere = pl.BlockSpec(memory_space=pl.ANY)
    whole = pl.BlockSpec(memory_space=pltpu.VMEM)
    shape = jax.ShapeDtypeStruct
    dma = pltpu.SemaphoreType.DMA
    results = pl.pallas_call(
        functools.partial(
            reduce_kernel, count, grp_count, number, len(bulk), tuple(small_axes)
        ),
        in_specs=[whole] * (number + len(smalls)) + [anywhere] * len(bulk),
        out_specs=[whole] * (number + len(smalls)) + [anywhere] * len(bulk),
        out_shape=[shape((size, width), F32)] * number
        + [shape(value.shape, value.dtype) for value in (*smalls, *bulk)],
        scratch_shapes=[pltpu.VMEM((half, size, width), BF16)] * (2 * number)
        + [pltpu.VMEM((k + 1, *value.shape), F32) for k, value in zip(stages, smalls)]
        + [pltpu.VMEM((k, *value.shape), F32) for k, value in zip(stages, smalls)]
        + [dma((number, half, 2))] * 2
        + [dma((2, k)) for k in stages]
        + [dma((2, max(len(bulk), 1)))],
        compiler_params=pltpu.CompilerParams(
            collective_id=call, has_side_effects=True, vmem_limit_bytes=56 * MIB
        ),
        cost_estimate=KERNEL_COST,
        name="reduce_rows",
    )(*parts, *smalls, *bulk)
    return (
        results[:number],
        results[number : number + len(smalls)],
        results[number + len(smalls) :],
    )


def reduce_and_weights_kernel(
    count, grp_count, part, x_in, cot_in, grad_e_in, act_e_in, grad_s_in, act_s_in, *refs
):
    refs = list(refs)

    def take(amount):
        taken = refs[:amount]
        del refs[:amount]
        return taken

    planes = grp_count // 2
    (summed,) = take(1)
    outs = [take(planes) for _ in range(4)]
    sources = (x_in, grad_e_in, cot_in, act_e_in, grad_s_in, act_s_in)
    held = take(6)
    x, grad_e, cot, act_e, grad_s, act_s = held
    to_right, to_left = take(2)
    staged, arrived = take(4), take(4)
    send_sems, recv_sems, load_sems, core_send, core_recv, out_sems = take(6)
    mine = lax.axis_index("grp")
    core, plane = mine % 2, mine // 2
    part_width = x.shape[1] // grp_count

    loads = [
        pltpu.make_async_copy(source, target, load_sems.at[i])
        for i, (source, target) in enumerate(zip(sources, held))
    ]
    for load in loads:
        load.start()
    greet("ep", count)
    greet("grp", grp_count)
    pl.semaphore_wait(pltpu.get_barrier_semaphore(), count - 1 + grp_count - 1)
    ring = RingSum(count, part, summed, to_right, to_left, send_sems, recv_sems)
    ring.start()

    def columns(order, side):
        member = 2 * ((plane + order) % planes) + (core if side == 0 else 1 - core)
        return pl.ds(pl.multiple_of(member * part_width, part_width), part_width)

    def products(kind, cut):
        if kind == 0:
            return [dot_tn(x[:, cut], grad_e[k]) for k in range(2)]
        if kind == 1:
            return [dot_tn(act_e[...], cot[:, cut])]
        if kind == 2:
            return [dot_tn(grad_s[k], x[:, cut]) for k in range(2)]
        return [dot_tn(act_s[...], cot[:, cut])]

    def to_core(kind, place):
        return pltpu.make_async_remote_copy(
            src_ref=staged[kind],
            dst_ref=arrived[kind].at[place],
            send_sem=core_send.at[kind, place],
            recv_sem=core_recv.at[kind, place],
            device_id={"grp": mine + 1 - 2 * core},
            device_id_type=MESH,
        )

    def store(kind, place):
        return pltpu.make_async_copy(staged[kind], outs[kind][place], out_sems.at[kind, place])

    orders = list(range(1, planes)) + [0]
    needs = ((0, 1), (2, 3), (4,), (5,))
    ring_step = 1
    number = 0
    for side in (1, 0):
        for place, order in enumerate(orders):
            for kind in range(4):
                if side == 1 and place == 0:
                    for i in needs[kind]:
                        loads[i].wait()
                pieces = products(kind, columns(order, side))
                if side == 1:
                    if place:
                        to_core(kind, place - 1).wait_send()
                else:
                    to_core(kind, place).wait_recv()
                    if place:
                        store(kind, place - 1).wait()
                    else:
                        to_core(kind, planes - 1).wait_send()
                for k, piece in enumerate(pieces):
                    whole = (k,) if len(pieces) > 1 else (Ellipsis,)
                    if side == 0:
                        piece = piece + arrived[kind][(place, *whole)].astype(F32)
                    staged[kind][whole] = piece.astype(BF16)
                if side == 1:
                    to_core(kind, place).start()
                else:
                    store(kind, place).start()
                number += 1
                if number % 4 == 2:
                    if ring_step < count // 2:
                        ring.advance(ring_step)
                    elif ring_step == count // 2:
                        ring.last()
                    ring_step += 1
    while ring_step <= count // 2:
        if ring_step < count // 2:
            ring.advance(ring_step)
        else:
            ring.last()
        ring_step += 1
    for kind in range(4):
        store(kind, planes - 1).wait()
    ring.finish()


def reduce_and_weights(
    count, grp_count, part, x, cot, grad_e, act_e, grad_s, act_s
):
    tokens, width = part.shape
    size, half, planes = tokens // count, count // 2, grp_count // 2
    part_width = width // grp_count
    wide, narrow = act_e.shape[1], act_s.shape[1]
    shapes = [
        (2, part_width, wide), (wide, part_width), (2, narrow, part_width), (narrow, part_width)
    ]
    anywhere = pl.BlockSpec(memory_space=pl.ANY)
    whole = pl.BlockSpec(memory_space=pltpu.VMEM)
    shape = jax.ShapeDtypeStruct
    dma = pltpu.SemaphoreType.DMA
    summed, *slices = pl.pallas_call(
        functools.partial(reduce_and_weights_kernel, count, grp_count),
        in_specs=[whole] + [anywhere] * 6,
        out_specs=[whole] + [anywhere] * (4 * planes),
        out_shape=[shape((size, width), F32)]
        + [shape(dims, BF16) for dims in shapes for _ in range(planes)],
        scratch_shapes=[
            pltpu.VMEM(value.shape, BF16) for value in (x, grad_e, cot, act_e, grad_s, act_s)
        ]
        + [pltpu.VMEM((half, size, width), BF16)] * 2
        + [pltpu.VMEM(dims, BF16) for dims in shapes]
        + [pltpu.VMEM((planes, *dims), BF16) for dims in shapes]
        + [dma((half, 2)), dma((half, 2)), dma((6,))]
        + [dma((4, planes))] * 3,
        compiler_params=pltpu.CompilerParams(
            collective_id=3, has_side_effects=True, vmem_limit_bytes=60 * MIB
        ),
        cost_estimate=KERNEL_COST,
        name="reduce_and_weights",
    )(part, x, cot, grad_e, act_e, grad_s, act_s)
    groups = [slices[i * planes : (i + 1) * planes] for i in range(4)]
    return summed, [group[:-1] for group in groups], [group[-1] for group in groups]


def tiles_of(width):
    tiles, start = [], 0
    while width - start > 384:
        tiles.append((start, 256))
        start += 256
    tiles.append((start, width - start))
    return tiles


def experts_kernel(
    count, expert_count, x_own, cot_own, routes, routes_w, gate_up_e, down_e, gate_up_s, down_s,
    act_e_out, grad_e_out, act_s_out, grad_s_out, part_out, branch_out, logits_out, x_out,
    cot_out,
    xs, cots, gate_e, up_e, held_e, gate_s, up_s, held_s, act_e, grad_e, act_s, grad_s, part,
    branch, logits_held, x_send, x_recv, cot_send, cot_recv, weight_sems, out_sems, x_sems,
):
    half = count // 2
    size = x_own.shape[0]
    rows = 2 * size
    ring_x = KernelRing(xs, count, size, x_send, x_recv)
    ring_cot = KernelRing(cots, count, size, cot_send, cot_recv)

    barrier = pltpu.get_barrier_semaphore()
    for neighbour in (ring_x.left, ring_x.right):
        pl.semaphore_signal(barrier, inc=1, device_id={"ep": neighbour}, device_id_type=MESH)
    loads = [
        pltpu.make_async_copy(source, target, weight_sems.at[i])
        for i, (source, target) in enumerate(
            [
                (gate_up_e.at[0, 0], gate_e),
                (gate_up_e.at[0, 1], up_e),
                (down_e.at[0], held_e),
                (gate_up_s.at[0], gate_s),
                (gate_up_s.at[1], up_s),
                (down_s, held_s),
            ]
        )
    ]
    for load in loads:
        load.start()
    xs[ring_x.own(), :] = x_own[...]
    cots[ring_x.own(), :] = cot_own[...]
    pl.semaphore_wait(barrier, 2)
    ring_x.start()
    ring_cot.start()

    def stores(i):
        here = rows_at(i, rows)
        slot = lax.rem(i, 2)
        pieces = [
            (act_e.at[slot], act_e_out.at[here]),
            (grad_e.at[slot, 0], grad_e_out.at[0, here]),
            (grad_e.at[slot, 1], grad_e_out.at[1, here]),
            (act_s.at[slot], act_s_out.at[here]),
            (grad_s.at[slot, 0], grad_s_out.at[0, here]),
            (grad_s.at[slot, 1], grad_s_out.at[1, here]),
            (part.at[slot], part_out.at[here]),
            (branch.at[slot], branch_out.at[here]),
            (logits_held.at[slot], logits_out.at[here]),
        ]
        return [
            pltpu.make_async_copy(source, target, out_sems.at[slot, k])
            for k, (source, target) in enumerate(pieces)
        ]

    def store_rows(i):
        here = rows_at(i, rows)
        return [
            pltpu.make_async_copy(xs.at[here], x_out.at[here], x_sems.at[0, i]),
            pltpu.make_async_copy(cots.at[here], cot_out.at[here], x_sems.at[1, i]),
        ]

    sections = (
        (gate_e, up_e, held_e, act_e, grad_e, dot, dot_nt),
        (gate_s, up_s, held_s, act_s, grad_s, dot_nt, dot),
    )
    mine = lax.axis_index("ep")
    onehot = (lax.broadcasted_iota(jnp.int32, (1, LANES), 1) == mine).astype(F32)

    def one_pair(i, carry):
        slot = lax.rem(i, 2)
        here = rows_at(i, rows)
        ring_x.arrive(i)
        ring_x.forward(i)
        ring_cot.arrive(i)
        ring_cot.forward(i)
        for copy in store_rows(i):
            copy.start()

        @pl.when(i == 0)
        def _():
            for load in loads:
                load.wait()

        @pl.when(i >= 2)
        def _():
            for copy in stores(i - 2):
                copy.wait()

        lane = lax.broadcasted_iota(jnp.int32, (rows, LANES), 1)
        inputs, cotangent = xs[here, :], cots[here, :]
        logits = dot(inputs, routes_w[...])
        routed = jnp.where(lane < expert_count, logits, NEGATIVE)
        expo = jnp.exp(routed - jnp.max(routed, -1, keepdims=True))
        probs = expo * (1.0 / jnp.sum(expo, -1, keepdims=True))
        named = jnp.concatenate(
            [routes[rows_at(slot_index(count, 2 * i + k), size), :] for k in range(2)], 0
        )
        hits = jnp.sum(jnp.where(named == mine, 1.0, 0.0), -1, keepdims=True)
        own_prob = jnp.sum(probs * onehot, -1, keepdims=True) * hits
        share_logit = jnp.sum(jnp.where(lane == expert_count, logits, 0.0), -1, keepdims=True)
        share = 1.0 / (1.0 + jnp.exp(-share_logit))

        inner = []
        total, out_total = None, None
        for s, (gate_w, up_w, down_w, act_out, grad_out, ahead, back_dot) in enumerate(sections):
            factor = own_prob if s == 0 else share
            dots = jnp.zeros((rows, 1), F32)
            for start, width in tiles_of(down_w.shape[0]):
                cut = pl.ds(start, width)
                piece = (slice(None), cut) if s == 0 else (cut, slice(None))
                gate = ahead(inputs, gate_w[piece])
                up = ahead(inputs, up_w[piece])
                grad = dot_nt(cotangent, down_w[cut, :])
                sigma = 0.5 * jnp.tanh(0.5 * gate) + 0.5
                silu = gate * sigma
                act = (silu * up).astype(BF16).astype(F32)
                dots = dots + jnp.sum(grad * act, -1, keepdims=True)
                scaled = grad * factor
                act_out[slot, :, cut] = (act * factor).astype(BF16)
                grad_out[slot, 0, :, cut] = (
                    scaled * up * (sigma + silu * (1.0 - sigma))
                ).astype(BF16)
                grad_out[slot, 1, :, cut] = (scaled * silu).astype(BF16)
            inner.append(dots)
            back = back_dot(grad_out[slot, 0], gate_w[...]) + back_dot(
                grad_out[slot, 1], up_w[...]
            )
            total = back if total is None else total + back
            out_piece = dot(act_out[slot], down_w[...])
            out_total = out_piece if out_total is None else out_total + out_piece
        branch[slot] = out_total.astype(BF16)
        grad_logits = own_prob * inner[0] * (onehot - probs)
        grad_share = share * (1.0 - share) * inner[1]
        grad_logits = grad_logits + jnp.where(lane == expert_count, grad_share, 0.0)
        high = grad_logits.astype(BF16)
        low = (grad_logits - high.astype(F32)).astype(BF16)
        total = total + dot_nt(high, routes_w[...]) + dot_nt(low, routes_w[...])
        logits_held[slot, :, :LANES] = high
        logits_held[slot, :, LANES:] = low
        part[slot] = total.astype(BF16)
        for copy in stores(i):
            copy.start()
        return carry

    lax.fori_loop(0, half, one_pair, 0)
    for i in range(half):
        for copy in store_rows(i):
            copy.wait()
    for i in range(max(half - 2, 0), half):
        for copy in stores(i):
            copy.wait()
    ring_x.finish()
    ring_cot.finish()


def experts(
    count, expert_count, x_own, cot_own, routes, routes_w, gate_up_e, down_e, gate_up_s, down_s
):
    size, width = x_own.shape
    tokens, rows, half = size * count, 2 * size, count // 2
    wide, narrow = down_e.shape[1], down_s.shape[0]
    anywhere = pl.BlockSpec(memory_space=pl.ANY)
    whole = pl.BlockSpec(memory_space=pltpu.VMEM)
    shape = jax.ShapeDtypeStruct
    dma = pltpu.SemaphoreType.DMA
    return pl.pallas_call(
        functools.partial(experts_kernel, count, expert_count),
        in_specs=[whole] * 4 + [anywhere] * 4,
        out_specs=[anywhere] * 9,
        out_shape=(
            shape((tokens, wide), BF16),
            shape((2, tokens, wide), BF16),
            shape((tokens, narrow), BF16),
            shape((2, tokens, narrow), BF16),
            shape((tokens, width), BF16),
            shape((tokens, width), BF16),
            shape((tokens, 2 * LANES), BF16),
            shape((tokens, width), BF16),
            shape((tokens, width), BF16),
        ),
        scratch_shapes=[
            pltpu.VMEM((tokens, width), BF16),
            pltpu.VMEM((tokens, width), BF16),
            pltpu.VMEM((width, wide), BF16),
            pltpu.VMEM((width, wide), BF16),
            pltpu.VMEM((wide, width), BF16),
            pltpu.VMEM((narrow, width), BF16),
            pltpu.VMEM((narrow, width), BF16),
            pltpu.VMEM((narrow, width), BF16),
            pltpu.VMEM((2, rows, wide), BF16),
            pltpu.VMEM((2, 2, rows, wide), BF16),
            pltpu.VMEM((2, rows, narrow), BF16),
            pltpu.VMEM((2, 2, rows, narrow), BF16),
            pltpu.VMEM((2, rows, width), BF16),
            pltpu.VMEM((2, rows, width), BF16),
            pltpu.VMEM((2, rows, 2 * LANES), BF16),
            dma((half, 2)),
            dma((half, 2)),
            dma((half, 2)),
            dma((half, 2)),
            dma((6,)),
            dma((2, 9)),
            dma((2, half)),
        ],
        compiler_params=pltpu.CompilerParams(
            collective_id=0, has_side_effects=True, vmem_limit_bytes=60 * MIB
        ),
        cost_estimate=KERNEL_COST,
        name="experts",
    )(x_own, cot_own, routes, routes_w, gate_up_e, down_e, gate_up_s, down_s)


def norm_of(values):
    factor = lax.rsqrt(jnp.mean(values * values, -1, keepdims=True) + EPS)
    return values * factor, factor


def norm_back(grad_out, normal, factor, gain):
    scaled = grad_out * gain
    return factor * (scaled - normal * jnp.mean(scaled * normal, -1, keepdims=True))


def local(
    hidden_in, segments, routes, cotangent, norm1_gain, w_qkv, b_qkv, w_out, norm2_gain, router,
    shared_gate_up, shared_down, shared_gate, expert_gate_up, expert_down,
):
    tokens_here, width = hidden_in.shape
    ep_count = lax.axis_size("ep")
    grp_count = lax.axis_size("grp")
    expert_count = router.shape[1]
    heads, qkv_dim = b_qkv.shape
    head_dim = qkv_dim // 3
    scale = 1.0 / math.sqrt(head_dim)
    slice_width = width // grp_count
    routes_w = jnp.concatenate(
        [router, shared_gate[:, None], jnp.zeros((width, LANES - 1 - expert_count), BF16)], 1
    )
    w_flat = w_qkv.reshape(width, heads * qkv_dim)
    b_flat = b_qkv.reshape(1, heads * qkv_dim)
    w_out_flat = w_out.reshape(heads * head_dim, width)

    (
        queries, key_rows, values, attended, logs, residual, normed_two, cosine, sine, starts,
        group_one, w_all,
    ) = attend_forward(
        ep_count, grp_count, hidden_in, norm1_gain, norm2_gain, w_flat, b_flat, w_out_flat,
        segments, scale,
    )

    (
        expert_act, expert_grad, shared_act, shared_grad, part, out_parts, grad_logits,
        group_two, group_cot,
    ) = experts(
        ep_count, expert_count, normed_two, cotangent, routes, routes_w,
        expert_gate_up, expert_down, jnp.swapaxes(shared_gate_up, 1, 2), shared_down,
    )

    def expert_gate_up_grad(rows, member):
        columns = columns_of(rows, member)
        return jnp.stack([dot_tn(columns, expert_grad[k]) for k in range(2)], 0)

    def shared_gate_up_grad(rows, member):
        columns = columns_of(rows, member)
        return jnp.stack([dot_tn(shared_grad[k], columns) for k in range(2)], 0)

    def down_grad(act):
        return lambda rows, member: dot_tn(act, columns_of(rows, member))

    normal_two, factor_two = norm_of(residual)
    grad_y = cotangent.astype(F32)
    if ep_count == 8:
        grad_normed_two, passed, sums_own = reduce_and_weights(
            ep_count, grp_count, part, group_two, group_cot, expert_grad, expert_act,
            shared_grad, shared_act,
        )
    else:
        sums = [
            GrpReduce(group_two, expert_gate_up_grad),
            GrpReduce(group_cot, down_grad(expert_act)),
            GrpReduce(group_two, shared_gate_up_grad),
            GrpReduce(group_cot, down_grad(shared_act)),
        ]
        arrived = [[item.to_partner(value) for value in item.away()] for item in sums]
        passed = [item.pass_on(values_) for item, values_ in zip(sums, arrived)]
        sums_own = [item.own() for item in sums]
        (grad_normed_two,), _, _ = reduce_rows(ep_count, grp_count, 3, [part])
    grad_residual = grad_y + norm_back(grad_normed_two, normal_two, factor_two, norm2_gain)
    grad_norm2 = jnp.sum(grad_normed_two * normal_two, 0)
    own_attn = grad_residual.astype(BF16)
    each = grp_count // 2 - 1

    grad_qkv, grad_bias, grad_branch, group_attn, *landed = attend_backward(
        ep_count, grp_count, own_attn, w_all, w_flat, cosine, sine, queries, key_rows, values,
        logs, starts, scale, passed[0],
    )
    from_planes = [landed]
    inners = []

    def w_qkv_grad(rows, member):
        piece = dot_tn(columns_of(rows, member), grad_qkv)
        start = member * slice_width
        weights = lax.dynamic_slice_in_dim(w_flat, start, slice_width, 0).astype(F32)
        place = (jnp.arange(grp_count) == member).astype(F32)
        inners.append(place[:, None] * jnp.sum(weights * piece, -1)[None, :])
        return piece

    more = [
        GrpReduce(group_one, w_qkv_grad),
        GrpReduce(group_attn, lambda rows, member: dot_tn(attended, columns_of(rows, member))),
    ]
    aways = [item.away() for item in more]
    arrived = [[item.to_partner(v) for v in values_] for item, values_ in zip(more, aways)]
    more_passed = [item.pass_on(values_) for item, values_ in zip(more, arrived)]
    more_own = [item.own() for item in more]
    grad_routes = dot_tn(grad_logits, group_two)
    grad_routes = grad_routes[: expert_count + 1] + grad_routes[LANES : LANES + expert_count + 1]
    grad_norm1 = sum(inners).reshape(width)
    small = jnp.concatenate([grad_norm2[None], (grad_norm1 / norm1_gain)[None], grad_routes], 0)
    bulk = [value for values_ in passed[1:] for value in values_]
    (grad_normed_one, out_sum), (small, bias_total), landed = reduce_rows(
        ep_count, grp_count, 4, [grad_branch, out_parts], [small, grad_bias],
        [("grp", "ep"), ("grp",)], bulk + [value for values_ in more_passed for value in values_],
    )
    from_planes += [landed[i * each : (i + 1) * each] for i in range(5)]
    layer_out = (residual + out_sum).astype(BF16)
    normal_one, factor_one = norm_of(hidden_in.astype(F32))
    grad_x = grad_residual + norm_back(grad_normed_one, normal_one, factor_one, norm1_gain)

    (
        grad_expert_gate_up, grad_expert_down, grad_shared_gate_up, grad_shared_down,
        grad_w_qkv, grad_w_out,
    ) = [
        add_all(own, values_)
        for own, values_ in zip(sums_own + more_own, from_planes)
    ]
    bias_total = bias_total.reshape(heads, grp_count, qkv_dim // grp_count)
    grad_b = lax.dynamic_index_in_dim(bias_total, lax.axis_index("grp"), 1, keepdims=False)
    grad_shared_gate_up = jnp.swapaxes(grad_shared_gate_up, 1, 2)

    return (
        layer_out,
        grad_x,
        small[1],
        grad_w_qkv.reshape(slice_width, heads, qkv_dim),
        grad_b,
        grad_w_out.reshape(heads, head_dim, slice_width),
        small[0],
        small[2 : expert_count + 2].T,
        grad_shared_gate_up,
        grad_shared_down,
        small[expert_count + 2],
        grad_expert_gate_up[None],
        grad_expert_down[None],
    )


def solution(mesh):
    in_specs = (
        P(("grp", "ep"), None),
        P("grp"),
        P("grp", None),
        P(("grp", "ep"), None),
        P(),
        P(None, "ep", None),
        P("ep", None),
        P("ep", None, None),
        P(),
        P(),
        P(None, None, "ep"),
        P("ep", None),
        P(),
        P("ep", None, None, None),
        P("ep", None, None),
    )
    out_specs = (
        P(("grp", "ep"), None),
        P(("grp", "ep"), None),
        P(),
        P("grp", "ep", None),
        P("ep", "grp"),
        P("ep", None, "grp"),
        P(),
        P(),
        P(None, "grp", "ep"),
        P("ep", "grp"),
        P(),
        P("ep", None, "grp", None),
        P("ep", None, "grp"),
    )
    return jax.shard_map(local, mesh=mesh, in_specs=in_specs, out_specs=out_specs, check_vma=False)
```

```python
import functools
import math

import jax
import jax.numpy as jnp
from jax import lax
from jax.experimental import pallas as pl
from jax.experimental.pallas import tpu as pltpu
from jax.sharding import PartitionSpec as P

EPS = 1e-06
THETA = 1000000.0
NEGATIVE = -1e30
BF16 = jnp.bfloat16
F32 = jnp.float32
LANES = 128
MIB = 1024 * 1024
KERNEL_COST = pl.CostEstimate(flops=10**6, bytes_accessed=10**5, transcendentals=0)


def dot(lhs, rhs):
    return jnp.dot(lhs, rhs, preferred_element_type=F32)


def dot_nt(lhs, rhs):
    return lax.dot_general(lhs, rhs, (((1,), (1,)), ((), ())), preferred_element_type=F32)


def dot_tn(lhs, rhs):
    return lax.dot_general(lhs, rhs, (((0,), (0,)), ((), ())), preferred_element_type=F32)


class GrpReduce:
    def __init__(self, rows, produce):
        self.rows, self.produce = rows, produce
        self.size = lax.axis_size("grp")
        self.planes = self.size // 2
        mine = lax.axis_index("grp")
        self.core, self.plane = mine % 2, mine // 2
        self.far = [(self.plane + k) % self.planes for k in range(1, self.planes)]

    def to_partner(self, value):
        return lax.ppermute(value, "grp", [(i, i ^ 1) for i in range(self.size)])

    def away(self):
        return [
            self.produce(self.rows, 2 * plane + 1 - self.core).astype(BF16) for plane in self.far
        ]

    def pass_on(self, arrived):
        return [
            (self.produce(self.rows, 2 * plane + self.core) + value.astype(F32)).astype(BF16)
            for plane, value in zip(self.far, arrived)
        ]

    def own(self):
        away = self.produce(self.rows, 2 * self.plane + 1 - self.core).astype(BF16)
        kept = self.produce(self.rows, 2 * self.plane + self.core)
        return kept + self.to_partner(away).astype(F32)


def add_all(value, others):
    value = value.astype(F32)
    for other in others:
        value = value + other.astype(F32)
    return value


def columns_of(array, member):
    size = array.shape[1] // lax.axis_size("grp")
    return lax.dynamic_slice_in_dim(array, member * size, size, 1)


MESH = pl.DeviceIdType.MESH


def ring_places(count):
    here = lax.axis_index("ep")
    if count != 8:
        return here, lambda spot: spot
    x, z = here % 2, here // 2

    def index_at(spot):
        side = spot // 4
        return 2 * (spot + side * (7 - 2 * spot)) + side

    return z + x * (7 - 2 * z), index_at


def slot_index(count, slot):
    place, index_at = ring_places(count)
    offset = jnp.where(slot == count - 1, count // 2, (slot // 2 + 1) * (2 * (slot % 2) - 1))
    offset = jnp.where(slot == count - 2, 0, offset)
    return index_at((place + offset + count) % count)


def when(condition):
    if isinstance(condition, bool):
        return (lambda run: run()) if condition else (lambda run: None)
    return pl.when(condition)


def rows_at(slot, size):
    return pl.ds(pl.multiple_of(slot * size, size), size)


class KernelRing:
    def __init__(self, buffer, count, size, send_sems, recv_sems):
        place, index_at = ring_places(count)
        self.buffer, self.count, self.size = buffer, count, size
        self.half = count // 2
        self.send_sems, self.recv_sems = send_sems, recv_sems
        self.right = index_at((place + 1) % count)
        self.left = index_at((place + count - 1) % count)

    def own(self):
        return slice((self.count - 2) * self.size, (self.count - 1) * self.size)

    def copy(self, source, target, neighbour, step, way):
        return pltpu.make_async_remote_copy(
            src_ref=self.buffer.at[source],
            dst_ref=self.buffer.at[target],
            send_sem=self.send_sems.at[step, way],
            recv_sem=self.recv_sems.at[step, way],
            device_id={"ep": neighbour},
            device_id_type=MESH,
        )

    def sends(self, step):
        before = lax.rem(step + self.half - 1, self.half)
        copies = []
        for way, neighbour in enumerate((self.right, self.left)):
            source = jnp.where(step == 0, self.count - 2, 2 * before + way)
            copies.append(
                self.copy(
                    rows_at(source, self.size), rows_at(2 * step + way, self.size),
                    neighbour, step, way,
                )
            )
        return copies

    def last_sends(self):
        middle = self.size // 2
        copies = []
        for way, neighbour in enumerate((self.right, self.left)):
            source = (self.count - 4 + way) * self.size + way * middle
            target = (self.count - 1) * self.size + way * middle
            copies.append(
                self.copy(
                    pl.ds(source, middle), pl.ds(target, middle), neighbour, self.half - 1, way
                )
            )
        return copies

    def start(self):
        for copy in self.sends(0):
            copy.start()

    def arrive(self, i):
        @when(i < self.half - 1)
        def _():
            for copy in self.sends(i):
                copy.wait_recv()

        @when(i == self.half - 1)
        def _():
            for copy in self.last_sends():
                copy.wait_recv()

    def forward(self, i):
        @when(i < self.half - 2)
        def _():
            for copy in self.sends(i + 1):
                copy.start()

        @when(i == self.half - 2)
        def _():
            for copy in self.last_sends():
                copy.start()

    def finish(self):
        for step in range(self.half - 1):
            for copy in self.sends(step):
                copy.wait_send()
        for copy in self.last_sends():
            copy.wait_send()


class Exchange:
    def __init__(self, count, source_at, target_at, send_sems, recv_sems):
        self.count = count
        self.place, self.index_at = ring_places(count)
        self.source_at, self.target_at = source_at, target_at
        self.send_sems, self.recv_sems = send_sems, recv_sems

    def copy(self, slot):
        way = slot % 2
        far = slot // 2 + 1
        farthest = slot == self.count - 1
        offset = jnp.where(farthest, self.count // 2, far * (2 * way - 1))
        landing = jnp.where(farthest, slot, slot + 1 - 2 * way)
        return pltpu.make_async_remote_copy(
            src_ref=self.source_at(slot),
            dst_ref=self.target_at(landing),
            send_sem=self.send_sems.at[slot],
            recv_sem=self.recv_sems.at[landing],
            device_id={"ep": self.index_at((self.place + offset + self.count) % self.count)},
            device_id_type=MESH,
        )

    def arrived(self, slot):
        return pltpu.make_async_remote_copy(
            src_ref=self.source_at(slot),
            dst_ref=self.target_at(slot),
            send_sem=self.send_sems.at[slot],
            recv_sem=self.recv_sems.at[slot],
            device_id={"ep": self.index_at((self.place + 1) % self.count)},
            device_id_type=MESH,
        )

    def others(self):
        return [slot for slot in range(self.count) if slot != self.count - 2]


class PlaneCopies:
    def __init__(self, sources, targets, planes, sems):
        mine, size = lax.axis_index("grp"), lax.axis_size("grp")
        self.copies = []
        for i, (source, target) in enumerate(zip(sources, targets)):
            shift = 2 * (i % (planes - 1) + 1)
            self.copies.append(
                pltpu.make_async_remote_copy(
                    src_ref=source,
                    dst_ref=target,
                    send_sem=sems.at[0, i],
                    recv_sem=sems.at[1, i],
                    device_id={"grp": (mine + shift) % size},
                    device_id_type=MESH,
                )
            )

    def start(self):
        for copy in self.copies:
            copy.start()

    def finish(self):
        for copy in self.copies:
            copy.wait()


def greet(axis, count):
    barrier = pltpu.get_barrier_semaphore()
    here = lax.axis_index(axis)
    for step in range(1, count):
        pl.semaphore_signal(
            barrier, inc=1, device_id={axis: (here + step) % count}, device_id_type=MESH
        )


def block_rows_of(count):
    return 256 if count % 256 == 0 else 128


def attend_forward_kernel(
    count, grp_count, heads, scale, hidden, first_gain, gain, w, b, segments, row_segments, w_out,
    q_out, k_out, v_out, attended_out, log_out, residual_out, normed_out, cosine, sine, row_starts,
    x_out, w_all_out, row_positions, starts, xs, w_all, received, x_send, x_recv, w_send, w_recv, plane_send, plane_recv, core_send,
    core_recv, hand_send, hand_recv, x_sems, w_sems, own_sem,
):
    size, width = hidden.shape
    half = count // 2
    rows = 2 * size
    dim = LANES
    inner_size = heads * dim
    planes = grp_count // 2
    mine = lax.axis_index("grp")
    core, plane = mine % 2, mine // 2
    part_width = width // grp_count

    own_columns = pl.ds(pl.multiple_of(mine * part_width, part_width), part_width)
    ring_x = KernelRing(xs, count, size, x_send, x_recv)
    ring_w = KernelRing(w_all.at[0], count, inner_size, w_send, w_recv)
    load = pltpu.make_async_copy(
        w_out.at[:, own_columns], w_all.at[0, ring_w.own()], own_sem.at[0]
    )
    load.start()
    greet("ep", count)
    greet("grp", grp_count)
    own_hidden = hidden[...].astype(F32)
    mean = jnp.sum(own_hidden * own_hidden, -1, keepdims=True) * (1.0 / width)
    xs[ring_x.own(), :] = (own_hidden * lax.rsqrt(mean + EPS) * first_gain[...]).astype(BF16)
    pl.semaphore_wait(pltpu.get_barrier_semaphore(), count - 1 + grp_count - 1)
    load.wait()
    ring_w.start()
    ring_x.start()

    for slot in range(count):
        row_positions[:, slot * size : (slot + 1) * size] = slot_index(
            count, slot
        ) * size + lax.broadcasted_iota(jnp.int32, (1, size), 1)
    lane = lax.broadcasted_iota(jnp.int32, (size, dim), 1)
    low_half = lane < dim // 2
    index = jnp.where(low_half, lane, lane - dim // 2).astype(F32)
    inverse = jnp.exp(index * (-2.0 * math.log(THETA) / dim))

    def tables(slot, carry):
        block = slot_index(count, slot)
        here, there = rows_at(slot, size), rows_at(block, size)
        before = jnp.where(row_segments[...] < segments[there, :], 1.0, 0.0)
        start = jnp.sum(before, -1, keepdims=True)
        starts[here, :] = start.astype(jnp.int32)
        own_row = row_segments[:, there]
        before = jnp.where(segments[...] < own_row, 1.0, 0.0)
        row_starts[:, here] = jnp.sum(before, 0, keepdims=True).astype(jnp.int32)
        position = (block * size + lax.broadcasted_iota(jnp.int32, (size, 1), 0)).astype(F32)
        angle = (position - start) * inverse
        cosine[here, :] = jnp.cos(angle)
        sine[here, :] = jnp.where(low_half, -jnp.sin(angle), jnp.sin(angle))
        return carry

    lax.fori_loop(0, count, tables, 0)

    def to_plane(step, i):
        here = rows_at(i, 2 * inner_size)
        landing = (planes - step) % planes
        return pltpu.make_async_remote_copy(
            src_ref=w_all.at[0, here],
            dst_ref=w_all.at[landing, here],
            send_sem=plane_send.at[step - 1, i],
            recv_sem=plane_recv.at[landing - 1, i],
            device_id={"grp": (mine + 2 * step) % grp_count},
            device_id_type=MESH,
        )

    def to_core(j):
        return pltpu.make_async_remote_copy(
            src_ref=w_all.at[j],
            dst_ref=w_all.at[planes + j],
            send_sem=core_send.at[j],
            recv_sem=core_recv.at[j],
            device_id={"grp": mine + 1 - 2 * core},
            device_id_type=MESH,
        )

    def store_x(i):
        here = rows_at(i, rows)
        return pltpu.make_async_copy(xs.at[here], x_out.at[here], x_sems.at[i])

    def store_w(j):
        return pltpu.make_async_copy(w_all.at[j], w_all_out.at[j], w_sems.at[j])

    def project(i, carry):
        here = rows_at(i, rows)
        ring_w.arrive(i)
        ring_w.forward(i)
        for step in range(1, planes):
            to_plane(step, i).start()
        ring_x.arrive(i)
        ring_x.forward(i)
        store_x(i).start()
        projected = dot(xs[here, :], w[...]) + b[...]
        cos, sin = cosine[here, :], sine[here, :]
        for h in range(heads):
            base = 3 * dim * h
            query = projected[:, base : base + dim]
            key = projected[:, base + dim : base + 2 * dim]
            q_out[h, here, :] = (query * cos + pltpu.roll(query, dim // 2, 1) * sin).astype(BF16)
            k_out[h, here, :] = (key * cos + pltpu.roll(key, dim // 2, 1) * sin).astype(BF16)
            v_out[h, here, :] = projected[:, base + 2 * dim : base + 3 * dim].astype(BF16)
        return carry

    lax.fori_loop(0, half, project, 0)
    to_core(0).start()
    store_w(0).start()

    exchange = Exchange(
        count,
        lambda slot: attended_out.at[rows_at(slot, size)],
        lambda slot: received.at[slot],
        hand_send,
        hand_recv,
    )

    def attend(step, carry):
        i = half - 1 - step
        here = rows_at(i, rows)
        count_up = lax.broadcasted_iota(jnp.int32, (size, 1), 0)
        own = jnp.concatenate(
            [slot_index(count, 2 * i + k) * size + count_up for k in range(2)], 0
        )
        start = starts[here, :]
        keys_at = row_positions[...]
        allowed = (keys_at <= own) & (keys_at >= start)
        for h in range(heads):
            scores = dot_nt(q_out[h, here, :], k_out[h]) * scale
            scores = jnp.where(allowed, scores, NEGATIVE)
            highest = jnp.max(scores, -1, keepdims=True)
            expo = jnp.exp(scores - highest)
            total = jnp.sum(expo, -1, keepdims=True)
            weights = (expo * (1.0 / total)).astype(BF16)
            attended_out[here, h * dim : (h + 1) * dim] = dot(weights, v_out[h]).astype(BF16)
            logs = jnp.broadcast_to(highest + jnp.log(total), (rows, LANES))
            log_out[h, :, here] = jnp.transpose(logs)[:1, :]
        exchange.copy(2 * i + 1).start()

        @pl.when(i < half - 1)
        def _():
            exchange.copy(2 * i).start()

        return carry

    lax.fori_loop(0, half, attend, 0)
    received[count - 2] = attended_out[ring_x.own(), :]
    for j in range(1, planes):
        for i in range(half):
            to_plane((planes - j) % planes, i).wait_recv()
        to_core(j).start()
        store_w(j).start()
    for slot in exchange.others():
        exchange.arrived(slot).wait_recv()
    for j in range(planes):
        to_core(j).wait_recv()
        store_w(planes + j).start()
    mixed = jnp.concatenate([received[slot] for slot in range(count)], 1)
    square = jnp.zeros((size, 1), F32)
    for j in range(grp_count):
        member = 2 * ((plane + j % planes) % planes) + (core if j < planes else 1 - core)
        columns = pl.ds(pl.multiple_of(member * part_width, part_width), part_width)
        piece = hidden[:, columns].astype(F32) + dot(mixed, w_all[j])
        residual_out[:, columns] = piece
        square = square + jnp.sum(piece * piece, -1, keepdims=True)
    factor = lax.rsqrt(square * (1.0 / width) + EPS)
    normed_out[...] = (residual_out[...] * factor * gain[...]).astype(BF16)

    for i in range(half):
        store_x(i).wait()
        for step in range(1, planes):
            to_plane(step, i).wait_send()
    for j in range(grp_count):
        store_w(j).wait()
    for j in range(planes):
        to_core(j).wait_send()
    for slot in exchange.others():
        exchange.copy(slot).wait_send()
    ring_x.finish()
    ring_w.finish()


def attend_forward(
    count, grp_count, hidden, first_gain, gain, w, b, w_out, segments, scale
):
    size, width = hidden.shape
    tokens = size * count
    heads = w.shape[1] // (3 * LANES)
    half, planes = count // 2, grp_count // 2
    anywhere = pl.BlockSpec(memory_space=pl.ANY)
    whole = pl.BlockSpec(memory_space=pltpu.VMEM)
    shape = jax.ShapeDtypeStruct
    w_all_shape = (grp_count, count * heads * LANES, width // grp_count)
    dma = pltpu.SemaphoreType.DMA
    return pl.pallas_call(
        functools.partial(attend_forward_kernel, count, grp_count, heads, scale),
        in_specs=[whole] * 7 + [anywhere],
        out_specs=[whole] * 10 + [anywhere] * 2,
        out_shape=(
            shape((heads, tokens, LANES), BF16),
            shape((heads, tokens, LANES), BF16),
            shape((heads, tokens, LANES), BF16),
            shape((tokens, heads * LANES), BF16),
            shape((heads, 1, tokens), F32),
            shape((size, width), F32),
            shape((size, width), BF16),
            shape((tokens, LANES), F32),
            shape((tokens, LANES), F32),
            shape((1, tokens), jnp.int32),
            shape((tokens, width), BF16),
            shape(w_all_shape, BF16),
        ),
        scratch_shapes=[
            pltpu.VMEM((1, tokens), jnp.int32),
            pltpu.VMEM((tokens, 1), jnp.int32),
            pltpu.VMEM((tokens, width), BF16),
            pltpu.VMEM(w_all_shape, BF16),
            pltpu.VMEM((count, size, heads * LANES), BF16),
            dma((half, 2)),
            dma((half, 2)),
            dma((half, 2)),
            dma((half, 2)),
            dma((max(planes - 1, 1), half)),
            dma((max(planes - 1, 1), half)),
            dma((planes,)),
            dma((planes,)),
            dma((count,)),
            dma((count,)),
            dma((half,)),
            dma((grp_count,)),
            dma((1,)),
        ],
        compiler_params=pltpu.CompilerParams(
            collective_id=1, has_side_effects=True, vmem_limit_bytes=56 * MIB
        ),
        cost_estimate=KERNEL_COST,
        name="attend_forward",
    )(hidden, first_gain[None, :], gain[None, :], w, b, segments[:, None], segments[None, :], w_out)


def attend_backward_kernel(
    count, grp_count, heads, scale, g_own, w_all, w, cosine, sine, q, k, v, row_logs, row_starts,
    *refs,
):
    number = (len(refs) - 17) // 2
    bulk, refs = refs[:number], refs[number:]
    g_out, bias_out, branch_out, group_out = refs[:4]
    landed = refs[4 : 4 + number]
    (
        row_positions, positions, g_att, dk, dv, outbox, gs, send_sems, recv_sems, ring_send,
        ring_recv, store_sems, plane_sems,
    ) = refs[4 + number :]
    size, width = g_own.shape
    tokens = size * count
    rows = block_rows_of(tokens)
    dim = LANES
    inner_size = heads * dim
    planes = grp_count // 2
    mine = lax.axis_index("grp")
    core, plane = mine % 2, mine // 2
    part_width = width // grp_count

    ring = KernelRing(gs, count, size, ring_send, ring_recv)

    def store(i):
        here = rows_at(i, 2 * size)
        return pltpu.make_async_copy(gs.at[here], group_out.at[here], store_sems.at[i])

    def next_pair(i):
        ring.arrive(i)
        ring.forward(i)
        store(i).start()

    greet("ep", count)
    greet("grp", grp_count)
    gs[ring.own(), :] = g_own[...]
    pl.semaphore_wait(pltpu.get_barrier_semaphore(), count - 1 + grp_count - 1)
    plane_copies = PlaneCopies(bulk, landed, grp_count // 2, plane_sems)
    ring.start()
    plane_copies.start()
    for slot in range(count):
        first = slot_index(count, slot) * size
        row_positions[:, slot * size : (slot + 1) * size] = first + lax.broadcasted_iota(
            jnp.int32, (1, size), 1
        )
        positions[slot * size : (slot + 1) * size, :] = first + lax.broadcasted_iota(
            jnp.int32, (size, 1), 0
        )
    own_rows = None
    for j in range(grp_count):
        member = 2 * ((plane + j % planes) % planes) + (core if j < planes else 1 - core)
        columns = pl.ds(pl.multiple_of(member * part_width, part_width), part_width)
        piece = dot_nt(g_own[:, columns], w_all[j])
        own_rows = piece if own_rows is None else own_rows + piece
    own_rows = own_rows.astype(BF16)
    for slot in range(count):
        outbox[slot] = own_rows[:, slot * inner_size : (slot + 1) * inner_size]
    exchange = Exchange(
        count,
        lambda slot: outbox.at[slot],
        lambda slot: g_att.at[rows_at(slot, size)],
        send_sems,
        recv_sems,
    )
    for slot in exchange.others():
        exchange.copy(slot).start()
    g_att[(count - 2) * size : (count - 1) * size, :] = outbox[count - 2]
    dk[...] = jnp.zeros_like(dk)
    dv[...] = jnp.zeros_like(dv)
    for slot in exchange.others():
        exchange.arrived(slot).wait_recv()

    def scores_back(i, carry):
        here = rows_at(i, rows)
        own, start = row_positions[:, here], row_starts[:, here]
        keys_at = positions[...]
        allowed = (keys_at <= own) & (keys_at >= start)
        cos, sin = cosine[here, :], sine[here, :]
        for h in range(heads):
            query = q[h, here, :]
            g_block = g_att[here, h * dim : (h + 1) * dim]
            scores = dot_nt(k[h], query) * scale - row_logs[h, :, here]
            weights = jnp.exp(jnp.where(allowed, scores, NEGATIVE))
            g_weights = dot_nt(v[h], g_block)
            inner = jnp.sum(weights * g_weights, 0, keepdims=True)
            g_scores = (weights * (g_weights - inner)).astype(BF16)
            g_query = dot_tn(g_scores, k[h]) * scale
            g_query = g_query * cos - pltpu.roll(g_query, dim // 2, 1) * sin
            g_out[here, 3 * dim * h : 3 * dim * h + dim] = g_query.astype(BF16)
            dk[h] += dot(g_scores, query)
            dv[h] += dot(weights.astype(BF16), g_block)

        @pl.when(i == 0)
        def _():
            next_pair(0)

        @pl.when(i == 2)
        def _():
            next_pair(1)

        return carry

    lax.fori_loop(0, tokens // rows, scores_back, 0)
    bias_out[...] = jnp.zeros_like(bias_out)

    def finish(i, carry):
        here = rows_at(i, rows)
        cos, sin = cosine[here, :], sine[here, :]
        for h in range(heads):
            base = 3 * dim * h
            g_key = dk[h, here, :] * scale
            g_key = g_key * cos - pltpu.roll(g_key, dim // 2, 1) * sin
            g_out[here, base + dim : base + 2 * dim] = g_key.astype(BF16)
            g_out[here, base + 2 * dim : base + 3 * dim] = dv[h, here, :].astype(BF16)
        g_here = g_out[here, :]
        bias_out[...] += jnp.sum(g_here.astype(F32), 0, keepdims=True)
        branch_out[here, :] = dot_nt(g_here, w[...]).astype(BF16)
        return carry

    lax.fori_loop(0, tokens // rows, finish, 0)
    for i in range(2, count // 2):
        next_pair(i)
    for slot in exchange.others():
        exchange.copy(slot).wait_send()
    ring.finish()
    for i in range(count // 2):
        store(i).wait()
    plane_copies.finish()


def attend_backward(
    count, grp_count, g_own, w_all, w, cosine, sine, q, k, v, logs, starts, scale, bulk
):
    size, width = g_own.shape
    heads, tokens, _ = q.shape
    anywhere = pl.BlockSpec(memory_space=pl.ANY)
    whole = pl.BlockSpec(memory_space=pltpu.VMEM)
    shape = jax.ShapeDtypeStruct
    dma = pltpu.SemaphoreType.DMA
    return pl.pallas_call(
        functools.partial(attend_backward_kernel, count, grp_count, heads, scale),
        in_specs=[whole] * 10 + [anywhere] * len(bulk),
        out_specs=[whole] * 3 + [anywhere] * (1 + len(bulk)),
        out_shape=(
            shape((tokens, 3 * LANES * heads), BF16),
            shape((1, 3 * LANES * heads), F32),
            shape((tokens, width), BF16),
            shape((tokens, width), BF16),
            *[shape(value.shape, value.dtype) for value in bulk],
        ),
        scratch_shapes=[
            pltpu.VMEM((1, tokens), jnp.int32),
            pltpu.VMEM((tokens, 1), jnp.int32),
            pltpu.VMEM((tokens, heads * LANES), BF16),
            pltpu.VMEM((heads, tokens, LANES), F32),
            pltpu.VMEM((heads, tokens, LANES), F32),
            pltpu.VMEM((count, size, heads * LANES), BF16),
            pltpu.VMEM((tokens, width), BF16),
            dma((count,)),
            dma((count,)),
            dma((count // 2, 2)),
            dma((count // 2, 2)),
            dma((count // 2,)),
            dma((2, max(len(bulk), 1))),
        ],
        compiler_params=pltpu.CompilerParams(
            collective_id=2, has_side_effects=True, vmem_limit_bytes=56 * MIB
        ),
        cost_estimate=KERNEL_COST,
        name="attend_backward",
    )(
        g_own, w_all, w, cosine, sine, q, k, v,
        logs, starts, *bulk,
    )


def doubling_stages(axes):
    stages = []
    for axis in axes:
        step = lax.axis_size(axis) // 2
        while step:
            stages.append((axis, step))
            step //= 2
    return stages


class Doubling:
    def __init__(self, held, arrived, stages, sems):
        self.held, self.arrived, self.stages, self.sems = held, arrived, stages, sems
        self.place = 0

    def copy(self, k):
        axis, step = self.stages[k]
        here = lax.axis_index(axis)
        return pltpu.make_async_remote_copy(
            src_ref=self.held.at[k],
            dst_ref=self.arrived.at[k],
            send_sem=self.sems.at[0, k],
            recv_sem=self.sems.at[1, k],
            device_id={axis: here + step * (1 - 2 * (here // step % 2))},
            device_id_type=MESH,
        )

    def start(self):
        self.copy(0).start()

    def advance(self):
        k = self.place
        if k < len(self.stages):
            self.copy(k).wait_recv()
            self.held[k + 1] = self.held[k] + self.arrived[k]
            if k + 1 < len(self.stages):
                self.copy(k + 1).start()
            self.place += 1

    def finish(self):
        while self.place < len(self.stages):
            self.advance()
        for k in range(len(self.stages)):
            self.copy(k).wait_send()
        return self.held[len(self.stages)]


class RingSum:
    def __init__(self, count, part, out, to_right, to_left, send_sems, recv_sems):
        place, index_at = ring_places(count)
        self.count, self.half, self.size = count, count // 2, out.shape[0]
        self.part, self.out, self.held = part, out, (to_right, to_left)
        self.send_sems, self.recv_sems = send_sems, recv_sems
        self.neighbours = (
            index_at((place + 1) % count), index_at((place + count - 1) % count)
        )

    def copy(self, step, way):
        held, middle = self.held[way], self.size // 2
        if step == 0:
            source = self.part.at[pl.ds((self.count - 1) * self.size + way * middle, middle)]
            target = held.at[0, pl.ds(way * middle, middle)]
        else:
            source, target = held.at[step - 1], held.at[step]
        return pltpu.make_async_remote_copy(
            src_ref=source,
            dst_ref=target,
            send_sem=self.send_sems.at[step, way],
            recv_sem=self.recv_sems.at[step, way],
            device_id={"ep": self.neighbours[way]},
            device_id_type=MESH,
        )

    def start(self):
        for way in range(2):
            self.copy(0, way).start()

    def advance(self, step):
        middle, part = self.size // 2, self.part
        for way in range(2):
            held = self.held[way]
            first = (2 * (self.half - step) - 1 - way) * self.size
            self.copy(step - 1, way).wait_recv()
            if step == 1:
                here = slice(way * middle, (way + 1) * middle)
                rest = slice((1 - way) * middle, (2 - way) * middle)
                own = part[first + way * middle : first + (way + 1) * middle, :]
                held[0, here] = (own.astype(F32) + held[0, here].astype(F32)).astype(BF16)
                held[0, rest] = part[first + (1 - way) * middle : first + (2 - way) * middle, :]
            else:
                own = part[first : first + self.size, :]
                held[step - 1] = (own.astype(F32) + held[step - 1].astype(F32)).astype(BF16)
            self.copy(step, way).start()

    def last(self):
        own = self.part[(self.count - 2) * self.size : (self.count - 1) * self.size, :]
        total = own.astype(F32)
        for way in range(2):
            self.copy(self.half - 1, way).wait_recv()
            total = total + self.held[way][self.half - 1].astype(F32)
        self.out[...] = total

    def finish(self):
        for step in range(self.half):
            for way in range(2):
                self.copy(step, way).wait_send()


def reduce_kernel(count, part, out, to_right, to_left, send_sems, recv_sems):
    greet("ep", count)
    pl.semaphore_wait(pltpu.get_barrier_semaphore(), count - 1)
    ring = RingSum(count, part, out, to_right, to_left, send_sems, recv_sems)
    ring.start()
    for step in range(1, count // 2):
        ring.advance(step)
    ring.last()
    ring.finish()


def reduce_rows(count, part):
    tokens, width = part.shape
    size, half = tokens // count, count // 2
    whole = pl.BlockSpec(memory_space=pltpu.VMEM)
    return pl.pallas_call(
        functools.partial(reduce_kernel, count),
        in_specs=[whole],
        out_specs=whole,
        out_shape=jax.ShapeDtypeStruct((size, width), F32),
        scratch_shapes=[pltpu.VMEM((half, size, width), BF16)] * 2
        + [pltpu.SemaphoreType.DMA((half, 2))] * 2,
        compiler_params=pltpu.CompilerParams(
            collective_id=3, has_side_effects=True, vmem_limit_bytes=56 * MIB
        ),
        cost_estimate=KERNEL_COST,
        name="reduce_rows",
    )(part)


def finish_kernel(
    count, grp_count, bulk_number, branch, out_parts, small, bias, gain, g_qkv, attended, w,
    x_in, attn_in, *refs
):
    refs = list(refs)

    def take(amount):
        taken = refs[:amount]
        del refs[:amount]
        return taken

    planes = grp_count // 2
    far_number = planes - 1
    bulk = take(bulk_number)
    branch_sum, out_sum, small_sum, bias_sum, own_q, own_o = take(6)
    landed = take(bulk_number + 2 * far_number)
    rings_held = take(4)
    x, attn = take(2)
    away, arrived, far = take(2), take(2), take(2)
    small_held, small_arrived, bias_held, bias_arrived = take(4)
    (
        send_sems, recv_sems, small_sems, bias_sems, plane_sems, load_sems, core_send, core_recv
    ) = take(8)
    mine = lax.axis_index("grp")
    core, plane = mine % 2, mine // 2
    part_width = x.shape[2]
    orders = list(range(1, planes)) + [0]
    units = [(side, place) for side in (1, 0) for place in range(planes)]

    def columns(unit):
        side, place = units[unit]
        member = 2 * ((plane + orders[place]) % planes) + (core if side == 0 else 1 - core)
        return pl.ds(pl.multiple_of(member * part_width, part_width), part_width)

    def loads(unit):
        slot = unit % 2
        return [
            pltpu.make_async_copy(
                source.at[:, columns(unit)], target.at[slot], load_sems.at[i, slot]
            )
            for i, (source, target) in enumerate(((x_in, x), (attn_in, attn)))
        ]

    for unit in range(2):
        for load in loads(unit):
            load.start()
    greet("ep", count)
    greet("grp", grp_count)
    small_held[0] = small[...]
    bias_held[0] = bias[...]
    pl.semaphore_wait(pltpu.get_barrier_semaphore(), count - 1 + grp_count - 1)
    rings = [
        RingSum(
            count, part, out, rings_held[2 * a], rings_held[2 * a + 1], send_sems.at[a],
            recv_sems.at[a],
        )
        for a, (part, out) in enumerate(((branch, branch_sum), (out_parts, out_sum)))
    ]
    for ring in rings:
        ring.start()
    sums = [
        Doubling(small_held, small_arrived, doubling_stages(("grp", "ep")), small_sems),
        Doubling(bias_held, bias_arrived, doubling_stages(("grp",)), bias_sems),
    ]
    sums[1].start()

    def to_core(kind, place):
        return pltpu.make_async_remote_copy(
            src_ref=away[kind].at[place],
            dst_ref=arrived[kind].at[place],
            send_sem=core_send.at[kind, place],
            recv_sem=core_recv.at[kind, place],
            device_id={"grp": mine + 1 - 2 * core},
            device_id_type=MESH,
        )

    for unit, (side, place) in enumerate(units):
        cut, slot = columns(unit), unit % 2
        for load in loads(unit):
            load.wait()
        q_piece = dot_tn(x[slot], g_qkv[...])
        inner = jnp.sum(q_piece * w[cut, :].astype(F32), -1, keepdims=True)
        inner = jnp.transpose(jnp.broadcast_to(inner, (part_width, LANES)))[:1, :]
        small_held[0, 1:2, cut] = inner / gain[:, cut]
        o_piece = dot_tn(attended[...], attn[slot])
        for kind, piece in enumerate((q_piece, o_piece)):
            if side == 1:
                away[kind][place] = piece.astype(BF16)
                to_core(kind, place).start()
            else:
                to_core(kind, place).wait_recv()
                piece = piece + arrived[kind][place].astype(F32)
                if orders[place]:
                    far[kind][place] = piece.astype(BF16)
                else:
                    (own_q, own_o)[kind][...] = piece
        if unit + 2 < len(units):
            for load in loads(unit + 2):
                load.start()
    sums[0].start()
    far_copies = PlaneCopies(
        [far[kind].at[place] for kind in range(2) for place in range(far_number)] + bulk,
        landed, planes, plane_sems,
    )
    far_copies.start()
    for step in range(1, count // 2):
        for ring in rings:
            ring.advance(step)
            for item in sums:
                item.advance()
    for ring in rings:
        ring.last()
    small_sum[...] = sums[0].finish()
    bias_sum[...] = sums[1].finish()
    for ring in rings:
        ring.finish()
    for kind in range(2):
        for place in range(planes):
            to_core(kind, place).wait_send()
    far_copies.finish()


def finish(
    count, grp_count, branch, out_parts, small, bias, gain, g_qkv, attended, w, x, attn, bulk
):
    tokens, width = branch.shape
    size, half, planes = tokens // count, count // 2, grp_count // 2
    part_width = width // grp_count
    q_shape, o_shape = (part_width, g_qkv.shape[1]), (attended.shape[1], part_width)
    stages = len(doubling_stages(("grp", "ep"))), len(doubling_stages(("grp",)))
    anywhere = pl.BlockSpec(memory_space=pl.ANY)
    whole = pl.BlockSpec(memory_space=pltpu.VMEM)
    shape = jax.ShapeDtypeStruct
    dma = pltpu.SemaphoreType.DMA
    landed = [shape(dims, BF16) for dims in (q_shape, o_shape) for _ in range(planes - 1)]
    landed += [shape(value.shape, value.dtype) for value in bulk]
    results = pl.pallas_call(
        functools.partial(finish_kernel, count, grp_count, len(bulk)),
        in_specs=[whole] * 8 + [anywhere] * (2 + len(bulk)),
        out_specs=[whole] * 6 + [anywhere] * len(landed),
        out_shape=[
            shape((size, width), F32),
            shape((size, width), F32),
            shape(small.shape, F32),
            shape(bias.shape, F32),
            shape(q_shape, F32),
            shape(o_shape, F32),
            *landed,
        ],
        scratch_shapes=[pltpu.VMEM((half, size, width), BF16)] * 4
        + [pltpu.VMEM((2, tokens, part_width), BF16)] * 2
        + [pltpu.VMEM((planes, *dims), BF16) for dims in (q_shape, o_shape)] * 2
        + [pltpu.VMEM((max(planes - 1, 1), *dims), BF16) for dims in (q_shape, o_shape)]
        + [
            pltpu.VMEM((stages[0] + 1, *small.shape), F32),
            pltpu.VMEM((stages[0], *small.shape), F32),
            pltpu.VMEM((stages[1] + 1, *bias.shape), F32),
            pltpu.VMEM((stages[1], *bias.shape), F32),
        ]
        + [dma((2, half, 2))] * 2
        + [dma((2, stages[0])), dma((2, stages[1])), dma((2, len(landed))), dma((2, 2))]
        + [dma((2, planes))] * 2,
        compiler_params=pltpu.CompilerParams(
            collective_id=4, has_side_effects=True, vmem_limit_bytes=60 * MIB
        ),
        cost_estimate=KERNEL_COST,
        name="finish",
    )(branch, out_parts, small, bias, gain, g_qkv, attended, w, x, attn, *bulk)
    return results[:6], results[6:]


def reduce_and_weights_kernel(
    count, grp_count, part, x_in, cot_in, grad_e_in, act_e_in, grad_s_in, act_s_in, *refs
):
    refs = list(refs)

    def take(amount):
        taken = refs[:amount]
        del refs[:amount]
        return taken

    planes = grp_count // 2
    (summed,) = take(1)
    outs = [take(planes) for _ in range(5)]
    landed = take(planes - 1)
    sources = (x_in, grad_e_in, cot_in, act_e_in, grad_s_in, act_s_in)
    held = take(6)
    x, grad_e, cot, act_e, grad_s, act_s = held
    to_right, to_left = take(2)
    staged, arrived = take(5), take(5)
    send_sems, recv_sems, load_sems, core_send, core_recv, out_sems, plane_sems = take(7)
    mine = lax.axis_index("grp")
    core, plane = mine % 2, mine // 2
    part_width = x.shape[1] // grp_count

    loads = [
        pltpu.make_async_copy(source, target, load_sems.at[i])
        for i, (source, target) in enumerate(zip(sources, held))
    ]
    for load in loads:
        load.start()
    greet("ep", count)
    greet("grp", grp_count)
    pl.semaphore_wait(pltpu.get_barrier_semaphore(), count - 1 + grp_count - 1)
    ring = RingSum(count, part, summed, to_right, to_left, send_sems, recv_sems)
    ring.start()

    def columns(order, side):
        member = 2 * ((plane + order) % planes) + (core if side == 0 else 1 - core)
        return pl.ds(pl.multiple_of(member * part_width, part_width), part_width)

    def products(kind, cut):
        if kind < 2:
            return [dot_tn(x[:, cut], grad_e[kind])]
        if kind == 2:
            return [dot_tn(act_e[...], cot[:, cut])]
        if kind == 3:
            return [dot_tn(grad_s[k], x[:, cut]) for k in range(2)]
        return [dot_tn(act_s[...], cot[:, cut])]

    def to_core(kind, place):
        return pltpu.make_async_remote_copy(
            src_ref=staged[kind],
            dst_ref=arrived[kind].at[place],
            send_sem=core_send.at[kind, place],
            recv_sem=core_recv.at[kind, place],
            device_id={"grp": mine + 1 - 2 * core},
            device_id_type=MESH,
        )

    def store(kind, place):
        return pltpu.make_async_copy(staged[kind], outs[kind][place], out_sems.at[kind, place])

    orders = list(range(1, planes)) + [0]
    needs = ((0, 1), (), (2, 3), (4,), (5,))
    plane_copies = PlaneCopies(outs[0][: planes - 1], landed, planes, plane_sems)
    ring_step = 1
    number = 0
    for place, order in enumerate(orders):
        for side in (1, 0):
            for kind in range(5):
                if side == 1 and place == 0:
                    for i in needs[kind]:
                        loads[i].wait()
                pieces = products(kind, columns(order, side))
                if side == 1:
                    if place and kind:
                        store(kind, place - 1).wait()
                else:
                    to_core(kind, place).wait_recv()
                    to_core(kind, place).wait_send()
                for k, piece in enumerate(pieces):
                    whole = (k,) if len(pieces) > 1 else (Ellipsis,)
                    if side == 0:
                        piece = piece + arrived[kind][(place, *whole)].astype(F32)
                    staged[kind][whole] = piece.astype(BF16)
                if side == 1:
                    to_core(kind, place).start()
                else:
                    store(kind, place).start()
                if side == 0 and kind == 1 and order:
                    store(0, place).wait()
                    plane_copies.copies[place].start()
                number += 1
                if number % 5 == 2:
                    if ring_step < count // 2:
                        ring.advance(ring_step)
                    elif ring_step == count // 2:
                        ring.last()
                    ring_step += 1
    while ring_step <= count // 2:
        if ring_step < count // 2:
            ring.advance(ring_step)
        else:
            ring.last()
        ring_step += 1
    for kind in range(5):
        store(kind, planes - 1).wait()
    ring.finish()
    plane_copies.finish()


def reduce_and_weights(
    count, grp_count, part, x, cot, grad_e, act_e, grad_s, act_s
):
    tokens, width = part.shape
    size, half, planes = tokens // count, count // 2, grp_count // 2
    part_width = width // grp_count
    wide, narrow = act_e.shape[1], act_s.shape[1]
    shapes = [
        (part_width, wide), (part_width, wide), (wide, part_width), (2, narrow, part_width),
        (narrow, part_width),
    ]
    anywhere = pl.BlockSpec(memory_space=pl.ANY)
    whole = pl.BlockSpec(memory_space=pltpu.VMEM)
    shape = jax.ShapeDtypeStruct
    dma = pltpu.SemaphoreType.DMA
    summed, *slices = pl.pallas_call(
        functools.partial(reduce_and_weights_kernel, count, grp_count),
        in_specs=[whole] + [anywhere] * 6,
        out_specs=[whole] + [anywhere] * (6 * planes - 1),
        out_shape=[shape((size, width), F32)]
        + [shape(dims, BF16) for dims in shapes for _ in range(planes)]
        + [shape(shapes[0], BF16)] * (planes - 1),
        scratch_shapes=[
            pltpu.VMEM(value.shape, BF16) for value in (x, grad_e, cot, act_e, grad_s, act_s)
        ]
        + [pltpu.VMEM((half, size, width), BF16)] * 2
        + [pltpu.VMEM(dims, BF16) for dims in shapes]
        + [pltpu.VMEM((planes, *dims), BF16) for dims in shapes]
        + [dma((half, 2)), dma((half, 2)), dma((6,))]
        + [dma((5, planes))] * 3
        + [dma((2, max(planes - 1, 1)))],
        compiler_params=pltpu.CompilerParams(
            collective_id=3, has_side_effects=True, vmem_limit_bytes=60 * MIB
        ),
        cost_estimate=KERNEL_COST,
        name="reduce_and_weights",
    )(part, x, cot, grad_e, act_e, grad_s, act_s)
    groups = [slices[i * planes : (i + 1) * planes] for i in range(5)]
    passed, own = [group[:-1] for group in groups], [group[-1] for group in groups]
    return summed, passed, own, slices[5 * planes :]


def tiles_of(width):
    tiles, start = [], 0
    while width - start > 384:
        tiles.append((start, 256))
        start += 256
    tiles.append((start, width - start))
    return tiles


def experts_kernel(
    count, expert_count, x_own, cot_own, routes, routes_w, gate_up_e, down_e, gate_up_s, down_s,
    act_e_out, grad_e_out, act_s_out, grad_s_out, part_out, branch_out, logits_out, x_out,
    cot_out,
    xs, cots, gate_e, up_e, held_e, gate_s, up_s, held_s, act_e, grad_e, act_s, grad_s, part,
    branch, logits_held, x_send, x_recv, cot_send, cot_recv, weight_sems, out_sems, x_sems,
):
    half = count // 2
    size = x_own.shape[0]
    rows = 2 * size
    ring_x = KernelRing(xs, count, size, x_send, x_recv)
    ring_cot = KernelRing(cots, count, size, cot_send, cot_recv)

    barrier = pltpu.get_barrier_semaphore()
    for neighbour in (ring_x.left, ring_x.right):
        pl.semaphore_signal(barrier, inc=1, device_id={"ep": neighbour}, device_id_type=MESH)
    loads = [
        pltpu.make_async_copy(source, target, weight_sems.at[i])
        for i, (source, target) in enumerate(
            [
                (gate_up_e.at[0, 0], gate_e),
                (gate_up_e.at[0, 1], up_e),
                (down_e.at[0], held_e),
                (gate_up_s.at[0], gate_s),
                (gate_up_s.at[1], up_s),
                (down_s, held_s),
            ]
        )
    ]
    for load in loads:
        load.start()
    xs[ring_x.own(), :] = x_own[...]
    cots[ring_x.own(), :] = cot_own[...]
    pl.semaphore_wait(barrier, 2)
    ring_x.start()
    ring_cot.start()

    def stores(i):
        here = rows_at(i, rows)
        slot = lax.rem(i, 2)
        pieces = [
            (act_e.at[slot], act_e_out.at[here]),
            (grad_e.at[slot, 0], grad_e_out.at[0, here]),
            (grad_e.at[slot, 1], grad_e_out.at[1, here]),
            (act_s.at[slot], act_s_out.at[here]),
            (grad_s.at[slot, 0], grad_s_out.at[0, here]),
            (grad_s.at[slot, 1], grad_s_out.at[1, here]),
            (part.at[slot], part_out.at[here]),
            (branch.at[slot], branch_out.at[here]),
            (logits_held.at[slot], logits_out.at[here]),
        ]
        return [
            pltpu.make_async_copy(source, target, out_sems.at[slot, k])
            for k, (source, target) in enumerate(pieces)
        ]

    def store_rows(i):
        here = rows_at(i, rows)
        return [
            pltpu.make_async_copy(xs.at[here], x_out.at[here], x_sems.at[0, i]),
            pltpu.make_async_copy(cots.at[here], cot_out.at[here], x_sems.at[1, i]),
        ]

    sections = (
        (gate_e, up_e, held_e, act_e, grad_e, dot, dot_nt),
        (gate_s, up_s, held_s, act_s, grad_s, dot_nt, dot),
    )
    mine = lax.axis_index("ep")
    onehot = (lax.broadcasted_iota(jnp.int32, (1, LANES), 1) == mine).astype(F32)

    def one_pair(i, carry):
        slot = lax.rem(i, 2)
        here = rows_at(i, rows)
        ring_x.arrive(i)
        ring_x.forward(i)
        ring_cot.arrive(i)
        ring_cot.forward(i)
        for copy in store_rows(i):
            copy.start()

        @pl.when(i == 0)
        def _():
            for load in loads:
                load.wait()

        @pl.when(i >= 2)
        def _():
            for copy in stores(i - 2):
                copy.wait()

        lane = lax.broadcasted_iota(jnp.int32, (rows, LANES), 1)
        inputs, cotangent = xs[here, :], cots[here, :]
        logits = dot(inputs, routes_w[...])
        routed = jnp.where(lane < expert_count, logits, NEGATIVE)
        expo = jnp.exp(routed - jnp.max(routed, -1, keepdims=True))
        probs = expo * (1.0 / jnp.sum(expo, -1, keepdims=True))
        named = jnp.concatenate(
            [routes[rows_at(slot_index(count, 2 * i + k), size), :] for k in range(2)], 0
        )
        hits = jnp.sum(jnp.where(named == mine, 1.0, 0.0), -1, keepdims=True)
        own_prob = jnp.sum(probs * onehot, -1, keepdims=True) * hits
        share_logit = jnp.sum(jnp.where(lane == expert_count, logits, 0.0), -1, keepdims=True)
        share = 1.0 / (1.0 + jnp.exp(-share_logit))

        inner = []
        total, out_total = None, None
        for s, (gate_w, up_w, down_w, act_out, grad_out, ahead, back_dot) in enumerate(sections):
            factor = own_prob if s == 0 else share
            dots = jnp.zeros((rows, 1), F32)
            for start, width in tiles_of(down_w.shape[0]):
                cut = pl.ds(start, width)
                piece = (slice(None), cut) if s == 0 else (cut, slice(None))
                gate = ahead(inputs, gate_w[piece])
                up = ahead(inputs, up_w[piece])
                grad = dot_nt(cotangent, down_w[cut, :])
                sigma = 0.5 * jnp.tanh(0.5 * gate) + 0.5
                silu = gate * sigma
                act = (silu * up).astype(BF16).astype(F32)
                dots = dots + jnp.sum(grad * act, -1, keepdims=True)
                scaled = grad * factor
                act_out[slot, :, cut] = (act * factor).astype(BF16)
                grad_out[slot, 0, :, cut] = (
                    scaled * up * (sigma + silu * (1.0 - sigma))
                ).astype(BF16)
                grad_out[slot, 1, :, cut] = (scaled * silu).astype(BF16)
            inner.append(dots)
            back = back_dot(grad_out[slot, 0], gate_w[...]) + back_dot(
                grad_out[slot, 1], up_w[...]
            )
            total = back if total is None else total + back
            out_piece = dot(act_out[slot], down_w[...])
            out_total = out_piece if out_total is None else out_total + out_piece
        branch[slot] = out_total.astype(BF16)
        grad_logits = own_prob * inner[0] * (onehot - probs)
        grad_share = share * (1.0 - share) * inner[1]
        grad_logits = grad_logits + jnp.where(lane == expert_count, grad_share, 0.0)
        high = grad_logits.astype(BF16)
        low = (grad_logits - high.astype(F32)).astype(BF16)
        total = total + dot_nt(high, routes_w[...]) + dot_nt(low, routes_w[...])
        logits_held[slot, :, :LANES] = high
        logits_held[slot, :, LANES:] = low
        part[slot] = total.astype(BF16)
        for copy in stores(i):
            copy.start()
        return carry

    lax.fori_loop(0, half, one_pair, 0)
    for i in range(half):
        for copy in store_rows(i):
            copy.wait()
    for i in range(max(half - 2, 0), half):
        for copy in stores(i):
            copy.wait()
    ring_x.finish()
    ring_cot.finish()


def experts(
    count, expert_count, x_own, cot_own, routes, routes_w, gate_up_e, down_e, gate_up_s, down_s
):
    size, width = x_own.shape
    tokens, rows, half = size * count, 2 * size, count // 2
    wide, narrow = down_e.shape[1], down_s.shape[0]
    anywhere = pl.BlockSpec(memory_space=pl.ANY)
    whole = pl.BlockSpec(memory_space=pltpu.VMEM)
    shape = jax.ShapeDtypeStruct
    dma = pltpu.SemaphoreType.DMA
    return pl.pallas_call(
        functools.partial(experts_kernel, count, expert_count),
        in_specs=[whole] * 4 + [anywhere] * 4,
        out_specs=[anywhere] * 9,
        out_shape=(
            shape((tokens, wide), BF16),
            shape((2, tokens, wide), BF16),
            shape((tokens, narrow), BF16),
            shape((2, tokens, narrow), BF16),
            shape((tokens, width), BF16),
            shape((tokens, width), BF16),
            shape((tokens, 2 * LANES), BF16),
            shape((tokens, width), BF16),
            shape((tokens, width), BF16),
        ),
        scratch_shapes=[
            pltpu.VMEM((tokens, width), BF16),
            pltpu.VMEM((tokens, width), BF16),
            pltpu.VMEM((width, wide), BF16),
            pltpu.VMEM((width, wide), BF16),
            pltpu.VMEM((wide, width), BF16),
            pltpu.VMEM((narrow, width), BF16),
            pltpu.VMEM((narrow, width), BF16),
            pltpu.VMEM((narrow, width), BF16),
            pltpu.VMEM((2, rows, wide), BF16),
            pltpu.VMEM((2, 2, rows, wide), BF16),
            pltpu.VMEM((2, rows, narrow), BF16),
            pltpu.VMEM((2, 2, rows, narrow), BF16),
            pltpu.VMEM((2, rows, width), BF16),
            pltpu.VMEM((2, rows, width), BF16),
            pltpu.VMEM((2, rows, 2 * LANES), BF16),
            dma((half, 2)),
            dma((half, 2)),
            dma((half, 2)),
            dma((half, 2)),
            dma((6,)),
            dma((2, 9)),
            dma((2, half)),
        ],
        compiler_params=pltpu.CompilerParams(
            collective_id=0, has_side_effects=True, vmem_limit_bytes=60 * MIB
        ),
        cost_estimate=KERNEL_COST,
        name="experts",
    )(x_own, cot_own, routes, routes_w, gate_up_e, down_e, gate_up_s, down_s)


def norm_of(values):
    factor = lax.rsqrt(jnp.mean(values * values, -1, keepdims=True) + EPS)
    return values * factor, factor


def norm_back(grad_out, normal, factor, gain):
    scaled = grad_out * gain
    return factor * (scaled - normal * jnp.mean(scaled * normal, -1, keepdims=True))


def local(
    hidden_in, segments, routes, cotangent, norm1_gain, w_qkv, b_qkv, w_out, norm2_gain, router,
    shared_gate_up, shared_down, shared_gate, expert_gate_up, expert_down,
):
    tokens_here, width = hidden_in.shape
    ep_count = lax.axis_size("ep")
    grp_count = lax.axis_size("grp")
    expert_count = router.shape[1]
    heads, qkv_dim = b_qkv.shape
    head_dim = qkv_dim // 3
    scale = 1.0 / math.sqrt(head_dim)
    slice_width = width // grp_count
    routes_w = jnp.concatenate(
        [router, shared_gate[:, None], jnp.zeros((width, LANES - 1 - expert_count), BF16)], 1
    )
    w_flat = w_qkv.reshape(width, heads * qkv_dim)
    b_flat = b_qkv.reshape(1, heads * qkv_dim)
    w_out_flat = w_out.reshape(heads * head_dim, width)

    (
        queries, key_rows, values, attended, logs, residual, normed_two, cosine, sine, starts,
        group_one, w_all,
    ) = attend_forward(
        ep_count, grp_count, hidden_in, norm1_gain, norm2_gain, w_flat, b_flat, w_out_flat,
        segments, scale,
    )

    (
        expert_act, expert_grad, shared_act, shared_grad, part, out_parts, grad_logits,
        group_two, group_cot,
    ) = experts(
        ep_count, expert_count, normed_two, cotangent, routes, routes_w,
        expert_gate_up, expert_down, jnp.swapaxes(shared_gate_up, 1, 2), shared_down,
    )

    if ep_count == 8:
        grad_normed_two, passed, sums_own, first_landed = reduce_and_weights(
            ep_count, grp_count, part, group_two, group_cot, expert_grad, expert_act,
            shared_grad, shared_act,
        )
    else:

        def up_grad(k):
            return lambda rows, member: dot_tn(columns_of(rows, member), expert_grad[k])

        def shared_gate_up_grad(rows, member):
            columns = columns_of(rows, member)
            return jnp.stack([dot_tn(shared_grad[k], columns) for k in range(2)], 0)

        def down_grad(act):
            return lambda rows, member: dot_tn(act, columns_of(rows, member))

        sums = [
            GrpReduce(group_two, up_grad(0)),
            GrpReduce(group_two, up_grad(1)),
            GrpReduce(group_cot, down_grad(expert_act)),
            GrpReduce(group_two, shared_gate_up_grad),
            GrpReduce(group_cot, down_grad(shared_act)),
        ]
        arrived = [[item.to_partner(value) for value in item.away()] for item in sums]
        passed = [item.pass_on(values_) for item, values_ in zip(sums, arrived)]
        sums_own = [item.own() for item in sums]
        grad_normed_two = reduce_rows(ep_count, part)
        first_landed = None
    normal_two, factor_two = norm_of(residual)
    grad_y = cotangent.astype(F32)
    grad_residual = grad_y + norm_back(grad_normed_two, normal_two, factor_two, norm2_gain)
    grad_norm2 = jnp.sum(grad_normed_two * normal_two, 0)
    own_attn = grad_residual.astype(BF16)
    each = grp_count // 2 - 1

    bulk = passed[1] + passed[4] + (passed[0] if first_landed is None else [])
    grad_qkv, grad_bias, grad_branch, group_attn, *landed = attend_backward(
        ep_count, grp_count, own_attn, w_all, w_flat, cosine, sine, queries, key_rows, values,
        logs, starts, scale, bulk,
    )
    from_planes = {1: landed[:each], 4: landed[each : 2 * each]}
    from_planes[0] = landed[2 * each :] if first_landed is None else first_landed

    grad_routes = dot_tn(grad_logits, group_two)
    grad_routes = grad_routes[: expert_count + 1] + grad_routes[LANES : LANES + expert_count + 1]
    small = jnp.concatenate([grad_norm2[None], jnp.zeros((1, width), F32), grad_routes], 0)
    (grad_normed_one, out_sum, small, bias_total, own_q, own_o), landed = finish(
        ep_count, grp_count, grad_branch, out_parts, small, grad_bias, norm1_gain[None, :],
        grad_qkv, attended, w_flat, group_one, group_attn, passed[2] + passed[3],
    )
    from_q, from_o, from_planes[2], from_planes[3] = [
        landed[i * each : (i + 1) * each] for i in range(4)
    ]
    layer_out = (residual + out_sum).astype(BF16)
    normal_one, factor_one = norm_of(hidden_in.astype(F32))
    grad_x = grad_residual + norm_back(grad_normed_one, normal_one, factor_one, norm1_gain)
    grad_gate, grad_up, grad_expert_down, grad_shared_gate_up, grad_shared_down = [
        add_all(own, from_planes[i]) for i, own in enumerate(sums_own)
    ]
    grad_w_qkv, grad_w_out = add_all(own_q, from_q), add_all(own_o, from_o)
    bias_total = bias_total.reshape(heads, grp_count, qkv_dim // grp_count)
    grad_b = lax.dynamic_index_in_dim(bias_total, lax.axis_index("grp"), 1, keepdims=False)

    return (
        layer_out,
        grad_x,
        small[1],
        grad_w_qkv.reshape(slice_width, heads, qkv_dim),
        grad_b,
        grad_w_out.reshape(heads, head_dim, slice_width),
        small[0],
        small[2 : expert_count + 2].T,
        jnp.swapaxes(grad_shared_gate_up, 1, 2),
        grad_shared_down,
        small[expert_count + 2],
        jnp.stack([grad_gate, grad_up], 0)[None],
        grad_expert_down[None],
    )


def solution(mesh):
    in_specs = (
        P(("grp", "ep"), None),
        P("grp"),
        P("grp", None),
        P(("grp", "ep"), None),
        P(),
        P(None, "ep", None),
        P("ep", None),
        P("ep", None, None),
        P(),
        P(),
        P(None, None, "ep"),
        P("ep", None),
        P(),
        P("ep", None, None, None),
        P("ep", None, None),
    )
    out_specs = (
        P(("grp", "ep"), None),
        P(("grp", "ep"), None),
        P(),
        P("grp", "ep", None),
        P("ep", "grp"),
        P("ep", None, "grp"),
        P(),
        P(),
        P(None, "grp", "ep"),
        P("ep", "grp"),
        P(),
        P("ep", None, "grp", None),
        P("ep", None, "grp"),
    )
    return jax.shard_map(local, mesh=mesh, in_specs=in_specs, out_specs=out_specs, check_vma=False)
```

```python
import functools
import math

import jax
import jax.numpy as jnp
from jax import lax
from jax.experimental import pallas as pl
from jax.experimental.pallas import tpu as pltpu
from jax.sharding import PartitionSpec as P

EPS = 1e-06
THETA = 1000000.0
NEGATIVE = -1e30
BF16 = jnp.bfloat16
F32 = jnp.float32
LANES = 128
MIB = 1024 * 1024
KERNEL_COST = pl.CostEstimate(flops=10**6, bytes_accessed=10**5, transcendentals=0)


def dot(lhs, rhs):
    return jnp.dot(lhs, rhs, preferred_element_type=F32)


def dot_nt(lhs, rhs):
    return lax.dot_general(lhs, rhs, (((1,), (1,)), ((), ())), preferred_element_type=F32)


def dot_tn(lhs, rhs):
    return lax.dot_general(lhs, rhs, (((0,), (0,)), ((), ())), preferred_element_type=F32)


class GrpReduce:
    def __init__(self, rows, produce):
        self.rows, self.produce = rows, produce
        self.size = lax.axis_size("grp")
        self.planes = self.size // 2
        mine = lax.axis_index("grp")
        self.core, self.plane = mine % 2, mine // 2
        self.far = [(self.plane + k) % self.planes for k in range(1, self.planes)]

    def to_partner(self, value):
        return lax.ppermute(value, "grp", [(i, i ^ 1) for i in range(self.size)])

    def away(self):
        return [
            self.produce(self.rows, 2 * plane + 1 - self.core).astype(BF16) for plane in self.far
        ]

    def pass_on(self, arrived):
        return [
            (self.produce(self.rows, 2 * plane + self.core) + value.astype(F32)).astype(BF16)
            for plane, value in zip(self.far, arrived)
        ]

    def own(self):
        away = self.produce(self.rows, 2 * self.plane + 1 - self.core).astype(BF16)
        kept = self.produce(self.rows, 2 * self.plane + self.core)
        return kept + self.to_partner(away).astype(F32)


def add_all(value, others):
    value = value.astype(F32)
    for other in others:
        value = value + other.astype(F32)
    return value


def columns_of(array, member):
    size = array.shape[1] // lax.axis_size("grp")
    return lax.dynamic_slice_in_dim(array, member * size, size, 1)


MESH = pl.DeviceIdType.MESH


def ring_places(count):
    here = lax.axis_index("ep")
    if count != 8:
        return here, lambda spot: spot
    x, z = here % 2, here // 2

    def index_at(spot):
        side = spot // 4
        return 2 * (spot + side * (7 - 2 * spot)) + side

    return z + x * (7 - 2 * z), index_at


def slot_index(count, slot):
    place, index_at = ring_places(count)
    offset = jnp.where(slot == count - 1, count // 2, (slot // 2 + 1) * (2 * (slot % 2) - 1))
    offset = jnp.where(slot == count - 2, 0, offset)
    return index_at((place + offset + count) % count)


def when(condition):
    if isinstance(condition, bool):
        return (lambda run: run()) if condition else (lambda run: None)
    return pl.when(condition)


def rows_at(slot, size):
    return pl.ds(pl.multiple_of(slot * size, size), size)


class KernelRing:
    def __init__(self, buffer, count, size, send_sems, recv_sems):
        place, index_at = ring_places(count)
        self.buffer, self.count, self.size = buffer, count, size
        self.half = count // 2
        self.send_sems, self.recv_sems = send_sems, recv_sems
        self.right = index_at((place + 1) % count)
        self.left = index_at((place + count - 1) % count)

    def own(self):
        return slice((self.count - 2) * self.size, (self.count - 1) * self.size)

    def copy(self, source, target, neighbour, step, way):
        return pltpu.make_async_remote_copy(
            src_ref=self.buffer.at[source],
            dst_ref=self.buffer.at[target],
            send_sem=self.send_sems.at[step, way],
            recv_sem=self.recv_sems.at[step, way],
            device_id={"ep": neighbour},
            device_id_type=MESH,
        )

    def sends(self, step):
        before = lax.rem(step + self.half - 1, self.half)
        copies = []
        for way, neighbour in enumerate((self.right, self.left)):
            source = jnp.where(step == 0, self.count - 2, 2 * before + way)
            copies.append(
                self.copy(
                    rows_at(source, self.size), rows_at(2 * step + way, self.size),
                    neighbour, step, way,
                )
            )
        return copies

    def last_sends(self):
        middle = self.size // 2
        copies = []
        for way, neighbour in enumerate((self.right, self.left)):
            source = (self.count - 4 + way) * self.size + way * middle
            target = (self.count - 1) * self.size + way * middle
            copies.append(
                self.copy(
                    pl.ds(source, middle), pl.ds(target, middle), neighbour, self.half - 1, way
                )
            )
        return copies

    def start(self):
        for copy in self.sends(0):
            copy.start()

    def arrive(self, i):
        @when(i < self.half - 1)
        def _():
            for copy in self.sends(i):
                copy.wait_recv()

        @when(i == self.half - 1)
        def _():
            for copy in self.last_sends():
                copy.wait_recv()

    def forward(self, i):
        @when(i < self.half - 2)
        def _():
            for copy in self.sends(i + 1):
                copy.start()

        @when(i == self.half - 2)
        def _():
            for copy in self.last_sends():
                copy.start()

    def finish(self, first=0):
        for step in range(first, self.half - 1):
            for copy in self.sends(step):
                copy.wait_send()
        for copy in self.last_sends():
            copy.wait_send()


class Exchange:
    def __init__(self, count, source_at, target_at, send_sems, recv_sems):
        self.count = count
        self.place, self.index_at = ring_places(count)
        self.source_at, self.target_at = source_at, target_at
        self.send_sems, self.recv_sems = send_sems, recv_sems

    def copy(self, slot):
        way = slot % 2
        far = slot // 2 + 1
        farthest = slot == self.count - 1
        offset = jnp.where(farthest, self.count // 2, far * (2 * way - 1))
        landing = jnp.where(farthest, slot, slot + 1 - 2 * way)
        return pltpu.make_async_remote_copy(
            src_ref=self.source_at(slot),
            dst_ref=self.target_at(landing),
            send_sem=self.send_sems.at[slot],
            recv_sem=self.recv_sems.at[landing],
            device_id={"ep": self.index_at((self.place + offset + self.count) % self.count)},
            device_id_type=MESH,
        )

    def arrived(self, slot):
        return pltpu.make_async_remote_copy(
            src_ref=self.source_at(slot),
            dst_ref=self.target_at(slot),
            send_sem=self.send_sems.at[slot],
            recv_sem=self.recv_sems.at[slot],
            device_id={"ep": self.index_at((self.place + 1) % self.count)},
            device_id_type=MESH,
        )

    def others(self):
        return [slot for slot in range(self.count) if slot != self.count - 2]


class PlaneCopies:
    def __init__(self, pairs, planes, sems):
        mine, size = lax.axis_index("grp"), lax.axis_size("grp")
        self.copies = []
        for i, (source, target) in enumerate(pairs):
            shift = 2 * (i % (planes - 1) + 1)
            self.copies.append(
                pltpu.make_async_remote_copy(
                    src_ref=source,
                    dst_ref=target,
                    send_sem=sems.at[0, i],
                    recv_sem=sems.at[1, i],
                    device_id={"grp": (mine + shift) % size},
                    device_id_type=MESH,
                )
            )

    def start(self, first=0, last=None):
        for copy in self.copies[first:last]:
            copy.start()

    def finish(self):
        for copy in self.copies:
            copy.wait()


def greet(axis, count):
    barrier = pltpu.get_barrier_semaphore()
    here = lax.axis_index(axis)
    for step in range(1, count):
        pl.semaphore_signal(
            barrier, inc=1, device_id={axis: (here + step) % count}, device_id_type=MESH
        )


def block_rows_of(count):
    return 256 if count % 256 == 0 else 128


def attend_forward_kernel(
    count, grp_count, heads, scale, hidden, cot_own, first_gain, gain, w, b, segments,
    row_segments, w_out,
    q_out, k_out, v_out, attended_out, log_out, residual_out, normed_out, cosine, sine, row_starts,
    x_out, w_all_out, near_out, row_positions, starts, near, xs, w_all, received, x_send, x_recv, w_send, w_recv, plane_send, plane_recv, core_send,
    core_recv, hand_send, hand_recv, near_send, near_recv, x_sems, w_sems, own_sem,
):
    size, width = hidden.shape
    half = count // 2
    rows = 2 * size
    dim = LANES
    inner_size = heads * dim
    planes = grp_count // 2
    mine = lax.axis_index("grp")
    core, plane = mine % 2, mine // 2
    part_width = width // grp_count

    own_columns = pl.ds(pl.multiple_of(mine * part_width, part_width), part_width)
    ring_x = KernelRing(xs, count, size, x_send, x_recv)
    ring_w = KernelRing(w_all.at[0], count, inner_size, w_send, w_recv)
    load = pltpu.make_async_copy(
        w_out.at[:, own_columns], w_all.at[0, ring_w.own()], own_sem.at[0]
    )
    load.start()
    greet("ep", count)
    greet("grp", grp_count)
    own_hidden = hidden[...].astype(F32)
    mean = jnp.sum(own_hidden * own_hidden, -1, keepdims=True) * (1.0 / width)
    xs[ring_x.own(), :] = (own_hidden * lax.rsqrt(mean + EPS) * first_gain[...]).astype(BF16)
    pl.semaphore_wait(pltpu.get_barrier_semaphore(), count - 1 + grp_count - 1)
    load.wait()
    ring_w.start()
    ring_x.start()

    for slot in range(count):
        row_positions[:, slot * size : (slot + 1) * size] = slot_index(
            count, slot
        ) * size + lax.broadcasted_iota(jnp.int32, (1, size), 1)
    lane = lax.broadcasted_iota(jnp.int32, (size, dim), 1)
    low_half = lane < dim // 2
    index = jnp.where(low_half, lane, lane - dim // 2).astype(F32)
    inverse = jnp.exp(index * (-2.0 * math.log(THETA) / dim))

    def tables(slot, carry):
        block = slot_index(count, slot)
        here, there = rows_at(slot, size), rows_at(block, size)
        before = jnp.where(row_segments[...] < segments[there, :], 1.0, 0.0)
        start = jnp.sum(before, -1, keepdims=True)
        starts[here, :] = start.astype(jnp.int32)
        own_row = row_segments[:, there]
        before = jnp.where(segments[...] < own_row, 1.0, 0.0)
        row_starts[:, here] = jnp.sum(before, 0, keepdims=True).astype(jnp.int32)
        position = (block * size + lax.broadcasted_iota(jnp.int32, (size, 1), 0)).astype(F32)
        angle = (position - start) * inverse
        cosine[here, :] = jnp.cos(angle)
        sine[here, :] = jnp.where(low_half, -jnp.sin(angle), jnp.sin(angle))
        return carry

    lax.fori_loop(0, count, tables, 0)

    def to_plane(step, i):
        here = rows_at(i, 2 * inner_size)
        landing = (planes - step) % planes
        return pltpu.make_async_remote_copy(
            src_ref=w_all.at[0, here],
            dst_ref=w_all.at[landing, here],
            send_sem=plane_send.at[step - 1, i],
            recv_sem=plane_recv.at[landing - 1, i],
            device_id={"grp": (mine + 2 * step) % grp_count},
            device_id_type=MESH,
        )

    def to_core(j):
        return pltpu.make_async_remote_copy(
            src_ref=w_all.at[j],
            dst_ref=w_all.at[planes + j],
            send_sem=core_send.at[j],
            recv_sem=core_recv.at[j],
            device_id={"grp": mine + 1 - 2 * core},
            device_id_type=MESH,
        )

    def store_x(i):
        here = rows_at(i, rows)
        return pltpu.make_async_copy(xs.at[here], x_out.at[here], x_sems.at[i])

    def store_w(j):
        return pltpu.make_async_copy(w_all.at[j], w_all_out.at[j], w_sems.at[j])

    def project(i, carry):
        here = rows_at(i, rows)
        ring_w.arrive(i)
        ring_w.forward(i)
        for step in range(1, planes):
            to_plane(step, i).start()
        ring_x.arrive(i)
        ring_x.forward(i)
        store_x(i).start()
        projected = dot(xs[here, :], w[...]) + b[...]
        cos, sin = cosine[here, :], sine[here, :]
        for h in range(heads):
            base = 3 * dim * h
            query = projected[:, base : base + dim]
            key = projected[:, base + dim : base + 2 * dim]
            q_out[h, here, :] = (query * cos + pltpu.roll(query, dim // 2, 1) * sin).astype(BF16)
            k_out[h, here, :] = (key * cos + pltpu.roll(key, dim // 2, 1) * sin).astype(BF16)
            v_out[h, here, :] = projected[:, base + 2 * dim : base + 3 * dim].astype(BF16)
        return carry

    def to_neighbour(way):
        return pltpu.make_async_remote_copy(
            src_ref=cot_own,
            dst_ref=near.at[pl.ds(way * size, size)],
            send_sem=near_send.at[way],
            recv_sem=near_recv.at[way],
            device_id={"ep": (ring_x.right, ring_x.left)[way]},
            device_id_type=MESH,
        )

    lax.fori_loop(0, half, project, 0)
    for way in range(2):
        to_neighbour(way).start()
    to_core(0).start()
    store_w(0).start()

    exchange = Exchange(
        count,
        lambda slot: attended_out.at[rows_at(slot, size)],
        lambda slot: received.at[slot],
        hand_send,
        hand_recv,
    )

    def attend(step, carry):
        i = half - 1 - step
        here = rows_at(i, rows)
        count_up = lax.broadcasted_iota(jnp.int32, (size, 1), 0)
        own = jnp.concatenate(
            [slot_index(count, 2 * i + k) * size + count_up for k in range(2)], 0
        )
        start = starts[here, :]
        keys_at = row_positions[...]
        allowed = (keys_at <= own) & (keys_at >= start)
        for h in range(heads):
            scores = dot_nt(q_out[h, here, :], k_out[h]) * scale
            scores = jnp.where(allowed, scores, NEGATIVE)
            highest = jnp.max(scores, -1, keepdims=True)
            expo = jnp.exp(scores - highest)
            total = jnp.sum(expo, -1, keepdims=True)
            weights = (expo * (1.0 / total)).astype(BF16)
            attended_out[here, h * dim : (h + 1) * dim] = dot(weights, v_out[h]).astype(BF16)
            logs = jnp.broadcast_to(highest + jnp.log(total), (rows, LANES))
            log_out[h, :, here] = jnp.transpose(logs)[:1, :]
        exchange.copy(2 * i + 1).start()

        @pl.when(i < half - 1)
        def _():
            exchange.copy(2 * i).start()

        return carry

    lax.fori_loop(0, half, attend, 0)
    received[count - 2] = attended_out[ring_x.own(), :]
    for j in range(1, planes):
        for i in range(half):
            to_plane((planes - j) % planes, i).wait_recv()
        to_core(j).start()
        store_w(j).start()
    for slot in exchange.others():
        exchange.arrived(slot).wait_recv()
    for j in range(planes):
        to_core(j).wait_recv()
        store_w(planes + j).start()
    store_near = pltpu.make_async_copy(near, near_out, own_sem.at[1])
    for way in range(2):
        to_neighbour(way).wait_recv()
    store_near.start()
    mixed = jnp.concatenate([received[slot] for slot in range(count)], 1)
    square = jnp.zeros((size, 1), F32)
    for j in range(grp_count):
        member = 2 * ((plane + j % planes) % planes) + (core if j < planes else 1 - core)
        columns = pl.ds(pl.multiple_of(member * part_width, part_width), part_width)
        piece = hidden[:, columns].astype(F32) + dot(mixed, w_all[j])
        residual_out[:, columns] = piece
        square = square + jnp.sum(piece * piece, -1, keepdims=True)
    factor = lax.rsqrt(square * (1.0 / width) + EPS)
    normed_out[...] = (residual_out[...] * factor * gain[...]).astype(BF16)

    for i in range(half):
        store_x(i).wait()
        for step in range(1, planes):
            to_plane(step, i).wait_send()
    for j in range(grp_count):
        store_w(j).wait()
    for j in range(planes):
        to_core(j).wait_send()
    for slot in exchange.others():
        exchange.copy(slot).wait_send()
    for way in range(2):
        to_neighbour(way).wait_send()
    store_near.wait()
    ring_x.finish()
    ring_w.finish()


def attend_forward(
    count, grp_count, hidden, cot_own, first_gain, gain, w, b, w_out, segments, scale
):
    size, width = hidden.shape
    tokens = size * count
    heads = w.shape[1] // (3 * LANES)
    half, planes = count // 2, grp_count // 2
    anywhere = pl.BlockSpec(memory_space=pl.ANY)
    whole = pl.BlockSpec(memory_space=pltpu.VMEM)
    shape = jax.ShapeDtypeStruct
    w_all_shape = (grp_count, count * heads * LANES, width // grp_count)
    dma = pltpu.SemaphoreType.DMA
    return pl.pallas_call(
        functools.partial(attend_forward_kernel, count, grp_count, heads, scale),
        in_specs=[whole] * 8 + [anywhere],
        out_specs=[whole] * 10 + [anywhere] * 3,
        out_shape=(
            shape((heads, tokens, LANES), BF16),
            shape((heads, tokens, LANES), BF16),
            shape((heads, tokens, LANES), BF16),
            shape((tokens, heads * LANES), BF16),
            shape((heads, 1, tokens), F32),
            shape((size, width), F32),
            shape((size, width), BF16),
            shape((tokens, LANES), F32),
            shape((tokens, LANES), F32),
            shape((1, tokens), jnp.int32),
            shape((tokens, width), BF16),
            shape(w_all_shape, BF16),
            shape((2 * size, width), BF16),
        ),
        scratch_shapes=[
            pltpu.VMEM((1, tokens), jnp.int32),
            pltpu.VMEM((tokens, 1), jnp.int32),
            pltpu.VMEM((2 * size, width), BF16),
            pltpu.VMEM((tokens, width), BF16),
            pltpu.VMEM(w_all_shape, BF16),
            pltpu.VMEM((count, size, heads * LANES), BF16),
            dma((half, 2)),
            dma((half, 2)),
            dma((half, 2)),
            dma((half, 2)),
            dma((max(planes - 1, 1), half)),
            dma((max(planes - 1, 1), half)),
            dma((planes,)),
            dma((planes,)),
            dma((count,)),
            dma((count,)),
            dma((2,)),
            dma((2,)),
            dma((half,)),
            dma((grp_count,)),
            dma((2,)),
        ],
        compiler_params=pltpu.CompilerParams(
            collective_id=1, has_side_effects=True, vmem_limit_bytes=56 * MIB
        ),
        cost_estimate=KERNEL_COST,
        name="attend_forward",
    )(
        hidden, cot_own, first_gain[None, :], gain[None, :], w, b, segments[:, None],
        segments[None, :], w_out,
    )


def attend_backward_kernel(
    count, grp_count, heads, scale, g_own, w_all, w, cosine, sine, q, k, v, row_logs, row_starts,
    *refs,
):
    number = (len(refs) - 17) // 2
    bulk, refs = refs[:number], refs[number:]
    g_out, bias_out, branch_out, group_out = refs[:4]
    landed = refs[4 : 4 + number]
    (
        row_positions, positions, g_att, dk, dv, outbox, gs, send_sems, recv_sems, ring_send,
        ring_recv, store_sems, plane_sems,
    ) = refs[4 + number :]
    size, width = g_own.shape
    tokens = size * count
    rows = block_rows_of(tokens)
    dim = LANES
    inner_size = heads * dim
    planes = grp_count // 2
    mine = lax.axis_index("grp")
    core, plane = mine % 2, mine // 2
    part_width = width // grp_count

    ring = KernelRing(gs, count, size, ring_send, ring_recv)

    def store(i):
        here = rows_at(i, 2 * size)
        return pltpu.make_async_copy(gs.at[here], group_out.at[here], store_sems.at[i])

    def next_pair(i):
        ring.arrive(i)
        ring.forward(i)
        store(i).start()

    greet("ep", count)
    greet("grp", grp_count)
    gs[ring.own(), :] = g_own[...]
    pl.semaphore_wait(pltpu.get_barrier_semaphore(), count - 1 + grp_count - 1)
    plane_copies = PlaneCopies(list(zip(bulk, landed)), grp_count // 2, plane_sems)
    plane_copies.start()
    for slot in range(count):
        first = slot_index(count, slot) * size
        row_positions[:, slot * size : (slot + 1) * size] = first + lax.broadcasted_iota(
            jnp.int32, (1, size), 1
        )
        positions[slot * size : (slot + 1) * size, :] = first + lax.broadcasted_iota(
            jnp.int32, (size, 1), 0
        )
    own_rows = None
    for j in range(grp_count):
        member = 2 * ((plane + j % planes) % planes) + (core if j < planes else 1 - core)
        columns = pl.ds(pl.multiple_of(member * part_width, part_width), part_width)
        piece = dot_nt(g_own[:, columns], w_all[j])
        own_rows = piece if own_rows is None else own_rows + piece
    own_rows = own_rows.astype(BF16)
    for slot in range(count):
        outbox[slot] = own_rows[:, slot * inner_size : (slot + 1) * inner_size]
    exchange = Exchange(
        count,
        lambda slot: outbox.at[slot],
        lambda slot: g_att.at[rows_at(slot, size)],
        send_sems,
        recv_sems,
    )
    for slot in exchange.others():
        exchange.copy(slot).start()
    ring.start()
    g_att[(count - 2) * size : (count - 1) * size, :] = outbox[count - 2]
    dk[...] = jnp.zeros_like(dk)
    dv[...] = jnp.zeros_like(dv)
    for slot in exchange.others():
        exchange.arrived(slot).wait_recv()

    def scores_back(i, carry):
        here = rows_at(i, rows)
        own, start = row_positions[:, here], row_starts[:, here]
        keys_at = positions[...]
        allowed = (keys_at <= own) & (keys_at >= start)
        cos, sin = cosine[here, :], sine[here, :]
        for h in range(heads):
            query = q[h, here, :]
            g_block = g_att[here, h * dim : (h + 1) * dim]
            scores = dot_nt(k[h], query) * scale - row_logs[h, :, here]
            weights = jnp.exp(jnp.where(allowed, scores, NEGATIVE))
            g_weights = dot_nt(v[h], g_block)
            inner = jnp.sum(weights * g_weights, 0, keepdims=True)
            g_scores = (weights * (g_weights - inner)).astype(BF16)
            g_query = dot_tn(g_scores, k[h]) * scale
            g_query = g_query * cos - pltpu.roll(g_query, dim // 2, 1) * sin
            g_out[here, 3 * dim * h : 3 * dim * h + dim] = g_query.astype(BF16)
            dk[h] += dot(g_scores, query)
            dv[h] += dot(weights.astype(BF16), g_block)

        @pl.when(i == 1)
        def _():
            next_pair(0)

        @pl.when(i == 3)
        def _():
            next_pair(1)

        return carry

    lax.fori_loop(0, tokens // rows, scores_back, 0)
    bias_out[...] = jnp.zeros_like(bias_out)

    def finish(i, carry):
        here = rows_at(i, rows)
        cos, sin = cosine[here, :], sine[here, :]
        for h in range(heads):
            base = 3 * dim * h
            g_key = dk[h, here, :] * scale
            g_key = g_key * cos - pltpu.roll(g_key, dim // 2, 1) * sin
            g_out[here, base + dim : base + 2 * dim] = g_key.astype(BF16)
            g_out[here, base + 2 * dim : base + 3 * dim] = dv[h, here, :].astype(BF16)
        g_here = g_out[here, :]
        bias_out[...] += jnp.sum(g_here.astype(F32), 0, keepdims=True)
        branch_out[here, :] = dot_nt(g_here, w[...]).astype(BF16)
        return carry

    lax.fori_loop(0, tokens // rows, finish, 0)
    for i in range(2, count // 2):
        next_pair(i)
    for slot in exchange.others():
        exchange.copy(slot).wait_send()
    ring.finish()
    for i in range(count // 2):
        store(i).wait()
    plane_copies.finish()


def attend_backward(
    count, grp_count, g_own, w_all, w, cosine, sine, q, k, v, logs, starts, scale, bulk
):
    size, width = g_own.shape
    heads, tokens, _ = q.shape
    anywhere = pl.BlockSpec(memory_space=pl.ANY)
    whole = pl.BlockSpec(memory_space=pltpu.VMEM)
    shape = jax.ShapeDtypeStruct
    dma = pltpu.SemaphoreType.DMA
    return pl.pallas_call(
        functools.partial(attend_backward_kernel, count, grp_count, heads, scale),
        in_specs=[whole] * 10 + [anywhere] * len(bulk),
        out_specs=[whole] * 3 + [anywhere] * (1 + len(bulk)),
        out_shape=(
            shape((tokens, 3 * LANES * heads), BF16),
            shape((1, 3 * LANES * heads), F32),
            shape((tokens, width), BF16),
            shape((tokens, width), BF16),
            *[shape(value.shape, value.dtype) for value in bulk],
        ),
        scratch_shapes=[
            pltpu.VMEM((1, tokens), jnp.int32),
            pltpu.VMEM((tokens, 1), jnp.int32),
            pltpu.VMEM((tokens, heads * LANES), BF16),
            pltpu.VMEM((heads, tokens, LANES), F32),
            pltpu.VMEM((heads, tokens, LANES), F32),
            pltpu.VMEM((count, size, heads * LANES), BF16),
            pltpu.VMEM((tokens, width), BF16),
            dma((count,)),
            dma((count,)),
            dma((count // 2, 2)),
            dma((count // 2, 2)),
            dma((count // 2,)),
            dma((2, max(len(bulk), 1))),
        ],
        compiler_params=pltpu.CompilerParams(
            collective_id=2, has_side_effects=True, vmem_limit_bytes=56 * MIB
        ),
        cost_estimate=KERNEL_COST,
        name="attend_backward",
    )(
        g_own, w_all, w, cosine, sine, q, k, v,
        logs, starts, *bulk,
    )


def doubling_stages(axes):
    stages = []
    for axis in axes:
        step = lax.axis_size(axis) // 2
        while step:
            stages.append((axis, step))
            step //= 2
    return stages


class Doubling:
    def __init__(self, held, arrived, stages, sems):
        self.held, self.arrived, self.stages, self.sems = held, arrived, stages, sems
        self.place = 0

    def copy(self, k):
        axis, step = self.stages[k]
        here = lax.axis_index(axis)
        return pltpu.make_async_remote_copy(
            src_ref=self.held.at[k],
            dst_ref=self.arrived.at[k],
            send_sem=self.sems.at[0, k],
            recv_sem=self.sems.at[1, k],
            device_id={axis: here + step * (1 - 2 * (here // step % 2))},
            device_id_type=MESH,
        )

    def start(self):
        self.copy(0).start()

    def advance(self):
        k = self.place
        if k < len(self.stages):
            self.copy(k).wait_recv()
            self.held[k + 1] = self.held[k] + self.arrived[k]
            if k + 1 < len(self.stages):
                self.copy(k + 1).start()
            self.place += 1

    def finish(self):
        while self.place < len(self.stages):
            self.advance()
        for k in range(len(self.stages)):
            self.copy(k).wait_send()
        return self.held[len(self.stages)]


class RingSum:
    def __init__(self, count, part, out, to_right, to_left, send_sems, recv_sems):
        place, index_at = ring_places(count)
        self.count, self.half, self.size = count, count // 2, out.shape[0]
        self.part, self.out, self.held = part, out, (to_right, to_left)
        self.send_sems, self.recv_sems = send_sems, recv_sems
        self.neighbours = (
            index_at((place + 1) % count), index_at((place + count - 1) % count)
        )

    def copy(self, step, way):
        held, middle = self.held[way], self.size // 2
        if step == 0:
            source = self.part.at[pl.ds((self.count - 1) * self.size + way * middle, middle)]
            target = held.at[0, pl.ds(way * middle, middle)]
        else:
            source, target = held.at[step - 1], held.at[step]
        return pltpu.make_async_remote_copy(
            src_ref=source,
            dst_ref=target,
            send_sem=self.send_sems.at[step, way],
            recv_sem=self.recv_sems.at[step, way],
            device_id={"ep": self.neighbours[way]},
            device_id_type=MESH,
        )

    def start(self):
        for way in range(2):
            self.copy(0, way).start()

    def advance(self, step):
        middle, part = self.size // 2, self.part
        for way in range(2):
            held = self.held[way]
            first = (2 * (self.half - step) - 1 - way) * self.size
            self.copy(step - 1, way).wait_recv()
            if step == 1:
                here = slice(way * middle, (way + 1) * middle)
                rest = slice((1 - way) * middle, (2 - way) * middle)
                own = part[first + way * middle : first + (way + 1) * middle, :]
                held[0, here] = (own.astype(F32) + held[0, here].astype(F32)).astype(BF16)
                held[0, rest] = part[first + (1 - way) * middle : first + (2 - way) * middle, :]
            else:
                own = part[first : first + self.size, :]
                held[step - 1] = (own.astype(F32) + held[step - 1].astype(F32)).astype(BF16)
            self.copy(step, way).start()

    def last(self):
        own = self.part[(self.count - 2) * self.size : (self.count - 1) * self.size, :]
        total = own.astype(F32)
        for way in range(2):
            self.copy(self.half - 1, way).wait_recv()
            total = total + self.held[way][self.half - 1].astype(F32)
        self.out[...] = total

    def finish(self):
        for step in range(self.half):
            for way in range(2):
                self.copy(step, way).wait_send()


def reduce_kernel(count, part, out, to_right, to_left, send_sems, recv_sems):
    greet("ep", count)
    pl.semaphore_wait(pltpu.get_barrier_semaphore(), count - 1)
    ring = RingSum(count, part, out, to_right, to_left, send_sems, recv_sems)
    ring.start()
    for step in range(1, count // 2):
        ring.advance(step)
    ring.last()
    ring.finish()


def reduce_rows(count, part):
    tokens, width = part.shape
    size, half = tokens // count, count // 2
    whole = pl.BlockSpec(memory_space=pltpu.VMEM)
    return pl.pallas_call(
        functools.partial(reduce_kernel, count),
        in_specs=[whole],
        out_specs=whole,
        out_shape=jax.ShapeDtypeStruct((size, width), F32),
        scratch_shapes=[pltpu.VMEM((half, size, width), BF16)] * 2
        + [pltpu.SemaphoreType.DMA((half, 2))] * 2,
        compiler_params=pltpu.CompilerParams(
            collective_id=3, has_side_effects=True, vmem_limit_bytes=56 * MIB
        ),
        cost_estimate=KERNEL_COST,
        name="reduce_rows",
    )(part)


def finish_kernel(
    count, grp_count, bulk_number, branch, out_parts, small, bias, gain, g_qkv, attended, w,
    x_in, attn_in, *refs
):
    refs = list(refs)

    def take(amount):
        taken = refs[:amount]
        del refs[:amount]
        return taken

    planes = grp_count // 2
    far_number = planes - 1
    bulk = take(bulk_number)
    branch_sum, out_sum, small_sum, bias_sum, own_q, own_o = take(6)
    landed = take(bulk_number + 2 * far_number)
    rings_held = take(4)
    x, attn = take(2)
    away, arrived, far = take(2), take(2), take(2)
    small_held, small_arrived, bias_held, bias_arrived = take(4)
    (
        send_sems, recv_sems, small_sems, bias_sems, plane_sems, load_sems, core_send, core_recv
    ) = take(8)
    mine = lax.axis_index("grp")
    core, plane = mine % 2, mine // 2
    part_width = x.shape[2]
    orders = list(range(1, planes)) + [0]
    units = [(side, place) for side in (1, 0) for place in range(planes)]

    def columns(unit):
        side, place = units[unit]
        member = 2 * ((plane + orders[place]) % planes) + (core if side == 0 else 1 - core)
        return pl.ds(pl.multiple_of(member * part_width, part_width), part_width)

    def loads(unit):
        slot = unit % 2
        return [
            pltpu.make_async_copy(
                source.at[:, columns(unit)], target.at[slot], load_sems.at[i, slot]
            )
            for i, (source, target) in enumerate(((x_in, x), (attn_in, attn)))
        ]

    for unit in range(2):
        for load in loads(unit):
            load.start()
    greet("ep", count)
    greet("grp", grp_count)
    small_held[0] = small[...]
    bias_held[0] = bias[...]
    pl.semaphore_wait(pltpu.get_barrier_semaphore(), count - 1 + grp_count - 1)
    rings = [
        RingSum(
            count, part, out, rings_held[2 * a], rings_held[2 * a + 1], send_sems.at[a],
            recv_sems.at[a],
        )
        for a, (part, out) in enumerate(((branch, branch_sum), (out_parts, out_sum)))
    ]
    for ring in rings:
        ring.start()
    sums = [
        Doubling(small_held, small_arrived, doubling_stages(("grp", "ep")), small_sems),
        Doubling(bias_held, bias_arrived, doubling_stages(("grp",)), bias_sems),
    ]
    sums[1].start()
    halves = bulk_number // 2
    sources = [bulk[i].at[0] for i in range(halves)]
    targets = [landed[2 * far_number + i].at[0] for i in range(halves)]
    for kind in range(2):
        for place in range(far_number):
            sources.append(far[kind].at[place])
            targets.append(landed[kind * far_number + place])
    sources += [bulk[i].at[1] for i in range(halves)] + bulk[halves:]
    targets += [landed[2 * far_number + i].at[1] for i in range(halves)]
    targets += landed[2 * far_number + halves :]
    far_copies = PlaneCopies(list(zip(sources, targets)), planes, plane_sems)
    far_copies.start(0, halves)

    def to_core(kind, place):
        return pltpu.make_async_remote_copy(
            src_ref=away[kind].at[place],
            dst_ref=arrived[kind].at[place],
            send_sem=core_send.at[kind, place],
            recv_sem=core_recv.at[kind, place],
            device_id={"grp": mine + 1 - 2 * core},
            device_id_type=MESH,
        )

    for unit, (side, place) in enumerate(units):
        cut, slot = columns(unit), unit % 2
        for load in loads(unit):
            load.wait()
        q_piece = dot_tn(x[slot], g_qkv[...])
        inner = jnp.sum(q_piece * w[cut, :].astype(F32), -1, keepdims=True)
        inner = jnp.transpose(jnp.broadcast_to(inner, (part_width, LANES)))[:1, :]
        small_held[0, small.shape[0] - 1 :, cut] = inner / gain[:, cut]
        o_piece = dot_tn(attended[...], attn[slot])
        for kind, piece in enumerate((q_piece, o_piece)):
            if side == 1:
                away[kind][place] = piece.astype(BF16)
                to_core(kind, place).start()
            else:
                to_core(kind, place).wait_recv()
                piece = piece + arrived[kind][place].astype(F32)
                if orders[place]:
                    far[kind][place] = piece.astype(BF16)
                else:
                    (own_q, own_o)[kind][...] = piece
        if unit + 2 < len(units):
            for load in loads(unit + 2):
                load.start()
    sums[0].start()
    far_copies.start(halves)
    for step in range(1, count // 2):
        for a, ring in enumerate(rings):
            ring.advance(step)
            if a or step == 1:
                for item in sums:
                    item.advance()
    for ring in rings:
        ring.last()
    small_sum[...] = sums[0].finish()
    bias_sum[...] = sums[1].finish()
    for ring in rings:
        ring.finish()
    for kind in range(2):
        for place in range(planes):
            to_core(kind, place).wait_send()
    far_copies.finish()


def finish(
    count, grp_count, branch, out_parts, small, bias, gain, g_qkv, attended, w, x, attn, bulk
):
    tokens, width = branch.shape
    size, half, planes = tokens // count, count // 2, grp_count // 2
    part_width = width // grp_count
    q_shape, o_shape = (part_width, g_qkv.shape[1]), (attended.shape[1], part_width)
    stages = len(doubling_stages(("grp", "ep"))), len(doubling_stages(("grp",)))
    anywhere = pl.BlockSpec(memory_space=pl.ANY)
    whole = pl.BlockSpec(memory_space=pltpu.VMEM)
    shape = jax.ShapeDtypeStruct
    dma = pltpu.SemaphoreType.DMA
    landed = [shape(dims, BF16) for dims in (q_shape, o_shape) for _ in range(planes - 1)]
    landed += [shape(value.shape, value.dtype) for value in bulk]
    results = pl.pallas_call(
        functools.partial(finish_kernel, count, grp_count, len(bulk)),
        in_specs=[whole] * 8 + [anywhere] * (2 + len(bulk)),
        out_specs=[whole] * 6 + [anywhere] * len(landed),
        out_shape=[
            shape((size, width), F32),
            shape((size, width), F32),
            shape(small.shape, F32),
            shape(bias.shape, F32),
            shape(q_shape, F32),
            shape(o_shape, F32),
            *landed,
        ],
        scratch_shapes=[pltpu.VMEM((half, size, width), BF16)] * 4
        + [pltpu.VMEM((2, tokens, part_width), BF16)] * 2
        + [pltpu.VMEM((planes, *dims), BF16) for dims in (q_shape, o_shape)] * 2
        + [pltpu.VMEM((max(planes - 1, 1), *dims), BF16) for dims in (q_shape, o_shape)]
        + [
            pltpu.VMEM((stages[0] + 1, *small.shape), F32),
            pltpu.VMEM((stages[0], *small.shape), F32),
            pltpu.VMEM((stages[1] + 1, *bias.shape), F32),
            pltpu.VMEM((stages[1], *bias.shape), F32),
        ]
        + [dma((2, half, 2))] * 2
        + [dma((2, stages[0])), dma((2, stages[1])), dma((2, len(landed) + len(bulk) // 2)), dma((2, 2))]
        + [dma((2, planes))] * 2,
        compiler_params=pltpu.CompilerParams(
            collective_id=4, has_side_effects=True, vmem_limit_bytes=60 * MIB
        ),
        cost_estimate=KERNEL_COST,
        name="finish",
    )(branch, out_parts, small, bias, gain, g_qkv, attended, w, x, attn, *bulk)
    return results[:6], results[6:]


def reduce_and_weights_kernel(
    count, grp_count, expert_count, part, residual, cot_own, gain, grad_logits, x_in, cot_in,
    grad_e_in, act_e_in, grad_s_in, act_s_in, *refs
):
    refs = list(refs)

    def take(amount):
        taken = refs[:amount]
        del refs[:amount]
        return taken

    planes = grp_count // 2
    grad_residual, own_attn, small = take(3)
    outs = [take(planes) for _ in range(5)]
    landed = take(planes - 1)
    sources = (x_in, grad_e_in, cot_in, act_e_in, grad_s_in, act_s_in)
    held = take(6)
    (summed,) = take(1)
    x, grad_e, cot, act_e, grad_s, act_s = held
    to_right, to_left = take(2)
    staged, arrived = take(5), take(5)
    send_sems, recv_sems, load_sems, core_send, core_recv, out_sems, plane_sems = take(7)
    mine = lax.axis_index("grp")
    core, plane = mine % 2, mine // 2
    part_width = x.shape[1] // grp_count

    loads = [
        pltpu.make_async_copy(source, target, load_sems.at[i])
        for i, (source, target) in enumerate(zip(sources, held))
    ]
    for load in loads:
        load.start()
    greet("ep", count)
    greet("grp", grp_count)
    pl.semaphore_wait(pltpu.get_barrier_semaphore(), count - 1 + grp_count - 1)
    ring = RingSum(count, part, summed, to_right, to_left, send_sems, recv_sems)
    ring.start()

    def columns(order, side):
        member = 2 * ((plane + order) % planes) + (core if side == 0 else 1 - core)
        return pl.ds(pl.multiple_of(member * part_width, part_width), part_width)

    def products(kind, cut):
        if kind < 2:
            return [dot_tn(x[:, cut], grad_e[kind])]
        if kind == 2:
            return [dot_tn(act_e[...], cot[:, cut])]
        if kind == 3:
            return [dot_tn(grad_s[k], x[:, cut]) for k in range(2)]
        return [dot_tn(act_s[...], cot[:, cut])]

    def to_core(kind, place):
        return pltpu.make_async_remote_copy(
            src_ref=staged[kind],
            dst_ref=arrived[kind].at[place],
            send_sem=core_send.at[kind, place],
            recv_sem=core_recv.at[kind, place],
            device_id={"grp": mine + 1 - 2 * core},
            device_id_type=MESH,
        )

    def store(kind, place):
        return pltpu.make_async_copy(staged[kind], outs[kind][place], out_sems.at[kind, place])

    orders = list(range(1, planes)) + [0]
    needs = ((0, 1), (), (2, 3), (4,), (5,))
    plane_copies = PlaneCopies(list(zip(outs[0][: planes - 1], landed)), planes, plane_sems)
    ring_step = 1
    number = 0
    for place, order in enumerate(orders):
        for side in (1, 0):
            for kind in range(5):
                if side == 1 and place == 0:
                    for i in needs[kind]:
                        loads[i].wait()
                pieces = products(kind, columns(order, side))
                if side == 1:
                    if place and kind:
                        store(kind, place - 1).wait()
                else:
                    to_core(kind, place).wait_recv()
                    to_core(kind, place).wait_send()
                for k, piece in enumerate(pieces):
                    whole = (k,) if len(pieces) > 1 else (Ellipsis,)
                    if side == 0:
                        piece = piece + arrived[kind][(place, *whole)].astype(F32)
                    staged[kind][whole] = piece.astype(BF16)
                if side == 1:
                    to_core(kind, place).start()
                else:
                    store(kind, place).start()
                if side == 0 and kind == 1 and order:
                    store(0, place).wait()
                    plane_copies.copies[place].start()
                number += 1
                if number % 5 == 2:
                    if ring_step < count // 2:
                        ring.advance(ring_step)
                    ring_step += 1
                if number == 5:
                    rows = dot_tn(grad_logits[:, :LANES], x[...])
                    rows = rows + dot_tn(grad_logits[:, LANES:], x[...])
                    small[: expert_count + 1, :] = rows[: expert_count + 1, :]
    while ring_step < count // 2:
        ring.advance(ring_step)
        ring_step += 1
    ring.last()
    normal, factor = norm_of(residual[...])
    total = summed[...]
    own = cot_own[...].astype(F32) + norm_back(total, normal, factor, gain[...])
    grad_residual[...] = own
    own_attn[...] = own.astype(BF16)
    small[expert_count + 1 : expert_count + 2, :] = jnp.sum(total * normal, 0, keepdims=True)
    small[expert_count + 2 :, :] = jnp.zeros((1, small.shape[1]), F32)
    for kind in range(5):
        store(kind, planes - 1).wait()
    ring.finish()
    plane_copies.finish()


def reduce_and_weights(
    count, grp_count, expert_count, part, residual, cot_own, gain, grad_logits, x, cot, grad_e,
    act_e, grad_s, act_s,
):
    tokens, width = part.shape
    size, half, planes = tokens // count, count // 2, grp_count // 2
    part_width = width // grp_count
    wide, narrow = act_e.shape[1], act_s.shape[1]
    shapes = [
        (part_width, wide), (part_width, wide), (wide, part_width), (2, narrow, part_width),
        (narrow, part_width),
    ]
    anywhere = pl.BlockSpec(memory_space=pl.ANY)
    whole = pl.BlockSpec(memory_space=pltpu.VMEM)
    shape = jax.ShapeDtypeStruct
    dma = pltpu.SemaphoreType.DMA
    rows = pl.pallas_call(
        functools.partial(reduce_and_weights_kernel, count, grp_count, expert_count),
        in_specs=[whole] * 5 + [anywhere] * 6,
        out_specs=[whole] * 3 + [anywhere] * (6 * planes - 1),
        out_shape=[
            shape((size, width), F32),
            shape((size, width), BF16),
            shape((expert_count + 3, width), F32),
        ]
        + [shape(dims, BF16) for dims in shapes for _ in range(planes)]
        + [shape(shapes[0], BF16)] * (planes - 1),
        scratch_shapes=[
            pltpu.VMEM(value.shape, BF16) for value in (x, grad_e, cot, act_e, grad_s, act_s)
        ]
        + [pltpu.VMEM((size, width), F32)]
        + [pltpu.VMEM((half, size, width), BF16)] * 2
        + [pltpu.VMEM(dims, BF16) for dims in shapes]
        + [pltpu.VMEM((planes, *dims), BF16) for dims in shapes]
        + [dma((half, 2)), dma((half, 2)), dma((6,))]
        + [dma((5, planes))] * 3
        + [dma((2, max(planes - 1, 1)))],
        compiler_params=pltpu.CompilerParams(
            collective_id=3, has_side_effects=True, vmem_limit_bytes=60 * MIB
        ),
        cost_estimate=KERNEL_COST,
        name="reduce_and_weights",
    )(part, residual, cot_own, gain, grad_logits, x, cot, grad_e, act_e, grad_s, act_s)
    rows, slices = rows[:3], list(rows[3:])
    groups = [slices[i * planes : (i + 1) * planes] for i in range(5)]
    passed, own = [group[:-1] for group in groups], [group[-1] for group in groups]
    return (*rows, passed, own, slices[5 * planes :])


def tiles_of(width):
    tiles, start = [], 0
    while width - start > 384:
        tiles.append((start, 256))
        start += 256
    tiles.append((start, width - start))
    return tiles


def experts_kernel(
    count, expert_count, x_own, cot_own, routes, routes_w, near, gate_up_e, down_e, gate_up_s,
    down_s, act_e_out, grad_e_out, act_s_out, grad_s_out, part_out, branch_out, logits_out, x_out,
    cot_out,
    xs, cots, gate_e, up_e, held_e, gate_s, up_s, held_s, act_e, grad_e, act_s, grad_s, part,
    branch, logits_held, x_send, x_recv, cot_send, cot_recv, weight_sems, out_sems, x_sems,
):
    half = count // 2
    size = x_own.shape[0]
    rows = 2 * size
    ring_x = KernelRing(xs, count, size, x_send, x_recv)
    ring_cot = KernelRing(cots, count, size, cot_send, cot_recv)

    barrier = pltpu.get_barrier_semaphore()
    for neighbour in (ring_x.left, ring_x.right):
        pl.semaphore_signal(barrier, inc=1, device_id={"ep": neighbour}, device_id_type=MESH)
    loads = [
        pltpu.make_async_copy(source, target, weight_sems.at[i])
        for i, (source, target) in enumerate(
            [
                (gate_up_e.at[0, 0], gate_e),
                (gate_up_e.at[0, 1], up_e),
                (down_e.at[0], held_e),
                (gate_up_s.at[0], gate_s),
                (gate_up_s.at[1], up_s),
                (down_s, held_s),
            ]
        )
    ]
    load_near = pltpu.make_async_copy(near, cots.at[pl.ds(0, rows)], weight_sems.at[6])
    load_near.start()
    for load in loads:
        load.start()
    xs[ring_x.own(), :] = x_own[...]
    cots[ring_x.own(), :] = cot_own[...]
    pl.semaphore_wait(barrier, 2)
    ring_x.start()
    load_near.wait()
    ring_cot.forward(0)

    def stores(i):
        here = rows_at(i, rows)
        slot = lax.rem(i, 2)
        pieces = [
            (act_e.at[slot], act_e_out.at[here]),
            (grad_e.at[slot, 0], grad_e_out.at[0, here]),
            (grad_e.at[slot, 1], grad_e_out.at[1, here]),
            (act_s.at[slot], act_s_out.at[here]),
            (grad_s.at[slot, 0], grad_s_out.at[0, here]),
            (grad_s.at[slot, 1], grad_s_out.at[1, here]),
            (part.at[slot], part_out.at[here]),
            (branch.at[slot], branch_out.at[here]),
            (logits_held.at[slot], logits_out.at[here]),
        ]
        return [
            pltpu.make_async_copy(source, target, out_sems.at[slot, k])
            for k, (source, target) in enumerate(pieces)
        ]

    def store_rows(i):
        here = rows_at(i, rows)
        return [
            pltpu.make_async_copy(xs.at[here], x_out.at[here], x_sems.at[0, i]),
            pltpu.make_async_copy(cots.at[here], cot_out.at[here], x_sems.at[1, i]),
        ]

    sections = (
        (gate_e, up_e, held_e, act_e, grad_e, dot, dot_nt),
        (gate_s, up_s, held_s, act_s, grad_s, dot_nt, dot),
    )
    mine = lax.axis_index("ep")
    onehot = (lax.broadcasted_iota(jnp.int32, (1, LANES), 1) == mine).astype(F32)

    def one_pair(i, carry):
        slot = lax.rem(i, 2)
        here = rows_at(i, rows)
        ring_x.arrive(i)
        ring_x.forward(i)

        @pl.when(i > 0)
        def _():
            ring_cot.arrive(i)
            ring_cot.forward(i)

        for copy in store_rows(i):
            copy.start()

        @pl.when(i == 0)
        def _():
            for load in loads:
                load.wait()

        @pl.when(i >= 2)
        def _():
            for copy in stores(i - 2):
                copy.wait()

        lane = lax.broadcasted_iota(jnp.int32, (rows, LANES), 1)
        inputs, cotangent = xs[here, :], cots[here, :]
        logits = dot(inputs, routes_w[...])
        routed = jnp.where(lane < expert_count, logits, NEGATIVE)
        expo = jnp.exp(routed - jnp.max(routed, -1, keepdims=True))
        probs = expo * (1.0 / jnp.sum(expo, -1, keepdims=True))
        named = jnp.concatenate(
            [routes[rows_at(slot_index(count, 2 * i + k), size), :] for k in range(2)], 0
        )
        hits = jnp.sum(jnp.where(named == mine, 1.0, 0.0), -1, keepdims=True)
        own_prob = jnp.sum(probs * onehot, -1, keepdims=True) * hits
        share_logit = jnp.sum(jnp.where(lane == expert_count, logits, 0.0), -1, keepdims=True)
        share = 1.0 / (1.0 + jnp.exp(-share_logit))

        inner = []
        total, out_total = None, None
        for s, (gate_w, up_w, down_w, act_out, grad_out, ahead, back_dot) in enumerate(sections):
            factor = own_prob if s == 0 else share
            dots = jnp.zeros((rows, 1), F32)
            for start, width in tiles_of(down_w.shape[0]):
                cut = pl.ds(start, width)
                piece = (slice(None), cut) if s == 0 else (cut, slice(None))
                gate = ahead(inputs, gate_w[piece])
                up = ahead(inputs, up_w[piece])
                grad = dot_nt(cotangent, down_w[cut, :])
                sigma = 0.5 * jnp.tanh(0.5 * gate) + 0.5
                silu = gate * sigma
                act = (silu * up).astype(BF16).astype(F32)
                dots = dots + jnp.sum(grad * act, -1, keepdims=True)
                scaled = grad * factor
                act_out[slot, :, cut] = (act * factor).astype(BF16)
                grad_out[slot, 0, :, cut] = (
                    scaled * up * (sigma + silu * (1.0 - sigma))
                ).astype(BF16)
                grad_out[slot, 1, :, cut] = (scaled * silu).astype(BF16)
            inner.append(dots)
            back = back_dot(grad_out[slot, 0], gate_w[...]) + back_dot(
                grad_out[slot, 1], up_w[...]
            )
            total = back if total is None else total + back
            out_piece = dot(act_out[slot], down_w[...])
            out_total = out_piece if out_total is None else out_total + out_piece
        branch[slot] = out_total.astype(BF16)
        grad_logits = own_prob * inner[0] * (onehot - probs)
        grad_share = share * (1.0 - share) * inner[1]
        grad_logits = grad_logits + jnp.where(lane == expert_count, grad_share, 0.0)
        high = grad_logits.astype(BF16)
        low = (grad_logits - high.astype(F32)).astype(BF16)
        total = total + dot_nt(high, routes_w[...]) + dot_nt(low, routes_w[...])
        logits_held[slot, :, :LANES] = high
        logits_held[slot, :, LANES:] = low
        part[slot] = total.astype(BF16)
        for copy in stores(i):
            copy.start()
        return carry

    lax.fori_loop(0, half, one_pair, 0)
    for i in range(half):
        for copy in store_rows(i):
            copy.wait()
    for i in range(max(half - 2, 0), half):
        for copy in stores(i):
            copy.wait()
    ring_x.finish()
    ring_cot.finish(1)


def experts(
    count, expert_count, x_own, cot_own, routes, routes_w, near, gate_up_e, down_e, gate_up_s,
    down_s,
):
    size, width = x_own.shape
    tokens, rows, half = size * count, 2 * size, count // 2
    wide, narrow = down_e.shape[1], down_s.shape[0]
    anywhere = pl.BlockSpec(memory_space=pl.ANY)
    whole = pl.BlockSpec(memory_space=pltpu.VMEM)
    shape = jax.ShapeDtypeStruct
    dma = pltpu.SemaphoreType.DMA
    return pl.pallas_call(
        functools.partial(experts_kernel, count, expert_count),
        in_specs=[whole] * 4 + [anywhere] * 5,
        out_specs=[anywhere] * 9,
        out_shape=(
            shape((tokens, wide), BF16),
            shape((2, tokens, wide), BF16),
            shape((tokens, narrow), BF16),
            shape((2, tokens, narrow), BF16),
            shape((tokens, width), BF16),
            shape((tokens, width), BF16),
            shape((tokens, 2 * LANES), BF16),
            shape((tokens, width), BF16),
            shape((tokens, width), BF16),
        ),
        scratch_shapes=[
            pltpu.VMEM((tokens, width), BF16),
            pltpu.VMEM((tokens, width), BF16),
            pltpu.VMEM((width, wide), BF16),
            pltpu.VMEM((width, wide), BF16),
            pltpu.VMEM((wide, width), BF16),
            pltpu.VMEM((narrow, width), BF16),
            pltpu.VMEM((narrow, width), BF16),
            pltpu.VMEM((narrow, width), BF16),
            pltpu.VMEM((2, rows, wide), BF16),
            pltpu.VMEM((2, 2, rows, wide), BF16),
            pltpu.VMEM((2, rows, narrow), BF16),
            pltpu.VMEM((2, 2, rows, narrow), BF16),
            pltpu.VMEM((2, rows, width), BF16),
            pltpu.VMEM((2, rows, width), BF16),
            pltpu.VMEM((2, rows, 2 * LANES), BF16),
            dma((half, 2)),
            dma((half, 2)),
            dma((half, 2)),
            dma((half, 2)),
            dma((7,)),
            dma((2, 9)),
            dma((2, half)),
        ],
        compiler_params=pltpu.CompilerParams(
            collective_id=0, has_side_effects=True, vmem_limit_bytes=60 * MIB
        ),
        cost_estimate=KERNEL_COST,
        name="experts",
    )(x_own, cot_own, routes, routes_w, near, gate_up_e, down_e, gate_up_s, down_s)


def norm_of(values):
    factor = lax.rsqrt(jnp.mean(values * values, -1, keepdims=True) + EPS)
    return values * factor, factor


def norm_back(grad_out, normal, factor, gain):
    scaled = grad_out * gain
    return factor * (scaled - normal * jnp.mean(scaled * normal, -1, keepdims=True))


def local(
    hidden_in, segments, routes, cotangent, norm1_gain, w_qkv, b_qkv, w_out, norm2_gain, router,
    shared_gate_up, shared_down, shared_gate, expert_gate_up, expert_down,
):
    tokens_here, width = hidden_in.shape
    ep_count = lax.axis_size("ep")
    grp_count = lax.axis_size("grp")
    expert_count = router.shape[1]
    heads, qkv_dim = b_qkv.shape
    head_dim = qkv_dim // 3
    scale = 1.0 / math.sqrt(head_dim)
    slice_width = width // grp_count
    routes_w = jnp.concatenate(
        [router, shared_gate[:, None], jnp.zeros((width, LANES - 1 - expert_count), BF16)], 1
    )
    w_flat = w_qkv.reshape(width, heads * qkv_dim)
    b_flat = b_qkv.reshape(1, heads * qkv_dim)
    w_out_flat = w_out.reshape(heads * head_dim, width)

    (
        queries, key_rows, values, attended, logs, residual, normed_two, cosine, sine, starts,
        group_one, w_all, near_cot,
    ) = attend_forward(
        ep_count, grp_count, hidden_in, cotangent, norm1_gain, norm2_gain, w_flat, b_flat, w_out_flat,
        segments, scale,
    )

    (
        expert_act, expert_grad, shared_act, shared_grad, part, out_parts, grad_logits,
        group_two, group_cot,
    ) = experts(
        ep_count, expert_count, normed_two, cotangent, routes, routes_w, near_cot,
        expert_gate_up, expert_down, jnp.swapaxes(shared_gate_up, 1, 2), shared_down,
    )

    if ep_count == 8:
        grad_residual, own_attn, small, passed, sums_own, first_landed = reduce_and_weights(
            ep_count, grp_count, expert_count, part, residual, cotangent, norm2_gain[None, :],
            grad_logits, group_two, group_cot, expert_grad, expert_act, shared_grad, shared_act,
        )
    else:

        def up_grad(k):
            return lambda rows, member: dot_tn(columns_of(rows, member), expert_grad[k])

        def shared_gate_up_grad(rows, member):
            columns = columns_of(rows, member)
            return jnp.stack([dot_tn(shared_grad[k], columns) for k in range(2)], 0)

        def down_grad(act):
            return lambda rows, member: dot_tn(act, columns_of(rows, member))

        sums = [
            GrpReduce(group_two, up_grad(0)),
            GrpReduce(group_two, up_grad(1)),
            GrpReduce(group_cot, down_grad(expert_act)),
            GrpReduce(group_two, shared_gate_up_grad),
            GrpReduce(group_cot, down_grad(shared_act)),
        ]
        arrived = [[item.to_partner(value) for value in item.away()] for item in sums]
        passed = [item.pass_on(values_) for item, values_ in zip(sums, arrived)]
        sums_own = [item.own() for item in sums]
        grad_normed_two = reduce_rows(ep_count, part)
        first_landed = None
        normal_two, factor_two = norm_of(residual)
        grad_residual = cotangent.astype(F32) + norm_back(
            grad_normed_two, normal_two, factor_two, norm2_gain
        )
        grad_norm2 = jnp.sum(grad_normed_two * normal_two, 0)
        own_attn = grad_residual.astype(BF16)
        rows = dot_tn(grad_logits, group_two)
        rows = rows[: expert_count + 1] + rows[LANES : LANES + expert_count + 1]
        small = jnp.concatenate([rows, grad_norm2[None], jnp.zeros((1, width), F32)], 0)
    each = grp_count // 2 - 1

    bulk = passed[1] + passed[4] + (passed[0] if first_landed is None else [])
    grad_qkv, grad_bias, grad_branch, group_attn, *landed = attend_backward(
        ep_count, grp_count, own_attn, w_all, w_flat, cosine, sine, queries, key_rows, values,
        logs, starts, scale, bulk,
    )
    from_planes = {1: landed[:each], 4: landed[each : 2 * each]}
    from_planes[0] = landed[2 * each :] if first_landed is None else first_landed

    (grad_normed_one, out_sum, small, bias_total, own_q, own_o), landed = finish(
        ep_count, grp_count, grad_branch, out_parts, small, grad_bias, norm1_gain[None, :],
        grad_qkv, attended, w_flat, group_one, group_attn, passed[3] + passed[2],
    )
    from_q, from_o, from_planes[3], from_planes[2] = [
        landed[i * each : (i + 1) * each] for i in range(4)
    ]
    layer_out = (residual + out_sum).astype(BF16)
    normal_one, factor_one = norm_of(hidden_in.astype(F32))
    grad_x = grad_residual + norm_back(grad_normed_one, normal_one, factor_one, norm1_gain)
    grad_gate, grad_up, grad_expert_down, grad_shared_gate_up, grad_shared_down = [
        add_all(own, from_planes[i]) for i, own in enumerate(sums_own)
    ]
    grad_w_qkv, grad_w_out = add_all(own_q, from_q), add_all(own_o, from_o)
    bias_total = bias_total.reshape(heads, grp_count, qkv_dim // grp_count)
    grad_b = lax.dynamic_index_in_dim(bias_total, lax.axis_index("grp"), 1, keepdims=False)

    return (
        layer_out,
        grad_x,
        small[expert_count + 2],
        grad_w_qkv.reshape(slice_width, heads, qkv_dim),
        grad_b,
        grad_w_out.reshape(heads, head_dim, slice_width),
        small[expert_count + 1],
        small[:expert_count].T,
        jnp.swapaxes(grad_shared_gate_up, 1, 2),
        grad_shared_down,
        small[expert_count],
        jnp.stack([grad_gate, grad_up], 0)[None],
        grad_expert_down[None],
    )


def solution(mesh):
    in_specs = (
        P(("grp", "ep"), None),
        P("grp"),
        P("grp", None),
        P(("grp", "ep"), None),
        P(),
        P(None, "ep", None),
        P("ep", None),
        P("ep", None, None),
        P(),
        P(),
        P(None, None, "ep"),
        P("ep", None),
        P(),
        P("ep", None, None, None),
        P("ep", None, None),
    )
    out_specs = (
        P(("grp", "ep"), None),
        P(("grp", "ep"), None),
        P(),
        P("grp", "ep", None),
        P("ep", "grp"),
        P("ep", None, "grp"),
        P(),
        P(),
        P(None, "grp", "ep"),
        P("ep", "grp"),
        P(),
        P("ep", None, "grp", None),
        P("ep", None, "grp"),
    )
    return jax.shard_map(local, mesh=mesh, in_specs=in_specs, out_specs=out_specs, check_vma=False)
```

```python
import functools
import math

import jax
import jax.numpy as jnp
from jax import lax
from jax.experimental import pallas as pl
from jax.experimental.pallas import tpu as pltpu
from jax.sharding import PartitionSpec as P

EPS = 1e-06
THETA = 1000000.0
NEGATIVE = -1e30
BF16 = jnp.bfloat16
F32 = jnp.float32
LANES = 128
MIB = 1024 * 1024
KERNEL_COST = pl.CostEstimate(flops=10**6, bytes_accessed=10**5, transcendentals=0)


def dot(lhs, rhs):
    return jnp.dot(lhs, rhs, preferred_element_type=F32)


def dot_nt(lhs, rhs):
    return lax.dot_general(lhs, rhs, (((1,), (1,)), ((), ())), preferred_element_type=F32)


def dot_tn(lhs, rhs):
    return lax.dot_general(lhs, rhs, (((0,), (0,)), ((), ())), preferred_element_type=F32)


class GrpReduce:
    def __init__(self, rows, produce):
        self.rows, self.produce = rows, produce
        self.size = lax.axis_size("grp")
        self.planes = self.size // 2
        mine = lax.axis_index("grp")
        self.core, self.plane = mine % 2, mine // 2
        self.far = [(self.plane + k) % self.planes for k in range(1, self.planes)]

    def to_partner(self, value):
        return lax.ppermute(value, "grp", [(i, i ^ 1) for i in range(self.size)])

    def away(self):
        return [
            self.produce(self.rows, 2 * plane + 1 - self.core).astype(BF16) for plane in self.far
        ]

    def pass_on(self, arrived):
        return [
            (self.produce(self.rows, 2 * plane + self.core) + value.astype(F32)).astype(BF16)
            for plane, value in zip(self.far, arrived)
        ]

    def own(self):
        away = self.produce(self.rows, 2 * self.plane + 1 - self.core).astype(BF16)
        kept = self.produce(self.rows, 2 * self.plane + self.core)
        return kept + self.to_partner(away).astype(F32)


def add_all(value, others):
    value = value.astype(F32)
    for other in others:
        value = value + other.astype(F32)
    return value


def columns_of(array, member):
    size = array.shape[1] // lax.axis_size("grp")
    return lax.dynamic_slice_in_dim(array, member * size, size, 1)


MESH = pl.DeviceIdType.MESH


def ring_places(count):
    here = lax.axis_index("ep")
    if count != 8:
        return here, lambda spot: spot
    x, z = here % 2, here // 2

    def index_at(spot):
        side = spot // 4
        return 2 * (spot + side * (7 - 2 * spot)) + side

    return z + x * (7 - 2 * z), index_at


def slot_index(count, slot):
    place, index_at = ring_places(count)
    offset = jnp.where(slot == count - 1, count // 2, (slot // 2 + 1) * (2 * (slot % 2) - 1))
    offset = jnp.where(slot == count - 2, 0, offset)
    return index_at((place + offset + count) % count)


def when(condition):
    if isinstance(condition, bool):
        return (lambda run: run()) if condition else (lambda run: None)
    return pl.when(condition)


def rows_at(slot, size):
    return pl.ds(pl.multiple_of(slot * size, size), size)


class KernelRing:
    def __init__(self, buffer, count, size, send_sems, recv_sems):
        place, index_at = ring_places(count)
        self.buffer, self.count, self.size = buffer, count, size
        self.half = count // 2
        self.send_sems, self.recv_sems = send_sems, recv_sems
        self.right = index_at((place + 1) % count)
        self.left = index_at((place + count - 1) % count)

    def own(self):
        return slice((self.count - 2) * self.size, (self.count - 1) * self.size)

    def copy(self, source, target, neighbour, step, way):
        return pltpu.make_async_remote_copy(
            src_ref=self.buffer.at[source],
            dst_ref=self.buffer.at[target],
            send_sem=self.send_sems.at[step, way],
            recv_sem=self.recv_sems.at[step, way],
            device_id={"ep": neighbour},
            device_id_type=MESH,
        )

    def sends(self, step):
        before = lax.rem(step + self.half - 1, self.half)
        copies = []
        for way, neighbour in enumerate((self.right, self.left)):
            source = jnp.where(step == 0, self.count - 2, 2 * before + way)
            copies.append(
                self.copy(
                    rows_at(source, self.size), rows_at(2 * step + way, self.size),
                    neighbour, step, way,
                )
            )
        return copies

    def last_sends(self):
        middle = self.size // 2
        copies = []
        for way, neighbour in enumerate((self.right, self.left)):
            source = (self.count - 4 + way) * self.size + way * middle
            target = (self.count - 1) * self.size + way * middle
            copies.append(
                self.copy(
                    pl.ds(source, middle), pl.ds(target, middle), neighbour, self.half - 1, way
                )
            )
        return copies

    def start(self):
        for copy in self.sends(0):
            copy.start()

    def arrive(self, i):
        @when(i < self.half - 1)
        def _():
            for copy in self.sends(i):
                copy.wait_recv()

        @when(i == self.half - 1)
        def _():
            for copy in self.last_sends():
                copy.wait_recv()

    def forward(self, i):
        @when(i < self.half - 2)
        def _():
            for copy in self.sends(i + 1):
                copy.start()

        @when(i == self.half - 2)
        def _():
            for copy in self.last_sends():
                copy.start()

    def finish(self):
        for step in range(self.half - 1):
            for copy in self.sends(step):
                copy.wait_send()
        for copy in self.last_sends():
            copy.wait_send()


class Exchange:
    def __init__(self, count, source_at, target_at, send_sems, recv_sems):
        self.count = count
        self.place, self.index_at = ring_places(count)
        self.source_at, self.target_at = source_at, target_at
        self.send_sems, self.recv_sems = send_sems, recv_sems

    def copy(self, slot):
        way = slot % 2
        far = slot // 2 + 1
        farthest = slot == self.count - 1
        offset = jnp.where(farthest, self.count // 2, far * (2 * way - 1))
        landing = jnp.where(farthest, slot, slot + 1 - 2 * way)
        return pltpu.make_async_remote_copy(
            src_ref=self.source_at(slot),
            dst_ref=self.target_at(landing),
            send_sem=self.send_sems.at[slot],
            recv_sem=self.recv_sems.at[landing],
            device_id={"ep": self.index_at((self.place + offset + self.count) % self.count)},
            device_id_type=MESH,
        )

    def arrived(self, slot):
        return pltpu.make_async_remote_copy(
            src_ref=self.source_at(slot),
            dst_ref=self.target_at(slot),
            send_sem=self.send_sems.at[slot],
            recv_sem=self.recv_sems.at[slot],
            device_id={"ep": self.index_at((self.place + 1) % self.count)},
            device_id_type=MESH,
        )

    def others(self):
        return [slot for slot in range(self.count) if slot != self.count - 2]


class PlaneCopies:
    def __init__(self, pairs, planes, sems):
        mine, size = lax.axis_index("grp"), lax.axis_size("grp")
        self.copies = []
        for i, (source, target) in enumerate(pairs):
            shift = 2 * (i % (planes - 1) + 1)
            self.copies.append(
                pltpu.make_async_remote_copy(
                    src_ref=source,
                    dst_ref=target,
                    send_sem=sems.at[0, i],
                    recv_sem=sems.at[1, i],
                    device_id={"grp": (mine + shift) % size},
                    device_id_type=MESH,
                )
            )

    def start(self, first=0, last=None):
        for copy in self.copies[first:last]:
            copy.start()

    def finish(self):
        for copy in self.copies:
            copy.wait()


def greet(axis, count):
    barrier = pltpu.get_barrier_semaphore()
    here = lax.axis_index(axis)
    for step in range(1, count):
        pl.semaphore_signal(
            barrier, inc=1, device_id={axis: (here + step) % count}, device_id_type=MESH
        )


def block_rows_of(count):
    return 256 if count % 256 == 0 else 128


def attend_forward_kernel(
    count, grp_count, heads, scale, hidden, first_gain, gain, w, b, segments, row_segments, w_out,
    q_out, k_out, v_out, attended_out, log_out, residual_out, normed_out, cosine, sine, row_starts,
    x_out, w_all_out, row_positions, starts, xs, w_all, received, x_send, x_recv, w_send, w_recv, plane_send, plane_recv, core_send,
    core_recv, hand_send, hand_recv, x_sems, w_sems, own_sem,
):
    size, width = hidden.shape
    half = count // 2
    rows = 2 * size
    dim = LANES
    inner_size = heads * dim
    planes = grp_count // 2
    mine = lax.axis_index("grp")
    core, plane = mine % 2, mine // 2
    part_width = width // grp_count

    own_columns = pl.ds(pl.multiple_of(mine * part_width, part_width), part_width)
    ring_x = KernelRing(xs, count, size, x_send, x_recv)
    ring_w = KernelRing(w_all.at[0], count, inner_size, w_send, w_recv)
    load = pltpu.make_async_copy(
        w_out.at[:, own_columns], w_all.at[0, ring_w.own()], own_sem.at[0]
    )
    load.start()
    greet("ep", count)
    greet("grp", grp_count)
    own_hidden = hidden[...].astype(F32)
    mean = jnp.sum(own_hidden * own_hidden, -1, keepdims=True) * (1.0 / width)
    xs[ring_x.own(), :] = (own_hidden * lax.rsqrt(mean + EPS) * first_gain[...]).astype(BF16)
    pl.semaphore_wait(pltpu.get_barrier_semaphore(), count - 1 + grp_count - 1)
    load.wait()
    ring_w.start()
    ring_x.start()

    for slot in range(count):
        row_positions[:, slot * size : (slot + 1) * size] = slot_index(
            count, slot
        ) * size + lax.broadcasted_iota(jnp.int32, (1, size), 1)
    lane = lax.broadcasted_iota(jnp.int32, (size, dim), 1)
    low_half = lane < dim // 2
    index = jnp.where(low_half, lane, lane - dim // 2).astype(F32)
    inverse = jnp.exp(index * (-2.0 * math.log(THETA) / dim))

    def tables(slot, carry):
        block = slot_index(count, slot)
        here, there = rows_at(slot, size), rows_at(block, size)
        before = jnp.where(row_segments[...] < segments[there, :], 1.0, 0.0)
        start = jnp.sum(before, -1, keepdims=True)
        starts[here, :] = start.astype(jnp.int32)
        own_row = row_segments[:, there]
        before = jnp.where(segments[...] < own_row, 1.0, 0.0)
        row_starts[:, here] = jnp.sum(before, 0, keepdims=True).astype(jnp.int32)
        position = (block * size + lax.broadcasted_iota(jnp.int32, (size, 1), 0)).astype(F32)
        angle = (position - start) * inverse
        cosine[here, :] = jnp.cos(angle)
        sine[here, :] = jnp.where(low_half, -jnp.sin(angle), jnp.sin(angle))
        return carry

    lax.fori_loop(0, count, tables, 0)

    def to_plane(step, i):
        here = rows_at(i, 2 * inner_size)
        landing = (planes - step) % planes
        return pltpu.make_async_remote_copy(
            src_ref=w_all.at[0, here],
            dst_ref=w_all.at[landing, here],
            send_sem=plane_send.at[step - 1, i],
            recv_sem=plane_recv.at[landing - 1, i],
            device_id={"grp": (mine + 2 * step) % grp_count},
            device_id_type=MESH,
        )

    def to_core(j):
        return pltpu.make_async_remote_copy(
            src_ref=w_all.at[j],
            dst_ref=w_all.at[planes + j],
            send_sem=core_send.at[j],
            recv_sem=core_recv.at[j],
            device_id={"grp": mine + 1 - 2 * core},
            device_id_type=MESH,
        )

    def store_x(i):
        here = rows_at(i, rows)
        return pltpu.make_async_copy(xs.at[here], x_out.at[here], x_sems.at[i])

    def store_w(j):
        return pltpu.make_async_copy(w_all.at[j], w_all_out.at[j], w_sems.at[j])

    def project(i, carry):
        here = rows_at(i, rows)
        ring_w.arrive(i)
        ring_w.forward(i)
        for step in range(1, planes):
            to_plane(step, i).start()
        ring_x.arrive(i)
        ring_x.forward(i)
        store_x(i).start()
        projected = dot(xs[here, :], w[...]) + b[...]
        cos, sin = cosine[here, :], sine[here, :]
        for h in range(heads):
            base = 3 * dim * h
            query = projected[:, base : base + dim]
            key = projected[:, base + dim : base + 2 * dim]
            q_out[h, here, :] = (query * cos + pltpu.roll(query, dim // 2, 1) * sin).astype(BF16)
            k_out[h, here, :] = (key * cos + pltpu.roll(key, dim // 2, 1) * sin).astype(BF16)
            v_out[h, here, :] = projected[:, base + 2 * dim : base + 3 * dim].astype(BF16)
        return carry

    lax.fori_loop(0, half, project, 0)
    to_core(0).start()
    store_w(0).start()

    exchange = Exchange(
        count,
        lambda slot: attended_out.at[rows_at(slot, size)],
        lambda slot: received.at[slot],
        hand_send,
        hand_recv,
    )

    def attend(step, carry):
        i = half - 1 - step
        here = rows_at(i, rows)
        count_up = lax.broadcasted_iota(jnp.int32, (size, 1), 0)
        own = jnp.concatenate(
            [slot_index(count, 2 * i + k) * size + count_up for k in range(2)], 0
        )
        start = starts[here, :]
        keys_at = row_positions[...]
        allowed = (keys_at <= own) & (keys_at >= start)
        for h in range(heads):
            scores = dot_nt(q_out[h, here, :], k_out[h]) * scale
            scores = jnp.where(allowed, scores, NEGATIVE)
            highest = jnp.max(scores, -1, keepdims=True)
            expo = jnp.exp(scores - highest)
            total = jnp.sum(expo, -1, keepdims=True)
            weights = (expo * (1.0 / total)).astype(BF16)
            attended_out[here, h * dim : (h + 1) * dim] = dot(weights, v_out[h]).astype(BF16)
            logs = jnp.broadcast_to(highest + jnp.log(total), (rows, LANES))
            log_out[h, :, here] = jnp.transpose(logs)[:1, :]
        exchange.copy(2 * i + 1).start()

        @pl.when(i < half - 1)
        def _():
            exchange.copy(2 * i).start()

        return carry

    lax.fori_loop(0, half, attend, 0)
    received[count - 2] = attended_out[ring_x.own(), :]
    for j in range(1, planes):
        for i in range(half):
            to_plane((planes - j) % planes, i).wait_recv()
        to_core(j).start()
        store_w(j).start()
    for slot in exchange.others():
        exchange.arrived(slot).wait_recv()
    for j in range(planes):
        to_core(j).wait_recv()
        store_w(planes + j).start()
    mixed = jnp.concatenate([received[slot] for slot in range(count)], 1)
    square = jnp.zeros((size, 1), F32)
    for j in range(grp_count):
        member = 2 * ((plane + j % planes) % planes) + (core if j < planes else 1 - core)
        columns = pl.ds(pl.multiple_of(member * part_width, part_width), part_width)
        piece = hidden[:, columns].astype(F32) + dot(mixed, w_all[j])
        residual_out[:, columns] = piece
        square = square + jnp.sum(piece * piece, -1, keepdims=True)
    factor = lax.rsqrt(square * (1.0 / width) + EPS)
    normed_out[...] = (residual_out[...] * factor * gain[...]).astype(BF16)

    for i in range(half):
        store_x(i).wait()
        for step in range(1, planes):
            to_plane(step, i).wait_send()
    for j in range(grp_count):
        store_w(j).wait()
    for j in range(planes):
        to_core(j).wait_send()
    for slot in exchange.others():
        exchange.copy(slot).wait_send()
    ring_x.finish()
    ring_w.finish()


def attend_forward(
    count, grp_count, hidden, first_gain, gain, w, b, w_out, segments, scale
):
    size, width = hidden.shape
    tokens = size * count
    heads = w.shape[1] // (3 * LANES)
    half, planes = count // 2, grp_count // 2
    anywhere = pl.BlockSpec(memory_space=pl.ANY)
    whole = pl.BlockSpec(memory_space=pltpu.VMEM)
    shape = jax.ShapeDtypeStruct
    w_all_shape = (grp_count, count * heads * LANES, width // grp_count)
    dma = pltpu.SemaphoreType.DMA
    return pl.pallas_call(
        functools.partial(attend_forward_kernel, count, grp_count, heads, scale),
        in_specs=[whole] * 7 + [anywhere],
        out_specs=[whole] * 10 + [anywhere] * 2,
        out_shape=(
            shape((heads, tokens, LANES), BF16),
            shape((heads, tokens, LANES), BF16),
            shape((heads, tokens, LANES), BF16),
            shape((tokens, heads * LANES), BF16),
            shape((heads, 1, tokens), F32),
            shape((size, width), F32),
            shape((size, width), BF16),
            shape((tokens, LANES), F32),
            shape((tokens, LANES), F32),
            shape((1, tokens), jnp.int32),
            shape((tokens, width), BF16),
            shape(w_all_shape, BF16),
        ),
        scratch_shapes=[
            pltpu.VMEM((1, tokens), jnp.int32),
            pltpu.VMEM((tokens, 1), jnp.int32),
            pltpu.VMEM((tokens, width), BF16),
            pltpu.VMEM(w_all_shape, BF16),
            pltpu.VMEM((count, size, heads * LANES), BF16),
            dma((half, 2)),
            dma((half, 2)),
            dma((half, 2)),
            dma((half, 2)),
            dma((max(planes - 1, 1), half)),
            dma((max(planes - 1, 1), half)),
            dma((planes,)),
            dma((planes,)),
            dma((count,)),
            dma((count,)),
            dma((half,)),
            dma((grp_count,)),
            dma((1,)),
        ],
        compiler_params=pltpu.CompilerParams(
            collective_id=1, has_side_effects=True, vmem_limit_bytes=56 * MIB
        ),
        cost_estimate=KERNEL_COST,
        name="attend_forward",
    )(hidden, first_gain[None, :], gain[None, :], w, b, segments[:, None], segments[None, :], w_out)


def attend_backward_kernel(
    count, grp_count, heads, scale, g_own, w_all, w, cosine, sine, q, k, v, row_logs, row_starts,
    *refs,
):
    number = (len(refs) - 17) // 2
    bulk, refs = refs[:number], refs[number:]
    g_out, bias_out, branch_out, group_out = refs[:4]
    landed = refs[4 : 4 + number]
    (
        row_positions, positions, g_att, dk, dv, outbox, gs, send_sems, recv_sems, ring_send,
        ring_recv, store_sems, plane_sems,
    ) = refs[4 + number :]
    size, width = g_own.shape
    tokens = size * count
    rows = block_rows_of(tokens)
    dim = LANES
    inner_size = heads * dim
    planes = grp_count // 2
    mine = lax.axis_index("grp")
    core, plane = mine % 2, mine // 2
    part_width = width // grp_count

    ring = KernelRing(gs, count, size, ring_send, ring_recv)

    def store(i):
        here = rows_at(i, 2 * size)
        return pltpu.make_async_copy(gs.at[here], group_out.at[here], store_sems.at[i])

    def next_pair(i):
        ring.arrive(i)
        ring.forward(i)
        store(i).start()

    greet("ep", count)
    greet("grp", grp_count)
    gs[ring.own(), :] = g_own[...]
    pl.semaphore_wait(pltpu.get_barrier_semaphore(), count - 1 + grp_count - 1)
    plane_copies = PlaneCopies(list(zip(bulk, landed)), grp_count // 2, plane_sems)
    ring.start()
    plane_copies.start()
    for slot in range(count):
        first = slot_index(count, slot) * size
        row_positions[:, slot * size : (slot + 1) * size] = first + lax.broadcasted_iota(
            jnp.int32, (1, size), 1
        )
        positions[slot * size : (slot + 1) * size, :] = first + lax.broadcasted_iota(
            jnp.int32, (size, 1), 0
        )
    own_rows = None
    for j in range(grp_count):
        member = 2 * ((plane + j % planes) % planes) + (core if j < planes else 1 - core)
        columns = pl.ds(pl.multiple_of(member * part_width, part_width), part_width)
        piece = dot_nt(g_own[:, columns], w_all[j])
        own_rows = piece if own_rows is None else own_rows + piece
    own_rows = own_rows.astype(BF16)
    for slot in range(count):
        outbox[slot] = own_rows[:, slot * inner_size : (slot + 1) * inner_size]
    exchange = Exchange(
        count,
        lambda slot: outbox.at[slot],
        lambda slot: g_att.at[rows_at(slot, size)],
        send_sems,
        recv_sems,
    )
    for slot in exchange.others():
        exchange.copy(slot).start()
    g_att[(count - 2) * size : (count - 1) * size, :] = outbox[count - 2]
    dk[...] = jnp.zeros_like(dk)
    dv[...] = jnp.zeros_like(dv)
    next_pair(0)
    for slot in exchange.others():
        exchange.arrived(slot).wait_recv()

    def scores_back(i, carry):
        here = rows_at(i, rows)
        own, start = row_positions[:, here], row_starts[:, here]
        keys_at = positions[...]
        allowed = (keys_at <= own) & (keys_at >= start)
        cos, sin = cosine[here, :], sine[here, :]
        for h in range(heads):
            query = q[h, here, :]
            g_block = g_att[here, h * dim : (h + 1) * dim]
            scores = dot_nt(k[h], query) * scale - row_logs[h, :, here]
            weights = jnp.exp(jnp.where(allowed, scores, NEGATIVE))
            g_weights = dot_nt(v[h], g_block)
            inner = jnp.sum(weights * g_weights, 0, keepdims=True)
            g_scores = (weights * (g_weights - inner)).astype(BF16)
            g_query = dot_tn(g_scores, k[h]) * scale
            g_query = g_query * cos - pltpu.roll(g_query, dim // 2, 1) * sin
            g_out[here, 3 * dim * h : 3 * dim * h + dim] = g_query.astype(BF16)
            dk[h] += dot(g_scores, query)
            dv[h] += dot(weights.astype(BF16), g_block)

        @pl.when(i == 1)
        def _():
            next_pair(1)

        return carry

    lax.fori_loop(0, tokens // rows, scores_back, 0)
    bias_out[...] = jnp.zeros_like(bias_out)

    def finish(i, carry):
        here = rows_at(i, rows)
        cos, sin = cosine[here, :], sine[here, :]
        for h in range(heads):
            base = 3 * dim * h
            g_key = dk[h, here, :] * scale
            g_key = g_key * cos - pltpu.roll(g_key, dim // 2, 1) * sin
            g_out[here, base + dim : base + 2 * dim] = g_key.astype(BF16)
            g_out[here, base + 2 * dim : base + 3 * dim] = dv[h, here, :].astype(BF16)
        g_here = g_out[here, :]
        bias_out[...] += jnp.sum(g_here.astype(F32), 0, keepdims=True)
        branch_out[here, :] = dot_nt(g_here, w[...]).astype(BF16)
        return carry

    lax.fori_loop(0, tokens // rows, finish, 0)
    for i in range(2, count // 2):
        next_pair(i)
    for slot in exchange.others():
        exchange.copy(slot).wait_send()
    ring.finish()
    for i in range(count // 2):
        store(i).wait()
    plane_copies.finish()


def attend_backward(
    count, grp_count, g_own, w_all, w, cosine, sine, q, k, v, logs, starts, scale, bulk
):
    size, width = g_own.shape
    heads, tokens, _ = q.shape
    anywhere = pl.BlockSpec(memory_space=pl.ANY)
    whole = pl.BlockSpec(memory_space=pltpu.VMEM)
    shape = jax.ShapeDtypeStruct
    dma = pltpu.SemaphoreType.DMA
    return pl.pallas_call(
        functools.partial(attend_backward_kernel, count, grp_count, heads, scale),
        in_specs=[whole] * 10 + [anywhere] * len(bulk),
        out_specs=[whole] * 3 + [anywhere] * (1 + len(bulk)),
        out_shape=(
            shape((tokens, 3 * LANES * heads), BF16),
            shape((1, 3 * LANES * heads), F32),
            shape((tokens, width), BF16),
            shape((tokens, width), BF16),
            *[shape(value.shape, value.dtype) for value in bulk],
        ),
        scratch_shapes=[
            pltpu.VMEM((1, tokens), jnp.int32),
            pltpu.VMEM((tokens, 1), jnp.int32),
            pltpu.VMEM((tokens, heads * LANES), BF16),
            pltpu.VMEM((heads, tokens, LANES), F32),
            pltpu.VMEM((heads, tokens, LANES), F32),
            pltpu.VMEM((count, size, heads * LANES), BF16),
            pltpu.VMEM((tokens, width), BF16),
            dma((count,)),
            dma((count,)),
            dma((count // 2, 2)),
            dma((count // 2, 2)),
            dma((count // 2,)),
            dma((2, max(len(bulk), 1))),
        ],
        compiler_params=pltpu.CompilerParams(
            collective_id=2, has_side_effects=True, vmem_limit_bytes=56 * MIB
        ),
        cost_estimate=KERNEL_COST,
        name="attend_backward",
    )(
        g_own, w_all, w, cosine, sine, q, k, v,
        logs, starts, *bulk,
    )


def doubling_stages(axes):
    stages = []
    for axis in axes:
        step = lax.axis_size(axis) // 2
        while step:
            stages.append((axis, step))
            step //= 2
    return stages


class Doubling:
    def __init__(self, held, arrived, stages, sems):
        self.held, self.arrived, self.stages, self.sems = held, arrived, stages, sems
        self.place = 0

    def copy(self, k):
        axis, step = self.stages[k]
        here = lax.axis_index(axis)
        return pltpu.make_async_remote_copy(
            src_ref=self.held.at[k],
            dst_ref=self.arrived.at[k],
            send_sem=self.sems.at[0, k],
            recv_sem=self.sems.at[1, k],
            device_id={axis: here + step * (1 - 2 * (here // step % 2))},
            device_id_type=MESH,
        )

    def start(self):
        self.copy(0).start()

    def advance(self):
        k = self.place
        if k < len(self.stages):
            self.copy(k).wait_recv()
            self.held[k + 1] = self.held[k] + self.arrived[k]
            if k + 1 < len(self.stages):
                self.copy(k + 1).start()
            self.place += 1

    def finish(self):
        while self.place < len(self.stages):
            self.advance()
        for k in range(len(self.stages)):
            self.copy(k).wait_send()
        return self.held[len(self.stages)]


class RingSum:
    def __init__(self, count, part, out, to_right, to_left, send_sems, recv_sems):
        place, index_at = ring_places(count)
        self.count, self.half, self.size = count, count // 2, out.shape[0]
        self.part, self.out, self.held = part, out, (to_right, to_left)
        self.send_sems, self.recv_sems = send_sems, recv_sems
        self.neighbours = (
            index_at((place + 1) % count), index_at((place + count - 1) % count)
        )

    def copy(self, step, way):
        held, middle = self.held[way], self.size // 2
        if step == 0:
            source = self.part.at[pl.ds((self.count - 1) * self.size + way * middle, middle)]
            target = held.at[0, pl.ds(way * middle, middle)]
        else:
            source, target = held.at[step - 1], held.at[step]
        return pltpu.make_async_remote_copy(
            src_ref=source,
            dst_ref=target,
            send_sem=self.send_sems.at[step, way],
            recv_sem=self.recv_sems.at[step, way],
            device_id={"ep": self.neighbours[way]},
            device_id_type=MESH,
        )

    def start(self):
        for way in range(2):
            self.copy(0, way).start()

    def advance(self, step):
        middle, part = self.size // 2, self.part
        for way in range(2):
            held = self.held[way]
            first = (2 * (self.half - step) - 1 - way) * self.size
            self.copy(step - 1, way).wait_recv()
            if step == 1:
                here = slice(way * middle, (way + 1) * middle)
                rest = slice((1 - way) * middle, (2 - way) * middle)
                own = part[first + way * middle : first + (way + 1) * middle, :]
                held[0, here] = (own.astype(F32) + held[0, here].astype(F32)).astype(BF16)
                held[0, rest] = part[first + (1 - way) * middle : first + (2 - way) * middle, :]
            else:
                own = part[first : first + self.size, :]
                held[step - 1] = (own.astype(F32) + held[step - 1].astype(F32)).astype(BF16)
            self.copy(step, way).start()

    def last(self):
        own = self.part[(self.count - 2) * self.size : (self.count - 1) * self.size, :]
        total = own.astype(F32)
        for way in range(2):
            self.copy(self.half - 1, way).wait_recv()
            total = total + self.held[way][self.half - 1].astype(F32)
        self.out[...] = total

    def finish(self):
        for step in range(self.half):
            for way in range(2):
                self.copy(step, way).wait_send()


def reduce_kernel(count, part, out, to_right, to_left, send_sems, recv_sems):
    greet("ep", count)
    pl.semaphore_wait(pltpu.get_barrier_semaphore(), count - 1)
    ring = RingSum(count, part, out, to_right, to_left, send_sems, recv_sems)
    ring.start()
    for step in range(1, count // 2):
        ring.advance(step)
    ring.last()
    ring.finish()


def reduce_rows(count, part):
    tokens, width = part.shape
    size, half = tokens // count, count // 2
    whole = pl.BlockSpec(memory_space=pltpu.VMEM)
    return pl.pallas_call(
        functools.partial(reduce_kernel, count),
        in_specs=[whole],
        out_specs=whole,
        out_shape=jax.ShapeDtypeStruct((size, width), F32),
        scratch_shapes=[pltpu.VMEM((half, size, width), BF16)] * 2
        + [pltpu.SemaphoreType.DMA((half, 2))] * 2,
        compiler_params=pltpu.CompilerParams(
            collective_id=3, has_side_effects=True, vmem_limit_bytes=56 * MIB
        ),
        cost_estimate=KERNEL_COST,
        name="reduce_rows",
    )(part)


def finish_kernel(
    count, grp_count, bulk_number, branch, out_parts, small, bias, gain, g_qkv, attended, w,
    x_in, attn_in, *refs
):
    refs = list(refs)

    def take(amount):
        taken = refs[:amount]
        del refs[:amount]
        return taken

    planes = grp_count // 2
    far_number = planes - 1
    bulk = take(bulk_number)
    branch_sum, out_sum, small_sum, bias_sum, own_q, own_o = take(6)
    landed = take(bulk_number + 2 * far_number)
    rings_held = take(4)
    x, attn = take(2)
    away, arrived, far = take(2), take(2), take(2)
    small_held, small_arrived, bias_held, bias_arrived = take(4)
    (
        send_sems, recv_sems, small_sems, bias_sems, plane_sems, load_sems, core_send, core_recv
    ) = take(8)
    mine = lax.axis_index("grp")
    core, plane = mine % 2, mine // 2
    part_width = x.shape[2]
    orders = list(range(1, planes)) + [0]
    units = [(side, place) for side in (1, 0) for place in range(planes)]

    def columns(unit):
        side, place = units[unit]
        member = 2 * ((plane + orders[place]) % planes) + (core if side == 0 else 1 - core)
        return pl.ds(pl.multiple_of(member * part_width, part_width), part_width)

    def loads(unit):
        slot = unit % 2
        return [
            pltpu.make_async_copy(
                source.at[:, columns(unit)], target.at[slot], load_sems.at[i, slot]
            )
            for i, (source, target) in enumerate(((x_in, x), (attn_in, attn)))
        ]

    for unit in range(2):
        for load in loads(unit):
            load.start()
    greet("ep", count)
    greet("grp", grp_count)
    small_held[0] = small[...]
    bias_held[0] = bias[...]
    pl.semaphore_wait(pltpu.get_barrier_semaphore(), count - 1 + grp_count - 1)
    rings = [
        RingSum(
            count, part, out, rings_held[2 * a], rings_held[2 * a + 1], send_sems.at[a],
            recv_sems.at[a],
        )
        for a, (part, out) in enumerate(((branch, branch_sum), (out_parts, out_sum)))
    ]
    for ring in rings:
        ring.start()
    sums = [
        Doubling(small_held, small_arrived, doubling_stages(("grp", "ep")), small_sems),
        Doubling(bias_held, bias_arrived, doubling_stages(("grp",)), bias_sems),
    ]
    sums[1].start()
    halves = bulk_number // 2
    sources = [bulk[i].at[0] for i in range(halves)]
    targets = [landed[2 * far_number + i].at[0] for i in range(halves)]
    for kind in range(2):
        for place in range(far_number):
            sources.append(far[kind].at[place])
            targets.append(landed[kind * far_number + place])
    sources += [bulk[i].at[1] for i in range(halves)] + bulk[halves:]
    targets += [landed[2 * far_number + i].at[1] for i in range(halves)]
    targets += landed[2 * far_number + halves :]
    far_copies = PlaneCopies(list(zip(sources, targets)), planes, plane_sems)
    far_copies.start(0, halves)

    def to_core(kind, place):
        return pltpu.make_async_remote_copy(
            src_ref=away[kind].at[place],
            dst_ref=arrived[kind].at[place],
            send_sem=core_send.at[kind, place],
            recv_sem=core_recv.at[kind, place],
            device_id={"grp": mine + 1 - 2 * core},
            device_id_type=MESH,
        )

    for unit, (side, place) in enumerate(units):
        cut, slot = columns(unit), unit % 2
        for load in loads(unit):
            load.wait()
        q_piece = dot_tn(x[slot], g_qkv[...])
        inner = jnp.sum(q_piece * w[cut, :].astype(F32), -1, keepdims=True)
        inner = jnp.transpose(jnp.broadcast_to(inner, (part_width, LANES)))[:1, :]
        small_held[0, small.shape[0] - 1 :, cut] = inner / gain[:, cut]
        o_piece = dot_tn(attended[...], attn[slot])
        for kind, piece in enumerate((q_piece, o_piece)):
            if side == 1:
                away[kind][place] = piece.astype(BF16)
                to_core(kind, place).start()
            else:
                to_core(kind, place).wait_recv()
                piece = piece + arrived[kind][place].astype(F32)
                if orders[place]:
                    far[kind][place] = piece.astype(BF16)
                else:
                    (own_q, own_o)[kind][...] = piece
        if unit + 2 < len(units):
            for load in loads(unit + 2):
                load.start()
    sums[0].start()
    far_copies.start(halves)
    for step in range(1, count // 2):
        for a, ring in enumerate(rings):
            ring.advance(step)
            if a or step == 1:
                for item in sums:
                    item.advance()
    for ring in rings:
        ring.last()
    small_sum[...] = sums[0].finish()
    bias_sum[...] = sums[1].finish()
    for ring in rings:
        ring.finish()
    for kind in range(2):
        for place in range(planes):
            to_core(kind, place).wait_send()
    far_copies.finish()


def finish(
    count, grp_count, branch, out_parts, small, bias, gain, g_qkv, attended, w, x, attn, bulk
):
    tokens, width = branch.shape
    size, half, planes = tokens // count, count // 2, grp_count // 2
    part_width = width // grp_count
    q_shape, o_shape = (part_width, g_qkv.shape[1]), (attended.shape[1], part_width)
    stages = len(doubling_stages(("grp", "ep"))), len(doubling_stages(("grp",)))
    anywhere = pl.BlockSpec(memory_space=pl.ANY)
    whole = pl.BlockSpec(memory_space=pltpu.VMEM)
    shape = jax.ShapeDtypeStruct
    dma = pltpu.SemaphoreType.DMA
    landed = [shape(dims, BF16) for dims in (q_shape, o_shape) for _ in range(planes - 1)]
    landed += [shape(value.shape, value.dtype) for value in bulk]
    results = pl.pallas_call(
        functools.partial(finish_kernel, count, grp_count, len(bulk)),
        in_specs=[whole] * 8 + [anywhere] * (2 + len(bulk)),
        out_specs=[whole] * 6 + [anywhere] * len(landed),
        out_shape=[
            shape((size, width), F32),
            shape((size, width), F32),
            shape(small.shape, F32),
            shape(bias.shape, F32),
            shape(q_shape, F32),
            shape(o_shape, F32),
            *landed,
        ],
        scratch_shapes=[pltpu.VMEM((half, size, width), BF16)] * 4
        + [pltpu.VMEM((2, tokens, part_width), BF16)] * 2
        + [pltpu.VMEM((planes, *dims), BF16) for dims in (q_shape, o_shape)] * 2
        + [pltpu.VMEM((max(planes - 1, 1), *dims), BF16) for dims in (q_shape, o_shape)]
        + [
            pltpu.VMEM((stages[0] + 1, *small.shape), F32),
            pltpu.VMEM((stages[0], *small.shape), F32),
            pltpu.VMEM((stages[1] + 1, *bias.shape), F32),
            pltpu.VMEM((stages[1], *bias.shape), F32),
        ]
        + [dma((2, half, 2))] * 2
        + [dma((2, stages[0])), dma((2, stages[1])), dma((2, len(landed) + len(bulk) // 2)), dma((2, 2))]
        + [dma((2, planes))] * 2,
        compiler_params=pltpu.CompilerParams(
            collective_id=4, has_side_effects=True, vmem_limit_bytes=60 * MIB
        ),
        cost_estimate=KERNEL_COST,
        name="finish",
    )(branch, out_parts, small, bias, gain, g_qkv, attended, w, x, attn, *bulk)
    return results[:6], results[6:]


def reduce_and_weights_kernel(
    count, grp_count, expert_count, part, residual, cot_own, gain, grad_logits, x_in, cot_in,
    grad_e_in, act_e_in, grad_s_in, act_s_in, *refs
):
    refs = list(refs)

    def take(amount):
        taken = refs[:amount]
        del refs[:amount]
        return taken

    planes = grp_count // 2
    grad_residual, own_attn, small = take(3)
    outs = [take(planes) for _ in range(5)]
    landed = take(planes - 1)
    sources = (x_in, grad_e_in, cot_in, act_e_in, grad_s_in, act_s_in)
    held = take(6)
    (summed,) = take(1)
    x, grad_e, cot, act_e, grad_s, act_s = held
    to_right, to_left = take(2)
    staged, arrived = take(5), take(5)
    send_sems, recv_sems, load_sems, core_send, core_recv, out_sems, plane_sems = take(7)
    mine = lax.axis_index("grp")
    core, plane = mine % 2, mine // 2
    part_width = x.shape[1] // grp_count

    loads = [
        pltpu.make_async_copy(source, target, load_sems.at[i])
        for i, (source, target) in enumerate(zip(sources, held))
    ]
    for load in loads:
        load.start()
    greet("ep", count)
    greet("grp", grp_count)
    pl.semaphore_wait(pltpu.get_barrier_semaphore(), count - 1 + grp_count - 1)
    ring = RingSum(count, part, summed, to_right, to_left, send_sems, recv_sems)
    ring.start()

    def columns(order, side):
        member = 2 * ((plane + order) % planes) + (core if side == 0 else 1 - core)
        return pl.ds(pl.multiple_of(member * part_width, part_width), part_width)

    def products(kind, cut):
        if kind < 2:
            return [dot_tn(x[:, cut], grad_e[kind])]
        if kind == 2:
            return [dot_tn(act_e[...], cot[:, cut])]
        if kind == 3:
            return [dot_tn(grad_s[k], x[:, cut]) for k in range(2)]
        return [dot_tn(act_s[...], cot[:, cut])]

    def to_core(kind, place):
        return pltpu.make_async_remote_copy(
            src_ref=staged[kind],
            dst_ref=arrived[kind].at[place],
            send_sem=core_send.at[kind, place],
            recv_sem=core_recv.at[kind, place],
            device_id={"grp": mine + 1 - 2 * core},
            device_id_type=MESH,
        )

    def store(kind, place):
        return pltpu.make_async_copy(staged[kind], outs[kind][place], out_sems.at[kind, place])

    orders = list(range(1, planes)) + [0]
    needs = ((0, 1), (), (2, 3), (4,), (5,))
    plane_copies = PlaneCopies(list(zip(outs[0][: planes - 1], landed)), planes, plane_sems)
    ring_step = 1
    number = 0
    for place, order in enumerate(orders):
        for side in (1, 0):
            for kind in range(5):
                if side == 1 and place == 0:
                    for i in needs[kind]:
                        loads[i].wait()
                pieces = products(kind, columns(order, side))
                if side == 1:
                    if place and kind:
                        store(kind, place - 1).wait()
                else:
                    to_core(kind, place).wait_recv()
                    to_core(kind, place).wait_send()
                for k, piece in enumerate(pieces):
                    whole = (k,) if len(pieces) > 1 else (Ellipsis,)
                    if side == 0:
                        piece = piece + arrived[kind][(place, *whole)].astype(F32)
                    staged[kind][whole] = piece.astype(BF16)
                if side == 1:
                    to_core(kind, place).start()
                else:
                    store(kind, place).start()
                if side == 0 and kind == 1 and order:
                    store(0, place).wait()
                    plane_copies.copies[place].start()
                number += 1
                if number % 5 == 2:
                    if ring_step < count // 2:
                        ring.advance(ring_step)
                    ring_step += 1
                if number == 5:
                    rows = dot_tn(grad_logits[:, :LANES], x[...])
                    rows = rows + dot_tn(grad_logits[:, LANES:], x[...])
                    small[: expert_count + 1, :] = rows[: expert_count + 1, :]
    while ring_step < count // 2:
        ring.advance(ring_step)
        ring_step += 1
    ring.last()
    normal, factor = norm_of(residual[...])
    total = summed[...]
    own = cot_own[...].astype(F32) + norm_back(total, normal, factor, gain[...])
    grad_residual[...] = own
    own_attn[...] = own.astype(BF16)
    small[expert_count + 1 : expert_count + 2, :] = jnp.sum(total * normal, 0, keepdims=True)
    small[expert_count + 2 :, :] = jnp.zeros((1, small.shape[1]), F32)
    for kind in range(5):
        store(kind, planes - 1).wait()
    ring.finish()
    plane_copies.finish()


def reduce_and_weights(
    count, grp_count, expert_count, part, residual, cot_own, gain, grad_logits, x, cot, grad_e,
    act_e, grad_s, act_s,
):
    tokens, width = part.shape
    size, half, planes = tokens // count, count // 2, grp_count // 2
    part_width = width // grp_count
    wide, narrow = act_e.shape[1], act_s.shape[1]
    shapes = [
        (part_width, wide), (part_width, wide), (wide, part_width), (2, narrow, part_width),
        (narrow, part_width),
    ]
    anywhere = pl.BlockSpec(memory_space=pl.ANY)
    whole = pl.BlockSpec(memory_space=pltpu.VMEM)
    shape = jax.ShapeDtypeStruct
    dma = pltpu.SemaphoreType.DMA
    rows = pl.pallas_call(
        functools.partial(reduce_and_weights_kernel, count, grp_count, expert_count),
        in_specs=[whole] * 5 + [anywhere] * 6,
        out_specs=[whole] * 3 + [anywhere] * (6 * planes - 1),
        out_shape=[
            shape((size, width), F32),
            shape((size, width), BF16),
            shape((expert_count + 3, width), F32),
        ]
        + [shape(dims, BF16) for dims in shapes for _ in range(planes)]
        + [shape(shapes[0], BF16)] * (planes - 1),
        scratch_shapes=[
            pltpu.VMEM(value.shape, BF16) for value in (x, grad_e, cot, act_e, grad_s, act_s)
        ]
        + [pltpu.VMEM((size, width), F32)]
        + [pltpu.VMEM((half, size, width), BF16)] * 2
        + [pltpu.VMEM(dims, BF16) for dims in shapes]
        + [pltpu.VMEM((planes, *dims), BF16) for dims in shapes]
        + [dma((half, 2)), dma((half, 2)), dma((6,))]
        + [dma((5, planes))] * 3
        + [dma((2, max(planes - 1, 1)))],
        compiler_params=pltpu.CompilerParams(
            collective_id=3, has_side_effects=True, vmem_limit_bytes=60 * MIB
        ),
        cost_estimate=KERNEL_COST,
        name="reduce_and_weights",
    )(part, residual, cot_own, gain, grad_logits, x, cot, grad_e, act_e, grad_s, act_s)
    rows, slices = rows[:3], list(rows[3:])
    groups = [slices[i * planes : (i + 1) * planes] for i in range(5)]
    passed, own = [group[:-1] for group in groups], [group[-1] for group in groups]
    return (*rows, passed, own, slices[5 * planes :])


def tiles_of(width):
    tiles, start = [], 0
    while width - start > 384:
        tiles.append((start, 256))
        start += 256
    tiles.append((start, width - start))
    return tiles


def experts_kernel(
    count, expert_count, x_own, cot_own, routes, routes_w, gate_up_e, down_e, gate_up_s, down_s,
    act_e_out, grad_e_out, act_s_out, grad_s_out, part_out, branch_out, logits_out, x_out,
    cot_out,
    xs, cots, gate_e, up_e, held_e, gate_s, up_s, held_s, act_e, grad_e, act_s, grad_s, part,
    branch, logits_held, x_send, x_recv, cot_send, cot_recv, weight_sems, out_sems, x_sems,
):
    half = count // 2
    size = x_own.shape[0]
    rows = 2 * size
    ring_x = KernelRing(xs, count, size, x_send, x_recv)
    ring_cot = KernelRing(cots, count, size, cot_send, cot_recv)

    barrier = pltpu.get_barrier_semaphore()
    for neighbour in (ring_x.left, ring_x.right):
        pl.semaphore_signal(barrier, inc=1, device_id={"ep": neighbour}, device_id_type=MESH)
    loads = [
        pltpu.make_async_copy(source, target, weight_sems.at[i])
        for i, (source, target) in enumerate(
            [
                (gate_up_e.at[0, 0], gate_e),
                (gate_up_e.at[0, 1], up_e),
                (down_e.at[0], held_e),
                (gate_up_s.at[0], gate_s),
                (gate_up_s.at[1], up_s),
                (down_s, held_s),
            ]
        )
    ]
    for load in loads:
        load.start()
    xs[ring_x.own(), :] = x_own[...]
    cots[ring_x.own(), :] = cot_own[...]
    pl.semaphore_wait(barrier, 2)
    ring_x.start()
    ring_cot.start()

    def stores(slot, length, here):
        cut = pl.ds(0, length)
        pieces = [
            (act_e.at[slot, cut], act_e_out.at[here]),
            (grad_e.at[slot, 0, cut], grad_e_out.at[0, here]),
            (grad_e.at[slot, 1, cut], grad_e_out.at[1, here]),
            (act_s.at[slot, cut], act_s_out.at[here]),
            (grad_s.at[slot, 0, cut], grad_s_out.at[0, here]),
            (grad_s.at[slot, 1, cut], grad_s_out.at[1, here]),
            (part.at[slot, cut], part_out.at[here]),
            (branch.at[slot, cut], branch_out.at[here]),
            (logits_held.at[slot, cut], logits_out.at[here]),
        ]
        return [
            pltpu.make_async_copy(source, target, out_sems.at[slot, k])
            for k, (source, target) in enumerate(pieces)
        ]

    def pair_stores(i):
        return stores(lax.rem(i, 2), rows, rows_at(i, rows))

    own_rows = pl.ds((count - 2) * size, size)
    far_rows = pl.ds((count - 1) * size, size)

    def store_rows(here, number):
        return [
            pltpu.make_async_copy(xs.at[here], x_out.at[here], x_sems.at[0, number]),
            pltpu.make_async_copy(cots.at[here], cot_out.at[here], x_sems.at[1, number]),
        ]

    sections = (
        (gate_e, up_e, held_e, act_e, grad_e, dot, dot_nt),
        (gate_s, up_s, held_s, act_s, grad_s, dot_nt, dot),
    )
    mine = lax.axis_index("ep")
    onehot = (lax.broadcasted_iota(jnp.int32, (1, LANES), 1) == mine).astype(F32)

    def compute(here, length, slot, blocks):
        lane = lax.broadcasted_iota(jnp.int32, (length, LANES), 1)
        inputs, cotangent = xs[here, :], cots[here, :]
        logits = dot(inputs, routes_w[...])
        routed = jnp.where(lane < expert_count, logits, NEGATIVE)
        expo = jnp.exp(routed - jnp.max(routed, -1, keepdims=True))
        probs = expo * (1.0 / jnp.sum(expo, -1, keepdims=True))
        named = jnp.concatenate(
            [routes[rows_at(slot_index(count, block), size), :] for block in blocks], 0
        )
        hits = jnp.sum(jnp.where(named == mine, 1.0, 0.0), -1, keepdims=True)
        own_prob = jnp.sum(probs * onehot, -1, keepdims=True) * hits
        share_logit = jnp.sum(jnp.where(lane == expert_count, logits, 0.0), -1, keepdims=True)
        share = 1.0 / (1.0 + jnp.exp(-share_logit))

        inner = []
        total, out_total = None, None
        for s, (gate_w, up_w, down_w, act_out, grad_out, ahead, back_dot) in enumerate(sections):
            factor = own_prob if s == 0 else share
            dots = jnp.zeros((length, 1), F32)
            for start, width in tiles_of(down_w.shape[0]):
                cut = pl.ds(start, width)
                piece = (slice(None), cut) if s == 0 else (cut, slice(None))
                gate = ahead(inputs, gate_w[piece])
                up = ahead(inputs, up_w[piece])
                grad = dot_nt(cotangent, down_w[cut, :])
                sigma = 0.5 * jnp.tanh(0.5 * gate) + 0.5
                silu = gate * sigma
                act = (silu * up).astype(BF16).astype(F32)
                dots = dots + jnp.sum(grad * act, -1, keepdims=True)
                scaled = grad * factor
                act_out[slot, :length, cut] = (act * factor).astype(BF16)
                grad_out[slot, 0, :length, cut] = (
                    scaled * up * (sigma + silu * (1.0 - sigma))
                ).astype(BF16)
                grad_out[slot, 1, :length, cut] = (scaled * silu).astype(BF16)
            inner.append(dots)
            back = back_dot(grad_out[slot, 0, :length], gate_w[...]) + back_dot(
                grad_out[slot, 1, :length], up_w[...]
            )
            total = back if total is None else total + back
            out_piece = dot(act_out[slot, :length], down_w[...])
            out_total = out_piece if out_total is None else out_total + out_piece
        branch[slot, :length] = out_total.astype(BF16)
        grad_logits = own_prob * inner[0] * (onehot - probs)
        grad_share = share * (1.0 - share) * inner[1]
        grad_logits = grad_logits + jnp.where(lane == expert_count, grad_share, 0.0)
        high = grad_logits.astype(BF16)
        low = (grad_logits - high.astype(F32)).astype(BF16)
        total = total + dot_nt(high, routes_w[...]) + dot_nt(low, routes_w[...])
        logits_held[slot, :length, :LANES] = high
        logits_held[slot, :length, LANES:] = low
        part[slot, :length] = total.astype(BF16)
        for copy in stores(slot, length, here):
            copy.start()

    def one_pair(i, carry):
        here = rows_at(i, rows)
        ring_x.arrive(i)
        ring_x.forward(i)
        ring_cot.arrive(i)
        ring_cot.forward(i)
        for copy in store_rows(here, i):
            copy.start()

        @pl.when(i == 1)
        def _():
            for copy in stores(1, size, own_rows):
                copy.wait()

        @pl.when(i >= 2)
        def _():
            for copy in pair_stores(i - 2):
                copy.wait()

        compute(here, rows, lax.rem(i, 2), [2 * i, 2 * i + 1])
        return carry

    for copy in store_rows(own_rows, half - 1):
        copy.start()
    for load in loads:
        load.wait()
    compute(own_rows, size, 1, [count - 2])
    lax.fori_loop(0, half - 1, one_pair, 0)
    ring_x.arrive(half - 1)
    ring_cot.arrive(half - 1)
    for copy in store_rows(far_rows, half):
        copy.start()
    last = (half - 1) % 2
    for copy in stores(last, rows, rows_at(half - 3, rows)):
        copy.wait()
    compute(far_rows, size, last, [count - 1])
    for i in range(half - 1):
        for copy in store_rows(rows_at(i, rows), i):
            copy.wait()
    for number, here in ((half - 1, own_rows), (half, far_rows)):
        for copy in store_rows(here, number):
            copy.wait()
    for copy in stores(1 - last, rows, rows_at(half - 2, rows)):
        copy.wait()
    for copy in stores(last, size, far_rows):
        copy.wait()
    ring_x.finish()
    ring_cot.finish()


def experts(
    count, expert_count, x_own, cot_own, routes, routes_w, gate_up_e, down_e, gate_up_s, down_s
):
    size, width = x_own.shape
    tokens, rows, half = size * count, 2 * size, count // 2
    wide, narrow = down_e.shape[1], down_s.shape[0]
    anywhere = pl.BlockSpec(memory_space=pl.ANY)
    whole = pl.BlockSpec(memory_space=pltpu.VMEM)
    shape = jax.ShapeDtypeStruct
    dma = pltpu.SemaphoreType.DMA
    return pl.pallas_call(
        functools.partial(experts_kernel, count, expert_count),
        in_specs=[whole] * 4 + [anywhere] * 4,
        out_specs=[anywhere] * 9,
        out_shape=(
            shape((tokens, wide), BF16),
            shape((2, tokens, wide), BF16),
            shape((tokens, narrow), BF16),
            shape((2, tokens, narrow), BF16),
            shape((tokens, width), BF16),
            shape((tokens, width), BF16),
            shape((tokens, 2 * LANES), BF16),
            shape((tokens, width), BF16),
            shape((tokens, width), BF16),
        ),
        scratch_shapes=[
            pltpu.VMEM((tokens, width), BF16),
            pltpu.VMEM((tokens, width), BF16),
            pltpu.VMEM((width, wide), BF16),
            pltpu.VMEM((width, wide), BF16),
            pltpu.VMEM((wide, width), BF16),
            pltpu.VMEM((narrow, width), BF16),
            pltpu.VMEM((narrow, width), BF16),
            pltpu.VMEM((narrow, width), BF16),
            pltpu.VMEM((2, rows, wide), BF16),
            pltpu.VMEM((2, 2, rows, wide), BF16),
            pltpu.VMEM((2, rows, narrow), BF16),
            pltpu.VMEM((2, 2, rows, narrow), BF16),
            pltpu.VMEM((2, rows, width), BF16),
            pltpu.VMEM((2, rows, width), BF16),
            pltpu.VMEM((2, rows, 2 * LANES), BF16),
            dma((half, 2)),
            dma((half, 2)),
            dma((half, 2)),
            dma((half, 2)),
            dma((6,)),
            dma((2, 9)),
            dma((2, half + 1)),
        ],
        compiler_params=pltpu.CompilerParams(
            collective_id=0, has_side_effects=True, vmem_limit_bytes=60 * MIB
        ),
        cost_estimate=KERNEL_COST,
        name="experts",
    )(x_own, cot_own, routes, routes_w, gate_up_e, down_e, gate_up_s, down_s)


def norm_of(values):
    factor = lax.rsqrt(jnp.mean(values * values, -1, keepdims=True) + EPS)
    return values * factor, factor


def norm_back(grad_out, normal, factor, gain):
    scaled = grad_out * gain
    return factor * (scaled - normal * jnp.mean(scaled * normal, -1, keepdims=True))


def local(
    hidden_in, segments, routes, cotangent, norm1_gain, w_qkv, b_qkv, w_out, norm2_gain, router,
    shared_gate_up, shared_down, shared_gate, expert_gate_up, expert_down,
):
    tokens_here, width = hidden_in.shape
    ep_count = lax.axis_size("ep")
    grp_count = lax.axis_size("grp")
    expert_count = router.shape[1]
    heads, qkv_dim = b_qkv.shape
    head_dim = qkv_dim // 3
    scale = 1.0 / math.sqrt(head_dim)
    slice_width = width // grp_count
    routes_w = jnp.concatenate(
        [router, shared_gate[:, None], jnp.zeros((width, LANES - 1 - expert_count), BF16)], 1
    )
    w_flat = w_qkv.reshape(width, heads * qkv_dim)
    b_flat = b_qkv.reshape(1, heads * qkv_dim)
    w_out_flat = w_out.reshape(heads * head_dim, width)

    (
        queries, key_rows, values, attended, logs, residual, normed_two, cosine, sine, starts,
        group_one, w_all,
    ) = attend_forward(
        ep_count, grp_count, hidden_in, norm1_gain, norm2_gain, w_flat, b_flat, w_out_flat,
        segments, scale,
    )

    (
        expert_act, expert_grad, shared_act, shared_grad, part, out_parts, grad_logits,
        group_two, group_cot,
    ) = experts(
        ep_count, expert_count, normed_two, cotangent, routes, routes_w,
        expert_gate_up, expert_down, jnp.swapaxes(shared_gate_up, 1, 2), shared_down,
    )

    if ep_count == 8:
        grad_residual, own_attn, small, passed, sums_own, first_landed = reduce_and_weights(
            ep_count, grp_count, expert_count, part, residual, cotangent, norm2_gain[None, :],
            grad_logits, group_two, group_cot, expert_grad, expert_act, shared_grad, shared_act,
        )
    else:

        def up_grad(k):
            return lambda rows, member: dot_tn(columns_of(rows, member), expert_grad[k])

        def shared_gate_up_grad(rows, member):
            columns = columns_of(rows, member)
            return jnp.stack([dot_tn(shared_grad[k], columns) for k in range(2)], 0)

        def down_grad(act):
            return lambda rows, member: dot_tn(act, columns_of(rows, member))

        sums = [
            GrpReduce(group_two, up_grad(0)),
            GrpReduce(group_two, up_grad(1)),
            GrpReduce(group_cot, down_grad(expert_act)),
            GrpReduce(group_two, shared_gate_up_grad),
            GrpReduce(group_cot, down_grad(shared_act)),
        ]
        arrived = [[item.to_partner(value) for value in item.away()] for item in sums]
        passed = [item.pass_on(values_) for item, values_ in zip(sums, arrived)]
        sums_own = [item.own() for item in sums]
        grad_normed_two = reduce_rows(ep_count, part)
        first_landed = None
        normal_two, factor_two = norm_of(residual)
        grad_residual = cotangent.astype(F32) + norm_back(
            grad_normed_two, normal_two, factor_two, norm2_gain
        )
        grad_norm2 = jnp.sum(grad_normed_two * normal_two, 0)
        own_attn = grad_residual.astype(BF16)
        rows = dot_tn(grad_logits, group_two)
        rows = rows[: expert_count + 1] + rows[LANES : LANES + expert_count + 1]
        small = jnp.concatenate([rows, grad_norm2[None], jnp.zeros((1, width), F32)], 0)
    each = grp_count // 2 - 1

    bulk = passed[1] + passed[4] + (passed[0] if first_landed is None else [])
    grad_qkv, grad_bias, grad_branch, group_attn, *landed = attend_backward(
        ep_count, grp_count, own_attn, w_all, w_flat, cosine, sine, queries, key_rows, values,
        logs, starts, scale, bulk,
    )
    from_planes = {1: landed[:each], 4: landed[each : 2 * each]}
    from_planes[0] = landed[2 * each :] if first_landed is None else first_landed

    (grad_normed_one, out_sum, small, bias_total, own_q, own_o), landed = finish(
        ep_count, grp_count, grad_branch, out_parts, small, grad_bias, norm1_gain[None, :],
        grad_qkv, attended, w_flat, group_one, group_attn, passed[3] + passed[2],
    )
    from_q, from_o, from_planes[3], from_planes[2] = [
        landed[i * each : (i + 1) * each] for i in range(4)
    ]
    layer_out = (residual + out_sum).astype(BF16)
    normal_one, factor_one = norm_of(hidden_in.astype(F32))
    grad_x = grad_residual + norm_back(grad_normed_one, normal_one, factor_one, norm1_gain)
    grad_gate, grad_up, grad_expert_down, grad_shared_gate_up, grad_shared_down = [
        add_all(own, from_planes[i]) for i, own in enumerate(sums_own)
    ]
    grad_w_qkv, grad_w_out = add_all(own_q, from_q), add_all(own_o, from_o)
    bias_total = bias_total.reshape(heads, grp_count, qkv_dim // grp_count)
    grad_b = lax.dynamic_index_in_dim(bias_total, lax.axis_index("grp"), 1, keepdims=False)

    return (
        layer_out,
        grad_x,
        small[expert_count + 2],
        grad_w_qkv.reshape(slice_width, heads, qkv_dim),
        grad_b,
        grad_w_out.reshape(heads, head_dim, slice_width),
        small[expert_count + 1],
        small[:expert_count].T,
        jnp.swapaxes(grad_shared_gate_up, 1, 2),
        grad_shared_down,
        small[expert_count],
        jnp.stack([grad_gate, grad_up], 0)[None],
        grad_expert_down[None],
    )


def solution(mesh):
    in_specs = (
        P(("grp", "ep"), None),
        P("grp"),
        P("grp", None),
        P(("grp", "ep"), None),
        P(),
        P(None, "ep", None),
        P("ep", None),
        P("ep", None, None),
        P(),
        P(),
        P(None, None, "ep"),
        P("ep", None),
        P(),
        P("ep", None, None, None),
        P("ep", None, None),
    )
    out_specs = (
        P(("grp", "ep"), None),
        P(("grp", "ep"), None),
        P(),
        P("grp", "ep", None),
        P("ep", "grp"),
        P("ep", None, "grp"),
        P(),
        P(),
        P(None, "grp", "ep"),
        P("ep", "grp"),
        P(),
        P("ep", None, "grp", None),
        P("ep", None, "grp"),
    )
    return jax.shard_map(local, mesh=mesh, in_specs=in_specs, out_specs=out_specs, check_vma=False)
```

```python
import functools
import math

import jax
import jax.numpy as jnp
from jax import lax
from jax.experimental import pallas as pl
from jax.experimental.pallas import tpu as pltpu
from jax.sharding import PartitionSpec as P

EPS = 1e-06
THETA = 1000000.0
NEGATIVE = -1e30
BF16 = jnp.bfloat16
F32 = jnp.float32
LANES = 128
MIB = 1024 * 1024
KERNEL_COST = pl.CostEstimate(flops=10**6, bytes_accessed=10**5, transcendentals=0)


def dot(lhs, rhs):
    return jnp.dot(lhs, rhs, preferred_element_type=F32)


def dot_nt(lhs, rhs):
    return lax.dot_general(lhs, rhs, (((1,), (1,)), ((), ())), preferred_element_type=F32)


def dot_tn(lhs, rhs):
    return lax.dot_general(lhs, rhs, (((0,), (0,)), ((), ())), preferred_element_type=F32)


class GrpReduce:
    def __init__(self, rows, produce):
        self.rows, self.produce = rows, produce
        self.size = lax.axis_size("grp")
        self.planes = self.size // 2
        mine = lax.axis_index("grp")
        self.core, self.plane = mine % 2, mine // 2
        self.far = [(self.plane + k) % self.planes for k in range(1, self.planes)]

    def to_partner(self, value):
        return lax.ppermute(value, "grp", [(i, i ^ 1) for i in range(self.size)])

    def away(self):
        return [
            self.produce(self.rows, 2 * plane + 1 - self.core).astype(BF16) for plane in self.far
        ]

    def pass_on(self, arrived):
        return [
            (self.produce(self.rows, 2 * plane + self.core) + value.astype(F32)).astype(BF16)
            for plane, value in zip(self.far, arrived)
        ]

    def own(self):
        away = self.produce(self.rows, 2 * self.plane + 1 - self.core).astype(BF16)
        kept = self.produce(self.rows, 2 * self.plane + self.core)
        return kept + self.to_partner(away).astype(F32)


def add_all(value, others):
    value = value.astype(F32)
    for other in others:
        value = value + other.astype(F32)
    return value


def columns_of(array, member):
    size = array.shape[1] // lax.axis_size("grp")
    return lax.dynamic_slice_in_dim(array, member * size, size, 1)


MESH = pl.DeviceIdType.MESH


def ring_places(count):
    here = lax.axis_index("ep")
    if count != 8:
        return here, lambda spot: spot
    x, z = here % 2, here // 2

    def index_at(spot):
        side = spot // 4
        return 2 * (spot + side * (7 - 2 * spot)) + side

    return z + x * (7 - 2 * z), index_at


def slot_index(count, slot):
    place, index_at = ring_places(count)
    offset = jnp.where(slot == count - 1, count // 2, (slot // 2 + 1) * (2 * (slot % 2) - 1))
    offset = jnp.where(slot == count - 2, 0, offset)
    return index_at((place + offset + count) % count)


def when(condition):
    if isinstance(condition, bool):
        return (lambda run: run()) if condition else (lambda run: None)
    return pl.when(condition)


def rows_at(slot, size):
    return pl.ds(pl.multiple_of(slot * size, size), size)


class KernelRing:
    def __init__(self, buffer, count, size, send_sems, recv_sems):
        place, index_at = ring_places(count)
        self.buffer, self.count, self.size = buffer, count, size
        self.half = count // 2
        self.send_sems, self.recv_sems = send_sems, recv_sems
        self.right = index_at((place + 1) % count)
        self.left = index_at((place + count - 1) % count)

    def own(self):
        return slice((self.count - 2) * self.size, (self.count - 1) * self.size)

    def copy(self, source, target, neighbour, step, way):
        return pltpu.make_async_remote_copy(
            src_ref=self.buffer.at[source],
            dst_ref=self.buffer.at[target],
            send_sem=self.send_sems.at[step, way],
            recv_sem=self.recv_sems.at[step, way],
            device_id={"ep": neighbour},
            device_id_type=MESH,
        )

    def sends(self, step):
        before = lax.rem(step + self.half - 1, self.half)
        copies = []
        for way, neighbour in enumerate((self.right, self.left)):
            source = jnp.where(step == 0, self.count - 2, 2 * before + way)
            copies.append(
                self.copy(
                    rows_at(source, self.size), rows_at(2 * step + way, self.size),
                    neighbour, step, way,
                )
            )
        return copies

    def last_sends(self):
        middle = self.size // 2
        copies = []
        for way, neighbour in enumerate((self.right, self.left)):
            source = (self.count - 4 + way) * self.size + way * middle
            target = (self.count - 1) * self.size + way * middle
            copies.append(
                self.copy(
                    pl.ds(source, middle), pl.ds(target, middle), neighbour, self.half - 1, way
                )
            )
        return copies

    def start(self):
        for copy in self.sends(0):
            copy.start()

    def arrive(self, i):
        @when(i < self.half - 1)
        def _():
            for copy in self.sends(i):
                copy.wait_recv()

        @when(i == self.half - 1)
        def _():
            for copy in self.last_sends():
                copy.wait_recv()

    def forward(self, i):
        @when(i < self.half - 2)
        def _():
            for copy in self.sends(i + 1):
                copy.start()

        @when(i == self.half - 2)
        def _():
            for copy in self.last_sends():
                copy.start()

    def finish(self):
        for step in range(self.half - 1):
            for copy in self.sends(step):
                copy.wait_send()
        for copy in self.last_sends():
            copy.wait_send()


class Exchange:
    def __init__(self, count, source_at, target_at, send_sems, recv_sems):
        self.count = count
        self.place, self.index_at = ring_places(count)
        self.source_at, self.target_at = source_at, target_at
        self.send_sems, self.recv_sems = send_sems, recv_sems

    def copy(self, slot):
        way = slot % 2
        far = slot // 2 + 1
        farthest = slot == self.count - 1
        offset = jnp.where(farthest, self.count // 2, far * (2 * way - 1))
        landing = jnp.where(farthest, slot, slot + 1 - 2 * way)
        return pltpu.make_async_remote_copy(
            src_ref=self.source_at(slot),
            dst_ref=self.target_at(landing),
            send_sem=self.send_sems.at[slot],
            recv_sem=self.recv_sems.at[landing],
            device_id={"ep": self.index_at((self.place + offset + self.count) % self.count)},
            device_id_type=MESH,
        )

    def arrived(self, slot):
        return pltpu.make_async_remote_copy(
            src_ref=self.source_at(slot),
            dst_ref=self.target_at(slot),
            send_sem=self.send_sems.at[slot],
            recv_sem=self.recv_sems.at[slot],
            device_id={"ep": self.index_at((self.place + 1) % self.count)},
            device_id_type=MESH,
        )

    def others(self):
        return [slot for slot in range(self.count) if slot != self.count - 2]


class PlaneCopies:
    def __init__(self, pairs, planes, sems):
        mine, size = lax.axis_index("grp"), lax.axis_size("grp")
        self.copies = []
        for i, (source, target) in enumerate(pairs):
            shift = 2 * (i % (planes - 1) + 1)
            self.copies.append(
                pltpu.make_async_remote_copy(
                    src_ref=source,
                    dst_ref=target,
                    send_sem=sems.at[0, i],
                    recv_sem=sems.at[1, i],
                    device_id={"grp": (mine + shift) % size},
                    device_id_type=MESH,
                )
            )

    def start(self, first=0, last=None):
        for copy in self.copies[first:last]:
            copy.start()

    def finish(self):
        for copy in self.copies:
            copy.wait()


def greet(axis, count):
    barrier = pltpu.get_barrier_semaphore()
    here = lax.axis_index(axis)
    for step in range(1, count):
        pl.semaphore_signal(
            barrier, inc=1, device_id={axis: (here + step) % count}, device_id_type=MESH
        )


def block_rows_of(count):
    return 256 if count % 256 == 0 else 128


def attend_forward_kernel(
    count, grp_count, heads, scale, hidden, first_gain, gain, w, b, segments, row_segments, w_out,
    q_out, k_out, v_out, attended_out, log_out, residual_out, normed_out, cosine, sine, row_starts,
    x_out, w_all_out, row_positions, starts, xs, w_all, received, x_send, x_recv, w_send, w_recv, plane_send, plane_recv, core_send,
    core_recv, hand_send, hand_recv, x_sems, w_sems, own_sem,
):
    size, width = hidden.shape
    half = count // 2
    rows = 2 * size
    dim = LANES
    inner_size = heads * dim
    planes = grp_count // 2
    mine = lax.axis_index("grp")
    core, plane = mine % 2, mine // 2
    part_width = width // grp_count

    own_columns = pl.ds(pl.multiple_of(mine * part_width, part_width), part_width)
    ring_x = KernelRing(xs, count, size, x_send, x_recv)
    ring_w = KernelRing(w_all.at[0], count, inner_size, w_send, w_recv)
    load = pltpu.make_async_copy(
        w_out.at[:, own_columns], w_all.at[0, ring_w.own()], own_sem.at[0]
    )
    load.start()
    greet("ep", count)
    greet("grp", grp_count)
    own_hidden = hidden[...].astype(F32)
    mean = jnp.sum(own_hidden * own_hidden, -1, keepdims=True) * (1.0 / width)
    xs[ring_x.own(), :] = (own_hidden * lax.rsqrt(mean + EPS) * first_gain[...]).astype(BF16)
    pl.semaphore_wait(pltpu.get_barrier_semaphore(), count - 1 + grp_count - 1)
    load.wait()
    ring_w.start()
    ring_x.start()

    for slot in range(count):
        row_positions[:, slot * size : (slot + 1) * size] = slot_index(
            count, slot
        ) * size + lax.broadcasted_iota(jnp.int32, (1, size), 1)
    lane = lax.broadcasted_iota(jnp.int32, (size, dim), 1)
    low_half = lane < dim // 2
    index = jnp.where(low_half, lane, lane - dim // 2).astype(F32)
    inverse = jnp.exp(index * (-2.0 * math.log(THETA) / dim))

    def tables(slot, carry):
        block = slot_index(count, slot)
        here, there = rows_at(slot, size), rows_at(block, size)
        before = jnp.where(row_segments[...] < segments[there, :], 1.0, 0.0)
        start = jnp.sum(before, -1, keepdims=True)
        starts[here, :] = start.astype(jnp.int32)
        own_row = row_segments[:, there]
        before = jnp.where(segments[...] < own_row, 1.0, 0.0)
        row_starts[:, here] = jnp.sum(before, 0, keepdims=True).astype(jnp.int32)
        position = (block * size + lax.broadcasted_iota(jnp.int32, (size, 1), 0)).astype(F32)
        angle = (position - start) * inverse
        cosine[here, :] = jnp.cos(angle)
        sine[here, :] = jnp.where(low_half, -jnp.sin(angle), jnp.sin(angle))
        return carry

    lax.fori_loop(0, count, tables, 0)

    def to_plane(step, i):
        here = rows_at(i, 2 * inner_size)
        landing = (planes - step) % planes
        return pltpu.make_async_remote_copy(
            src_ref=w_all.at[0, here],
            dst_ref=w_all.at[landing, here],
            send_sem=plane_send.at[step - 1, i],
            recv_sem=plane_recv.at[landing - 1, i],
            device_id={"grp": (mine + 2 * step) % grp_count},
            device_id_type=MESH,
        )

    def to_core(j):
        return pltpu.make_async_remote_copy(
            src_ref=w_all.at[j],
            dst_ref=w_all.at[planes + j],
            send_sem=core_send.at[j],
            recv_sem=core_recv.at[j],
            device_id={"grp": mine + 1 - 2 * core},
            device_id_type=MESH,
        )

    def store_x(i):
        here = rows_at(i, rows)
        return pltpu.make_async_copy(xs.at[here], x_out.at[here], x_sems.at[i])

    def store_w(j):
        return pltpu.make_async_copy(w_all.at[j], w_all_out.at[j], w_sems.at[j])

    def project(i, carry):
        here = rows_at(i, rows)
        ring_w.arrive(i)
        ring_w.forward(i)
        for step in range(1, planes):
            to_plane(step, i).start()
        ring_x.arrive(i)
        ring_x.forward(i)
        store_x(i).start()
        projected = dot(xs[here, :], w[...]) + b[...]
        cos, sin = cosine[here, :], sine[here, :]
        for h in range(heads):
            base = 3 * dim * h
            query = projected[:, base : base + dim]
            key = projected[:, base + dim : base + 2 * dim]
            q_out[h, here, :] = (query * cos + pltpu.roll(query, dim // 2, 1) * sin).astype(BF16)
            k_out[h, here, :] = (key * cos + pltpu.roll(key, dim // 2, 1) * sin).astype(BF16)
            v_out[h, here, :] = projected[:, base + 2 * dim : base + 3 * dim].astype(BF16)
        return carry

    lax.fori_loop(0, half, project, 0)
    to_core(0).start()
    store_w(0).start()

    exchange = Exchange(
        count,
        lambda slot: attended_out.at[rows_at(slot, size)],
        lambda slot: received.at[slot],
        hand_send,
        hand_recv,
    )

    def attend(step, carry):
        i = half - 1 - step
        here = rows_at(i, rows)
        count_up = lax.broadcasted_iota(jnp.int32, (size, 1), 0)
        own = jnp.concatenate(
            [slot_index(count, 2 * i + k) * size + count_up for k in range(2)], 0
        )
        start = starts[here, :]
        keys_at = row_positions[...]
        allowed = (keys_at <= own) & (keys_at >= start)
        for h in range(heads):
            scores = dot_nt(q_out[h, here, :], k_out[h]) * scale
            scores = jnp.where(allowed, scores, NEGATIVE)
            highest = jnp.max(scores, -1, keepdims=True)
            expo = jnp.exp(scores - highest)
            total = jnp.sum(expo, -1, keepdims=True)
            weights = (expo * (1.0 / total)).astype(BF16)
            attended_out[here, h * dim : (h + 1) * dim] = dot(weights, v_out[h]).astype(BF16)
            logs = jnp.broadcast_to(highest + jnp.log(total), (rows, LANES))
            log_out[h, :, here] = jnp.transpose(logs)[:1, :]
        exchange.copy(2 * i + 1).start()

        @pl.when(i < half - 1)
        def _():
            exchange.copy(2 * i).start()

        return carry

    lax.fori_loop(0, half, attend, 0)
    received[count - 2] = attended_out[ring_x.own(), :]
    for j in range(1, planes):
        for i in range(half):
            to_plane((planes - j) % planes, i).wait_recv()
        to_core(j).start()
        store_w(j).start()
    for slot in exchange.others():
        exchange.arrived(slot).wait_recv()
    for j in range(planes):
        to_core(j).wait_recv()
        store_w(planes + j).start()
    mixed = jnp.concatenate([received[slot] for slot in range(count)], 1)
    square = jnp.zeros((size, 1), F32)
    for j in range(grp_count):
        member = 2 * ((plane + j % planes) % planes) + (core if j < planes else 1 - core)
        columns = pl.ds(pl.multiple_of(member * part_width, part_width), part_width)
        piece = hidden[:, columns].astype(F32) + dot(mixed, w_all[j])
        residual_out[:, columns] = piece
        square = square + jnp.sum(piece * piece, -1, keepdims=True)
    factor = lax.rsqrt(square * (1.0 / width) + EPS)
    normed_out[...] = (residual_out[...] * factor * gain[...]).astype(BF16)

    for i in range(half):
        store_x(i).wait()
        for step in range(1, planes):
            to_plane(step, i).wait_send()
    for j in range(grp_count):
        store_w(j).wait()
    for j in range(planes):
        to_core(j).wait_send()
    for slot in exchange.others():
        exchange.copy(slot).wait_send()
    ring_x.finish()
    ring_w.finish()


def attend_forward(
    count, grp_count, hidden, first_gain, gain, w, b, w_out, segments, scale
):
    size, width = hidden.shape
    tokens = size * count
    heads = w.shape[1] // (3 * LANES)
    half, planes = count // 2, grp_count // 2
    anywhere = pl.BlockSpec(memory_space=pl.ANY)
    whole = pl.BlockSpec(memory_space=pltpu.VMEM)
    shape = jax.ShapeDtypeStruct
    w_all_shape = (grp_count, count * heads * LANES, width // grp_count)
    dma = pltpu.SemaphoreType.DMA
    return pl.pallas_call(
        functools.partial(attend_forward_kernel, count, grp_count, heads, scale),
        in_specs=[whole] * 7 + [anywhere],
        out_specs=[whole] * 10 + [anywhere] * 2,
        out_shape=(
            shape((heads, tokens, LANES), BF16),
            shape((heads, tokens, LANES), BF16),
            shape((heads, tokens, LANES), BF16),
            shape((tokens, heads * LANES), BF16),
            shape((heads, 1, tokens), F32),
            shape((size, width), F32),
            shape((size, width), BF16),
            shape((tokens, LANES), F32),
            shape((tokens, LANES), F32),
            shape((1, tokens), jnp.int32),
            shape((tokens, width), BF16),
            shape(w_all_shape, BF16),
        ),
        scratch_shapes=[
            pltpu.VMEM((1, tokens), jnp.int32),
            pltpu.VMEM((tokens, 1), jnp.int32),
            pltpu.VMEM((tokens, width), BF16),
            pltpu.VMEM(w_all_shape, BF16),
            pltpu.VMEM((count, size, heads * LANES), BF16),
            dma((half, 2)),
            dma((half, 2)),
            dma((half, 2)),
            dma((half, 2)),
            dma((max(planes - 1, 1), half)),
            dma((max(planes - 1, 1), half)),
            dma((planes,)),
            dma((planes,)),
            dma((count,)),
            dma((count,)),
            dma((half,)),
            dma((grp_count,)),
            dma((1,)),
        ],
        compiler_params=pltpu.CompilerParams(
            collective_id=1, has_side_effects=True, vmem_limit_bytes=56 * MIB
        ),
        cost_estimate=KERNEL_COST,
        name="attend_forward",
    )(hidden, first_gain[None, :], gain[None, :], w, b, segments[:, None], segments[None, :], w_out)


def attend_backward_kernel(
    count, grp_count, heads, scale, g_own, cosine, sine, q, k, v, row_logs, row_starts, w_all_in,
    w_in, *refs,
):
    number = (len(refs) - 20) // 2
    bulk, refs = refs[:number], refs[number:]
    g_out, bias_out, branch_out, group_out = refs[:4]
    landed = refs[4 : 4 + number]
    (
        row_positions, positions, g_att, dk, dv, outbox, gs, send_sems, recv_sems, ring_send,
        ring_recv, store_sems, plane_sems, w_all, w, w_sems,
    ) = refs[4 + number :]
    size, width = g_own.shape
    tokens = size * count
    rows = block_rows_of(tokens)
    dim = LANES
    inner_size = heads * dim
    planes = grp_count // 2
    mine = lax.axis_index("grp")
    core, plane = mine % 2, mine // 2
    part_width = width // grp_count

    ring = KernelRing(gs, count, size, ring_send, ring_recv)

    load_all = pltpu.make_async_copy(w_all_in, w_all, w_sems.at[0])
    load_w = pltpu.make_async_copy(w_in, w, w_sems.at[1])
    load_all.start()
    load_w.start()

    def store(i):
        here = rows_at(i, 2 * size)
        return pltpu.make_async_copy(gs.at[here], group_out.at[here], store_sems.at[i])

    def next_pair(i):
        ring.arrive(i)
        ring.forward(i)
        store(i).start()

    greet("ep", count)
    greet("grp", grp_count)
    gs[ring.own(), :] = g_own[...]
    pl.semaphore_wait(pltpu.get_barrier_semaphore(), count - 1 + grp_count - 1)
    plane_copies = PlaneCopies(list(zip(bulk, landed)), grp_count // 2, plane_sems)
    ring.start()
    plane_copies.start()
    for slot in range(count):
        first = slot_index(count, slot) * size
        row_positions[:, slot * size : (slot + 1) * size] = first + lax.broadcasted_iota(
            jnp.int32, (1, size), 1
        )
        positions[slot * size : (slot + 1) * size, :] = first + lax.broadcasted_iota(
            jnp.int32, (size, 1), 0
        )
    load_all.wait()
    own_rows = None
    for j in range(grp_count):
        member = 2 * ((plane + j % planes) % planes) + (core if j < planes else 1 - core)
        columns = pl.ds(pl.multiple_of(member * part_width, part_width), part_width)
        piece = dot_nt(g_own[:, columns], w_all[j])
        own_rows = piece if own_rows is None else own_rows + piece
    own_rows = own_rows.astype(BF16)
    for slot in range(count):
        outbox[slot] = own_rows[:, slot * inner_size : (slot + 1) * inner_size]
    exchange = Exchange(
        count,
        lambda slot: outbox.at[slot],
        lambda slot: g_att.at[rows_at(slot, size)],
        send_sems,
        recv_sems,
    )
    for slot in exchange.others():
        exchange.copy(slot).start()
    g_att[(count - 2) * size : (count - 1) * size, :] = outbox[count - 2]
    dk[...] = jnp.zeros_like(dk)
    dv[...] = jnp.zeros_like(dv)
    next_pair(0)
    for slot in exchange.others():
        exchange.arrived(slot).wait_recv()

    def scores_back(i, carry):
        here = rows_at(i, rows)
        own, start = row_positions[:, here], row_starts[:, here]
        keys_at = positions[...]
        allowed = (keys_at <= own) & (keys_at >= start)
        cos, sin = cosine[here, :], sine[here, :]
        for h in range(heads):
            query = q[h, here, :]
            g_block = g_att[here, h * dim : (h + 1) * dim]
            scores = dot_nt(k[h], query) * scale - row_logs[h, :, here]
            weights = jnp.exp(jnp.where(allowed, scores, NEGATIVE))
            g_weights = dot_nt(v[h], g_block)
            inner = jnp.sum(weights * g_weights, 0, keepdims=True)
            g_scores = (weights * (g_weights - inner)).astype(BF16)
            g_query = dot_tn(g_scores, k[h]) * scale
            g_query = g_query * cos - pltpu.roll(g_query, dim // 2, 1) * sin
            g_out[here, 3 * dim * h : 3 * dim * h + dim] = g_query.astype(BF16)
            dk[h] += dot(g_scores, query)
            dv[h] += dot(weights.astype(BF16), g_block)

        @pl.when(i == 1)
        def _():
            next_pair(1)

        return carry

    lax.fori_loop(0, tokens // rows, scores_back, 0)
    load_w.wait()
    bias_out[...] = jnp.zeros_like(bias_out)

    def finish(i, carry):
        here = rows_at(i, rows)
        cos, sin = cosine[here, :], sine[here, :]
        for h in range(heads):
            base = 3 * dim * h
            g_key = dk[h, here, :] * scale
            g_key = g_key * cos - pltpu.roll(g_key, dim // 2, 1) * sin
            g_out[here, base + dim : base + 2 * dim] = g_key.astype(BF16)
            g_out[here, base + 2 * dim : base + 3 * dim] = dv[h, here, :].astype(BF16)
        g_here = g_out[here, :]
        bias_out[...] += jnp.sum(g_here.astype(F32), 0, keepdims=True)
        branch_out[here, :] = dot_nt(g_here, w[...]).astype(BF16)
        return carry

    lax.fori_loop(0, tokens // rows, finish, 0)
    for i in range(2, count // 2):
        next_pair(i)
    for slot in exchange.others():
        exchange.copy(slot).wait_send()
    ring.finish()
    for i in range(count // 2):
        store(i).wait()
    plane_copies.finish()


def attend_backward(
    count, grp_count, g_own, w_all, w, cosine, sine, q, k, v, logs, starts, scale, bulk
):
    size, width = g_own.shape
    heads, tokens, _ = q.shape
    anywhere = pl.BlockSpec(memory_space=pl.ANY)
    whole = pl.BlockSpec(memory_space=pltpu.VMEM)
    shape = jax.ShapeDtypeStruct
    dma = pltpu.SemaphoreType.DMA
    return pl.pallas_call(
        functools.partial(attend_backward_kernel, count, grp_count, heads, scale),
        in_specs=[whole] * 8 + [anywhere] * (2 + len(bulk)),
        out_specs=[whole] * 3 + [anywhere] * (1 + len(bulk)),
        out_shape=(
            shape((tokens, 3 * LANES * heads), BF16),
            shape((1, 3 * LANES * heads), F32),
            shape((tokens, width), BF16),
            shape((tokens, width), BF16),
            *[shape(value.shape, value.dtype) for value in bulk],
        ),
        scratch_shapes=[
            pltpu.VMEM((1, tokens), jnp.int32),
            pltpu.VMEM((tokens, 1), jnp.int32),
            pltpu.VMEM((tokens, heads * LANES), BF16),
            pltpu.VMEM((heads, tokens, LANES), F32),
            pltpu.VMEM((heads, tokens, LANES), F32),
            pltpu.VMEM((count, size, heads * LANES), BF16),
            pltpu.VMEM((tokens, width), BF16),
            dma((count,)),
            dma((count,)),
            dma((count // 2, 2)),
            dma((count // 2, 2)),
            dma((count // 2,)),
            dma((2, max(len(bulk), 1))),
            pltpu.VMEM(w_all.shape, BF16),
            pltpu.VMEM(w.shape, BF16),
            dma((2,)),
        ],
        compiler_params=pltpu.CompilerParams(
            collective_id=2, has_side_effects=True, vmem_limit_bytes=56 * MIB
        ),
        cost_estimate=KERNEL_COST,
        name="attend_backward",
    )(
        g_own, cosine, sine, q, k, v, logs, starts, w_all, w, *bulk,
    )


def doubling_stages(axes):
    stages = []
    for axis in axes:
        step = lax.axis_size(axis) // 2
        while step:
            stages.append((axis, step))
            step //= 2
    return stages


class Doubling:
    def __init__(self, held, arrived, stages, sems):
        self.held, self.arrived, self.stages, self.sems = held, arrived, stages, sems
        self.place = 0

    def copy(self, k):
        axis, step = self.stages[k]
        here = lax.axis_index(axis)
        return pltpu.make_async_remote_copy(
            src_ref=self.held.at[k],
            dst_ref=self.arrived.at[k],
            send_sem=self.sems.at[0, k],
            recv_sem=self.sems.at[1, k],
            device_id={axis: here + step * (1 - 2 * (here // step % 2))},
            device_id_type=MESH,
        )

    def start(self):
        self.copy(0).start()

    def advance(self):
        k = self.place
        if k < len(self.stages):
            self.copy(k).wait_recv()
            self.held[k + 1] = self.held[k] + self.arrived[k]
            if k + 1 < len(self.stages):
                self.copy(k + 1).start()
            self.place += 1

    def finish(self):
        while self.place < len(self.stages):
            self.advance()
        for k in range(len(self.stages)):
            self.copy(k).wait_send()
        return self.held[len(self.stages)]


class RingSum:
    def __init__(self, count, part, out, to_right, to_left, send_sems, recv_sems, near=None):
        place, index_at = ring_places(count)
        self.near = near
        self.count, self.half, self.size = count, count // 2, out.shape[0]
        self.part, self.out, self.held = part, out, (to_right, to_left)
        self.send_sems, self.recv_sems = send_sems, recv_sems
        self.neighbours = (
            index_at((place + 1) % count), index_at((place + count - 1) % count)
        )

    def copy(self, step, way):
        held, middle = self.held[way], self.size // 2
        if step == 0:
            source = self.part.at[pl.ds((self.count - 1) * self.size + way * middle, middle)]
            target = held.at[0, pl.ds(way * middle, middle)]
        else:
            source, target = held.at[step - 1], held.at[step]
        return pltpu.make_async_remote_copy(
            src_ref=source,
            dst_ref=target,
            send_sem=self.send_sems.at[step, way],
            recv_sem=self.recv_sems.at[step, way],
            device_id={"ep": self.neighbours[way]},
            device_id_type=MESH,
        )

    def start(self):
        if self.near is None:
            for way in range(2):
                self.copy(0, way).start()
        else:
            self.advance(1)

    def advance(self, step):
        middle, part = self.size // 2, self.part
        for way in range(2):
            held = self.held[way]
            first = (2 * (self.half - step) - 1 - way) * self.size
            if step > 1 or self.near is None:
                self.copy(step - 1, way).wait_recv()
            if step == 1:
                here = slice(way * middle, (way + 1) * middle)
                rest = slice((1 - way) * middle, (2 - way) * middle)
                own = part[first + way * middle : first + (way + 1) * middle, :]
                before = held[0, here] if self.near is None else self.near[here, :]
                held[0, here] = (own.astype(F32) + before.astype(F32)).astype(BF16)
                held[0, rest] = part[first + (1 - way) * middle : first + (2 - way) * middle, :]
            else:
                own = part[first : first + self.size, :]
                held[step - 1] = (own.astype(F32) + held[step - 1].astype(F32)).astype(BF16)
            self.copy(step, way).start()

    def last(self):
        own = self.part[(self.count - 2) * self.size : (self.count - 1) * self.size, :]
        total = own.astype(F32)
        for way in range(2):
            self.copy(self.half - 1, way).wait_recv()
            total = total + self.held[way][self.half - 1].astype(F32)
        self.out[...] = total

    def finish(self):
        for step in range(0 if self.near is None else 1, self.half):
            for way in range(2):
                self.copy(step, way).wait_send()


def reduce_kernel(count, part, out, to_right, to_left, send_sems, recv_sems):
    greet("ep", count)
    pl.semaphore_wait(pltpu.get_barrier_semaphore(), count - 1)
    ring = RingSum(count, part, out, to_right, to_left, send_sems, recv_sems)
    ring.start()
    for step in range(1, count // 2):
        ring.advance(step)
    ring.last()
    ring.finish()


def reduce_rows(count, part):
    tokens, width = part.shape
    size, half = tokens // count, count // 2
    whole = pl.BlockSpec(memory_space=pltpu.VMEM)
    return pl.pallas_call(
        functools.partial(reduce_kernel, count),
        in_specs=[whole],
        out_specs=whole,
        out_shape=jax.ShapeDtypeStruct((size, width), F32),
        scratch_shapes=[pltpu.VMEM((half, size, width), BF16)] * 2
        + [pltpu.SemaphoreType.DMA((half, 2))] * 2,
        compiler_params=pltpu.CompilerParams(
            collective_id=3, has_side_effects=True, vmem_limit_bytes=56 * MIB
        ),
        cost_estimate=KERNEL_COST,
        name="reduce_rows",
    )(part)


def finish_kernel(
    count, grp_count, bulk_number, has_near, branch, small, bias, gain, g_qkv, attended, *refs
):
    refs = list(refs)

    def take(amount):
        taken = refs[:amount]
        del refs[:amount]
        return taken

    planes = grp_count // 2
    far_number = planes - 1
    near = take(1)[0] if has_near else None
    out_in, w_in, x_in, attn_in = take(4)
    bulk = take(bulk_number)
    branch_sum, out_sum, small_sum, bias_sum, own_q, own_o = take(6)
    landed = take(bulk_number + 2 * far_number)
    rings_held = take(4)
    out_parts, w = take(2)
    x, attn = take(2)
    away, arrived, far = take(2), take(2), take(2)
    small_held, small_arrived, bias_held, bias_arrived = take(4)
    (
        send_sems, recv_sems, small_sems, bias_sems, plane_sems, load_sems, core_send, core_recv
    ) = take(8)
    mine = lax.axis_index("grp")
    core, plane = mine % 2, mine // 2
    part_width = x.shape[2]
    orders = list(range(1, planes)) + [0]
    units = [(side, place) for side in (1, 0) for place in range(planes)]

    def columns(unit):
        side, place = units[unit]
        member = 2 * ((plane + orders[place]) % planes) + (core if side == 0 else 1 - core)
        return pl.ds(pl.multiple_of(member * part_width, part_width), part_width)

    def loads(unit):
        slot = unit % 2
        return [
            pltpu.make_async_copy(
                source.at[:, columns(unit)], target.at[slot], load_sems.at[i, slot]
            )
            for i, (source, target) in enumerate(((x_in, x), (attn_in, attn)))
        ]

    load_out = pltpu.make_async_copy(out_in, out_parts, load_sems.at[2, 0])
    load_w = pltpu.make_async_copy(w_in, w, load_sems.at[2, 1])
    load_out.start()
    for unit in range(2):
        for load in loads(unit):
            load.start()
    load_w.start()
    greet("ep", count)
    greet("grp", grp_count)
    small_held[0] = small[...]
    bias_held[0] = bias[...]
    pl.semaphore_wait(pltpu.get_barrier_semaphore(), count - 1 + grp_count - 1)
    rings = [
        RingSum(
            count, part, out, rings_held[2 * a], rings_held[2 * a + 1], send_sems.at[a],
            recv_sems.at[a], first,
        )
        for a, (part, out, first) in enumerate(
            ((branch, branch_sum, None), (out_parts, out_sum, near))
        )
    ]
    rings[0].start()
    load_out.wait()
    rings[1].start()
    sums = [
        Doubling(small_held, small_arrived, doubling_stages(("grp", "ep")), small_sems),
        Doubling(bias_held, bias_arrived, doubling_stages(("grp",)), bias_sems),
    ]
    sums[1].start()
    halves = bulk_number // 2
    sources = [bulk[i].at[0] for i in range(halves)]
    targets = [landed[2 * far_number + i].at[0] for i in range(halves)]
    for kind in range(2):
        for place in range(far_number):
            sources.append(far[kind].at[place])
            targets.append(landed[kind * far_number + place])
    sources += [bulk[i].at[1] for i in range(halves)] + bulk[halves:]
    targets += [landed[2 * far_number + i].at[1] for i in range(halves)]
    targets += landed[2 * far_number + halves :]
    far_copies = PlaneCopies(list(zip(sources, targets)), planes, plane_sems)
    far_copies.start(0, halves)

    def to_core(kind, place):
        return pltpu.make_async_remote_copy(
            src_ref=away[kind].at[place],
            dst_ref=arrived[kind].at[place],
            send_sem=core_send.at[kind, place],
            recv_sem=core_recv.at[kind, place],
            device_id={"grp": mine + 1 - 2 * core},
            device_id_type=MESH,
        )

    load_w.wait()
    for unit, (side, place) in enumerate(units):
        cut, slot = columns(unit), unit % 2
        for load in loads(unit):
            load.wait()
        q_piece = dot_tn(x[slot], g_qkv[...])
        inner = jnp.sum(q_piece * w[cut, :].astype(F32), -1, keepdims=True)
        inner = jnp.transpose(jnp.broadcast_to(inner, (part_width, LANES)))[:1, :]
        small_held[0, small.shape[0] - 1 :, cut] = inner / gain[:, cut]
        o_piece = dot_tn(attended[...], attn[slot])
        for kind, piece in enumerate((q_piece, o_piece)):
            if side == 1:
                away[kind][place] = piece.astype(BF16)
                to_core(kind, place).start()
            else:
                to_core(kind, place).wait_recv()
                piece = piece + arrived[kind][place].astype(F32)
                if orders[place]:
                    far[kind][place] = piece.astype(BF16)
                else:
                    (own_q, own_o)[kind][...] = piece
        if unit + 2 < len(units):
            for load in loads(unit + 2):
                load.start()
    sums[0].start()
    far_copies.start(halves)
    for step in range(1, count // 2):
        for a, ring in enumerate(rings):
            if step > 1 or ring.near is None:
                ring.advance(step)
            if a or step == 1:
                for item in sums:
                    item.advance()
    for ring in rings:
        ring.last()
    small_sum[...] = sums[0].finish()
    bias_sum[...] = sums[1].finish()
    for ring in rings:
        ring.finish()
    for kind in range(2):
        for place in range(planes):
            to_core(kind, place).wait_send()
    far_copies.finish()


def finish(
    count, grp_count, branch, out_parts, small, bias, gain, g_qkv, attended, w, x, attn, bulk,
    near,
):
    tokens, width = branch.shape
    size, half, planes = tokens // count, count // 2, grp_count // 2
    part_width = width // grp_count
    q_shape, o_shape = (part_width, g_qkv.shape[1]), (attended.shape[1], part_width)
    stages = len(doubling_stages(("grp", "ep"))), len(doubling_stages(("grp",)))
    anywhere = pl.BlockSpec(memory_space=pl.ANY)
    whole = pl.BlockSpec(memory_space=pltpu.VMEM)
    shape = jax.ShapeDtypeStruct
    dma = pltpu.SemaphoreType.DMA
    first = [] if near is None else [near]
    landed = [shape(dims, BF16) for dims in (q_shape, o_shape) for _ in range(planes - 1)]
    landed += [shape(value.shape, value.dtype) for value in bulk]
    results = pl.pallas_call(
        functools.partial(finish_kernel, count, grp_count, len(bulk), bool(first)),
        in_specs=[whole] * (6 + len(first)) + [anywhere] * (4 + len(bulk)),
        out_specs=[whole] * 6 + [anywhere] * len(landed),
        out_shape=[
            shape((size, width), F32),
            shape((size, width), F32),
            shape(small.shape, F32),
            shape(bias.shape, F32),
            shape(q_shape, F32),
            shape(o_shape, F32),
            *landed,
        ],
        scratch_shapes=[pltpu.VMEM((half, size, width), BF16)] * 4
        + [pltpu.VMEM((tokens, width), BF16), pltpu.VMEM(w.shape, BF16)]
        + [pltpu.VMEM((2, tokens, part_width), BF16)] * 2
        + [pltpu.VMEM((planes, *dims), BF16) for dims in (q_shape, o_shape)] * 2
        + [pltpu.VMEM((max(planes - 1, 1), *dims), BF16) for dims in (q_shape, o_shape)]
        + [
            pltpu.VMEM((stages[0] + 1, *small.shape), F32),
            pltpu.VMEM((stages[0], *small.shape), F32),
            pltpu.VMEM((stages[1] + 1, *bias.shape), F32),
            pltpu.VMEM((stages[1], *bias.shape), F32),
        ]
        + [dma((2, half, 2))] * 2
        + [dma((2, stages[0])), dma((2, stages[1])), dma((2, len(landed) + len(bulk) // 2)), dma((3, 2))]
        + [dma((2, planes))] * 2,
        compiler_params=pltpu.CompilerParams(
            collective_id=4, has_side_effects=True, vmem_limit_bytes=60 * MIB
        ),
        cost_estimate=KERNEL_COST,
        name="finish",
    )(branch, small, bias, gain, g_qkv, attended, *first, out_parts, w, x, attn, *bulk)
    return results[:6], results[6:]


def reduce_and_weights_kernel(
    count, grp_count, expert_count, part, residual, cot_own, gain, grad_logits, x_in, cot_in,
    grad_e_in, act_e_in, grad_s_in, act_s_in, out_parts, *refs
):
    refs = list(refs)

    def take(amount):
        taken = refs[:amount]
        del refs[:amount]
        return taken

    planes = grp_count // 2
    grad_residual, own_attn, small, out_near = take(4)
    outs = [take(planes) for _ in range(5)]
    landed = take(planes - 1)
    sources = (x_in, grad_e_in, cot_in, act_e_in, grad_s_in, act_s_in)
    held = take(6)
    summed, out_far, landing = take(3)
    x, grad_e, cot, act_e, grad_s, act_s = held
    to_right, to_left = take(2)
    staged, arrived = take(5), take(5)
    (
        send_sems, recv_sems, load_sems, core_send, core_recv, out_sems, plane_sems, near_sems
    ) = take(8)
    mine = lax.axis_index("grp")
    core, plane = mine % 2, mine // 2
    part_width = x.shape[1] // grp_count

    loads = [
        pltpu.make_async_copy(source, target, load_sems.at[i])
        for i, (source, target) in enumerate(zip(sources, held))
    ]
    for load in loads:
        load.start()
    size = out_far.shape[0]
    load_far = pltpu.make_async_copy(
        out_parts.at[pl.ds((count - 1) * size, size)], out_far, load_sems.at[6]
    )
    load_far.start()
    greet("ep", count)
    greet("grp", grp_count)
    pl.semaphore_wait(pltpu.get_barrier_semaphore(), count - 1 + grp_count - 1)
    ring = RingSum(count, part, summed, to_right, to_left, send_sems, recv_sems)
    ring.start()

    def near_copy(way):
        half_rows = pl.ds(way * (size // 2), size // 2)
        return pltpu.make_async_remote_copy(
            src_ref=out_far.at[half_rows],
            dst_ref=landing.at[half_rows],
            send_sem=near_sems.at[0, way],
            recv_sem=near_sems.at[1, way],
            device_id={"ep": ring.neighbours[way]},
            device_id_type=MESH,
        )

    def columns(order, side):
        member = 2 * ((plane + order) % planes) + (core if side == 0 else 1 - core)
        return pl.ds(pl.multiple_of(member * part_width, part_width), part_width)

    def products(kind, cut):
        if kind < 2:
            return [dot_tn(x[:, cut], grad_e[kind])]
        if kind == 2:
            return [dot_tn(act_e[...], cot[:, cut])]
        if kind == 3:
            return [dot_tn(grad_s[k], x[:, cut]) for k in range(2)]
        return [dot_tn(act_s[...], cot[:, cut])]

    def to_core(kind, place):
        return pltpu.make_async_remote_copy(
            src_ref=staged[kind],
            dst_ref=arrived[kind].at[place],
            send_sem=core_send.at[kind, place],
            recv_sem=core_recv.at[kind, place],
            device_id={"grp": mine + 1 - 2 * core},
            device_id_type=MESH,
        )

    def store(kind, place):
        return pltpu.make_async_copy(staged[kind], outs[kind][place], out_sems.at[kind, place])

    orders = list(range(1, planes)) + [0]
    needs = ((0, 1), (), (2, 3), (4,), (5,))
    plane_copies = PlaneCopies(list(zip(outs[0][: planes - 1], landed)), planes, plane_sems)
    ring_step = 1
    number = 0
    for place, order in enumerate(orders):
        for side in (1, 0):
            for kind in range(5):
                if side == 1 and place == 0:
                    for i in needs[kind]:
                        loads[i].wait()
                pieces = products(kind, columns(order, side))
                if side == 1:
                    if place and kind:
                        store(kind, place - 1).wait()
                else:
                    to_core(kind, place).wait_recv()
                    to_core(kind, place).wait_send()
                for k, piece in enumerate(pieces):
                    whole = (k,) if len(pieces) > 1 else (Ellipsis,)
                    if side == 0:
                        piece = piece + arrived[kind][(place, *whole)].astype(F32)
                    staged[kind][whole] = piece.astype(BF16)
                if side == 1:
                    to_core(kind, place).start()
                else:
                    store(kind, place).start()
                if side == 0 and kind == 1 and order:
                    store(0, place).wait()
                    plane_copies.copies[place].start()
                number += 1
                if number % 5 == 2:
                    if ring_step < count // 2:
                        ring.advance(ring_step)
                    if ring_step == count // 2 - 1:
                        load_far.wait()
                        near_copy(0).start()
                        near_copy(1).start()
                    ring_step += 1
                if number == 5:
                    rows = dot_tn(grad_logits[:, :LANES], x[...])
                    rows = rows + dot_tn(grad_logits[:, LANES:], x[...])
                    small[: expert_count + 1, :] = rows[: expert_count + 1, :]
    ring.last()
    normal, factor = norm_of(residual[...])
    total = summed[...]
    own = cot_own[...].astype(F32) + norm_back(total, normal, factor, gain[...])
    grad_residual[...] = own
    own_attn[...] = own.astype(BF16)
    small[expert_count + 1 : expert_count + 2, :] = jnp.sum(total * normal, 0, keepdims=True)
    small[expert_count + 2 :, :] = jnp.zeros((1, small.shape[1]), F32)
    for way in range(2):
        near_copy(way).wait()
    out_near[...] = landing[...]
    for kind in range(5):
        store(kind, planes - 1).wait()
    ring.finish()
    plane_copies.finish()


def reduce_and_weights(
    count, grp_count, expert_count, part, residual, cot_own, gain, grad_logits, x, cot, grad_e,
    act_e, grad_s, act_s, out_parts,
):
    tokens, width = part.shape
    size, half, planes = tokens // count, count // 2, grp_count // 2
    part_width = width // grp_count
    wide, narrow = act_e.shape[1], act_s.shape[1]
    shapes = [
        (part_width, wide), (part_width, wide), (wide, part_width), (2, narrow, part_width),
        (narrow, part_width),
    ]
    anywhere = pl.BlockSpec(memory_space=pl.ANY)
    whole = pl.BlockSpec(memory_space=pltpu.VMEM)
    shape = jax.ShapeDtypeStruct
    dma = pltpu.SemaphoreType.DMA
    rows = pl.pallas_call(
        functools.partial(reduce_and_weights_kernel, count, grp_count, expert_count),
        in_specs=[whole] * 5 + [anywhere] * 7,
        out_specs=[whole] * 4 + [anywhere] * (6 * planes - 1),
        out_shape=[
            shape((size, width), F32),
            shape((size, width), BF16),
            shape((expert_count + 3, width), F32),
            shape((size, width), BF16),
        ]
        + [shape(dims, BF16) for dims in shapes for _ in range(planes)]
        + [shape(shapes[0], BF16)] * (planes - 1),
        scratch_shapes=[
            pltpu.VMEM(value.shape, BF16) for value in (x, grad_e, cot, act_e, grad_s, act_s)
        ]
        + [pltpu.VMEM((size, width), F32)]
        + [pltpu.VMEM((size, width), BF16)] * 2
        + [pltpu.VMEM((half, size, width), BF16)] * 2
        + [pltpu.VMEM(dims, BF16) for dims in shapes]
        + [pltpu.VMEM((planes, *dims), BF16) for dims in shapes]
        + [dma((half, 2)), dma((half, 2)), dma((7,))]
        + [dma((5, planes))] * 3
        + [dma((2, max(planes - 1, 1))), dma((2, 2))],
        compiler_params=pltpu.CompilerParams(
            collective_id=3, has_side_effects=True, vmem_limit_bytes=62 * MIB
        ),
        cost_estimate=KERNEL_COST,
        name="reduce_and_weights",
    )(part, residual, cot_own, gain, grad_logits, x, cot, grad_e, act_e, grad_s, act_s, out_parts)
    rows, slices = rows[:4], list(rows[4:])
    groups = [slices[i * planes : (i + 1) * planes] for i in range(5)]
    passed, own = [group[:-1] for group in groups], [group[-1] for group in groups]
    return (*rows, passed, own, slices[5 * planes :])


def tiles_of(width):
    tiles, start = [], 0
    while width - start > 384:
        tiles.append((start, 256))
        start += 256
    tiles.append((start, width - start))
    return tiles


def experts_kernel(
    count, expert_count, x_own, cot_own, routes, routes_w, gate_up_e, down_e, gate_up_s, down_s,
    act_e_out, grad_e_out, act_s_out, grad_s_out, part_out, branch_out, logits_out, x_out,
    cot_out,
    xs, cots, gate_e, up_e, held_e, gate_s, up_s, held_s, act_e, grad_e, act_s, grad_s, part,
    branch, logits_held, x_send, x_recv, cot_send, cot_recv, weight_sems, out_sems, x_sems,
):
    half = count // 2
    size = x_own.shape[0]
    rows = 2 * size
    ring_x = KernelRing(xs, count, size, x_send, x_recv)
    ring_cot = KernelRing(cots, count, size, cot_send, cot_recv)

    barrier = pltpu.get_barrier_semaphore()
    for neighbour in (ring_x.left, ring_x.right):
        pl.semaphore_signal(barrier, inc=1, device_id={"ep": neighbour}, device_id_type=MESH)
    loads = [
        pltpu.make_async_copy(source, target, weight_sems.at[i])
        for i, (source, target) in enumerate(
            [
                (gate_up_e.at[0, 0], gate_e),
                (gate_up_e.at[0, 1], up_e),
                (down_e.at[0], held_e),
                (gate_up_s.at[0], gate_s),
                (gate_up_s.at[1], up_s),
                (down_s, held_s),
            ]
        )
    ]
    for load in loads:
        load.start()
    xs[ring_x.own(), :] = x_own[...]
    cots[ring_x.own(), :] = cot_own[...]
    pl.semaphore_wait(barrier, 2)
    ring_x.start()
    ring_cot.start()

    def stores(slot, length, here):
        cut = pl.ds(0, length)
        pieces = [
            (act_e.at[slot, cut], act_e_out.at[here]),
            (grad_e.at[slot, 0, cut], grad_e_out.at[0, here]),
            (grad_e.at[slot, 1, cut], grad_e_out.at[1, here]),
            (act_s.at[slot, cut], act_s_out.at[here]),
            (grad_s.at[slot, 0, cut], grad_s_out.at[0, here]),
            (grad_s.at[slot, 1, cut], grad_s_out.at[1, here]),
            (part.at[slot, cut], part_out.at[here]),
            (branch.at[slot, cut], branch_out.at[here]),
            (logits_held.at[slot, cut], logits_out.at[here]),
        ]
        return [
            pltpu.make_async_copy(source, target, out_sems.at[slot, k])
            for k, (source, target) in enumerate(pieces)
        ]

    def pair_stores(i):
        return stores(lax.rem(i, 2), rows, rows_at(i, rows))

    own_rows = pl.ds((count - 2) * size, size)
    far_rows = pl.ds((count - 1) * size, size)

    def store_rows(here, number):
        return [
            pltpu.make_async_copy(xs.at[here], x_out.at[here], x_sems.at[0, number]),
            pltpu.make_async_copy(cots.at[here], cot_out.at[here], x_sems.at[1, number]),
        ]

    sections = (
        (gate_e, up_e, held_e, act_e, grad_e, dot, dot_nt),
        (gate_s, up_s, held_s, act_s, grad_s, dot_nt, dot),
    )
    mine = lax.axis_index("ep")
    onehot = (lax.broadcasted_iota(jnp.int32, (1, LANES), 1) == mine).astype(F32)

    def compute(here, length, slot, blocks):
        lane = lax.broadcasted_iota(jnp.int32, (length, LANES), 1)
        inputs, cotangent = xs[here, :], cots[here, :]
        logits = dot(inputs, routes_w[...])
        routed = jnp.where(lane < expert_count, logits, NEGATIVE)
        expo = jnp.exp(routed - jnp.max(routed, -1, keepdims=True))
        probs = expo * (1.0 / jnp.sum(expo, -1, keepdims=True))
        named = jnp.concatenate(
            [routes[rows_at(slot_index(count, block), size), :] for block in blocks], 0
        )
        hits = jnp.sum(jnp.where(named == mine, 1.0, 0.0), -1, keepdims=True)
        own_prob = jnp.sum(probs * onehot, -1, keepdims=True) * hits
        share_logit = jnp.sum(jnp.where(lane == expert_count, logits, 0.0), -1, keepdims=True)
        share = 1.0 / (1.0 + jnp.exp(-share_logit))

        inner = []
        total, out_total = None, None
        for s, (gate_w, up_w, down_w, act_out, grad_out, ahead, back_dot) in enumerate(sections):
            factor = own_prob if s == 0 else share
            dots = jnp.zeros((length, 1), F32)
            for start, width in tiles_of(down_w.shape[0]):
                cut = pl.ds(start, width)
                piece = (slice(None), cut) if s == 0 else (cut, slice(None))
                gate = ahead(inputs, gate_w[piece])
                up = ahead(inputs, up_w[piece])
                grad = dot_nt(cotangent, down_w[cut, :])
                sigma = 0.5 * jnp.tanh(0.5 * gate) + 0.5
                silu = gate * sigma
                act = (silu * up).astype(BF16).astype(F32)
                dots = dots + jnp.sum(grad * act, -1, keepdims=True)
                scaled = grad * factor
                act_out[slot, :length, cut] = (act * factor).astype(BF16)
                grad_out[slot, 0, :length, cut] = (
                    scaled * up * (sigma + silu * (1.0 - sigma))
                ).astype(BF16)
                grad_out[slot, 1, :length, cut] = (scaled * silu).astype(BF16)
            inner.append(dots)
            back = back_dot(grad_out[slot, 0, :length], gate_w[...]) + back_dot(
                grad_out[slot, 1, :length], up_w[...]
            )
            total = back if total is None else total + back
            out_piece = dot(act_out[slot, :length], down_w[...])
            out_total = out_piece if out_total is None else out_total + out_piece
        branch[slot, :length] = out_total.astype(BF16)
        grad_logits = own_prob * inner[0] * (onehot - probs)
        grad_share = share * (1.0 - share) * inner[1]
        grad_logits = grad_logits + jnp.where(lane == expert_count, grad_share, 0.0)
        high = grad_logits.astype(BF16)
        low = (grad_logits - high.astype(F32)).astype(BF16)
        total = total + dot_nt(high, routes_w[...]) + dot_nt(low, routes_w[...])
        logits_held[slot, :length, :LANES] = high
        logits_held[slot, :length, LANES:] = low
        part[slot, :length] = total.astype(BF16)
        for copy in stores(slot, length, here):
            copy.start()

    def one_pair(i, carry):
        here = rows_at(i, rows)
        ring_x.arrive(i)
        ring_x.forward(i)
        ring_cot.arrive(i)
        ring_cot.forward(i)
        for copy in store_rows(here, i):
            copy.start()

        @pl.when(i == 1)
        def _():
            for copy in stores(1, size, own_rows):
                copy.wait()

        @pl.when(i >= 2)
        def _():
            for copy in pair_stores(i - 2):
                copy.wait()

        compute(here, rows, lax.rem(i, 2), [2 * i, 2 * i + 1])
        return carry

    for copy in store_rows(own_rows, half - 1):
        copy.start()
    for load in loads:
        load.wait()
    compute(own_rows, size, 1, [count - 2])
    lax.fori_loop(0, half - 1, one_pair, 0)
    ring_x.arrive(half - 1)
    ring_cot.arrive(half - 1)
    for copy in store_rows(far_rows, half):
        copy.start()
    last = (half - 1) % 2
    for copy in stores(last, rows, rows_at(half - 3, rows)):
        copy.wait()
    compute(far_rows, size, last, [count - 1])
    for i in range(half - 1):
        for copy in store_rows(rows_at(i, rows), i):
            copy.wait()
    for number, here in ((half - 1, own_rows), (half, far_rows)):
        for copy in store_rows(here, number):
            copy.wait()
    for copy in stores(1 - last, rows, rows_at(half - 2, rows)):
        copy.wait()
    for copy in stores(last, size, far_rows):
        copy.wait()
    ring_x.finish()
    ring_cot.finish()


def experts(
    count, expert_count, x_own, cot_own, routes, routes_w, gate_up_e, down_e, gate_up_s, down_s
):
    size, width = x_own.shape
    tokens, rows, half = size * count, 2 * size, count // 2
    wide, narrow = down_e.shape[1], down_s.shape[0]
    anywhere = pl.BlockSpec(memory_space=pl.ANY)
    whole = pl.BlockSpec(memory_space=pltpu.VMEM)
    shape = jax.ShapeDtypeStruct
    dma = pltpu.SemaphoreType.DMA
    return pl.pallas_call(
        functools.partial(experts_kernel, count, expert_count),
        in_specs=[whole] * 4 + [anywhere] * 4,
        out_specs=[anywhere] * 9,
        out_shape=(
            shape((tokens, wide), BF16),
            shape((2, tokens, wide), BF16),
            shape((tokens, narrow), BF16),
            shape((2, tokens, narrow), BF16),
            shape((tokens, width), BF16),
            shape((tokens, width), BF16),
            shape((tokens, 2 * LANES), BF16),
            shape((tokens, width), BF16),
            shape((tokens, width), BF16),
        ),
        scratch_shapes=[
            pltpu.VMEM((tokens, width), BF16),
            pltpu.VMEM((tokens, width), BF16),
            pltpu.VMEM((width, wide), BF16),
            pltpu.VMEM((width, wide), BF16),
            pltpu.VMEM((wide, width), BF16),
            pltpu.VMEM((narrow, width), BF16),
            pltpu.VMEM((narrow, width), BF16),
            pltpu.VMEM((narrow, width), BF16),
            pltpu.VMEM((2, rows, wide), BF16),
            pltpu.VMEM((2, 2, rows, wide), BF16),
            pltpu.VMEM((2, rows, narrow), BF16),
            pltpu.VMEM((2, 2, rows, narrow), BF16),
            pltpu.VMEM((2, rows, width), BF16),
            pltpu.VMEM((2, rows, width), BF16),
            pltpu.VMEM((2, rows, 2 * LANES), BF16),
            dma((half, 2)),
            dma((half, 2)),
            dma((half, 2)),
            dma((half, 2)),
            dma((6,)),
            dma((2, 9)),
            dma((2, half + 1)),
        ],
        compiler_params=pltpu.CompilerParams(
            collective_id=0, has_side_effects=True, vmem_limit_bytes=60 * MIB
        ),
        cost_estimate=KERNEL_COST,
        name="experts",
    )(x_own, cot_own, routes, routes_w, gate_up_e, down_e, gate_up_s, down_s)


def norm_of(values):
    factor = lax.rsqrt(jnp.mean(values * values, -1, keepdims=True) + EPS)
    return values * factor, factor


def norm_back(grad_out, normal, factor, gain):
    scaled = grad_out * gain
    return factor * (scaled - normal * jnp.mean(scaled * normal, -1, keepdims=True))


def local(
    hidden_in, segments, routes, cotangent, norm1_gain, w_qkv, b_qkv, w_out, norm2_gain, router,
    shared_gate_up, shared_down, shared_gate, expert_gate_up, expert_down,
):
    tokens_here, width = hidden_in.shape
    ep_count = lax.axis_size("ep")
    grp_count = lax.axis_size("grp")
    expert_count = router.shape[1]
    heads, qkv_dim = b_qkv.shape
    head_dim = qkv_dim // 3
    scale = 1.0 / math.sqrt(head_dim)
    slice_width = width // grp_count
    routes_w = jnp.concatenate(
        [router, shared_gate[:, None], jnp.zeros((width, LANES - 1 - expert_count), BF16)], 1
    )
    w_flat = w_qkv.reshape(width, heads * qkv_dim)
    b_flat = b_qkv.reshape(1, heads * qkv_dim)
    w_out_flat = w_out.reshape(heads * head_dim, width)

    (
        queries, key_rows, values, attended, logs, residual, normed_two, cosine, sine, starts,
        group_one, w_all,
    ) = attend_forward(
        ep_count, grp_count, hidden_in, norm1_gain, norm2_gain, w_flat, b_flat, w_out_flat,
        segments, scale,
    )

    (
        expert_act, expert_grad, shared_act, shared_grad, part, out_parts, grad_logits,
        group_two, group_cot,
    ) = experts(
        ep_count, expert_count, normed_two, cotangent, routes, routes_w,
        expert_gate_up, expert_down, jnp.swapaxes(shared_gate_up, 1, 2), shared_down,
    )

    if ep_count == 8:
        (
            grad_residual, own_attn, small, out_near, passed, sums_own, first_landed
        ) = reduce_and_weights(
            ep_count, grp_count, expert_count, part, residual, cotangent, norm2_gain[None, :],
            grad_logits, group_two, group_cot, expert_grad, expert_act, shared_grad, shared_act,
            out_parts,
        )
    else:

        def up_grad(k):
            return lambda rows, member: dot_tn(columns_of(rows, member), expert_grad[k])

        def shared_gate_up_grad(rows, member):
            columns = columns_of(rows, member)
            return jnp.stack([dot_tn(shared_grad[k], columns) for k in range(2)], 0)

        def down_grad(act):
            return lambda rows, member: dot_tn(act, columns_of(rows, member))

        sums = [
            GrpReduce(group_two, up_grad(0)),
            GrpReduce(group_two, up_grad(1)),
            GrpReduce(group_cot, down_grad(expert_act)),
            GrpReduce(group_two, shared_gate_up_grad),
            GrpReduce(group_cot, down_grad(shared_act)),
        ]
        arrived = [[item.to_partner(value) for value in item.away()] for item in sums]
        passed = [item.pass_on(values_) for item, values_ in zip(sums, arrived)]
        sums_own = [item.own() for item in sums]
        grad_normed_two = reduce_rows(ep_count, part)
        first_landed = out_near = None
        normal_two, factor_two = norm_of(residual)
        grad_residual = cotangent.astype(F32) + norm_back(
            grad_normed_two, normal_two, factor_two, norm2_gain
        )
        grad_norm2 = jnp.sum(grad_normed_two * normal_two, 0)
        own_attn = grad_residual.astype(BF16)
        rows = dot_tn(grad_logits, group_two)
        rows = rows[: expert_count + 1] + rows[LANES : LANES + expert_count + 1]
        small = jnp.concatenate([rows, grad_norm2[None], jnp.zeros((1, width), F32)], 0)
    each = grp_count // 2 - 1

    bulk = passed[1] + passed[4] + (passed[0] if first_landed is None else [])
    grad_qkv, grad_bias, grad_branch, group_attn, *landed = attend_backward(
        ep_count, grp_count, own_attn, w_all, w_flat, cosine, sine, queries, key_rows, values,
        logs, starts, scale, bulk,
    )
    from_planes = {1: landed[:each], 4: landed[each : 2 * each]}
    from_planes[0] = landed[2 * each :] if first_landed is None else first_landed

    (grad_normed_one, out_sum, small, bias_total, own_q, own_o), landed = finish(
        ep_count, grp_count, grad_branch, out_parts, small, grad_bias, norm1_gain[None, :],
        grad_qkv, attended, w_flat, group_one, group_attn, passed[3] + passed[2], out_near,
    )
    from_q, from_o, from_planes[3], from_planes[2] = [
        landed[i * each : (i + 1) * each] for i in range(4)
    ]
    layer_out = (residual + out_sum).astype(BF16)
    normal_one, factor_one = norm_of(hidden_in.astype(F32))
    grad_x = grad_residual + norm_back(grad_normed_one, normal_one, factor_one, norm1_gain)
    grad_gate, grad_up, grad_expert_down, grad_shared_gate_up, grad_shared_down = [
        add_all(own, from_planes[i]) for i, own in enumerate(sums_own)
    ]
    grad_w_qkv, grad_w_out = add_all(own_q, from_q), add_all(own_o, from_o)
    bias_total = bias_total.reshape(heads, grp_count, qkv_dim // grp_count)
    grad_b = lax.dynamic_index_in_dim(bias_total, lax.axis_index("grp"), 1, keepdims=False)

    return (
        layer_out,
        grad_x,
        small[expert_count + 2],
        grad_w_qkv.reshape(slice_width, heads, qkv_dim),
        grad_b,
        grad_w_out.reshape(heads, head_dim, slice_width),
        small[expert_count + 1],
        small[:expert_count].T,
        jnp.swapaxes(grad_shared_gate_up, 1, 2),
        grad_shared_down,
        small[expert_count],
        jnp.stack([grad_gate, grad_up], 0)[None],
        grad_expert_down[None],
    )


def solution(mesh):
    in_specs = (
        P(("grp", "ep"), None),
        P("grp"),
        P("grp", None),
        P(("grp", "ep"), None),
        P(),
        P(None, "ep", None),
        P("ep", None),
        P("ep", None, None),
        P(),
        P(),
        P(None, None, "ep"),
        P("ep", None),
        P(),
        P("ep", None, None, None),
        P("ep", None, None),
    )
    out_specs = (
        P(("grp", "ep"), None),
        P(("grp", "ep"), None),
        P(),
        P("grp", "ep", None),
        P("ep", "grp"),
        P("ep", None, "grp"),
        P(),
        P(),
        P(None, "grp", "ep"),
        P("ep", "grp"),
        P(),
        P("ep", None, "grp", None),
        P("ep", None, "grp"),
    )
    return jax.shard_map(local, mesh=mesh, in_specs=in_specs, out_specs=out_specs, check_vma=False)
```

```python
import functools
import math

import jax
import jax.numpy as jnp
from jax import lax
from jax.experimental import pallas as pl
from jax.experimental.pallas import tpu as pltpu
from jax.sharding import PartitionSpec as P

EPS = 1e-06
THETA = 1000000.0
NEGATIVE = -1e30
BF16 = jnp.bfloat16
F32 = jnp.float32
LANES = 128
MIB = 1024 * 1024
KERNEL_COST = pl.CostEstimate(flops=10**6, bytes_accessed=10**5, transcendentals=0)


def dot(lhs, rhs):
    return jnp.dot(lhs, rhs, preferred_element_type=F32)


def dot_nt(lhs, rhs):
    return lax.dot_general(lhs, rhs, (((1,), (1,)), ((), ())), preferred_element_type=F32)


def dot_tn(lhs, rhs):
    return lax.dot_general(lhs, rhs, (((0,), (0,)), ((), ())), preferred_element_type=F32)


class GrpReduce:
    def __init__(self, rows, produce):
        self.rows, self.produce = rows, produce
        self.size = lax.axis_size("grp")
        self.planes = self.size // 2
        mine = lax.axis_index("grp")
        self.core, self.plane = mine % 2, mine // 2
        self.far = [(self.plane + k) % self.planes for k in range(1, self.planes)]

    def to_partner(self, value):
        return lax.ppermute(value, "grp", [(i, i ^ 1) for i in range(self.size)])

    def away(self):
        return [
            self.produce(self.rows, 2 * plane + 1 - self.core).astype(BF16) for plane in self.far
        ]

    def pass_on(self, arrived):
        return [
            (self.produce(self.rows, 2 * plane + self.core) + value.astype(F32)).astype(BF16)
            for plane, value in zip(self.far, arrived)
        ]

    def own(self):
        away = self.produce(self.rows, 2 * self.plane + 1 - self.core).astype(BF16)
        kept = self.produce(self.rows, 2 * self.plane + self.core)
        return kept + self.to_partner(away).astype(F32)


def add_all(value, others):
    value = value.astype(F32)
    for other in others:
        value = value + other.astype(F32)
    return value


def columns_of(array, member):
    size = array.shape[1] // lax.axis_size("grp")
    return lax.dynamic_slice_in_dim(array, member * size, size, 1)


MESH = pl.DeviceIdType.MESH


def ring_places(count):
    here = lax.axis_index("ep")
    if count != 8:
        return here, lambda spot: spot
    x, z = here % 2, here // 2

    def index_at(spot):
        side = spot // 4
        return 2 * (spot + side * (7 - 2 * spot)) + side

    return z + x * (7 - 2 * z), index_at


def slot_index(count, slot):
    place, index_at = ring_places(count)
    offset = jnp.where(slot == count - 1, count // 2, (slot // 2 + 1) * (2 * (slot % 2) - 1))
    offset = jnp.where(slot == count - 2, 0, offset)
    return index_at((place + offset + count) % count)


def when(condition):
    if isinstance(condition, bool):
        return (lambda run: run()) if condition else (lambda run: None)
    return pl.when(condition)


def rows_at(slot, size):
    return pl.ds(pl.multiple_of(slot * size, size), size)


class KernelRing:
    def __init__(self, buffer, count, size, send_sems, recv_sems):
        place, index_at = ring_places(count)
        self.buffer, self.count, self.size = buffer, count, size
        self.half = count // 2
        self.send_sems, self.recv_sems = send_sems, recv_sems
        self.right = index_at((place + 1) % count)
        self.left = index_at((place + count - 1) % count)

    def own(self):
        return slice((self.count - 2) * self.size, (self.count - 1) * self.size)

    def copy(self, source, target, neighbour, step, way):
        return pltpu.make_async_remote_copy(
            src_ref=self.buffer.at[source],
            dst_ref=self.buffer.at[target],
            send_sem=self.send_sems.at[step, way],
            recv_sem=self.recv_sems.at[step, way],
            device_id={"ep": neighbour},
            device_id_type=MESH,
        )

    def sends(self, step):
        before = lax.rem(step + self.half - 1, self.half)
        copies = []
        for way, neighbour in enumerate((self.right, self.left)):
            source = jnp.where(step == 0, self.count - 2, 2 * before + way)
            copies.append(
                self.copy(
                    rows_at(source, self.size), rows_at(2 * step + way, self.size),
                    neighbour, step, way,
                )
            )
        return copies

    def last_sends(self):
        middle = self.size // 2
        copies = []
        for way, neighbour in enumerate((self.right, self.left)):
            source = (self.count - 4 + way) * self.size + way * middle
            target = (self.count - 1) * self.size + way * middle
            copies.append(
                self.copy(
                    pl.ds(source, middle), pl.ds(target, middle), neighbour, self.half - 1, way
                )
            )
        return copies

    def start(self):
        for copy in self.sends(0):
            copy.start()

    def arrive(self, i):
        @when(i < self.half - 1)
        def _():
            for copy in self.sends(i):
                copy.wait_recv()

        @when(i == self.half - 1)
        def _():
            for copy in self.last_sends():
                copy.wait_recv()

    def forward(self, i):
        @when(i < self.half - 2)
        def _():
            for copy in self.sends(i + 1):
                copy.start()

        @when(i == self.half - 2)
        def _():
            for copy in self.last_sends():
                copy.start()

    def finish(self):
        for step in range(self.half - 1):
            for copy in self.sends(step):
                copy.wait_send()
        for copy in self.last_sends():
            copy.wait_send()


class Exchange:
    def __init__(self, count, source_at, target_at, send_sems, recv_sems):
        self.count = count
        self.place, self.index_at = ring_places(count)
        self.source_at, self.target_at = source_at, target_at
        self.send_sems, self.recv_sems = send_sems, recv_sems

    def copy(self, slot):
        way = slot % 2
        far = slot // 2 + 1
        farthest = slot == self.count - 1
        offset = jnp.where(farthest, self.count // 2, far * (2 * way - 1))
        landing = jnp.where(farthest, slot, slot + 1 - 2 * way)
        return pltpu.make_async_remote_copy(
            src_ref=self.source_at(slot),
            dst_ref=self.target_at(landing),
            send_sem=self.send_sems.at[slot],
            recv_sem=self.recv_sems.at[landing],
            device_id={"ep": self.index_at((self.place + offset + self.count) % self.count)},
            device_id_type=MESH,
        )

    def arrived(self, slot):
        return pltpu.make_async_remote_copy(
            src_ref=self.source_at(slot),
            dst_ref=self.target_at(slot),
            send_sem=self.send_sems.at[slot],
            recv_sem=self.recv_sems.at[slot],
            device_id={"ep": self.index_at((self.place + 1) % self.count)},
            device_id_type=MESH,
        )

    def others(self):
        return [slot for slot in range(self.count) if slot != self.count - 2]


class PlaneCopies:
    def __init__(self, pairs, planes, sems):
        mine, size = lax.axis_index("grp"), lax.axis_size("grp")
        self.copies = []
        for i, (source, target) in enumerate(pairs):
            shift = 2 * (i % (planes - 1) + 1)
            self.copies.append(
                pltpu.make_async_remote_copy(
                    src_ref=source,
                    dst_ref=target,
                    send_sem=sems.at[0, i],
                    recv_sem=sems.at[1, i],
                    device_id={"grp": (mine + shift) % size},
                    device_id_type=MESH,
                )
            )

    def start(self, first=0, last=None):
        for copy in self.copies[first:last]:
            copy.start()

    def finish(self):
        for copy in self.copies:
            copy.wait()


def rows_ahead(length):
    return length * 2 // 3 // 16 * 16


def greet(axis, count):
    barrier = pltpu.get_barrier_semaphore()
    here = lax.axis_index(axis)
    for step in range(1, count):
        pl.semaphore_signal(
            barrier, inc=1, device_id={axis: (here + step) % count}, device_id_type=MESH
        )


def block_rows_of(count):
    return 256 if count % 256 == 0 else 128


def attend_forward_kernel(
    count, grp_count, heads, scale, hidden, first_gain, gain, w, b, segments, row_segments, w_out,
    q_out, k_out, v_out, attended_out, log_out, residual_out, normed_out, cosine, sine, row_starts,
    x_out, w_all_out, row_positions, starts, xs, w_all, received, x_send, x_recv, w_send, w_recv, plane_send, plane_recv, core_send,
    core_recv, hand_send, hand_recv, x_sems, w_sems, own_sem,
):
    size, width = hidden.shape
    half = count // 2
    rows = 2 * size
    dim = LANES
    inner_size = heads * dim
    planes = grp_count // 2
    mine = lax.axis_index("grp")
    core, plane = mine % 2, mine // 2
    part_width = width // grp_count

    own_columns = pl.ds(pl.multiple_of(mine * part_width, part_width), part_width)
    ring_x = KernelRing(xs, count, size, x_send, x_recv)
    ring_w = KernelRing(w_all.at[0], count, inner_size, w_send, w_recv)
    load = pltpu.make_async_copy(
        w_out.at[:, own_columns], w_all.at[0, ring_w.own()], own_sem.at[0]
    )
    load.start()
    greet("ep", count)
    greet("grp", grp_count)
    own_hidden = hidden[...].astype(F32)
    mean = jnp.sum(own_hidden * own_hidden, -1, keepdims=True) * (1.0 / width)
    xs[ring_x.own(), :] = (own_hidden * lax.rsqrt(mean + EPS) * first_gain[...]).astype(BF16)
    pl.semaphore_wait(pltpu.get_barrier_semaphore(), count - 1 + grp_count - 1)
    load.wait()
    ring_w.start()
    ring_x.start()

    for slot in range(count):
        row_positions[:, slot * size : (slot + 1) * size] = slot_index(
            count, slot
        ) * size + lax.broadcasted_iota(jnp.int32, (1, size), 1)
    lane = lax.broadcasted_iota(jnp.int32, (size, dim), 1)
    low_half = lane < dim // 2
    index = jnp.where(low_half, lane, lane - dim // 2).astype(F32)
    inverse = jnp.exp(index * (-2.0 * math.log(THETA) / dim))

    def tables(slot, carry):
        block = slot_index(count, slot)
        here, there = rows_at(slot, size), rows_at(block, size)
        before = jnp.where(row_segments[...] < segments[there, :], 1.0, 0.0)
        start = jnp.sum(before, -1, keepdims=True)
        starts[here, :] = start.astype(jnp.int32)
        own_row = row_segments[:, there]
        before = jnp.where(segments[...] < own_row, 1.0, 0.0)
        row_starts[:, here] = jnp.sum(before, 0, keepdims=True).astype(jnp.int32)
        position = (block * size + lax.broadcasted_iota(jnp.int32, (size, 1), 0)).astype(F32)
        angle = (position - start) * inverse
        cosine[here, :] = jnp.cos(angle)
        sine[here, :] = jnp.where(low_half, -jnp.sin(angle), jnp.sin(angle))
        return carry

    lax.fori_loop(0, count, tables, 0)

    def to_plane(step, i):
        here = rows_at(i, 2 * inner_size)
        landing = (planes - step) % planes
        return pltpu.make_async_remote_copy(
            src_ref=w_all.at[0, here],
            dst_ref=w_all.at[landing, here],
            send_sem=plane_send.at[step - 1, i],
            recv_sem=plane_recv.at[landing - 1, i],
            device_id={"grp": (mine + 2 * step) % grp_count},
            device_id_type=MESH,
        )

    def to_core(j):
        return pltpu.make_async_remote_copy(
            src_ref=w_all.at[j],
            dst_ref=w_all.at[planes + j],
            send_sem=core_send.at[j],
            recv_sem=core_recv.at[j],
            device_id={"grp": mine + 1 - 2 * core},
            device_id_type=MESH,
        )

    def store_x(i):
        here = rows_at(i, rows)
        return pltpu.make_async_copy(xs.at[here], x_out.at[here], x_sems.at[i])

    def store_w(j):
        return pltpu.make_async_copy(w_all.at[j], w_all_out.at[j], w_sems.at[j])

    def project(i, carry):
        here = rows_at(i, rows)
        ring_w.arrive(i)
        ring_w.forward(i)
        for step in range(1, planes):
            to_plane(step, i).start()
        ring_x.arrive(i)
        ring_x.forward(i)
        store_x(i).start()
        projected = dot(xs[here, :], w[...]) + b[...]
        cos, sin = cosine[here, :], sine[here, :]
        for h in range(heads):
            base = 3 * dim * h
            query = projected[:, base : base + dim]
            key = projected[:, base + dim : base + 2 * dim]
            q_out[h, here, :] = (query * cos + pltpu.roll(query, dim // 2, 1) * sin).astype(BF16)
            k_out[h, here, :] = (key * cos + pltpu.roll(key, dim // 2, 1) * sin).astype(BF16)
            v_out[h, here, :] = projected[:, base + 2 * dim : base + 3 * dim].astype(BF16)
        return carry

    lax.fori_loop(0, half, project, 0)
    to_core(0).start()
    store_w(0).start()

    exchange = Exchange(
        count,
        lambda slot: attended_out.at[rows_at(slot, size)],
        lambda slot: received.at[slot],
        hand_send,
        hand_recv,
    )

    def attend(step, carry):
        i = half - 1 - step
        here = rows_at(i, rows)
        count_up = lax.broadcasted_iota(jnp.int32, (size, 1), 0)
        own = jnp.concatenate(
            [slot_index(count, 2 * i + k) * size + count_up for k in range(2)], 0
        )
        start = starts[here, :]
        keys_at = row_positions[...]
        allowed = (keys_at <= own) & (keys_at >= start)
        for h in range(heads):
            scores = dot_nt(q_out[h, here, :], k_out[h]) * scale
            scores = jnp.where(allowed, scores, NEGATIVE)
            highest = jnp.max(scores, -1, keepdims=True)
            expo = jnp.exp(scores - highest)
            total = jnp.sum(expo, -1, keepdims=True)
            weights = (expo * (1.0 / total)).astype(BF16)
            attended_out[here, h * dim : (h + 1) * dim] = dot(weights, v_out[h]).astype(BF16)
            logs = jnp.broadcast_to(highest + jnp.log(total), (rows, LANES))
            log_out[h, :, here] = jnp.transpose(logs)[:1, :]
        exchange.copy(2 * i + 1).start()

        @pl.when(i < half - 1)
        def _():
            exchange.copy(2 * i).start()

        return carry

    lax.fori_loop(0, half, attend, 0)
    received[count - 2] = attended_out[ring_x.own(), :]
    for j in range(1, planes):
        for i in range(half):
            to_plane((planes - j) % planes, i).wait_recv()
        to_core(j).start()
        store_w(j).start()
    for slot in exchange.others():
        exchange.arrived(slot).wait_recv()
    for j in range(planes):
        to_core(j).wait_recv()
        store_w(planes + j).start()
    mixed = jnp.concatenate([received[slot] for slot in range(count)], 1)
    square = jnp.zeros((size, 1), F32)
    for j in range(grp_count):
        member = 2 * ((plane + j % planes) % planes) + (core if j < planes else 1 - core)
        columns = pl.ds(pl.multiple_of(member * part_width, part_width), part_width)
        piece = hidden[:, columns].astype(F32) + dot(mixed, w_all[j])
        residual_out[:, columns] = piece
        square = square + jnp.sum(piece * piece, -1, keepdims=True)
    factor = lax.rsqrt(square * (1.0 / width) + EPS)
    normed_out[...] = (residual_out[...] * factor * gain[...]).astype(BF16)

    for i in range(half):
        store_x(i).wait()
        for step in range(1, planes):
            to_plane(step, i).wait_send()
    for j in range(grp_count):
        store_w(j).wait()
    for j in range(planes):
        to_core(j).wait_send()
    for slot in exchange.others():
        exchange.copy(slot).wait_send()
    ring_x.finish()
    ring_w.finish()


def attend_forward(
    count, grp_count, hidden, first_gain, gain, w, b, w_out, segments, scale
):
    size, width = hidden.shape
    tokens = size * count
    heads = w.shape[1] // (3 * LANES)
    half, planes = count // 2, grp_count // 2
    anywhere = pl.BlockSpec(memory_space=pl.ANY)
    whole = pl.BlockSpec(memory_space=pltpu.VMEM)
    shape = jax.ShapeDtypeStruct
    w_all_shape = (grp_count, count * heads * LANES, width // grp_count)
    dma = pltpu.SemaphoreType.DMA
    return pl.pallas_call(
        functools.partial(attend_forward_kernel, count, grp_count, heads, scale),
        in_specs=[whole] * 7 + [anywhere],
        out_specs=[whole] * 10 + [anywhere] * 2,
        out_shape=(
            shape((heads, tokens, LANES), BF16),
            shape((heads, tokens, LANES), BF16),
            shape((heads, tokens, LANES), BF16),
            shape((tokens, heads * LANES), BF16),
            shape((heads, 1, tokens), F32),
            shape((size, width), F32),
            shape((size, width), BF16),
            shape((tokens, LANES), F32),
            shape((tokens, LANES), F32),
            shape((1, tokens), jnp.int32),
            shape((tokens, width), BF16),
            shape(w_all_shape, BF16),
        ),
        scratch_shapes=[
            pltpu.VMEM((1, tokens), jnp.int32),
            pltpu.VMEM((tokens, 1), jnp.int32),
            pltpu.VMEM((tokens, width), BF16),
            pltpu.VMEM(w_all_shape, BF16),
            pltpu.VMEM((count, size, heads * LANES), BF16),
            dma((half, 2)),
            dma((half, 2)),
            dma((half, 2)),
            dma((half, 2)),
            dma((max(planes - 1, 1), half)),
            dma((max(planes - 1, 1), half)),
            dma((planes,)),
            dma((planes,)),
            dma((count,)),
            dma((count,)),
            dma((half,)),
            dma((grp_count,)),
            dma((1,)),
        ],
        compiler_params=pltpu.CompilerParams(
            collective_id=1, has_side_effects=True, vmem_limit_bytes=56 * MIB
        ),
        cost_estimate=KERNEL_COST,
        name="attend_forward",
    )(hidden, first_gain[None, :], gain[None, :], w, b, segments[:, None], segments[None, :], w_out)


def attend_backward_kernel(
    count, grp_count, heads, scale, g_own, cosine, sine, q, k, v, row_logs, row_starts, w_all_in,
    w_in, *refs,
):
    number = (len(refs) - 20) // 2
    bulk, refs = refs[:number], refs[number:]
    g_out, bias_out, branch_out, group_out = refs[:4]
    landed = refs[4 : 4 + number]
    (
        row_positions, positions, g_att, dk, dv, outbox, gs, send_sems, recv_sems, ring_send,
        ring_recv, store_sems, plane_sems, w_all, w, w_sems,
    ) = refs[4 + number :]
    size, width = g_own.shape
    tokens = size * count
    rows = block_rows_of(tokens)
    dim = LANES
    inner_size = heads * dim
    planes = grp_count // 2
    mine = lax.axis_index("grp")
    core, plane = mine % 2, mine // 2
    part_width = width // grp_count

    ring = KernelRing(gs, count, size, ring_send, ring_recv)

    load_all = pltpu.make_async_copy(w_all_in, w_all, w_sems.at[0])
    load_w = pltpu.make_async_copy(w_in, w, w_sems.at[1])
    load_all.start()
    load_w.start()

    def store(i):
        here = rows_at(i, 2 * size)
        return pltpu.make_async_copy(gs.at[here], group_out.at[here], store_sems.at[i])

    def next_pair(i):
        ring.arrive(i)
        ring.forward(i)
        store(i).start()

    greet("ep", count)
    greet("grp", grp_count)
    gs[ring.own(), :] = g_own[...]
    pl.semaphore_wait(pltpu.get_barrier_semaphore(), count - 1 + grp_count - 1)
    pairs = list(zip(bulk, landed))
    for i in range(number - (grp_count // 2 - 1), number):
        cut = pl.ds(0, rows_ahead(bulk[i].shape[1]))
        pairs[i] = bulk[i].at[0, cut], landed[i].at[0, cut]
    plane_copies = PlaneCopies(pairs, grp_count // 2, plane_sems)
    ring.start()
    plane_copies.start()
    for slot in range(count):
        first = slot_index(count, slot) * size
        row_positions[:, slot * size : (slot + 1) * size] = first + lax.broadcasted_iota(
            jnp.int32, (1, size), 1
        )
        positions[slot * size : (slot + 1) * size, :] = first + lax.broadcasted_iota(
            jnp.int32, (size, 1), 0
        )
    load_all.wait()
    own_rows = None
    for j in range(grp_count):
        member = 2 * ((plane + j % planes) % planes) + (core if j < planes else 1 - core)
        columns = pl.ds(pl.multiple_of(member * part_width, part_width), part_width)
        piece = dot_nt(g_own[:, columns], w_all[j])
        own_rows = piece if own_rows is None else own_rows + piece
    own_rows = own_rows.astype(BF16)
    for slot in range(count):
        outbox[slot] = own_rows[:, slot * inner_size : (slot + 1) * inner_size]
    exchange = Exchange(
        count,
        lambda slot: outbox.at[slot],
        lambda slot: g_att.at[rows_at(slot, size)],
        send_sems,
        recv_sems,
    )
    for slot in exchange.others():
        exchange.copy(slot).start()
    g_att[(count - 2) * size : (count - 1) * size, :] = outbox[count - 2]
    dk[...] = jnp.zeros_like(dk)
    dv[...] = jnp.zeros_like(dv)
    next_pair(0)
    for slot in exchange.others():
        exchange.arrived(slot).wait_recv()

    def scores_back(i, carry):
        here = rows_at(i, rows)
        own, start = row_positions[:, here], row_starts[:, here]
        keys_at = positions[...]
        allowed = (keys_at <= own) & (keys_at >= start)
        cos, sin = cosine[here, :], sine[here, :]
        for h in range(heads):
            query = q[h, here, :]
            g_block = g_att[here, h * dim : (h + 1) * dim]
            scores = dot_nt(k[h], query) * scale - row_logs[h, :, here]
            weights = jnp.exp(jnp.where(allowed, scores, NEGATIVE))
            g_weights = dot_nt(v[h], g_block)
            inner = jnp.sum(weights * g_weights, 0, keepdims=True)
            g_scores = (weights * (g_weights - inner)).astype(BF16)
            g_query = dot_tn(g_scores, k[h]) * scale
            g_query = g_query * cos - pltpu.roll(g_query, dim // 2, 1) * sin
            g_out[here, 3 * dim * h : 3 * dim * h + dim] = g_query.astype(BF16)
            dk[h] += dot(g_scores, query)
            dv[h] += dot(weights.astype(BF16), g_block)

        @pl.when(i == 1)
        def _():
            next_pair(1)

        return carry

    lax.fori_loop(0, tokens // rows, scores_back, 0)
    load_w.wait()
    bias_out[...] = jnp.zeros_like(bias_out)

    def finish(i, carry):
        here = rows_at(i, rows)
        cos, sin = cosine[here, :], sine[here, :]
        for h in range(heads):
            base = 3 * dim * h
            g_key = dk[h, here, :] * scale
            g_key = g_key * cos - pltpu.roll(g_key, dim // 2, 1) * sin
            g_out[here, base + dim : base + 2 * dim] = g_key.astype(BF16)
            g_out[here, base + 2 * dim : base + 3 * dim] = dv[h, here, :].astype(BF16)
        g_here = g_out[here, :]
        bias_out[...] += jnp.sum(g_here.astype(F32), 0, keepdims=True)
        branch_out[here, :] = dot_nt(g_here, w[...]).astype(BF16)
        return carry

    lax.fori_loop(0, tokens // rows, finish, 0)
    for i in range(2, count // 2):
        next_pair(i)
    for slot in exchange.others():
        exchange.copy(slot).wait_send()
    ring.finish()
    for i in range(count // 2):
        store(i).wait()
    plane_copies.finish()


def attend_backward(
    count, grp_count, g_own, w_all, w, cosine, sine, q, k, v, logs, starts, scale, bulk
):
    size, width = g_own.shape
    heads, tokens, _ = q.shape
    anywhere = pl.BlockSpec(memory_space=pl.ANY)
    whole = pl.BlockSpec(memory_space=pltpu.VMEM)
    shape = jax.ShapeDtypeStruct
    dma = pltpu.SemaphoreType.DMA
    return pl.pallas_call(
        functools.partial(attend_backward_kernel, count, grp_count, heads, scale),
        in_specs=[whole] * 8 + [anywhere] * (2 + len(bulk)),
        out_specs=[whole] * 3 + [anywhere] * (1 + len(bulk)),
        out_shape=(
            shape((tokens, 3 * LANES * heads), BF16),
            shape((1, 3 * LANES * heads), F32),
            shape((tokens, width), BF16),
            shape((tokens, width), BF16),
            *[shape(value.shape, value.dtype) for value in bulk],
        ),
        scratch_shapes=[
            pltpu.VMEM((1, tokens), jnp.int32),
            pltpu.VMEM((tokens, 1), jnp.int32),
            pltpu.VMEM((tokens, heads * LANES), BF16),
            pltpu.VMEM((heads, tokens, LANES), F32),
            pltpu.VMEM((heads, tokens, LANES), F32),
            pltpu.VMEM((count, size, heads * LANES), BF16),
            pltpu.VMEM((tokens, width), BF16),
            dma((count,)),
            dma((count,)),
            dma((count // 2, 2)),
            dma((count // 2, 2)),
            dma((count // 2,)),
            dma((2, max(len(bulk), 1))),
            pltpu.VMEM(w_all.shape, BF16),
            pltpu.VMEM(w.shape, BF16),
            dma((2,)),
        ],
        compiler_params=pltpu.CompilerParams(
            collective_id=2, has_side_effects=True, vmem_limit_bytes=56 * MIB
        ),
        cost_estimate=KERNEL_COST,
        name="attend_backward",
    )(
        g_own, cosine, sine, q, k, v, logs, starts, w_all, w, *bulk,
    )


def doubling_stages(axes):
    stages = []
    for axis in axes:
        step = lax.axis_size(axis) // 2
        while step:
            stages.append((axis, step))
            step //= 2
    return stages


class Doubling:
    def __init__(self, held, arrived, stages, sems):
        self.held, self.arrived, self.stages, self.sems = held, arrived, stages, sems
        self.place = 0

    def copy(self, k):
        axis, step = self.stages[k]
        here = lax.axis_index(axis)
        return pltpu.make_async_remote_copy(
            src_ref=self.held.at[k],
            dst_ref=self.arrived.at[k],
            send_sem=self.sems.at[0, k],
            recv_sem=self.sems.at[1, k],
            device_id={axis: here + step * (1 - 2 * (here // step % 2))},
            device_id_type=MESH,
        )

    def start(self):
        self.copy(0).start()

    def advance(self):
        k = self.place
        if k < len(self.stages):
            self.copy(k).wait_recv()
            self.held[k + 1] = self.held[k] + self.arrived[k]
            if k + 1 < len(self.stages):
                self.copy(k + 1).start()
            self.place += 1

    def finish(self):
        while self.place < len(self.stages):
            self.advance()
        for k in range(len(self.stages)):
            self.copy(k).wait_send()
        return self.held[len(self.stages)]


class RingSum:
    def __init__(self, count, part, out, to_right, to_left, send_sems, recv_sems, near=None):
        place, index_at = ring_places(count)
        self.near = near
        self.count, self.half, self.size = count, count // 2, out.shape[0]
        self.part, self.out, self.held = part, out, (to_right, to_left)
        self.send_sems, self.recv_sems = send_sems, recv_sems
        self.neighbours = (
            index_at((place + 1) % count), index_at((place + count - 1) % count)
        )

    def copy(self, step, way):
        held, middle = self.held[way], self.size // 2
        if step == 0:
            source = self.part.at[pl.ds((self.count - 1) * self.size + way * middle, middle)]
            target = held.at[0, pl.ds(way * middle, middle)]
        else:
            source, target = held.at[step - 1], held.at[step]
        return pltpu.make_async_remote_copy(
            src_ref=source,
            dst_ref=target,
            send_sem=self.send_sems.at[step, way],
            recv_sem=self.recv_sems.at[step, way],
            device_id={"ep": self.neighbours[way]},
            device_id_type=MESH,
        )

    def start(self):
        if self.near is None:
            for way in range(2):
                self.copy(0, way).start()
        else:
            self.advance(1)

    def advance(self, step):
        middle, part = self.size // 2, self.part
        for way in range(2):
            held = self.held[way]
            first = (2 * (self.half - step) - 1 - way) * self.size
            if step > 1 or self.near is None:
                self.copy(step - 1, way).wait_recv()
            if step == 1:
                here = slice(way * middle, (way + 1) * middle)
                rest = slice((1 - way) * middle, (2 - way) * middle)
                own = part[first + way * middle : first + (way + 1) * middle, :]
                before = held[0, here] if self.near is None else self.near[here, :]
                held[0, here] = (own.astype(F32) + before.astype(F32)).astype(BF16)
                held[0, rest] = part[first + (1 - way) * middle : first + (2 - way) * middle, :]
            else:
                own = part[first : first + self.size, :]
                held[step - 1] = (own.astype(F32) + held[step - 1].astype(F32)).astype(BF16)
            self.copy(step, way).start()

    def last(self):
        own = self.part[(self.count - 2) * self.size : (self.count - 1) * self.size, :]
        total = own.astype(F32)
        for way in range(2):
            self.copy(self.half - 1, way).wait_recv()
            total = total + self.held[way][self.half - 1].astype(F32)
        self.out[...] = total

    def finish(self):
        for step in range(0 if self.near is None else 1, self.half):
            for way in range(2):
                self.copy(step, way).wait_send()


def reduce_kernel(count, part, out, to_right, to_left, send_sems, recv_sems):
    greet("ep", count)
    pl.semaphore_wait(pltpu.get_barrier_semaphore(), count - 1)
    ring = RingSum(count, part, out, to_right, to_left, send_sems, recv_sems)
    ring.start()
    for step in range(1, count // 2):
        ring.advance(step)
    ring.last()
    ring.finish()


def reduce_rows(count, part):
    tokens, width = part.shape
    size, half = tokens // count, count // 2
    whole = pl.BlockSpec(memory_space=pltpu.VMEM)
    return pl.pallas_call(
        functools.partial(reduce_kernel, count),
        in_specs=[whole],
        out_specs=whole,
        out_shape=jax.ShapeDtypeStruct((size, width), F32),
        scratch_shapes=[pltpu.VMEM((half, size, width), BF16)] * 2
        + [pltpu.SemaphoreType.DMA((half, 2))] * 2,
        compiler_params=pltpu.CompilerParams(
            collective_id=3, has_side_effects=True, vmem_limit_bytes=56 * MIB
        ),
        cost_estimate=KERNEL_COST,
        name="reduce_rows",
    )(part)


def finish_kernel(
    count, grp_count, bulk_number, has_near, branch, small, bias, gain, g_qkv, attended, *refs
):
    refs = list(refs)

    def take(amount):
        taken = refs[:amount]
        del refs[:amount]
        return taken

    planes = grp_count // 2
    far_number = planes - 1
    near = take(1)[0] if has_near else None
    out_in, w_in, x_in, attn_in = take(4)
    bulk = take(bulk_number)
    branch_sum, out_sum, small_sum, bias_sum, own_q, own_o = take(6)
    landed = take(bulk_number + 2 * far_number)
    rings_held = take(4)
    out_parts, w = take(2)
    x, attn = take(2)
    away, arrived, far = take(2), take(2), take(2)
    small_held, small_arrived, bias_held, bias_arrived = take(4)
    (
        send_sems, recv_sems, small_sems, bias_sems, plane_sems, load_sems, core_send, core_recv
    ) = take(8)
    mine = lax.axis_index("grp")
    core, plane = mine % 2, mine // 2
    part_width = x.shape[2]
    orders = list(range(1, planes)) + [0]
    units = [(side, place) for side in (1, 0) for place in range(planes)]

    def columns(unit):
        side, place = units[unit]
        member = 2 * ((plane + orders[place]) % planes) + (core if side == 0 else 1 - core)
        return pl.ds(pl.multiple_of(member * part_width, part_width), part_width)

    def loads(unit):
        slot = unit % 2
        return [
            pltpu.make_async_copy(
                source.at[:, columns(unit)], target.at[slot], load_sems.at[i, slot]
            )
            for i, (source, target) in enumerate(((x_in, x), (attn_in, attn)))
        ]

    load_out = pltpu.make_async_copy(out_in, out_parts, load_sems.at[2, 0])
    load_w = pltpu.make_async_copy(w_in, w, load_sems.at[2, 1])
    load_out.start()
    for unit in range(2):
        for load in loads(unit):
            load.start()
    load_w.start()
    greet("ep", count)
    greet("grp", grp_count)
    small_held[0] = small[...]
    bias_held[0] = bias[...]
    pl.semaphore_wait(pltpu.get_barrier_semaphore(), count - 1 + grp_count - 1)
    rings = [
        RingSum(
            count, part, out, rings_held[2 * a], rings_held[2 * a + 1], send_sems.at[a],
            recv_sems.at[a], first,
        )
        for a, (part, out, first) in enumerate(
            ((branch, branch_sum, None), (out_parts, out_sum, near))
        )
    ]
    rings[0].start()
    load_out.wait()
    rings[1].start()
    sums = [
        Doubling(small_held, small_arrived, doubling_stages(("grp", "ep")), small_sems),
        Doubling(bias_held, bias_arrived, doubling_stages(("grp",)), bias_sems),
    ]
    sums[1].start()
    halves = bulk_number // 2
    sources = [bulk[i].at[1] for i in range(halves)]
    targets = [landed[2 * far_number + i].at[1] for i in range(halves)]
    for kind in range(2):
        for place in range(far_number):
            sources.append(far[kind].at[place])
            targets.append(landed[kind * far_number + place])
    length = bulk[0].shape[1]
    ahead = rows_ahead(length)
    rest = pl.ds(ahead, length - ahead)
    sources += [bulk[i].at[0, rest] for i in range(halves)] + bulk[halves:]
    targets += [landed[2 * far_number + i].at[0, rest] for i in range(halves)]
    targets += landed[2 * far_number + halves :]
    far_copies = PlaneCopies(list(zip(sources, targets)), planes, plane_sems)
    far_copies.start(0, halves)

    def to_core(kind, place):
        return pltpu.make_async_remote_copy(
            src_ref=away[kind].at[place],
            dst_ref=arrived[kind].at[place],
            send_sem=core_send.at[kind, place],
            recv_sem=core_recv.at[kind, place],
            device_id={"grp": mine + 1 - 2 * core},
            device_id_type=MESH,
        )

    load_w.wait()
    for unit, (side, place) in enumerate(units):
        cut, slot = columns(unit), unit % 2
        for load in loads(unit):
            load.wait()
        q_piece = dot_tn(x[slot], g_qkv[...])
        inner = jnp.sum(q_piece * w[cut, :].astype(F32), -1, keepdims=True)
        inner = jnp.transpose(jnp.broadcast_to(inner, (part_width, LANES)))[:1, :]
        small_held[0, small.shape[0] - 1 :, cut] = inner / gain[:, cut]
        o_piece = dot_tn(attended[...], attn[slot])
        for kind, piece in enumerate((q_piece, o_piece)):
            if side == 1:
                away[kind][place] = piece.astype(BF16)
                to_core(kind, place).start()
            else:
                to_core(kind, place).wait_recv()
                piece = piece + arrived[kind][place].astype(F32)
                if orders[place]:
                    far[kind][place] = piece.astype(BF16)
                else:
                    (own_q, own_o)[kind][...] = piece
        if unit + 2 < len(units):
            for load in loads(unit + 2):
                load.start()
    sums[0].start()
    far_copies.start(halves)
    for step in range(1, count // 2):
        for a, ring in enumerate(rings):
            if step > 1 or ring.near is None:
                ring.advance(step)
            if a or step == 1:
                for item in sums:
                    item.advance()
    for ring in rings:
        ring.last()
    small_sum[...] = sums[0].finish()
    bias_sum[...] = sums[1].finish()
    for ring in rings:
        ring.finish()
    for kind in range(2):
        for place in range(planes):
            to_core(kind, place).wait_send()
    far_copies.finish()


def finish(
    count, grp_count, branch, out_parts, small, bias, gain, g_qkv, attended, w, x, attn, bulk,
    near,
):
    tokens, width = branch.shape
    size, half, planes = tokens // count, count // 2, grp_count // 2
    part_width = width // grp_count
    q_shape, o_shape = (part_width, g_qkv.shape[1]), (attended.shape[1], part_width)
    stages = len(doubling_stages(("grp", "ep"))), len(doubling_stages(("grp",)))
    anywhere = pl.BlockSpec(memory_space=pl.ANY)
    whole = pl.BlockSpec(memory_space=pltpu.VMEM)
    shape = jax.ShapeDtypeStruct
    dma = pltpu.SemaphoreType.DMA
    first = [] if near is None else [near]
    landed = [shape(dims, BF16) for dims in (q_shape, o_shape) for _ in range(planes - 1)]
    landed += [shape(value.shape, value.dtype) for value in bulk]
    results = pl.pallas_call(
        functools.partial(finish_kernel, count, grp_count, len(bulk), bool(first)),
        in_specs=[whole] * (6 + len(first)) + [anywhere] * (4 + len(bulk)),
        out_specs=[whole] * 6 + [anywhere] * len(landed),
        out_shape=[
            shape((size, width), F32),
            shape((size, width), F32),
            shape(small.shape, F32),
            shape(bias.shape, F32),
            shape(q_shape, F32),
            shape(o_shape, F32),
            *landed,
        ],
        scratch_shapes=[pltpu.VMEM((half, size, width), BF16)] * 4
        + [pltpu.VMEM((tokens, width), BF16), pltpu.VMEM(w.shape, BF16)]
        + [pltpu.VMEM((2, tokens, part_width), BF16)] * 2
        + [pltpu.VMEM((planes, *dims), BF16) for dims in (q_shape, o_shape)] * 2
        + [pltpu.VMEM((max(planes - 1, 1), *dims), BF16) for dims in (q_shape, o_shape)]
        + [
            pltpu.VMEM((stages[0] + 1, *small.shape), F32),
            pltpu.VMEM((stages[0], *small.shape), F32),
            pltpu.VMEM((stages[1] + 1, *bias.shape), F32),
            pltpu.VMEM((stages[1], *bias.shape), F32),
        ]
        + [dma((2, half, 2))] * 2
        + [dma((2, stages[0])), dma((2, stages[1])), dma((2, len(landed) + len(bulk) // 2)), dma((3, 2))]
        + [dma((2, planes))] * 2,
        compiler_params=pltpu.CompilerParams(
            collective_id=4, has_side_effects=True, vmem_limit_bytes=60 * MIB
        ),
        cost_estimate=KERNEL_COST,
        name="finish",
    )(branch, small, bias, gain, g_qkv, attended, *first, out_parts, w, x, attn, *bulk)
    return results[:6], results[6:]


def reduce_and_weights_kernel(
    count, grp_count, expert_count, part, residual, cot_own, gain, grad_logits, x_in, cot_in,
    grad_e_in, act_e_in, grad_s_in, act_s_in, out_parts, *refs
):
    refs = list(refs)

    def take(amount):
        taken = refs[:amount]
        del refs[:amount]
        return taken

    planes = grp_count // 2
    grad_residual, own_attn, small, out_near = take(4)
    outs = [take(planes) for _ in range(5)]
    landed = take(planes - 1)
    sources = (x_in, grad_e_in, cot_in, act_e_in, grad_s_in, act_s_in)
    held = take(6)
    summed, out_far, landing = take(3)
    x, grad_e, cot, act_e, grad_s, act_s = held
    to_right, to_left = take(2)
    staged, arrived = take(5), take(5)
    (
        send_sems, recv_sems, load_sems, core_send, core_recv, out_sems, plane_sems, near_sems
    ) = take(8)
    mine = lax.axis_index("grp")
    core, plane = mine % 2, mine // 2
    part_width = x.shape[1] // grp_count

    loads = [
        pltpu.make_async_copy(source, target, load_sems.at[i])
        for i, (source, target) in enumerate(zip(sources, held))
    ]
    for load in loads:
        load.start()
    size = out_far.shape[0]
    load_far = pltpu.make_async_copy(
        out_parts.at[pl.ds((count - 1) * size, size)], out_far, load_sems.at[6]
    )
    load_far.start()
    greet("ep", count)
    greet("grp", grp_count)
    pl.semaphore_wait(pltpu.get_barrier_semaphore(), count - 1 + grp_count - 1)
    ring = RingSum(count, part, summed, to_right, to_left, send_sems, recv_sems)
    ring.start()

    def near_copy(way):
        half_rows = pl.ds(way * (size // 2), size // 2)
        return pltpu.make_async_remote_copy(
            src_ref=out_far.at[half_rows],
            dst_ref=landing.at[half_rows],
            send_sem=near_sems.at[0, way],
            recv_sem=near_sems.at[1, way],
            device_id={"ep": ring.neighbours[way]},
            device_id_type=MESH,
        )

    def columns(order, side):
        member = 2 * ((plane + order) % planes) + (core if side == 0 else 1 - core)
        return pl.ds(pl.multiple_of(member * part_width, part_width), part_width)

    def products(kind, cut):
        if kind < 2:
            return [dot_tn(x[:, cut], grad_e[kind])]
        if kind == 2:
            return [dot_tn(act_e[...], cot[:, cut])]
        if kind == 3:
            return [dot_tn(grad_s[k], x[:, cut]) for k in range(2)]
        return [dot_tn(act_s[...], cot[:, cut])]

    def to_core(kind, place):
        return pltpu.make_async_remote_copy(
            src_ref=staged[kind],
            dst_ref=arrived[kind].at[place],
            send_sem=core_send.at[kind, place],
            recv_sem=core_recv.at[kind, place],
            device_id={"grp": mine + 1 - 2 * core},
            device_id_type=MESH,
        )

    def store(kind, place):
        return pltpu.make_async_copy(staged[kind], outs[kind][place], out_sems.at[kind, place])

    orders = list(range(1, planes)) + [0]
    needs = ((0, 1), (), (2, 3), (4,), (5,))
    plane_copies = PlaneCopies(list(zip(outs[0][: planes - 1], landed)), planes, plane_sems)
    ring_step = 1
    number = 0
    for place, order in enumerate(orders):
        for side in (1, 0):
            for kind in range(5):
                if side == 1 and place == 0:
                    for i in needs[kind]:
                        loads[i].wait()
                pieces = products(kind, columns(order, side))
                if side == 1:
                    if place and kind:
                        store(kind, place - 1).wait()
                else:
                    to_core(kind, place).wait_recv()
                    to_core(kind, place).wait_send()
                for k, piece in enumerate(pieces):
                    whole = (k,) if len(pieces) > 1 else (Ellipsis,)
                    if side == 0:
                        piece = piece + arrived[kind][(place, *whole)].astype(F32)
                    staged[kind][whole] = piece.astype(BF16)
                if side == 1:
                    to_core(kind, place).start()
                else:
                    store(kind, place).start()
                if side == 0 and kind == 1 and order:
                    store(0, place).wait()
                    plane_copies.copies[place].start()
                number += 1
                if number % 5 == 2:
                    if ring_step < count // 2:
                        ring.advance(ring_step)
                    if ring_step == count // 2 - 1:
                        load_far.wait()
                        near_copy(0).start()
                        near_copy(1).start()
                    ring_step += 1
                if number == 5:
                    rows = dot_tn(grad_logits[:, :LANES], x[...])
                    rows = rows + dot_tn(grad_logits[:, LANES:], x[...])
                    small[: expert_count + 1, :] = rows[: expert_count + 1, :]
    ring.last()
    normal, factor = norm_of(residual[...])
    total = summed[...]
    own = cot_own[...].astype(F32) + norm_back(total, normal, factor, gain[...])
    grad_residual[...] = own
    own_attn[...] = own.astype(BF16)
    small[expert_count + 1 : expert_count + 2, :] = jnp.sum(total * normal, 0, keepdims=True)
    small[expert_count + 2 :, :] = jnp.zeros((1, small.shape[1]), F32)
    for way in range(2):
        near_copy(way).wait()
    out_near[...] = landing[...]
    for kind in range(5):
        store(kind, planes - 1).wait()
    ring.finish()
    plane_copies.finish()


def reduce_and_weights(
    count, grp_count, expert_count, part, residual, cot_own, gain, grad_logits, x, cot, grad_e,
    act_e, grad_s, act_s, out_parts,
):
    tokens, width = part.shape
    size, half, planes = tokens // count, count // 2, grp_count // 2
    part_width = width // grp_count
    wide, narrow = act_e.shape[1], act_s.shape[1]
    shapes = [
        (part_width, wide), (part_width, wide), (wide, part_width), (2, narrow, part_width),
        (narrow, part_width),
    ]
    anywhere = pl.BlockSpec(memory_space=pl.ANY)
    whole = pl.BlockSpec(memory_space=pltpu.VMEM)
    shape = jax.ShapeDtypeStruct
    dma = pltpu.SemaphoreType.DMA
    rows = pl.pallas_call(
        functools.partial(reduce_and_weights_kernel, count, grp_count, expert_count),
        in_specs=[whole] * 5 + [anywhere] * 7,
        out_specs=[whole] * 4 + [anywhere] * (6 * planes - 1),
        out_shape=[
            shape((size, width), F32),
            shape((size, width), BF16),
            shape((expert_count + 3, width), F32),
            shape((size, width), BF16),
        ]
        + [shape(dims, BF16) for dims in shapes for _ in range(planes)]
        + [shape(shapes[0], BF16)] * (planes - 1),
        scratch_shapes=[
            pltpu.VMEM(value.shape, BF16) for value in (x, grad_e, cot, act_e, grad_s, act_s)
        ]
        + [pltpu.VMEM((size, width), F32)]
        + [pltpu.VMEM((size, width), BF16)] * 2
        + [pltpu.VMEM((half, size, width), BF16)] * 2
        + [pltpu.VMEM(dims, BF16) for dims in shapes]
        + [pltpu.VMEM((planes, *dims), BF16) for dims in shapes]
        + [dma((half, 2)), dma((half, 2)), dma((7,))]
        + [dma((5, planes))] * 3
        + [dma((2, max(planes - 1, 1))), dma((2, 2))],
        compiler_params=pltpu.CompilerParams(
            collective_id=3, has_side_effects=True, vmem_limit_bytes=62 * MIB
        ),
        cost_estimate=KERNEL_COST,
        name="reduce_and_weights",
    )(part, residual, cot_own, gain, grad_logits, x, cot, grad_e, act_e, grad_s, act_s, out_parts)
    rows, slices = rows[:4], list(rows[4:])
    groups = [slices[i * planes : (i + 1) * planes] for i in range(5)]
    passed, own = [group[:-1] for group in groups], [group[-1] for group in groups]
    return (*rows, passed, own, slices[5 * planes :])


def tiles_of(width):
    tiles, start = [], 0
    while width - start > 384:
        tiles.append((start, 256))
        start += 256
    tiles.append((start, width - start))
    return tiles


def experts_kernel(
    count, expert_count, x_own, cot_own, routes, routes_w, gate_up_e, down_e, gate_up_s, down_s,
    act_e_out, grad_e_out, act_s_out, grad_s_out, part_out, branch_out, logits_out, x_out,
    cot_out,
    xs, cots, gate_e, up_e, held_e, gate_s, up_s, held_s, act_e, grad_e, act_s, grad_s, part,
    branch, logits_held, x_send, x_recv, cot_send, cot_recv, weight_sems, out_sems, x_sems,
):
    half = count // 2
    size = x_own.shape[0]
    rows = 2 * size
    ring_x = KernelRing(xs, count, size, x_send, x_recv)
    ring_cot = KernelRing(cots, count, size, cot_send, cot_recv)

    barrier = pltpu.get_barrier_semaphore()
    for neighbour in (ring_x.left, ring_x.right):
        pl.semaphore_signal(barrier, inc=1, device_id={"ep": neighbour}, device_id_type=MESH)
    loads = [
        pltpu.make_async_copy(source, target, weight_sems.at[i])
        for i, (source, target) in enumerate(
            [
                (gate_up_e.at[0, 0], gate_e),
                (gate_up_e.at[0, 1], up_e),
                (down_e.at[0], held_e),
                (gate_up_s.at[0], gate_s),
                (gate_up_s.at[1], up_s),
                (down_s, held_s),
            ]
        )
    ]
    for load in loads:
        load.start()
    xs[ring_x.own(), :] = x_own[...]
    cots[ring_x.own(), :] = cot_own[...]
    pl.semaphore_wait(barrier, 2)
    ring_x.start()
    ring_cot.start()

    def stores(slot, length, here):
        cut = pl.ds(0, length)
        pieces = [
            (act_e.at[slot, cut], act_e_out.at[here]),
            (grad_e.at[slot, 0, cut], grad_e_out.at[0, here]),
            (grad_e.at[slot, 1, cut], grad_e_out.at[1, here]),
            (act_s.at[slot, cut], act_s_out.at[here]),
            (grad_s.at[slot, 0, cut], grad_s_out.at[0, here]),
            (grad_s.at[slot, 1, cut], grad_s_out.at[1, here]),
            (part.at[slot, cut], part_out.at[here]),
            (branch.at[slot, cut], branch_out.at[here]),
            (logits_held.at[slot, cut], logits_out.at[here]),
        ]
        return [
            pltpu.make_async_copy(source, target, out_sems.at[slot, k])
            for k, (source, target) in enumerate(pieces)
        ]

    def pair_stores(i):
        return stores(lax.rem(i, 2), rows, rows_at(i, rows))

    own_rows = pl.ds((count - 2) * size, size)
    far_rows = pl.ds((count - 1) * size, size)

    def store_rows(here, number):
        return [
            pltpu.make_async_copy(xs.at[here], x_out.at[here], x_sems.at[0, number]),
            pltpu.make_async_copy(cots.at[here], cot_out.at[here], x_sems.at[1, number]),
        ]

    sections = (
        (gate_e, up_e, held_e, act_e, grad_e, dot, dot_nt),
        (gate_s, up_s, held_s, act_s, grad_s, dot_nt, dot),
    )
    mine = lax.axis_index("ep")
    onehot = (lax.broadcasted_iota(jnp.int32, (1, LANES), 1) == mine).astype(F32)

    def compute(here, length, slot, blocks):
        lane = lax.broadcasted_iota(jnp.int32, (length, LANES), 1)
        inputs, cotangent = xs[here, :], cots[here, :]
        logits = dot(inputs, routes_w[...])
        routed = jnp.where(lane < expert_count, logits, NEGATIVE)
        expo = jnp.exp(routed - jnp.max(routed, -1, keepdims=True))
        probs = expo * (1.0 / jnp.sum(expo, -1, keepdims=True))
        named = jnp.concatenate(
            [routes[rows_at(slot_index(count, block), size), :] for block in blocks], 0
        )
        hits = jnp.sum(jnp.where(named == mine, 1.0, 0.0), -1, keepdims=True)
        own_prob = jnp.sum(probs * onehot, -1, keepdims=True) * hits
        share_logit = jnp.sum(jnp.where(lane == expert_count, logits, 0.0), -1, keepdims=True)
        share = 1.0 / (1.0 + jnp.exp(-share_logit))

        inner = []
        total, out_total = None, None
        for s, (gate_w, up_w, down_w, act_out, grad_out, ahead, back_dot) in enumerate(sections):
            factor = own_prob if s == 0 else share
            dots = jnp.zeros((length, 1), F32)
            for start, width in tiles_of(down_w.shape[0]):
                cut = pl.ds(start, width)
                piece = (slice(None), cut) if s == 0 else (cut, slice(None))
                gate = ahead(inputs, gate_w[piece])
                up = ahead(inputs, up_w[piece])
                grad = dot_nt(cotangent, down_w[cut, :])
                sigma = 0.5 * jnp.tanh(0.5 * gate) + 0.5
                silu = gate * sigma
                act = (silu * up).astype(BF16).astype(F32)
                dots = dots + jnp.sum(grad * act, -1, keepdims=True)
                scaled = grad * factor
                act_out[slot, :length, cut] = (act * factor).astype(BF16)
                grad_out[slot, 0, :length, cut] = (
                    scaled * up * (sigma + silu * (1.0 - sigma))
                ).astype(BF16)
                grad_out[slot, 1, :length, cut] = (scaled * silu).astype(BF16)
            inner.append(dots)
            back = back_dot(grad_out[slot, 0, :length], gate_w[...]) + back_dot(
                grad_out[slot, 1, :length], up_w[...]
            )
            total = back if total is None else total + back
            out_piece = dot(act_out[slot, :length], down_w[...])
            out_total = out_piece if out_total is None else out_total + out_piece
        branch[slot, :length] = out_total.astype(BF16)
        grad_logits = own_prob * inner[0] * (onehot - probs)
        grad_share = share * (1.0 - share) * inner[1]
        grad_logits = grad_logits + jnp.where(lane == expert_count, grad_share, 0.0)
        high = grad_logits.astype(BF16)
        low = (grad_logits - high.astype(F32)).astype(BF16)
        total = total + dot_nt(high, routes_w[...]) + dot_nt(low, routes_w[...])
        logits_held[slot, :length, :LANES] = high
        logits_held[slot, :length, LANES:] = low
        part[slot, :length] = total.astype(BF16)
        for copy in stores(slot, length, here):
            copy.start()

    def one_pair(i, carry):
        here = rows_at(i, rows)
        ring_x.arrive(i)
        ring_x.forward(i)
        ring_cot.arrive(i)
        ring_cot.forward(i)
        for copy in store_rows(here, i):
            copy.start()

        @pl.when(i == 1)
        def _():
            for copy in stores(1, size, own_rows):
                copy.wait()

        @pl.when(i >= 2)
        def _():
            for copy in pair_stores(i - 2):
                copy.wait()

        compute(here, rows, lax.rem(i, 2), [2 * i, 2 * i + 1])
        return carry

    for copy in store_rows(own_rows, half - 1):
        copy.start()
    for load in loads:
        load.wait()
    compute(own_rows, size, 1, [count - 2])
    lax.fori_loop(0, half - 1, one_pair, 0)
    ring_x.arrive(half - 1)
    ring_cot.arrive(half - 1)
    for copy in store_rows(far_rows, half):
        copy.start()
    last = (half - 1) % 2
    for copy in stores(last, rows, rows_at(half - 3, rows)):
        copy.wait()
    compute(far_rows, size, last, [count - 1])
    for i in range(half - 1):
        for copy in store_rows(rows_at(i, rows), i):
            copy.wait()
    for number, here in ((half - 1, own_rows), (half, far_rows)):
        for copy in store_rows(here, number):
            copy.wait()
    for copy in stores(1 - last, rows, rows_at(half - 2, rows)):
        copy.wait()
    for copy in stores(last, size, far_rows):
        copy.wait()
    ring_x.finish()
    ring_cot.finish()


def experts(
    count, expert_count, x_own, cot_own, routes, routes_w, gate_up_e, down_e, gate_up_s, down_s
):
    size, width = x_own.shape
    tokens, rows, half = size * count, 2 * size, count // 2
    wide, narrow = down_e.shape[1], down_s.shape[0]
    anywhere = pl.BlockSpec(memory_space=pl.ANY)
    whole = pl.BlockSpec(memory_space=pltpu.VMEM)
    shape = jax.ShapeDtypeStruct
    dma = pltpu.SemaphoreType.DMA
    return pl.pallas_call(
        functools.partial(experts_kernel, count, expert_count),
        in_specs=[whole] * 4 + [anywhere] * 4,
        out_specs=[anywhere] * 9,
        out_shape=(
            shape((tokens, wide), BF16),
            shape((2, tokens, wide), BF16),
            shape((tokens, narrow), BF16),
            shape((2, tokens, narrow), BF16),
            shape((tokens, width), BF16),
            shape((tokens, width), BF16),
            shape((tokens, 2 * LANES), BF16),
            shape((tokens, width), BF16),
            shape((tokens, width), BF16),
        ),
        scratch_shapes=[
            pltpu.VMEM((tokens, width), BF16),
            pltpu.VMEM((tokens, width), BF16),
            pltpu.VMEM((width, wide), BF16),
            pltpu.VMEM((width, wide), BF16),
            pltpu.VMEM((wide, width), BF16),
            pltpu.VMEM((narrow, width), BF16),
            pltpu.VMEM((narrow, width), BF16),
            pltpu.VMEM((narrow, width), BF16),
            pltpu.VMEM((2, rows, wide), BF16),
            pltpu.VMEM((2, 2, rows, wide), BF16),
            pltpu.VMEM((2, rows, narrow), BF16),
            pltpu.VMEM((2, 2, rows, narrow), BF16),
            pltpu.VMEM((2, rows, width), BF16),
            pltpu.VMEM((2, rows, width), BF16),
            pltpu.VMEM((2, rows, 2 * LANES), BF16),
            dma((half, 2)),
            dma((half, 2)),
            dma((half, 2)),
            dma((half, 2)),
            dma((6,)),
            dma((2, 9)),
            dma((2, half + 1)),
        ],
        compiler_params=pltpu.CompilerParams(
            collective_id=0, has_side_effects=True, vmem_limit_bytes=60 * MIB
        ),
        cost_estimate=KERNEL_COST,
        name="experts",
    )(x_own, cot_own, routes, routes_w, gate_up_e, down_e, gate_up_s, down_s)


def norm_of(values):
    factor = lax.rsqrt(jnp.mean(values * values, -1, keepdims=True) + EPS)
    return values * factor, factor


def norm_back(grad_out, normal, factor, gain):
    scaled = grad_out * gain
    return factor * (scaled - normal * jnp.mean(scaled * normal, -1, keepdims=True))


def local(
    hidden_in, segments, routes, cotangent, norm1_gain, w_qkv, b_qkv, w_out, norm2_gain, router,
    shared_gate_up, shared_down, shared_gate, expert_gate_up, expert_down,
):
    tokens_here, width = hidden_in.shape
    ep_count = lax.axis_size("ep")
    grp_count = lax.axis_size("grp")
    expert_count = router.shape[1]
    heads, qkv_dim = b_qkv.shape
    head_dim = qkv_dim // 3
    scale = 1.0 / math.sqrt(head_dim)
    slice_width = width // grp_count
    routes_w = jnp.concatenate(
        [router, shared_gate[:, None], jnp.zeros((width, LANES - 1 - expert_count), BF16)], 1
    )
    w_flat = w_qkv.reshape(width, heads * qkv_dim)
    b_flat = b_qkv.reshape(1, heads * qkv_dim)
    w_out_flat = w_out.reshape(heads * head_dim, width)

    (
        queries, key_rows, values, attended, logs, residual, normed_two, cosine, sine, starts,
        group_one, w_all,
    ) = attend_forward(
        ep_count, grp_count, hidden_in, norm1_gain, norm2_gain, w_flat, b_flat, w_out_flat,
        segments, scale,
    )

    (
        expert_act, expert_grad, shared_act, shared_grad, part, out_parts, grad_logits,
        group_two, group_cot,
    ) = experts(
        ep_count, expert_count, normed_two, cotangent, routes, routes_w,
        expert_gate_up, expert_down, jnp.swapaxes(shared_gate_up, 1, 2), shared_down,
    )

    if ep_count == 8:
        (
            grad_residual, own_attn, small, out_near, passed, sums_own, first_landed
        ) = reduce_and_weights(
            ep_count, grp_count, expert_count, part, residual, cotangent, norm2_gain[None, :],
            grad_logits, group_two, group_cot, expert_grad, expert_act, shared_grad, shared_act,
            out_parts,
        )
    else:

        def up_grad(k):
            return lambda rows, member: dot_tn(columns_of(rows, member), expert_grad[k])

        def shared_gate_up_grad(rows, member):
            columns = columns_of(rows, member)
            return jnp.stack([dot_tn(shared_grad[k], columns) for k in range(2)], 0)

        def down_grad(act):
            return lambda rows, member: dot_tn(act, columns_of(rows, member))

        sums = [
            GrpReduce(group_two, up_grad(0)),
            GrpReduce(group_two, up_grad(1)),
            GrpReduce(group_cot, down_grad(expert_act)),
            GrpReduce(group_two, shared_gate_up_grad),
            GrpReduce(group_cot, down_grad(shared_act)),
        ]
        arrived = [[item.to_partner(value) for value in item.away()] for item in sums]
        passed = [item.pass_on(values_) for item, values_ in zip(sums, arrived)]
        sums_own = [item.own() for item in sums]
        grad_normed_two = reduce_rows(ep_count, part)
        first_landed = out_near = None
        normal_two, factor_two = norm_of(residual)
        grad_residual = cotangent.astype(F32) + norm_back(
            grad_normed_two, normal_two, factor_two, norm2_gain
        )
        grad_norm2 = jnp.sum(grad_normed_two * normal_two, 0)
        own_attn = grad_residual.astype(BF16)
        rows = dot_tn(grad_logits, group_two)
        rows = rows[: expert_count + 1] + rows[LANES : LANES + expert_count + 1]
        small = jnp.concatenate([rows, grad_norm2[None], jnp.zeros((1, width), F32)], 0)
    each = grp_count // 2 - 1

    bulk = passed[1] + passed[4] + (passed[0] if first_landed is None else []) + passed[3]
    grad_qkv, grad_bias, grad_branch, group_attn, *landed = attend_backward(
        ep_count, grp_count, own_attn, w_all, w_flat, cosine, sine, queries, key_rows, values,
        logs, starts, scale, bulk,
    )
    from_planes = {1: landed[:each], 4: landed[each : 2 * each]}
    from_planes[0] = landed[2 * each : 3 * each] if first_landed is None else first_landed
    early = landed[-each:]

    (grad_normed_one, out_sum, small, bias_total, own_q, own_o), landed = finish(
        ep_count, grp_count, grad_branch, out_parts, small, grad_bias, norm1_gain[None, :],
        grad_qkv, attended, w_flat, group_one, group_attn, passed[3] + passed[2], out_near,
    )
    from_q, from_o, from_planes[3], from_planes[2] = [
        landed[i * each : (i + 1) * each] for i in range(4)
    ]
    narrow = shared_down.shape[0]
    went = (jnp.arange(2) == 0)[:, None, None] & (
        jnp.arange(narrow) < rows_ahead(narrow)
    )[None, :, None]
    from_planes[3] = [
        jnp.where(went, before, value) for before, value in zip(early, from_planes[3])
    ]
    layer_out = (residual + out_sum).astype(BF16)
    normal_one, factor_one = norm_of(hidden_in.astype(F32))
    grad_x = grad_residual + norm_back(grad_normed_one, normal_one, factor_one, norm1_gain)
    grad_gate, grad_up, grad_expert_down, grad_shared_gate_up, grad_shared_down = [
        add_all(own, from_planes[i]) for i, own in enumerate(sums_own)
    ]
    grad_w_qkv, grad_w_out = add_all(own_q, from_q), add_all(own_o, from_o)
    bias_total = bias_total.reshape(heads, grp_count, qkv_dim // grp_count)
    grad_b = lax.dynamic_index_in_dim(bias_total, lax.axis_index("grp"), 1, keepdims=False)

    return (
        layer_out,
        grad_x,
        small[expert_count + 2],
        grad_w_qkv.reshape(slice_width, heads, qkv_dim),
        grad_b,
        grad_w_out.reshape(heads, head_dim, slice_width),
        small[expert_count + 1],
        small[:expert_count].T,
        jnp.swapaxes(grad_shared_gate_up, 1, 2),
        grad_shared_down,
        small[expert_count],
        jnp.stack([grad_gate, grad_up], 0)[None],
        grad_expert_down[None],
    )


def solution(mesh):
    in_specs = (
        P(("grp", "ep"), None),
        P("grp"),
        P("grp", None),
        P(("grp", "ep"), None),
        P(),
        P(None, "ep", None),
        P("ep", None),
        P("ep", None, None),
        P(),
        P(),
        P(None, None, "ep"),
        P("ep", None),
        P(),
        P("ep", None, None, None),
        P("ep", None, None),
    )
    out_specs = (
        P(("grp", "ep"), None),
        P(("grp", "ep"), None),
        P(),
        P("grp", "ep", None),
        P("ep", "grp"),
        P("ep", None, "grp"),
        P(),
        P(),
        P(None, "grp", "ep"),
        P("ep", "grp"),
        P(),
        P("ep", None, "grp", None),
        P("ep", None, "grp"),
    )
    return jax.shard_map(local, mesh=mesh, in_specs=in_specs, out_specs=out_specs, check_vma=False)
```
